32 devices in a mesh: img: 4 (over z), gx: 4 (over y, core), gy: 2 (over x).
Axes of the slice: x: 2, y: 2, z: 4, core: 2. Of those that a mesh axis runs over, the one named last changes fastest.
Arguments:
- magnetization: float32 [4, 3, 16, 32, 512], P('img', None, None, 'gy', 'gx'), may hold values from -1 to 1, as said below
- lower_image: int32 [4], replicated, may hold values from 0 to 2, as said below
- image_weights: float32 [3], replicated, may hold values from 0.5 to 2
- regions: int32 [16, 32, 512], P(None, 'gy', 'gx'), may hold values from 0 to 7
- anisotropy: float32 [8], replicated, may hold values from 0.5 to 4
- damping: float32 [8], replicated, may hold values from 0.05 to 0.5
Outputs:
- evolved: float32 [4, 3, 16, 32, 512], P('img', None, None, 'gy', 'gx')
The draws below stay inside these ranges and needn't reach their ends.
Inputs may be any that keep to these rules, and one draw needn't show every extreme that they name: `lower_image`: lower_image_j is j - 1 or j; it is 0 for image 0 and 2 for the last image. `magnetization`: every cell holds a unit vector, and in every cell neighbouring images make an angle under 90 degrees.
All inputs are finite; a program needn't handle non-finite values.
Results may differ from the reference program's by a relative error of at most 0.000024.
Values sent between devices are 32-bit elements; how exact they have to be, the bound alone decides.
No kernel may reach another device: no remote copies, remote signals or barrier semaphores. Data moves between devices by JAX's collectives and lax.ppermute only.
A program may use at most 64 MiB of HBM per device.

```python
import math
import jax
import jax.numpy as jnp
from jax import lax

NZ = 16
STEPS = 4
REGIONS = 8
IMAGES = 4
NX = 512
NY = 32


def draw_magnetization(key, part):
    base_key = jax.random.fold_in(key, 11)
    noise_key = jax.random.fold_in(key, 12)
    base = jax.random.normal(base_key, (3, NZ, NY, NX), jnp.float32)
    base = base * jax.lax.rsqrt(jnp.sum(base * base, axis=0, keepdims=True) + 1e-06)
    amplitude = 0.08 * (1.0 + 2.0 * jnp.arange(IMAGES, dtype=jnp.float32) / (IMAGES - 1))
    noise = jax.random.uniform(noise_key, (IMAGES, 3, NZ, NY, NX), jnp.float32, -1.0, 1.0)
    field = base[None] + amplitude[:, None, None, None, None] * noise
    return field * jax.lax.rsqrt(jnp.sum(field * field, axis=1, keepdims=True))


def draw_lower_image(key, part):
    step_back = jax.random.randint(jax.random.fold_in(key, 21), (IMAGES,), 0, 2)
    position = jnp.arange(IMAGES, dtype=jnp.int32)
    return jnp.clip(position - step_back, 0, IMAGES - 2).astype(jnp.int32)


def set_ends(values, stream_key, least, largest):
    place = [jax.random.randint(jax.random.fold_in(stream_key, axis), (), 0, length) for axis, length in enumerate(values.shape)]
    longest = values.shape.index(max(values.shape))
    neighbour = place[:longest] + [(place[longest] + 1) % values.shape[longest]] + place[longest + 1:]
    return values.at[tuple(place)].set(least).at[tuple(neighbour)].set(largest)


def setup_inputs(seed: int = 0) -> dict:
    arg_keys = jax.random.split(jax.random.key(seed), 7)
    return {
        "magnetization": draw_magnetization(jax.random.fold_in(arg_keys[6], 71), 0),
        "lower_image": draw_lower_image(jax.random.fold_in(arg_keys[6], 71), 0),
        "image_weights": jnp.clip(jnp.exp(jax.random.uniform(arg_keys[2], (IMAGES - 1,), jnp.float32, math.log(0.5), math.log(2.0))), 0.5, 2.0),
        "regions": set_ends(jax.random.randint(arg_keys[3], (NZ, NY, NX), 0, REGIONS), jax.random.fold_in(arg_keys[3], 1), 0, REGIONS - 1).astype(jnp.int32),
        "anisotropy": jnp.clip(jnp.exp(jax.random.uniform(arg_keys[4], (REGIONS,), jnp.float32, math.log(0.5), math.log(4.0))), 0.5, 4.0),
        "damping": jnp.clip(jnp.exp(jax.random.uniform(arg_keys[5], (REGIONS,), jnp.float32, math.log(0.05), math.log(0.5))), 0.05, 0.5),
    }


eps = 1e-06
time_step = 0.05

def normalize(field):
    return field * lax.rsqrt(field[..., 0, :, :, :] ** 2 + field[..., 1, :, :, :] ** 2 + field[..., 2, :, :, :] ** 2)[..., None, :, :, :]

def laplacian(field):
    plane = jnp.roll(field, 1, -1) + jnp.roll(field, -1, -1) + jnp.roll(field, 1, -2) + jnp.roll(field, -1, -2) - 4.0 * field
    upper = jnp.concatenate([field[..., 1:, :, :], field[..., -1:, :, :]], axis=-3)
    lower = jnp.concatenate([field[..., :1, :, :], field[..., :-1, :, :]], axis=-3)
    return plane + (upper + lower - 2.0 * field)

def torque_rate(field, lap, aniso, damp):
    mx, my, mz = (field[..., 0, :, :, :], field[..., 1, :, :, :], field[..., 2, :, :, :])
    hx, hy = (lap[..., 0, :, :, :], lap[..., 1, :, :, :])
    hz = lap[..., 2, :, :, :] + 2.0 * aniso * mz
    cx = my * hz - mz * hy
    cy = mz * hx - mx * hz
    cz = mx * hy - my * hx
    dx = my * cz - mz * cy
    dy = mz * cx - mx * cz
    dz = mx * cy - my * cx
    scale = -1.0 / (1.0 + damp * damp)
    return jnp.stack([scale * (cx + damp * dx), scale * (cy + damp * dy), scale * (cz + damp * dz)], axis=-4)

def evolve(field, aniso, damp):
    for step in range(STEPS):
        first = torque_rate(field, laplacian(field), aniso, damp)
        predicted = field + time_step * first
        second = torque_rate(predicted, laplacian(predicted), aniso, damp)
        field = normalize(field + 0.5 * time_step * (first + second))
    return field

def reference(magnetization, lower_image, image_weights, regions, anisotropy, damping):
    squares = lax.optimization_barrier(jnp.sum((magnetization[1:] - magnetization[:-1]) ** 2, axis=(1, 2, 3, 4)))
    lengths = jnp.concatenate([jnp.zeros((1,), jnp.float32), jnp.sqrt(squares + eps)])
    arc = jnp.cumsum(lengths)
    total = arc[-1]
    shares = jnp.concatenate([jnp.zeros((1,), jnp.float32), jnp.cumsum(image_weights)])
    target = shares / shares[-1]
    upper_image = lower_image + 1
    weight = jnp.clip((target * total - arc[lower_image]) / lengths[upper_image], -0.5, 1.5)
    weight = weight[:, None, None, None, None]
    start = normalize((1.0 - weight) * magnetization[lower_image] + weight * magnetization[upper_image])
    aniso = anisotropy[regions]
    damp = damping[regions]
    return lax.map(lambda field: evolve(field, aniso, damp), start)
```

```python
import functools

import jax
import jax.numpy as jnp
from jax import lax
from jax.experimental import pallas as pl
from jax.experimental.pallas import tpu as pltpu
from jax.sharding import PartitionSpec as P

STEPS = 4
DEPTH = 2 * STEPS

eps = 1e-06
time_step = 0.05

SUB = 8
LANES = 128
COMPS = 3


def lane_iota():
    return lax.broadcasted_iota(jnp.int32, (SUB, LANES), 1)


def sub_iota():
    return lax.broadcasted_iota(jnp.int32, (SUB, LANES), 0)


def rows_at(ny, tiles, y, t):
    return pl.ds(y + ny * t, SUB, stride=ny * tiles)


def gather_kernel(ny, tiles, lower_ref, m_ref, up_ref, down_ref, reg_ref, part_ref, near_ref, left_ref, right_ref):
    here = lax.axis_index("img")
    take_up = lower_ref[here] < here
    lane = lane_iota()

    near_ref[...] = jnp.where(take_up, up_ref[...], down_ref[...])
    diff = m_ref[...] - up_ref[...]
    total = jnp.sum(jnp.sum(diff * diff, axis=(0, 1), keepdims=True)[0], axis=1, keepdims=True)
    slot = lax.broadcasted_iota(jnp.int32, (1, LANES), 1)
    part_ref[...] = jnp.where((slot == here) & (here > 0), total, 0.0)

    for t in range(tiles):
        for c in range(2 * COMPS + 1):
            left = jnp.zeros((SUB, LANES), jnp.float32)
            right = jnp.zeros((SUB, LANES), jnp.float32)
            for y in range(ny):
                rows = rows_at(ny, tiles, y, t)
                if c < COMPS:
                    cells = m_ref[c, rows, :]
                elif c < 2 * COMPS:
                    cells = near_ref[c - COMPS, rows, :]
                else:
                    cells = reg_ref[rows, :].astype(jnp.float32)
                cells = pltpu.roll(cells, (DEPTH * (y + 1)) % LANES, 1)
                left = jnp.where(lane // DEPTH == (y + 1) % ny, cells, left)
                right = jnp.where(lane // DEPTH == y, cells, right)
            left_ref[c, t] = left
            right_ref[c, t] = right


def turn(m, h, a2, b, sc):
    mx, my, mz = m
    hx, hy, hz = h
    hz = hz + a2 * mz
    gx = hx + b * (my * hz - mz * hy)
    gy = hy + b * (mz * hx - mx * hz)
    gz = hz + b * (mx * hy - my * hx)
    return (
        sc * (my * gz - mz * gy),
        sc * (mz * gx - mx * gz),
        sc * (mx * gy - my * gx),
    )


def normal(v):
    scale = lax.rsqrt(v[0] * v[0] + v[1] * v[1] + v[2] * v[2])
    return tuple(x * scale for x in v)


def evolve_kernel(
    ny,
    tiles,
    images,
    regions,
    lower_ref,
    aniso_ref,
    damp_ref,
    sq_ref,
    share_ref,
    m_ref,
    mp_ref,
    n_ref,
    np_ref,
    reg_ref,
    regp_ref,
    left_ref,
    right_ref,
    leftp_ref,
    rightp_ref,
    out_ref,
    main,
    strip,
    edge,
    seam,
    par,
    spar,
):
    window = ny + 2 * DEPTH
    here = lax.axis_index("img")
    lane = lane_iota()
    sub = sub_iota()
    block = lane // DEPTH
    first_lane = lane == 0
    last_lane = lane == LANES - 1
    head_lane = lane % DEPTH == 0
    tail_lane = lane % DEPTH == DEPTH - 1
    top = sub == SUB - 1
    bottom = sub == 0

    lo = lower_ref[here]
    slot = lax.broadcasted_iota(jnp.int32, (1, LANES), 1)
    lengths = jnp.where((slot >= 1) & (slot < images), jnp.sqrt(sq_ref[...] + eps), 0.0)
    total = jnp.sum(lengths, axis=1, keepdims=True)
    arc = jnp.sum(jnp.where(slot <= lo, lengths, 0.0), axis=1, keepdims=True)
    gap = jnp.sum(jnp.where(slot == lo + 1, lengths, 0.0), axis=1, keepdims=True)
    share = share_ref[...]
    spot = lax.broadcasted_iota(jnp.int32, share.shape, 1)
    target = jnp.sum(jnp.where(spot < here, share, 0.0), axis=1, keepdims=True) / jnp.sum(
        share, axis=1, keepdims=True
    )
    weight = jnp.clip((target * total - arc) / gap, -0.5, 1.5)
    weight = jnp.broadcast_to(weight, (SUB, LANES))
    below = lo < here
    w_own = jnp.where(below, weight, 1.0 - weight)
    w_near = jnp.where(below, 1.0 - weight, weight)

    def params(region):
        a = jnp.full((SUB, LANES), aniso_ref[0], jnp.float32)
        d = jnp.full((SUB, LANES), damp_ref[0], jnp.float32)
        for i in range(1, regions):
            inside = region == i
            a = jnp.where(inside, aniso_ref[i], a)
            d = jnp.where(inside, damp_ref[i], d)
        return 2.0 * a, d, -time_step / (1.0 + d * d)

    def merge(old, new, k):
        mask = ((lane - (DEPTH * k + DEPTH - 1)) & (LANES - 1)) < 2
        shift = (DEPTH * (k + 1)) & (LANES - 1)
        return jnp.where(mask, pltpu.roll(new, shift, 1), old)

    zero = jnp.zeros((SUB, LANES), jnp.float32)
    zeros = tuple(zero for _ in range(COMPS * tiles))
    for g, (own, near, reg) in enumerate(((m_ref, n_ref, reg_ref), (mp_ref, np_ref, regp_ref))):

        def fill(k, edges, g=g, own=own, near=near, reg=reg):
            edges = list(edges)
            for t in range(tiles):
                rows = rows_at(ny, tiles, k, t)
                v = normal(
                    [w_own * own[c, rows, :] + w_near * near[c, rows, :] for c in range(COMPS)]
                )
                for c in range(COMPS):
                    main[0, c, g * ny + k, t] = v[c]
                    edges[c * tiles + t] = merge(edges[c * tiles + t], v[c], k)
                p = params(reg[rows, :])
                for i in range(3):
                    par[i, g * ny + k, t] = p[i]
            return tuple(edges)

        edges = lax.fori_loop(0, ny, fill, zeros)
        for c in range(COMPS):
            for t in range(tiles):
                edge[0, c, g, t] = edges[c * tiles + t]
    for side, pair in enumerate(((left_ref, leftp_ref), (right_ref, rightp_ref))):
        for g in range(2):
            for t in range(tiles):
                v = normal(
                    [w_own * pair[g][c, t] + w_near * pair[g][COMPS + c, t] for c in range(COMPS)]
                )
                for c in range(COMPS):
                    strip[0, c, side, g, t] = v[c]
                p = params(pair[g][2 * COMPS, t].astype(jnp.int32))
                for i in range(3):
                    spar[i, side, g, t] = p[i]

    def seams(state):
        for c in range(COMPS):
            for g in range(2):
                for t in range(tiles):
                    seam[state, c, g, t] = jnp.where(
                        tail_lane, strip[state, c, 0, g, t], strip[state, c, 1, g, t]
                    )

    seams(0)

    def around_z(cells, t):
        if t + 1 < tiles:
            above = cells[t + 1]
        else:
            above = jnp.where(top, 0.0, pltpu.roll(cells[0], SUB - 1, 0))
        if t > 0:
            under = cells[t - 1]
        else:
            under = jnp.where(bottom, 0.0, pltpu.roll(cells[tiles - 1], 1, 0))
        return above + under

    def main_row(state, g, k):
        r = g * ny + k
        after = (r + 1) & (window - 1)
        before = (r - 1) & (window - 1)
        shift = (LANES - DEPTH * (k + 1)) & (LANES - 1)
        center = [[main[state, c, r, t] for t in range(tiles)] for c in range(COMPS)]
        result = []
        for t in range(tiles):
            h = []
            for c in range(COMPS):
                cells = center[c][t]
                ends = pltpu.roll(seam[state, c, g, t], shift, 1)
                s = pltpu.roll(jnp.where(last_lane, ends, cells), 1, 1)
                s = s + pltpu.roll(jnp.where(first_lane, ends, cells), LANES - 1, 1)
                s = s + (main[state, c, after, t] + main[state, c, before, t])
                h.append(s + around_z(center[c], t))
            m = [center[c][t] for c in range(COMPS)]
            rate = turn(m, h, par[0, r, t], par[1, r, t], par[2, r, t])
            if state == 0:
                new = [m[c] + rate[c] for c in range(COMPS)]
            else:
                new = normal([main[0, c, r, t] + (m[c] + rate[c]) for c in range(COMPS)])
            result.append(new)
        return r, result

    def strip_rows(state):
        for side in range(2):
            for g in range(2):
                center = [[strip[state, c, side, g, t] for t in range(tiles)] for c in range(COMPS)]
                for t in range(tiles):
                    h = []
                    for c in range(COMPS):
                        cells = center[c][t]
                        inner = edge[state, c, g, t]
                        other = strip[state, c, side, 1 - g, t]
                        if side == 0:
                            s = pltpu.roll(cells, 1, 1)
                            s = s + pltpu.roll(jnp.where(head_lane, inner, cells), LANES - 1, 1)
                        else:
                            s = pltpu.roll(jnp.where(tail_lane, inner, cells), 1, 1)
                            s = s + pltpu.roll(cells, LANES - 1, 1)
                        start = block == side
                        stop = block == (side + ny - 1) % ny
                        s = s + pltpu.roll(jnp.where(start, other, cells), LANES - DEPTH, 1)
                        s = s + pltpu.roll(jnp.where(stop, other, cells), DEPTH, 1)
                        h.append(s + around_z(center[c], t))
                    m = [center[c][t] for c in range(COMPS)]
                    rate = turn(
                        m, h, spar[0, side, g, t], spar[1, side, g, t], spar[2, side, g, t]
                    )
                    if state == 0:
                        new = [m[c] + rate[c] for c in range(COMPS)]
                    else:
                        new = normal(
                            [strip[0, c, side, g, t] + (m[c] + rate[c]) for c in range(COMPS)]
                        )
                    for c in range(COMPS):
                        strip[1 - state, c, side, g, t] = new[c]
        seams(1 - state)

    def main_rows(state, g, count, pick):
        def body(i, edges):
            edges = list(edges)
            for k in pick(i):
                r, result = main_row(state, g, k)
                for t in range(tiles):
                    for c in range(COMPS):
                        main[1 - state, c, r, t] = result[t][c]
                        edges[c * tiles + t] = merge(edges[c * tiles + t], result[t][c], k)
            return tuple(edges)

        edges = lax.fori_loop(0, count, body, zeros)
        for c in range(COMPS):
            for t in range(tiles):
                edge[1 - state, c, g, t] = edges[c * tiles + t]

    for stage in range(1, 2 * STEPS + 1):
        state = (stage + 1) % 2
        if stage == 2 * STEPS:

            def last(i, carry):
                for k in (i, i + ny // 2):
                    _, result = main_row(1, 0, k)
                    for t in range(tiles):
                        for c in range(COMPS):
                            out_ref[c, rows_at(ny, tiles, k, t), :] = result[t][c]
                return carry

            lax.fori_loop(0, ny // 2, last, 0)
        else:
            main_rows(state, 0, ny // 2, lambda i: (i, i + ny // 2))
            main_rows(state, 1, DEPTH - stage, lambda i: (i, ny - 1 - i))
            strip_rows(state)


def shifted(cells, axis, step, closed):
    count = lax.axis_size(axis)
    pairs = [(i, (i + step) % count) for i in range(count) if closed or 0 <= i + step < count]
    return lax.ppermute(cells, axis, pairs)


def around(cells, dim):
    ny = cells.shape[dim]
    if lax.axis_size("gy") == 2:
        return shifted(cells, "gy", 1, True)
    head = lax.slice_in_dim(cells, 0, DEPTH, axis=dim)
    tail = lax.slice_in_dim(cells, ny - DEPTH, ny, axis=dim)
    return jnp.concatenate([shifted(head, "gy", -1, True), shifted(tail, "gy", 1, True)], axis=dim)


def around_strip(cells, side):
    if lax.axis_size("gy") == 2:
        return shifted(cells, "gy", 1, True)
    block = (lax.broadcasted_iota(jnp.int32, cells.shape, cells.ndim - 1) // DEPTH - side) % (LANES // DEPTH)
    return jnp.where(block < DEPTH, shifted(cells, "gy", -1, True), shifted(cells, "gy", 1, True))


def body(magnetization, lower_image, image_weights, regions, anisotropy, damping):
    local, comps, nz, ny, nx = magnetization.shape
    images = local * lax.axis_size("img")
    tiles = nz // SUB
    assert local == 1 and comps == COMPS and nx == LANES
    assert ny == 2 * DEPTH and ny * DEPTH == LANES and tiles >= 2
    flat = (comps, nz * ny, nx)
    own = magnetization[0]
    up = shifted(own, "img", 1, False)
    down = shifted(own, "img", -1, False)
    own_p = around(own, 2)
    reg_p = around(regions, 1)

    smem = pl.BlockSpec(memory_space=pltpu.SMEM)
    vmem = pl.BlockSpec(memory_space=pltpu.VMEM)
    f32 = jnp.float32
    limit = pltpu.CompilerParams(vmem_limit_bytes=32 * 1024 * 1024)
    packed = jax.ShapeDtypeStruct((2 * comps + 1, tiles, SUB, LANES), f32)
    part, near, left, right = pl.pallas_call(
        functools.partial(gather_kernel, ny, tiles),
        out_shape=(
            jax.ShapeDtypeStruct((1, LANES), f32),
            jax.ShapeDtypeStruct(flat, f32),
            packed,
            packed,
        ),
        in_specs=[smem] + [vmem] * 4,
        out_specs=(vmem,) * 4,
        compiler_params=limit,
        name="gather_images",
    )(lower_image, own.reshape(flat), up.reshape(flat), down.reshape(flat), regions.reshape(flat[1:]))
    near_p = around(near.reshape(own.shape), 2)
    strip_r = shifted(left, "gx", -1, True)
    strip_l = shifted(right, "gx", 1, True)
    strip_lp = around_strip(strip_l, 0)
    strip_rp = around_strip(strip_r, 1)
    squares = lax.psum(part, ("img", "gx", "gy"))

    window = ny + 2 * DEPTH
    vreg = (SUB, LANES)
    out = pl.pallas_call(
        functools.partial(evolve_kernel, ny, tiles, images, anisotropy.shape[0]),
        out_shape=jax.ShapeDtypeStruct(flat, f32),
        in_specs=[smem] * 3 + [vmem] * 12,
        out_specs=vmem,
        scratch_shapes=[
            pltpu.VMEM((2, comps, window, tiles) + vreg, f32),
            pltpu.VMEM((2, comps, 2, 2, tiles) + vreg, f32),
            pltpu.VMEM((2, comps, 2, tiles) + vreg, f32),
            pltpu.VMEM((2, comps, 2, tiles) + vreg, f32),
            pltpu.VMEM((3, window, tiles) + vreg, f32),
            pltpu.VMEM((3, 2, 2, tiles) + vreg, f32),
        ],
        compiler_params=limit,
        name="evolve",
    )(
        lower_image,
        anisotropy,
        damping,
        squares,
        image_weights.reshape(1, -1),
        own.reshape(flat),
        own_p.reshape(flat),
        near,
        near_p.reshape(flat),
        regions.reshape(flat[1:]),
        reg_p.reshape(flat[1:]),
        strip_l,
        strip_r,
        strip_lp,
        strip_rp,
    )
    return out.reshape(magnetization.shape)


def solution(mesh):
    placed = (P("img", None, None, "gy", "gx"), P(), P(), P(None, "gy", "gx"), P(), P())
    return jax.shard_map(
        body,
        mesh=mesh,
        in_specs=placed,
        out_specs=P("img", None, None, "gy", "gx"),
        check_vma=False,
    )
```

```python
import functools

import jax
import jax.numpy as jnp
from jax import lax
from jax.experimental import pallas as pl
from jax.experimental.pallas import tpu as pltpu
from jax.sharding import PartitionSpec as P

STEPS = 4
DEPTH = 2 * STEPS

eps = 1e-06
time_step = 0.05

SUB = 8
LANES = 128
COMPS = 3


def lane_iota():
    return lax.broadcasted_iota(jnp.int32, (SUB, LANES), 1)


def sub_iota():
    return lax.broadcasted_iota(jnp.int32, (SUB, LANES), 0)


def rows_at(ny, tiles, y, t):
    return pl.ds(y + ny * t, SUB, stride=ny * tiles)


def gather_kernel(ny, tiles, lower_ref, m_ref, up_ref, down_ref, reg_ref, part_ref, near_ref, left_ref, right_ref):
    here = lax.axis_index("img")
    take_up = lower_ref[here] < here
    lane = lane_iota()

    near_ref[...] = jnp.where(take_up, up_ref[...], down_ref[...])
    diff = m_ref[...] - up_ref[...]
    total = jnp.sum(jnp.sum(diff * diff, axis=(0, 1), keepdims=True)[0], axis=1, keepdims=True)
    slot = lax.broadcasted_iota(jnp.int32, part_ref.shape, 1)
    part_ref[...] = jnp.where((slot == here) & (here > 0), total, 0.0)

    for t in range(tiles):
        for c in range(2 * COMPS + 1):
            left = jnp.zeros((SUB, LANES), jnp.float32)
            right = jnp.zeros((SUB, LANES), jnp.float32)
            for y in range(ny):
                rows = rows_at(ny, tiles, y, t)
                if c < COMPS:
                    cells = m_ref[c, rows, :]
                elif c < 2 * COMPS:
                    cells = near_ref[c - COMPS, rows, :]
                else:
                    cells = reg_ref[rows, :].astype(jnp.float32)
                cells = pltpu.roll(cells, (DEPTH * (y + 1)) % LANES, 1)
                left = jnp.where(lane // DEPTH == (y + 1) % ny, cells, left)
                right = jnp.where(lane // DEPTH == y, cells, right)
            left_ref[c, t] = left
            right_ref[c, t] = right


def turn(m, h, a2, b, sc):
    mx, my, mz = m
    hx, hy, hz = h
    hz = hz + a2 * mz
    gx = hx + b * (my * hz - mz * hy)
    gy = hy + b * (mz * hx - mx * hz)
    gz = hz + b * (mx * hy - my * hx)
    return (
        sc * (my * gz - mz * gy),
        sc * (mz * gx - mx * gz),
        sc * (mx * gy - my * gx),
    )


def normal(v):
    scale = lax.rsqrt(v[0] * v[0] + v[1] * v[1] + v[2] * v[2])
    return tuple(x * scale for x in v)


def evolve_kernel(
    ny,
    tiles,
    regions,
    lower_ref,
    aniso_ref,
    damp_ref,
    sq_ref,
    share_ref,
    m_ref,
    mp_ref,
    n_ref,
    np_ref,
    reg_ref,
    regp_ref,
    left_ref,
    right_ref,
    leftp_ref,
    rightp_ref,
    out_ref,
    main,
    strip,
    edge,
    seam,
    par,
    spar,
):
    window = ny + 2 * DEPTH
    here = lax.axis_index("img")
    lane = lane_iota()
    sub = sub_iota()
    block = lane // DEPTH
    first_lane = lane == 0
    last_lane = lane == LANES - 1
    head_lane = lane % DEPTH == 0
    tail_lane = lane % DEPTH == DEPTH - 1
    top = sub == SUB - 1
    bottom = sub == 0

    lo = lower_ref[here]
    slot = lax.broadcasted_iota(jnp.int32, sq_ref.shape, 1)
    lengths = jnp.where(slot >= 1, jnp.sqrt(sq_ref[...] + eps), 0.0)
    total = jnp.sum(lengths, axis=1, keepdims=True)
    arc = jnp.sum(jnp.where(slot <= lo, lengths, 0.0), axis=1, keepdims=True)
    gap = jnp.sum(jnp.where(slot == lo + 1, lengths, 0.0), axis=1, keepdims=True)
    share = share_ref[...]
    spot = lax.broadcasted_iota(jnp.int32, share.shape, 1)
    target = jnp.sum(jnp.where(spot < here, share, 0.0), axis=1, keepdims=True) / jnp.sum(
        share, axis=1, keepdims=True
    )
    weight = jnp.clip((target * total - arc) / gap, -0.5, 1.5)
    weight = jnp.broadcast_to(weight, (SUB, LANES))
    below = lo < here
    w_own = jnp.where(below, weight, 1.0 - weight)
    w_near = jnp.where(below, 1.0 - weight, weight)

    def params(region):
        a = jnp.full((SUB, LANES), aniso_ref[0], jnp.float32)
        d = jnp.full((SUB, LANES), damp_ref[0], jnp.float32)
        for i in range(1, regions):
            inside = region == i
            a = jnp.where(inside, aniso_ref[i], a)
            d = jnp.where(inside, damp_ref[i], d)
        return 2.0 * a, d, -time_step / (1.0 + d * d)

    def merge(old, new, k):
        mask = ((lane - (DEPTH * k + DEPTH - 1)) & (LANES - 1)) < 2
        shift = (DEPTH * (k + 1)) & (LANES - 1)
        return jnp.where(mask, pltpu.roll(new, shift, 1), old)

    zero = jnp.zeros((SUB, LANES), jnp.float32)
    zeros = tuple(zero for _ in range(COMPS * tiles))
    for g, (own, near, reg) in enumerate(((m_ref, n_ref, reg_ref), (mp_ref, np_ref, regp_ref))):

        edges = list(zeros)
        for k in range(ny):
            for t in range(tiles):
                rows = rows_at(ny, tiles, k, t)
                v = normal(
                    [w_own * own[c, rows, :] + w_near * near[c, rows, :] for c in range(COMPS)]
                )
                for c in range(COMPS):
                    main[0, c, g * ny + k, t] = v[c]
                    edges[c * tiles + t] = merge(edges[c * tiles + t], v[c], k)
                p = params(reg[rows, :])
                for i in range(3):
                    par[i, g * ny + k, t] = p[i]
        for c in range(COMPS):
            for t in range(tiles):
                edge[0, c, g, t] = edges[c * tiles + t]
    for side, pair in enumerate(((left_ref, leftp_ref), (right_ref, rightp_ref))):
        for g in range(2):
            for t in range(tiles):
                v = normal(
                    [w_own * pair[g][c, t] + w_near * pair[g][COMPS + c, t] for c in range(COMPS)]
                )
                for c in range(COMPS):
                    strip[0, c, side, g, t] = v[c]
                p = params(pair[g][2 * COMPS, t].astype(jnp.int32))
                for i in range(3):
                    spar[i, side, g, t] = p[i]

    def seams(state):
        for c in range(COMPS):
            for g in range(2):
                for t in range(tiles):
                    seam[state, c, g, t] = jnp.where(
                        tail_lane, strip[state, c, 0, g, t], strip[state, c, 1, g, t]
                    )

    seams(0)

    def around_z(cells, t):
        if t + 1 < tiles:
            above = cells[t + 1]
        else:
            above = jnp.where(top, 0.0, pltpu.roll(cells[0], SUB - 1, 0))
        if t > 0:
            under = cells[t - 1]
        else:
            under = jnp.where(bottom, 0.0, pltpu.roll(cells[tiles - 1], 1, 0))
        return above + under

    def main_row(state, g, k):
        r = g * ny + k
        after = (r + 1) & (window - 1)
        before = (r - 1) & (window - 1)
        shift = (LANES - DEPTH * (k + 1)) & (LANES - 1)
        center = [[main[state, c, r, t] for t in range(tiles)] for c in range(COMPS)]
        result = []
        for t in range(tiles):
            h = []
            for c in range(COMPS):
                cells = center[c][t]
                ends = pltpu.roll(seam[state, c, g, t], shift, 1)
                s = pltpu.roll(jnp.where(last_lane, ends, cells), 1, 1)
                s = s + pltpu.roll(jnp.where(first_lane, ends, cells), LANES - 1, 1)
                s = s + (main[state, c, after, t] + main[state, c, before, t])
                h.append(s + around_z(center[c], t))
            m = [center[c][t] for c in range(COMPS)]
            rate = turn(m, h, par[0, r, t], par[1, r, t], par[2, r, t])
            if state == 0:
                new = [m[c] + rate[c] for c in range(COMPS)]
            else:
                new = normal([main[0, c, r, t] + (m[c] + rate[c]) for c in range(COMPS)])
            result.append(new)
        return r, result

    def strip_rows(state):
        for side in range(2):
            for g in range(2):
                center = [[strip[state, c, side, g, t] for t in range(tiles)] for c in range(COMPS)]
                for t in range(tiles):
                    h = []
                    for c in range(COMPS):
                        cells = center[c][t]
                        inner = edge[state, c, g, t]
                        other = strip[state, c, side, 1 - g, t]
                        if side == 0:
                            s = pltpu.roll(cells, 1, 1)
                            s = s + pltpu.roll(jnp.where(head_lane, inner, cells), LANES - 1, 1)
                        else:
                            s = pltpu.roll(jnp.where(tail_lane, inner, cells), 1, 1)
                            s = s + pltpu.roll(cells, LANES - 1, 1)
                        start = block == side
                        stop = block == (side + ny - 1) % ny
                        s = s + pltpu.roll(jnp.where(start, other, cells), LANES - DEPTH, 1)
                        s = s + pltpu.roll(jnp.where(stop, other, cells), DEPTH, 1)
                        h.append(s + around_z(center[c], t))
                    m = [center[c][t] for c in range(COMPS)]
                    rate = turn(
                        m, h, spar[0, side, g, t], spar[1, side, g, t], spar[2, side, g, t]
                    )
                    if state == 0:
                        new = [m[c] + rate[c] for c in range(COMPS)]
                    else:
                        new = normal(
                            [strip[0, c, side, g, t] + (m[c] + rate[c]) for c in range(COMPS)]
                        )
                    for c in range(COMPS):
                        strip[1 - state, c, side, g, t] = new[c]
        seams(1 - state)

    def main_rows(state, g, rows):
        edges = list(zeros)
        for k in rows:
            r, result = main_row(state, g, k)
            for t in range(tiles):
                for c in range(COMPS):
                    main[1 - state, c, r, t] = result[t][c]
                    edges[c * tiles + t] = merge(edges[c * tiles + t], result[t][c], k)
        for c in range(COMPS):
            for t in range(tiles):
                edge[1 - state, c, g, t] = edges[c * tiles + t]

    for stage in range(1, 2 * STEPS):
        state = (stage + 1) % 2
        main_rows(state, 0, range(ny))
        main_rows(state, 1, [k for k in range(ny) if not DEPTH - stage <= k < DEPTH + stage])
        strip_rows(state)
    for k in range(ny):
        _, result = main_row(1, 0, k)
        for t in range(tiles):
            for c in range(COMPS):
                out_ref[c, rows_at(ny, tiles, k, t), :] = result[t][c]


def shifted(cells, axis, step, closed):
    count = lax.axis_size(axis)
    pairs = [(i, (i + step) % count) for i in range(count) if closed or 0 <= i + step < count]
    return lax.ppermute(cells, axis, pairs)


def around(cells, dim):
    ny = cells.shape[dim]
    if lax.axis_size("gy") == 2:
        return shifted(cells, "gy", 1, True)
    head = lax.slice_in_dim(cells, 0, DEPTH, axis=dim)
    tail = lax.slice_in_dim(cells, ny - DEPTH, ny, axis=dim)
    return jnp.concatenate([shifted(head, "gy", -1, True), shifted(tail, "gy", 1, True)], axis=dim)


def around_strip(cells, side):
    if lax.axis_size("gy") == 2:
        return shifted(cells, "gy", 1, True)
    block = (lax.broadcasted_iota(jnp.int32, cells.shape, cells.ndim - 1) // DEPTH - side) % (LANES // DEPTH)
    return jnp.where(block < DEPTH, shifted(cells, "gy", -1, True), shifted(cells, "gy", 1, True))


def body(magnetization, lower_image, image_weights, regions, anisotropy, damping):
    local, comps, nz, ny, nx = magnetization.shape
    images = local * lax.axis_size("img")
    tiles = nz // SUB
    assert local == 1 and comps == COMPS and nx == LANES
    assert ny == 2 * DEPTH and ny * DEPTH == LANES and tiles >= 2
    flat = (comps, nz * ny, nx)
    own = magnetization[0]
    up = shifted(own, "img", 1, False)
    down = shifted(own, "img", -1, False)
    own_p = around(own, 2)
    reg_p = around(regions, 1)

    smem = pl.BlockSpec(memory_space=pltpu.SMEM)
    vmem = pl.BlockSpec(memory_space=pltpu.VMEM)
    f32 = jnp.float32
    limit = pltpu.CompilerParams(vmem_limit_bytes=32 * 1024 * 1024)
    packed = jax.ShapeDtypeStruct((2 * comps + 1, tiles, SUB, LANES), f32)
    part, near, left, right = pl.pallas_call(
        functools.partial(gather_kernel, ny, tiles),
        out_shape=(
            jax.ShapeDtypeStruct((1, images), f32),
            jax.ShapeDtypeStruct(flat, f32),
            packed,
            packed,
        ),
        in_specs=[smem] + [vmem] * 4,
        out_specs=(vmem,) * 4,
        compiler_params=limit,
        name="gather_images",
    )(lower_image, own.reshape(flat), up.reshape(flat), down.reshape(flat), regions.reshape(flat[1:]))
    near_p = around(near.reshape(own.shape), 2)
    strip_r = shifted(left, "gx", -1, True)
    strip_l = shifted(right, "gx", 1, True)
    strip_lp = around_strip(strip_l, 0)
    strip_rp = around_strip(strip_r, 1)
    squares = lax.psum(part.reshape(images), ("img", "gx", "gy"))

    window = ny + 2 * DEPTH
    vreg = (SUB, LANES)
    out = pl.pallas_call(
        functools.partial(evolve_kernel, ny, tiles, anisotropy.shape[0]),
        out_shape=jax.ShapeDtypeStruct(flat, f32),
        in_specs=[smem] * 3 + [vmem] * 12,
        out_specs=vmem,
        scratch_shapes=[
            pltpu.VMEM((2, comps, window, tiles) + vreg, f32),
            pltpu.VMEM((2, comps, 2, 2, tiles) + vreg, f32),
            pltpu.VMEM((2, comps, 2, tiles) + vreg, f32),
            pltpu.VMEM((2, comps, 2, tiles) + vreg, f32),
            pltpu.VMEM((3, window, tiles) + vreg, f32),
            pltpu.VMEM((3, 2, 2, tiles) + vreg, f32),
        ],
        compiler_params=limit,
        name="evolve",
    )(
        lower_image,
        anisotropy,
        damping,
        squares.reshape(1, images),
        image_weights.reshape(1, -1),
        own.reshape(flat),
        own_p.reshape(flat),
        near,
        near_p.reshape(flat),
        regions.reshape(flat[1:]),
        reg_p.reshape(flat[1:]),
        strip_l,
        strip_r,
        strip_lp,
        strip_rp,
    )
    return out.reshape(magnetization.shape)


def solution(mesh):
    placed = (P("img", None, None, "gy", "gx"), P(), P(), P(None, "gy", "gx"), P(), P())
    return jax.shard_map(
        body,
        mesh=mesh,
        in_specs=placed,
        out_specs=P("img", None, None, "gy", "gx"),
        check_vma=False,
    )
```

```python
import functools

import jax
import jax.numpy as jnp
from jax import lax
from jax.experimental import pallas as pl
from jax.experimental.pallas import tpu as pltpu
from jax.sharding import PartitionSpec as P

STEPS = 4
DEPTH = 2 * STEPS

eps = 1e-06
time_step = 0.05

SUB = 8
LANES = 128
COMPS = 3
ROWS = 2


def lane_iota():
    return lax.broadcasted_iota(jnp.int32, (SUB, LANES), 1)


def sub_iota():
    return lax.broadcasted_iota(jnp.int32, (SUB, LANES), 0)


def rows_at(ny, tiles, y, t):
    return pl.ds(y + ny * t, SUB, stride=ny * tiles)


def gather_kernel(ny, tiles, lower_ref, m_ref, up_ref, down_ref, reg_ref, part_ref, near_ref, left_ref, right_ref):
    here = lax.axis_index("img")
    take_up = lower_ref[here] < here
    block = lane_iota() // DEPTH

    def squares(i, sums):
        sums = list(sums)
        for u in range(2):
            rows = pl.ds(pl.multiple_of((2 * i + u) * SUB, SUB), SUB)
            for c in range(COMPS):
                up = up_ref[c, rows, :]
                near_ref[c, rows, :] = jnp.where(take_up, up, down_ref[c, rows, :])
                diff = m_ref[c, rows, :] - up
                sums[c + COMPS * u] = sums[c + COMPS * u] + diff * diff
        return tuple(sums)

    zero = jnp.zeros((SUB, LANES), jnp.float32)
    sums = lax.fori_loop(0, m_ref.shape[1] // (2 * SUB), squares, (zero,) * (2 * COMPS))
    total = jnp.sum(functools.reduce(jnp.add, sums), axis=(0, 1), keepdims=True)
    slot = lax.broadcasted_iota(jnp.int32, part_ref.shape, 1)
    part_ref[...] = jnp.where((slot == here) & (here > 0), total, 0.0)

    def pack(y, carry):
        shift = (DEPTH * (y + 1)) & (LANES - 1)
        left = block == ((y + 1) & (ny - 1))
        right = block == y
        for t in range(tiles):
            rows = rows_at(ny, tiles, y, t)
            for c in range(2 * COMPS + 1):
                if c < COMPS:
                    cells = m_ref[c, rows, :]
                elif c < 2 * COMPS:
                    cells = near_ref[c - COMPS, rows, :]
                else:
                    cells = reg_ref[rows, :].astype(jnp.float32)
                cells = pltpu.roll(cells, shift, 1)
                pltpu.store(left_ref.at[c, t], cells, mask=left)
                pltpu.store(right_ref.at[c, t], cells, mask=right)
        return carry

    lax.fori_loop(0, ny, pack, 0)


def turn(m, h, a2, b, sc):
    mx, my, mz = m
    hx, hy, hz = h
    hz = hz + a2 * mz
    gx = hx + b * (my * hz - mz * hy)
    gy = hy + b * (mz * hx - mx * hz)
    gz = hz + b * (mx * hy - my * hx)
    return (
        sc * (my * gz - mz * gy),
        sc * (mz * gx - mx * gz),
        sc * (mx * gy - my * gx),
    )


def normal(v):
    scale = lax.rsqrt(v[0] * v[0] + v[1] * v[1] + v[2] * v[2])
    return tuple(x * scale for x in v)


def evolve_kernel(
    ny,
    tiles,
    images,
    regions,
    lower_ref,
    aniso_ref,
    damp_ref,
    sq_ref,
    share_ref,
    m_ref,
    mp_ref,
    n_ref,
    np_ref,
    reg_ref,
    regp_ref,
    left_ref,
    right_ref,
    leftp_ref,
    rightp_ref,
    out_ref,
    main,
    strip,
    edge,
    seam,
    par,
    spar,
):
    window = ny + 2 * DEPTH
    here = lax.axis_index("img")
    lane = lane_iota()
    sub = sub_iota()
    block = lane // DEPTH
    first_lane = lane == 0
    last_lane = lane == LANES - 1
    head_lane = lane % DEPTH == 0
    tail_lane = lane % DEPTH == DEPTH - 1
    top = sub == SUB - 1
    bottom = sub == 0

    lo = lower_ref[here]
    slot = lax.broadcasted_iota(jnp.int32, (1, LANES), 1)
    squares = jnp.sum(sq_ref[...], axis=0, keepdims=True)
    lengths = jnp.where((slot >= 1) & (slot < images), jnp.sqrt(squares + eps), 0.0)
    total = jnp.sum(lengths, axis=1, keepdims=True)
    arc = jnp.sum(jnp.where(slot <= lo, lengths, 0.0), axis=1, keepdims=True)
    gap = jnp.sum(jnp.where(slot == lo + 1, lengths, 0.0), axis=1, keepdims=True)
    share = share_ref[...]
    spot = lax.broadcasted_iota(jnp.int32, share.shape, 1)
    target = jnp.sum(jnp.where(spot < here, share, 0.0), axis=1, keepdims=True) / jnp.sum(
        share, axis=1, keepdims=True
    )
    weight = jnp.clip((target * total - arc) / gap, -0.5, 1.5)
    weight = jnp.broadcast_to(weight, (SUB, LANES))
    below = lo < here
    w_own = jnp.where(below, weight, 1.0 - weight)
    w_near = jnp.where(below, 1.0 - weight, weight)

    table_a = jnp.zeros((SUB, LANES), jnp.float32)
    table_d = jnp.zeros((SUB, LANES), jnp.float32)
    for i in range(regions):
        table_a = jnp.where(lane == i, 2.0 * aniso_ref[i], table_a)
        table_d = jnp.where(lane == i, damp_ref[i], table_d)
    tables = (table_a, table_d, -time_step / (1.0 + table_d * table_d))

    def params(region):
        return [jnp.take_along_axis(table, region, axis=1) for table in tables]

    def keep_ends(state, g, k, t, new):
        mask = ((lane - (DEPTH * k + DEPTH - 1)) & (LANES - 1)) < 2
        shift = (DEPTH * (k + 1)) & (LANES - 1)
        for c in range(COMPS):
            pltpu.store(edge.at[state, c, g, t], pltpu.roll(new[c], shift, 1), mask=mask)

    def fill(k, carry):
        for g, (own, near, reg) in enumerate(((m_ref, n_ref, reg_ref), (mp_ref, np_ref, regp_ref))):
            for t in range(tiles):
                rows = rows_at(ny, tiles, k, t)
                v = normal(
                    [w_own * own[c, rows, :] + w_near * near[c, rows, :] for c in range(COMPS)]
                )
                for c in range(COMPS):
                    main[0, c, g * ny + k, t] = v[c]
                keep_ends(0, g, k, t, v)
                p = params(reg[rows, :])
                for i in range(3):
                    par[i, g * ny + k, t] = p[i]
        return carry

    lax.fori_loop(0, ny, fill, 0)

    def fill_strips(t, carry):
        for g, pair in enumerate(((left_ref, right_ref), (leftp_ref, rightp_ref))):
            ends = []
            for side in range(2):
                cells = pair[side]
                v = normal(
                    [w_own * cells[c, t] + w_near * cells[COMPS + c, t] for c in range(COMPS)]
                )
                for c in range(COMPS):
                    strip[0, c, side, g, t] = v[c]
                p = params(cells[2 * COMPS, t].astype(jnp.int32))
                for i in range(3):
                    spar[i, side, g, t] = p[i]
                ends.append(v)
            for c in range(COMPS):
                seam[0, c, g, t] = jnp.where(tail_lane, ends[0][c], ends[1][c])
        return carry

    lax.fori_loop(0, tiles, fill_strips, 0)

    def around_z(cells, t):
        if t + 1 < tiles:
            above = cells[t + 1]
        else:
            above = jnp.where(top, 0.0, pltpu.roll(cells[0], SUB - 1, 0))
        if t > 0:
            under = cells[t - 1]
        else:
            under = jnp.where(bottom, 0.0, pltpu.roll(cells[tiles - 1], 1, 0))
        return above + under

    def main_row(state, r):
        g = r // ny
        k = r & (ny - 1)
        after = (r + 1) & (window - 1)
        before = (r - 1) & (window - 1)
        shift = (LANES - DEPTH * (k + 1)) & (LANES - 1)
        center = [[main[state, c, r, t] for t in range(tiles)] for c in range(COMPS)]
        for t in range(tiles):
            h = []
            for c in range(COMPS):
                cells = center[c][t]
                ends = pltpu.roll(seam[state, c, g, t], shift, 1)
                s = pltpu.roll(jnp.where(last_lane, ends, cells), 1, 1)
                s = s + pltpu.roll(jnp.where(first_lane, ends, cells), LANES - 1, 1)
                s = s + (main[state, c, after, t] + main[state, c, before, t])
                h.append(s + around_z(center[c], t))
            m = [center[c][t] for c in range(COMPS)]
            rate = turn(m, h, par[0, r, t], par[1, r, t], par[2, r, t])
            if state == 0:
                new = [m[c] + rate[c] for c in range(COMPS)]
            else:
                new = normal([main[0, c, r, t] + (m[c] + rate[c]) for c in range(COMPS)])
            for c in range(COMPS):
                main[1 - state, c, r, t] = new[c]
            keep_ends(1 - state, g, k, t, new)

    def strip_rows(state):
        def group(g, carry):
            ends = [[None] * tiles, [None] * tiles]
            for side in range(2):
                start = block == side
                stop = block == (side + ny - 1) % ny
                center = [[strip[state, c, side, g, t] for t in range(tiles)] for c in range(COMPS)]
                for t in range(tiles):
                    h = []
                    for c in range(COMPS):
                        cells = center[c][t]
                        inner = edge[state, c, g, t]
                        other = strip[state, c, side, 1 - g, t]
                        if side == 0:
                            s = pltpu.roll(cells, 1, 1)
                            s = s + pltpu.roll(jnp.where(head_lane, inner, cells), LANES - 1, 1)
                        else:
                            s = pltpu.roll(jnp.where(tail_lane, inner, cells), 1, 1)
                            s = s + pltpu.roll(cells, LANES - 1, 1)
                        s = s + pltpu.roll(jnp.where(start, other, cells), LANES - DEPTH, 1)
                        s = s + pltpu.roll(jnp.where(stop, other, cells), DEPTH, 1)
                        h.append(s + around_z(center[c], t))
                    m = [center[c][t] for c in range(COMPS)]
                    rate = turn(
                        m, h, spar[0, side, g, t], spar[1, side, g, t], spar[2, side, g, t]
                    )
                    if state == 0:
                        new = [m[c] + rate[c] for c in range(COMPS)]
                    else:
                        new = normal(
                            [strip[0, c, side, g, t] + (m[c] + rate[c]) for c in range(COMPS)]
                        )
                    for c in range(COMPS):
                        strip[1 - state, c, side, g, t] = new[c]
                    ends[side][t] = new
            for t in range(tiles):
                for c in range(COMPS):
                    seam[1 - state, c, g, t] = jnp.where(tail_lane, ends[0][t][c], ends[1][t][c])
            return carry

        lax.fori_loop(0, 2, group, 0)

    def main_rows(state, first, count):
        def rows(i, carry):
            for u in range(ROWS):
                main_row(state, (first + ROWS * i + u) & (window - 1))
            return carry

        lax.fori_loop(0, count // ROWS, rows, 0)

    def step(i, carry):
        for state in range(2):
            margin = DEPTH - 1 - state - 2 * i
            main_rows(state, -margin, ny + 2 * margin)
            strip_rows(state)
        return carry

    lax.fori_loop(0, STEPS, step, 0)

    def hand_out(k, carry):
        for t in range(tiles):
            for c in range(COMPS):
                out_ref[c, rows_at(ny, tiles, k, t), :] = main[0, c, k, t]
        return carry

    lax.fori_loop(0, ny, hand_out, 0)


def shifted(cells, axis, step, closed):
    count = lax.axis_size(axis)
    pairs = [(i, (i + step) % count) for i in range(count) if closed or 0 <= i + step < count]
    return lax.ppermute(cells, axis, pairs)


def around(cells, dim):
    ny = cells.shape[dim]
    if lax.axis_size("gy") == 2:
        return shifted(cells, "gy", 1, True)
    head = lax.slice_in_dim(cells, 0, DEPTH, axis=dim)
    tail = lax.slice_in_dim(cells, ny - DEPTH, ny, axis=dim)
    return jnp.concatenate([shifted(head, "gy", -1, True), shifted(tail, "gy", 1, True)], axis=dim)


def diagonal(cells, step_x, step_y):
    nx, ny = lax.axis_size("gx"), lax.axis_size("gy")
    pairs = [
        (x * ny + y, (x + step_x) % nx * ny + (y + step_y) % ny) for x in range(nx) for y in range(ny)
    ]
    return lax.ppermute(cells, ("gx", "gy"), pairs)


def around_strip(cells, step_x, side):
    if lax.axis_size("gy") == 2:
        return diagonal(cells, step_x, 1)
    block = (lax.broadcasted_iota(jnp.int32, cells.shape, cells.ndim - 1) // DEPTH - side) % (LANES // DEPTH)
    return jnp.where(block < DEPTH, diagonal(cells, step_x, -1), diagonal(cells, step_x, 1))


def body(magnetization, lower_image, image_weights, regions, anisotropy, damping):
    local, comps, nz, ny, nx = magnetization.shape
    images = local * lax.axis_size("img")
    tiles = nz // SUB
    devices = lax.axis_size(("img", "gx", "gy"))
    assert local == 1 and comps == COMPS and nx == LANES
    assert ny == 2 * DEPTH and ny * DEPTH == LANES and tiles >= 2
    flat = (comps, nz * ny, nx)
    own = magnetization[0]
    up = shifted(own, "img", 1, False)
    down = shifted(own, "img", -1, False)
    own_p = around(own, 2)
    reg_p = around(regions, 1)

    smem = pl.BlockSpec(memory_space=pltpu.SMEM)
    vmem = pl.BlockSpec(memory_space=pltpu.VMEM)
    f32 = jnp.float32
    limit = pltpu.CompilerParams(vmem_limit_bytes=32 * 1024 * 1024)
    packed = jax.ShapeDtypeStruct((2 * comps + 1, tiles, SUB, LANES), f32)
    part, near, left, right = pl.pallas_call(
        functools.partial(gather_kernel, ny, tiles),
        out_shape=(
            jax.ShapeDtypeStruct((devices, LANES), f32),
            jax.ShapeDtypeStruct(flat, f32),
            packed,
            packed,
        ),
        in_specs=[smem] + [vmem] * 4,
        out_specs=(vmem,) * 4,
        compiler_params=limit,
        name="gather_images",
    )(lower_image, own.reshape(flat), up.reshape(flat), down.reshape(flat), regions.reshape(flat[1:]))
    near_p = around(near.reshape(own.shape), 2)
    strip_r = shifted(left, "gx", -1, True)
    strip_l = shifted(right, "gx", 1, True)
    strip_lp = around_strip(right, 1, 0)
    strip_rp = around_strip(left, -1, 1)
    squares = lax.all_to_all(part, ("img", "gx", "gy"), 0, 0, tiled=True)

    window = ny + 2 * DEPTH
    vreg = (SUB, LANES)
    out = pl.pallas_call(
        functools.partial(evolve_kernel, ny, tiles, images, anisotropy.shape[0]),
        out_shape=jax.ShapeDtypeStruct(flat, f32),
        in_specs=[smem] * 3 + [vmem] * 12,
        out_specs=vmem,
        scratch_shapes=[
            pltpu.VMEM((2, comps, window, tiles) + vreg, f32),
            pltpu.VMEM((2, comps, 2, 2, tiles) + vreg, f32),
            pltpu.VMEM((2, comps, 2, tiles) + vreg, f32),
            pltpu.VMEM((2, comps, 2, tiles) + vreg, f32),
            pltpu.VMEM((3, window, tiles) + vreg, f32),
            pltpu.VMEM((3, 2, 2, tiles) + vreg, f32),
        ],
        compiler_params=limit,
        name="evolve",
    )(
        lower_image,
        anisotropy,
        damping,
        squares,
        image_weights.reshape(1, -1),
        own.reshape(flat),
        own_p.reshape(flat),
        near,
        near_p.reshape(flat),
        regions.reshape(flat[1:]),
        reg_p.reshape(flat[1:]),
        strip_l,
        strip_r,
        strip_lp,
        strip_rp,
    )
    return out.reshape(magnetization.shape)


def solution(mesh):
    placed = (P("img", None, None, "gy", "gx"), P(), P(), P(None, "gy", "gx"), P(), P())
    return jax.shard_map(
        body,
        mesh=mesh,
        in_specs=placed,
        out_specs=P("img", None, None, "gy", "gx"),
        check_vma=False,
    )
```

```python
import functools

import jax
import jax.numpy as jnp
from jax import lax
from jax.experimental import pallas as pl
from jax.experimental.pallas import tpu as pltpu
from jax.sharding import PartitionSpec as P

STEPS = 4
DEPTH = 2 * STEPS

eps = 1e-06
time_step = 0.05

SUB = 8
LANES = 128
COMPS = 3
ROWS = 4


def lane_iota():
    return lax.broadcasted_iota(jnp.int32, (SUB, LANES), 1)


def sub_iota():
    return lax.broadcasted_iota(jnp.int32, (SUB, LANES), 0)


def rows_at(ny, tiles, y, t):
    return pl.ds(y + ny * t, SUB, stride=ny * tiles)


def gather_kernel(ny, tiles, lower_ref, m_ref, up_ref, down_ref, reg_ref, part_ref, near_ref, left_ref, right_ref):
    here = lax.axis_index("img")
    take_up = lower_ref[here] < here
    block = lane_iota() // DEPTH

    def squares(i, sums):
        sums = list(sums)
        for u in range(2):
            rows = pl.ds(pl.multiple_of((2 * i + u) * SUB, SUB), SUB)
            for c in range(COMPS):
                up = up_ref[c, rows, :]
                near_ref[c, rows, :] = jnp.where(take_up, up, down_ref[c, rows, :])
                diff = m_ref[c, rows, :] - up
                sums[c + COMPS * u] = sums[c + COMPS * u] + diff * diff
        return tuple(sums)

    zero = jnp.zeros((SUB, LANES), jnp.float32)
    sums = lax.fori_loop(0, m_ref.shape[1] // (2 * SUB), squares, (zero,) * (2 * COMPS))
    total = jnp.sum(functools.reduce(jnp.add, sums), axis=(0, 1), keepdims=True)
    slot = lax.broadcasted_iota(jnp.int32, part_ref.shape, 1)
    part_ref[...] = jnp.where((slot == here) & (here > 0), total, 0.0)

    def pack(y, carry):
        shift = (DEPTH * (y + 1)) & (LANES - 1)
        left = block == ((y + 1) & (ny - 1))
        right = block == y
        done = []
        for t in range(tiles):
            rows = rows_at(ny, tiles, y, t)
            for c in range(2 * COMPS + 1):
                if c < COMPS:
                    cells = m_ref[c, rows, :]
                elif c < 2 * COMPS:
                    cells = near_ref[c - COMPS, rows, :]
                else:
                    cells = reg_ref[rows, :].astype(jnp.float32)
                done.append((c, t, pltpu.roll(cells, shift, 1)))
        for c, t, cells in done:
            pltpu.store(left_ref.at[c, t], cells, mask=left)
            pltpu.store(right_ref.at[c, t], cells, mask=right)
        return carry

    lax.fori_loop(0, ny, pack, 0)


def turn(m, h, a2, b, sc):
    mx, my, mz = m
    hx, hy, hz = h
    hz = hz + a2 * mz
    gx = hx + b * (my * hz - mz * hy)
    gy = hy + b * (mz * hx - mx * hz)
    gz = hz + b * (mx * hy - my * hx)
    return (
        sc * (my * gz - mz * gy),
        sc * (mz * gx - mx * gz),
        sc * (mx * gy - my * gx),
    )


def normal(v):
    scale = lax.rsqrt(v[0] * v[0] + v[1] * v[1] + v[2] * v[2])
    return tuple(x * scale for x in v)


def evolve_kernel(
    ny,
    tiles,
    images,
    regions,
    lower_ref,
    aniso_ref,
    damp_ref,
    sq_ref,
    share_ref,
    m_ref,
    mp_ref,
    n_ref,
    np_ref,
    reg_ref,
    regp_ref,
    left_ref,
    right_ref,
    leftp_ref,
    rightp_ref,
    out_ref,
    main0,
    main1,
    strip0,
    strip1,
    edge0,
    edge1,
    seam0,
    seam1,
    par,
    spar,
):
    main, strip, edge, seam = (main0, main1), (strip0, strip1), (edge0, edge1), (seam0, seam1)
    window = ny + 2 * DEPTH
    here = lax.axis_index("img")
    lane = lane_iota()
    sub = sub_iota()
    block = lane // DEPTH
    first_lane = lane == 0
    last_lane = lane == LANES - 1
    head_lane = lane % DEPTH == 0
    tail_lane = lane % DEPTH == DEPTH - 1
    top = sub == SUB - 1
    bottom = sub == 0

    lo = lower_ref[here]
    slot = lax.broadcasted_iota(jnp.int32, (1, LANES), 1)
    squares = jnp.sum(sq_ref[...], axis=0, keepdims=True)
    lengths = jnp.where((slot >= 1) & (slot < images), jnp.sqrt(squares + eps), 0.0)
    total = jnp.sum(lengths, axis=1, keepdims=True)
    arc = jnp.sum(jnp.where(slot <= lo, lengths, 0.0), axis=1, keepdims=True)
    gap = jnp.sum(jnp.where(slot == lo + 1, lengths, 0.0), axis=1, keepdims=True)
    share = share_ref[...]
    spot = lax.broadcasted_iota(jnp.int32, share.shape, 1)
    target = jnp.sum(jnp.where(spot < here, share, 0.0), axis=1, keepdims=True) / jnp.sum(
        share, axis=1, keepdims=True
    )
    weight = jnp.clip((target * total - arc) / gap, -0.5, 1.5)
    weight = jnp.broadcast_to(weight, (SUB, LANES))
    below = lo < here
    w_own = jnp.where(below, weight, 1.0 - weight)
    w_near = jnp.where(below, 1.0 - weight, weight)

    table_a = jnp.zeros((SUB, LANES), jnp.float32)
    table_d = jnp.zeros((SUB, LANES), jnp.float32)
    for i in range(regions):
        table_a = jnp.where(lane == i, 2.0 * aniso_ref[i], table_a)
        table_d = jnp.where(lane == i, damp_ref[i], table_d)
    tables = (table_a, table_d, -time_step / (1.0 + table_d * table_d))

    def params(region):
        return [jnp.take_along_axis(table, region, axis=1) for table in tables]

    def ends_of(k, new):
        shift = (DEPTH * (k + 1)) & (LANES - 1)
        return [pltpu.roll(new[c], shift, 1) for c in range(COMPS)]

    def keep(state, r, t, new, ends):
        k = r & (ny - 1)
        mask = ((lane - (DEPTH * k + DEPTH - 1)) & (LANES - 1)) < 2
        for c in range(COMPS):
            main[state][c, r, t] = new[c]
            pltpu.store(edge[state].at[c, r // ny, t], ends[c], mask=mask)

    def fill(k, carry):
        done = []
        for g, (own, near, reg) in enumerate(((m_ref, n_ref, reg_ref), (mp_ref, np_ref, regp_ref))):
            for t in range(tiles):
                rows = rows_at(ny, tiles, k, t)
                v = normal(
                    [w_own * own[c, rows, :] + w_near * near[c, rows, :] for c in range(COMPS)]
                )
                done.append((g * ny + k, t, v, ends_of(k, v), params(reg[rows, :])))
        for r, t, v, ends, p in done:
            keep(0, r, t, v, ends)
            for i in range(3):
                par[i, r, t] = p[i]
        return carry

    lax.fori_loop(0, ny, fill, 0)

    def fill_strips(t, carry):
        for g, pair in enumerate(((left_ref, right_ref), (leftp_ref, rightp_ref))):
            ends = []
            for side in range(2):
                cells = pair[side]
                v = normal(
                    [w_own * cells[c, t] + w_near * cells[COMPS + c, t] for c in range(COMPS)]
                )
                for c in range(COMPS):
                    strip[0][c, side, g, t] = v[c]
                p = params(cells[2 * COMPS, t].astype(jnp.int32))
                for i in range(3):
                    spar[i, side, g, t] = p[i]
                ends.append(v)
            for c in range(COMPS):
                seam[0][c, g, t] = jnp.where(tail_lane, ends[0][c], ends[1][c])
        return carry

    lax.fori_loop(0, tiles, fill_strips, 0)

    def around_z(cells, t):
        if t + 1 < tiles:
            above = cells[t + 1]
        else:
            above = jnp.where(top, 0.0, pltpu.roll(cells[0], SUB - 1, 0))
        if t > 0:
            under = cells[t - 1]
        else:
            under = jnp.where(bottom, 0.0, pltpu.roll(cells[tiles - 1], 1, 0))
        return above + under

    def main_row(state, r):
        g = r // ny
        k = r & (ny - 1)
        after = (r + 1) & (window - 1)
        before = (r - 1) & (window - 1)
        shift = (LANES - DEPTH * (k + 1)) & (LANES - 1)
        center = [[main[state][c, r, t] for t in range(tiles)] for c in range(COMPS)]
        done = []
        for t in range(tiles):
            h = []
            for c in range(COMPS):
                cells = center[c][t]
                ends = pltpu.roll(seam[state][c, g, t], shift, 1)
                s = pltpu.roll(jnp.where(last_lane, ends, cells), 1, 1)
                s = s + pltpu.roll(jnp.where(first_lane, ends, cells), LANES - 1, 1)
                s = s + (main[state][c, after, t] + main[state][c, before, t])
                h.append(s + around_z(center[c], t))
            m = [center[c][t] for c in range(COMPS)]
            rate = turn(m, h, par[0, r, t], par[1, r, t], par[2, r, t])
            if state == 0:
                new = [m[c] + rate[c] for c in range(COMPS)]
            else:
                new = normal([main[0][c, r, t] + (m[c] + rate[c]) for c in range(COMPS)])
            done.append((r, t, new, ends_of(k, new)))
        return done

    def strip_rows(state):
        def group(g, carry):
            ends = [[None] * tiles, [None] * tiles]
            done = []
            for side in range(2):
                start = block == side
                stop = block == (side + ny - 1) % ny
                center = [[strip[state][c, side, g, t] for t in range(tiles)] for c in range(COMPS)]
                for t in range(tiles):
                    h = []
                    for c in range(COMPS):
                        cells = center[c][t]
                        inner = edge[state][c, g, t]
                        other = strip[state][c, side, 1 - g, t]
                        if side == 0:
                            s = pltpu.roll(cells, 1, 1)
                            s = s + pltpu.roll(jnp.where(head_lane, inner, cells), LANES - 1, 1)
                        else:
                            s = pltpu.roll(jnp.where(tail_lane, inner, cells), 1, 1)
                            s = s + pltpu.roll(cells, LANES - 1, 1)
                        s = s + pltpu.roll(jnp.where(start, other, cells), LANES - DEPTH, 1)
                        s = s + pltpu.roll(jnp.where(stop, other, cells), DEPTH, 1)
                        h.append(s + around_z(center[c], t))
                    m = [center[c][t] for c in range(COMPS)]
                    rate = turn(
                        m, h, spar[0, side, g, t], spar[1, side, g, t], spar[2, side, g, t]
                    )
                    if state == 0:
                        new = [m[c] + rate[c] for c in range(COMPS)]
                    else:
                        new = normal(
                            [strip[0][c, side, g, t] + (m[c] + rate[c]) for c in range(COMPS)]
                        )
                    done.append((side, t, new))
                    ends[side][t] = new
            for side, t, new in done:
                for c in range(COMPS):
                    strip[1 - state][c, side, g, t] = new[c]
            for t in range(tiles):
                for c in range(COMPS):
                    seam[1 - state][c, g, t] = jnp.where(tail_lane, ends[0][t][c], ends[1][t][c])
            return carry

        lax.fori_loop(0, 2, group, 0)

    def main_rows(state, first, count):
        def rows(i, carry):
            done = []
            for u in range(ROWS):
                done += main_row(state, (first + ROWS * i + u) & (window - 1))
            for r, t, new, ends in done:
                keep(1 - state, r, t, new, ends)
            return carry

        lax.fori_loop(0, count // ROWS, rows, 0)

    def step(i, carry):
        for state in range(2):
            margin = DEPTH - 2 * state - 2 * i
            main_rows(state, -margin, ny + 2 * margin)
            strip_rows(state)
        return carry

    lax.fori_loop(0, STEPS, step, 0)

    def hand_out(k, carry):
        for t in range(tiles):
            for c in range(COMPS):
                out_ref[c, rows_at(ny, tiles, k, t), :] = main[0][c, k, t]
        return carry

    lax.fori_loop(0, ny, hand_out, 0)


def shifted(cells, axis, step, closed):
    count = lax.axis_size(axis)
    pairs = [(i, (i + step) % count) for i in range(count) if closed or 0 <= i + step < count]
    return lax.ppermute(cells, axis, pairs)


def around(cells, dim):
    ny = cells.shape[dim]
    if lax.axis_size("gy") == 2:
        return shifted(cells, "gy", 1, True)
    head = lax.slice_in_dim(cells, 0, DEPTH, axis=dim)
    tail = lax.slice_in_dim(cells, ny - DEPTH, ny, axis=dim)
    return jnp.concatenate([shifted(head, "gy", -1, True), shifted(tail, "gy", 1, True)], axis=dim)


def diagonal(cells, step_x, step_y):
    nx, ny = lax.axis_size("gx"), lax.axis_size("gy")
    pairs = [
        (x * ny + y, (x + step_x) % nx * ny + (y + step_y) % ny) for x in range(nx) for y in range(ny)
    ]
    return lax.ppermute(cells, ("gx", "gy"), pairs)


def around_strip(cells, step_x, side):
    if lax.axis_size("gy") == 2:
        return diagonal(cells, step_x, 1)
    block = (lax.broadcasted_iota(jnp.int32, cells.shape, cells.ndim - 1) // DEPTH - side) % (LANES // DEPTH)
    return jnp.where(block < DEPTH, diagonal(cells, step_x, -1), diagonal(cells, step_x, 1))


def body(magnetization, lower_image, image_weights, regions, anisotropy, damping):
    local, comps, nz, ny, nx = magnetization.shape
    images = local * lax.axis_size("img")
    tiles = nz // SUB
    devices = lax.axis_size(("img", "gx", "gy"))
    assert local == 1 and comps == COMPS and nx == LANES
    assert ny == 2 * DEPTH and ny * DEPTH == LANES and tiles >= 2
    flat = (comps, nz * ny, nx)
    own = magnetization[0]
    up = shifted(own, "img", 1, False)
    down = shifted(own, "img", -1, False)
    own_p = around(own, 2)
    reg_p = around(regions, 1)

    up, down, own_p, reg_p = lax.optimization_barrier((up, down, own_p, reg_p))

    smem = pl.BlockSpec(memory_space=pltpu.SMEM)
    vmem = pl.BlockSpec(memory_space=pltpu.VMEM)
    f32 = jnp.float32
    limit = pltpu.CompilerParams(vmem_limit_bytes=32 * 1024 * 1024)
    packed = jax.ShapeDtypeStruct((2 * comps + 1, tiles, SUB, LANES), f32)
    part, near, left, right = pl.pallas_call(
        functools.partial(gather_kernel, ny, tiles),
        out_shape=(
            jax.ShapeDtypeStruct((devices, LANES), f32),
            jax.ShapeDtypeStruct(flat, f32),
            packed,
            packed,
        ),
        in_specs=[smem] + [vmem] * 4,
        out_specs=(vmem,) * 4,
        compiler_params=limit,
        name="gather_images",
    )(lower_image, own.reshape(flat), up.reshape(flat), down.reshape(flat), regions.reshape(flat[1:]))
    near_p = around(near.reshape(own.shape), 2)
    strip_r = shifted(left, "gx", -1, True)
    strip_l = shifted(right, "gx", 1, True)
    strip_lp = around_strip(right, 1, 0)
    strip_rp = around_strip(left, -1, 1)
    squares = lax.all_to_all(part, ("img", "gx", "gy"), 0, 0, tiled=True)

    window = ny + 2 * DEPTH
    vreg = (SUB, LANES)
    out = pl.pallas_call(
        functools.partial(evolve_kernel, ny, tiles, images, anisotropy.shape[0]),
        out_shape=jax.ShapeDtypeStruct(flat, f32),
        in_specs=[smem] * 3 + [vmem] * 12,
        out_specs=vmem,
        scratch_shapes=[
            pltpu.VMEM((comps, window, tiles) + vreg, f32),
            pltpu.VMEM((comps, window, tiles) + vreg, f32),
            pltpu.VMEM((comps, 2, 2, tiles) + vreg, f32),
            pltpu.VMEM((comps, 2, 2, tiles) + vreg, f32),
            pltpu.VMEM((comps, 2, tiles) + vreg, f32),
            pltpu.VMEM((comps, 2, tiles) + vreg, f32),
            pltpu.VMEM((comps, 2, tiles) + vreg, f32),
            pltpu.VMEM((comps, 2, tiles) + vreg, f32),
            pltpu.VMEM((3, window, tiles) + vreg, f32),
            pltpu.VMEM((3, 2, 2, tiles) + vreg, f32),
        ],
        compiler_params=limit,
        name="evolve",
    )(
        lower_image,
        anisotropy,
        damping,
        squares,
        image_weights.reshape(1, -1),
        own.reshape(flat),
        own_p.reshape(flat),
        near,
        near_p.reshape(flat),
        regions.reshape(flat[1:]),
        reg_p.reshape(flat[1:]),
        strip_l,
        strip_r,
        strip_lp,
        strip_rp,
    )
    return out.reshape(magnetization.shape)


def solution(mesh):
    placed = (P("img", None, None, "gy", "gx"), P(), P(), P(None, "gy", "gx"), P(), P())
    return jax.shard_map(
        body,
        mesh=mesh,
        in_specs=placed,
        out_specs=P("img", None, None, "gy", "gx"),
        check_vma=False,
    )
```

```python
import functools

import jax
import jax.numpy as jnp
from jax import lax
from jax.experimental import pallas as pl
from jax.experimental.pallas import tpu as pltpu
from jax.sharding import PartitionSpec as P

STEPS = 4
DEPTH = 2 * STEPS

eps = 1e-06
time_step = 0.05

SUB = 8
LANES = 128
COMPS = 3
ROWS = 4


def lane_iota():
    return lax.broadcasted_iota(jnp.int32, (SUB, LANES), 1)


def sub_iota():
    return lax.broadcasted_iota(jnp.int32, (SUB, LANES), 0)


def rows_at(ny, tiles, y, t):
    return pl.ds(y + ny * t, SUB, stride=ny * tiles)


def gather_kernel(ny, tiles, lower_ref, m_ref, up_ref, down_ref, reg_ref, part_ref, near_ref, left_ref, right_ref):
    here = lax.axis_index("img")
    take_up = lower_ref[here] < here
    block = lane_iota() // DEPTH

    def squares(i, sums):
        sums = list(sums)
        for u in range(2):
            rows = pl.ds(pl.multiple_of((2 * i + u) * SUB, SUB), SUB)
            for c in range(COMPS):
                up = up_ref[c, rows, :]
                near_ref[c, rows, :] = jnp.where(take_up, up, down_ref[c, rows, :])
                diff = m_ref[c, rows, :] - up
                sums[c + COMPS * u] = sums[c + COMPS * u] + diff * diff
        return tuple(sums)

    zero = jnp.zeros((SUB, LANES), jnp.float32)
    sums = lax.fori_loop(0, m_ref.shape[1] // (2 * SUB), squares, (zero,) * (2 * COMPS))
    total = jnp.sum(functools.reduce(jnp.add, sums), axis=(0, 1), keepdims=True)
    slot = lax.broadcasted_iota(jnp.int32, part_ref.shape, 1)
    part_ref[...] = jnp.where((slot == here) & (here > 0), total, 0.0)

    def pack(y, carry):
        shift = (DEPTH * (y + 1)) & (LANES - 1)
        left = block == ((y + 1) & (ny - 1))
        right = block == y
        done = []
        for t in range(tiles):
            rows = rows_at(ny, tiles, y, t)
            for c in range(2 * COMPS + 1):
                if c < COMPS:
                    cells = m_ref[c, rows, :]
                elif c < 2 * COMPS:
                    cells = near_ref[c - COMPS, rows, :]
                else:
                    cells = reg_ref[rows, :].astype(jnp.float32)
                done.append((c, t, pltpu.roll(cells, shift, 1)))
        for c, t, cells in done:
            pltpu.store(left_ref.at[c, t], cells, mask=left)
            pltpu.store(right_ref.at[c, t], cells, mask=right)
        return carry

    lax.fori_loop(0, ny, pack, 0)


def turn(m, h, a2, b, sc):
    mx, my, mz = m
    hx, hy, hz = h
    hz = hz + a2 * mz
    gx = hx + b * (my * hz - mz * hy)
    gy = hy + b * (mz * hx - mx * hz)
    gz = hz + b * (mx * hy - my * hx)
    return (
        sc * (my * gz - mz * gy),
        sc * (mz * gx - mx * gz),
        sc * (mx * gy - my * gx),
    )


def normal(v):
    scale = lax.rsqrt(v[0] * v[0] + v[1] * v[1] + v[2] * v[2])
    return tuple(x * scale for x in v)


def evolve_kernel(
    ny,
    tiles,
    images,
    regions,
    lower_ref,
    aniso_ref,
    damp_ref,
    sq_ref,
    share_ref,
    m_ref,
    mp_ref,
    n_ref,
    np_ref,
    reg_ref,
    regp_ref,
    left_ref,
    right_ref,
    leftp_ref,
    rightp_ref,
    out_ref,
    main0,
    main1,
    strip0,
    strip1,
    edge,
    seam0,
    seam1,
    par,
    spar,
):
    main, strip, seam = (main0, main1), (strip0, strip1), (seam0, seam1)
    window = ny + 2 * DEPTH
    here = lax.axis_index("img")
    lane = lane_iota()
    sub = sub_iota()
    block = lane // DEPTH
    first_lane = lane == 0
    last_lane = lane == LANES - 1
    head_lane = lane % DEPTH == 0
    tail_lane = lane % DEPTH == DEPTH - 1
    top = sub == SUB - 1
    bottom = sub == 0

    lo = lower_ref[here]
    slot = lax.broadcasted_iota(jnp.int32, (1, LANES), 1)
    squares = jnp.sum(sq_ref[...], axis=0, keepdims=True)
    lengths = jnp.where((slot >= 1) & (slot < images), jnp.sqrt(squares + eps), 0.0)
    total = jnp.sum(lengths, axis=1, keepdims=True)
    arc = jnp.sum(jnp.where(slot <= lo, lengths, 0.0), axis=1, keepdims=True)
    gap = jnp.sum(jnp.where(slot == lo + 1, lengths, 0.0), axis=1, keepdims=True)
    share = share_ref[...]
    spot = lax.broadcasted_iota(jnp.int32, share.shape, 1)
    target = jnp.sum(jnp.where(spot < here, share, 0.0), axis=1, keepdims=True) / jnp.sum(
        share, axis=1, keepdims=True
    )
    weight = jnp.clip((target * total - arc) / gap, -0.5, 1.5)
    weight = jnp.broadcast_to(weight, (SUB, LANES))
    below = lo < here
    w_own = jnp.where(below, weight, 1.0 - weight)
    w_near = jnp.where(below, 1.0 - weight, weight)

    table_a = jnp.zeros((SUB, LANES), jnp.float32)
    table_d = jnp.zeros((SUB, LANES), jnp.float32)
    for i in range(regions):
        table_a = jnp.where(lane == i, 2.0 * aniso_ref[i], table_a)
        table_d = jnp.where(lane == i, damp_ref[i], table_d)
    tables = (table_a, table_d, -time_step / (1.0 + table_d * table_d))

    def params(region):
        return [jnp.take_along_axis(table, region, axis=1) for table in tables]

    def ends_of(k, new):
        shift = (DEPTH * (k + 1)) & (LANES - 1)
        return [pltpu.roll(new[c], shift, 1) for c in range(COMPS)]

    def fill(k, carry):
        done = []
        for g, (own, near, reg) in enumerate(((m_ref, n_ref, reg_ref), (mp_ref, np_ref, regp_ref))):
            for t in range(tiles):
                rows = rows_at(ny, tiles, k, t)
                v = normal(
                    [w_own * own[c, rows, :] + w_near * near[c, rows, :] for c in range(COMPS)]
                )
                done.append((g * ny + k, t, v, params(reg[rows, :])))
        for r, t, v, p in done:
            for c in range(COMPS):
                main0[c, r, t] = v[c]
            for i in range(3):
                par[i, r, t] = p[i]
        return carry

    lax.fori_loop(0, ny, fill, 0)

    def seam_of(left, right):
        return jnp.where(head_lane, pltpu.roll(left, 1, 1), pltpu.roll(right, LANES - 1, 1))

    def fill_strips(t, carry):
        for g, pair in enumerate(((left_ref, right_ref), (leftp_ref, rightp_ref))):
            ends = []
            for side in range(2):
                cells = pair[side]
                v = normal(
                    [w_own * cells[c, t] + w_near * cells[COMPS + c, t] for c in range(COMPS)]
                )
                for c in range(COMPS):
                    strip[0][c, side, g, t] = v[c]
                p = params(cells[2 * COMPS, t].astype(jnp.int32))
                for i in range(3):
                    spar[i, side, g, t] = p[i]
                ends.append(v)
            for c in range(COMPS):
                seam[0][c, g, t] = seam_of(ends[0][c], ends[1][c])
        return carry

    lax.fori_loop(0, tiles, fill_strips, 0)

    def around_z(cells, t):
        if t + 1 < tiles:
            above = cells[t + 1]
        else:
            above = jnp.where(top, 0.0, pltpu.roll(cells[0], SUB - 1, 0))
        if t > 0:
            under = cells[t - 1]
        else:
            under = jnp.where(bottom, 0.0, pltpu.roll(cells[tiles - 1], 1, 0))
        return above + under

    def main_row(state, r):
        g = r // ny
        k = r & (ny - 1)
        after = (r + 1) & (window - 1)
        before = (r - 1) & (window - 1)
        shift = (LANES - DEPTH * (k + 1)) & (LANES - 1)
        center = [[main[state][c, r, t] for t in range(tiles)] for c in range(COMPS)]
        done = []
        for t in range(tiles):
            h = []
            for c in range(COMPS):
                cells = center[c][t]
                ends = pltpu.roll(seam[state][c, g, t], shift, 1)
                s = jnp.where(first_lane, ends, pltpu.roll(cells, 1, 1))
                s = s + jnp.where(last_lane, ends, pltpu.roll(cells, LANES - 1, 1))
                s = s + (main[state][c, after, t] + main[state][c, before, t])
                h.append(s + around_z(center[c], t))
            m = [center[c][t] for c in range(COMPS)]
            rate = turn(m, h, par[0, r, t], par[1, r, t], par[2, r, t])
            if state == 0:
                new = [m[c] + rate[c] for c in range(COMPS)]
            else:
                new = normal([main[0][c, r, t] + (m[c] + rate[c]) for c in range(COMPS)])
            done.append((r, t, new, ends_of(k, m)))
        return done

    def strip_rows(state):
        done = []
        for g in range(2):
            for side in range(2):
                start = block == side
                stop = block == (side + ny - 1) % ny
                center = [[strip[state][c, side, g, t] for t in range(tiles)] for c in range(COMPS)]
                for t in range(tiles):
                    h = []
                    for c in range(COMPS):
                        cells = center[c][t]
                        inner = edge[c, g, t]
                        other = strip[state][c, side, 1 - g, t]
                        if side == 0:
                            s = pltpu.roll(cells, 1, 1)
                            s = s + pltpu.roll(jnp.where(head_lane, inner, cells), LANES - 1, 1)
                        else:
                            s = pltpu.roll(jnp.where(tail_lane, inner, cells), 1, 1)
                            s = s + pltpu.roll(cells, LANES - 1, 1)
                        s = s + pltpu.roll(jnp.where(start, other, cells), LANES - DEPTH, 1)
                        s = s + pltpu.roll(jnp.where(stop, other, cells), DEPTH, 1)
                        h.append(s + around_z(center[c], t))
                    m = [center[c][t] for c in range(COMPS)]
                    rate = turn(
                        m, h, spar[0, side, g, t], spar[1, side, g, t], spar[2, side, g, t]
                    )
                    if state == 0:
                        new = [m[c] + rate[c] for c in range(COMPS)]
                    else:
                        new = normal(
                            [strip[0][c, side, g, t] + (m[c] + rate[c]) for c in range(COMPS)]
                        )
                    done.append((side, g, t, new))
        for side, g, t, new in done:
            for c in range(COMPS):
                strip[1 - state][c, side, g, t] = new[c]
        for g in range(2):
            for t in range(tiles):
                left, right = (new for _, h, u, new in done if (h, u) == (g, t))
                for c in range(COMPS):
                    seam[1 - state][c, g, t] = seam_of(left[c], right[c])

    def main_rows(state, first, count):
        def rows(i, carry):
            done = []
            for u in range(ROWS):
                done += main_row(state, (first + ROWS * i + u) & (window - 1))
            for r, t, new, ends in done:
                k = r & (ny - 1)
                mask = ((lane - (DEPTH * k + DEPTH - 1)) & (LANES - 1)) < 2
                for c in range(COMPS):
                    main[1 - state][c, r, t] = new[c]
                    pltpu.store(edge.at[c, r // ny, t], ends[c], mask=mask)
            return carry

        lax.fori_loop(0, count // ROWS, rows, 0)

    def step(i, carry):
        for state in range(2):
            margin = DEPTH - 2 * state - 2 * i
            main_rows(state, -margin, ny + 2 * margin)
            strip_rows(state)
        return carry

    lax.fori_loop(0, STEPS, step, 0)

    def hand_out(k, carry):
        for t in range(tiles):
            for c in range(COMPS):
                out_ref[c, rows_at(ny, tiles, k, t), :] = main[0][c, k, t]
        return carry

    lax.fori_loop(0, ny, hand_out, 0)


def shifted(cells, axis, step, closed):
    count = lax.axis_size(axis)
    pairs = [(i, (i + step) % count) for i in range(count) if closed or 0 <= i + step < count]
    return lax.ppermute(cells, axis, pairs)


def around(cells, dim):
    ny = cells.shape[dim]
    if lax.axis_size("gy") == 2:
        return shifted(cells, "gy", 1, True)
    head = lax.slice_in_dim(cells, 0, DEPTH, axis=dim)
    tail = lax.slice_in_dim(cells, ny - DEPTH, ny, axis=dim)
    return jnp.concatenate([shifted(head, "gy", -1, True), shifted(tail, "gy", 1, True)], axis=dim)


def diagonal(cells, step_x, step_y):
    nx, ny = lax.axis_size("gx"), lax.axis_size("gy")
    pairs = [
        (x * ny + y, (x + step_x) % nx * ny + (y + step_y) % ny) for x in range(nx) for y in range(ny)
    ]
    return lax.ppermute(cells, ("gx", "gy"), pairs)


def around_strip(cells, step_x, side):
    if lax.axis_size("gy") == 2:
        return diagonal(cells, step_x, 1)
    block = (lax.broadcasted_iota(jnp.int32, cells.shape, cells.ndim - 1) // DEPTH - side) % (LANES // DEPTH)
    return jnp.where(block < DEPTH, diagonal(cells, step_x, -1), diagonal(cells, step_x, 1))


def body(magnetization, lower_image, image_weights, regions, anisotropy, damping):
    local, comps, nz, ny, nx = magnetization.shape
    images = local * lax.axis_size("img")
    tiles = nz // SUB
    devices = lax.axis_size(("img", "gx", "gy"))
    assert local == 1 and comps == COMPS and nx == LANES
    assert ny == 2 * DEPTH and ny * DEPTH == LANES and tiles >= 2
    flat = (comps, nz * ny, nx)
    own = magnetization[0]
    up = shifted(own, "img", 1, False)
    down = shifted(own, "img", -1, False)
    own_p = around(own, 2)
    reg_p = around(regions, 1)

    up, down, own_p, reg_p = lax.optimization_barrier((up, down, own_p, reg_p))

    smem = pl.BlockSpec(memory_space=pltpu.SMEM)
    vmem = pl.BlockSpec(memory_space=pltpu.VMEM)
    f32 = jnp.float32
    limit = pltpu.CompilerParams(vmem_limit_bytes=32 * 1024 * 1024)
    packed = jax.ShapeDtypeStruct((2 * comps + 1, tiles, SUB, LANES), f32)
    part, near, left, right = pl.pallas_call(
        functools.partial(gather_kernel, ny, tiles),
        out_shape=(
            jax.ShapeDtypeStruct((devices, LANES), f32),
            jax.ShapeDtypeStruct(flat, f32),
            packed,
            packed,
        ),
        in_specs=[smem] + [vmem] * 4,
        out_specs=(vmem,) * 4,
        compiler_params=limit,
        name="gather_images",
    )(lower_image, own.reshape(flat), up.reshape(flat), down.reshape(flat), regions.reshape(flat[1:]))
    near_p = around(near.reshape(own.shape), 2)
    strip_r = shifted(left, "gx", -1, True)
    strip_l = shifted(right, "gx", 1, True)
    strip_lp = around_strip(right, 1, 0)
    strip_rp = around_strip(left, -1, 1)
    squares = lax.all_to_all(part, ("img", "gx", "gy"), 0, 0, tiled=True)

    window = ny + 2 * DEPTH
    vreg = (SUB, LANES)
    out = pl.pallas_call(
        functools.partial(evolve_kernel, ny, tiles, images, anisotropy.shape[0]),
        out_shape=jax.ShapeDtypeStruct(flat, f32),
        in_specs=[smem] * 3 + [vmem] * 12,
        out_specs=vmem,
        scratch_shapes=[
            pltpu.VMEM((comps, window, tiles) + vreg, f32),
            pltpu.VMEM((comps, window, tiles) + vreg, f32),
            pltpu.VMEM((comps, 2, 2, tiles) + vreg, f32),
            pltpu.VMEM((comps, 2, 2, tiles) + vreg, f32),
            pltpu.VMEM((comps, 2, tiles) + vreg, f32),
            pltpu.VMEM((comps, 2, tiles) + vreg, f32),
            pltpu.VMEM((comps, 2, tiles) + vreg, f32),
            pltpu.VMEM((3, window, tiles) + vreg, f32),
            pltpu.VMEM((3, 2, 2, tiles) + vreg, f32),
        ],
        compiler_params=limit,
        name="evolve",
    )(
        lower_image,
        anisotropy,
        damping,
        squares,
        image_weights.reshape(1, -1),
        own.reshape(flat),
        own_p.reshape(flat),
        near,
        near_p.reshape(flat),
        regions.reshape(flat[1:]),
        reg_p.reshape(flat[1:]),
        strip_l,
        strip_r,
        strip_lp,
        strip_rp,
    )
    return out.reshape(magnetization.shape)


def solution(mesh):
    placed = (P("img", None, None, "gy", "gx"), P(), P(), P(None, "gy", "gx"), P(), P())
    return jax.shard_map(
        body,
        mesh=mesh,
        in_specs=placed,
        out_specs=P("img", None, None, "gy", "gx"),
        check_vma=False,
    )
```

```python
import functools

import jax
import jax.numpy as jnp
from jax import lax
from jax.experimental import pallas as pl
from jax.experimental.pallas import tpu as pltpu
from jax.sharding import PartitionSpec as P

STEPS = 4
DEPTH = 2 * STEPS

eps = 1e-06
time_step = 0.05

SUB = 8
LANES = 128
COMPS = 3
ROWS = 4


def lane_iota():
    return lax.broadcasted_iota(jnp.int32, (SUB, LANES), 1)


def sub_iota():
    return lax.broadcasted_iota(jnp.int32, (SUB, LANES), 0)


def rows_at(ny, tiles, y, t):
    return pl.ds(y + ny * t, SUB, stride=ny * tiles)


def pack_kernel(
    ny, tiles, regions, lower_ref, aniso_ref, damp_ref, share_ref, m_ref, reg_ref, both_ref, info_ref
):
    here = lax.axis_index("img")
    lane = lane_iota()
    block = lane // DEPTH

    def pack(i, carry):
        done = []
        for u in range(2):
            y = 2 * i + u
            shift = (DEPTH * (y + 1)) & (LANES - 1)
            left = block == ((y + 1) & (ny - 1))
            right = block == y
            for t in range(tiles):
                rows = rows_at(ny, tiles, y, t)
                for c in range(COMPS + 1):
                    cells = m_ref[c, rows, :] if c < COMPS else reg_ref[rows, :].astype(jnp.float32)
                    done.append((c, t, left, right, pltpu.roll(cells, shift, 1)))
        for c, t, left, right, cells in done:
            pltpu.store(both_ref.at[0, c, t], cells, mask=left)
            pltpu.store(both_ref.at[1, c, t], cells, mask=right)
        return carry

    lax.fori_loop(0, ny // 2, pack, 0)

    table_a = jnp.zeros((SUB, LANES), jnp.float32)
    table_d = jnp.zeros((SUB, LANES), jnp.float32)
    for i in range(regions):
        table_a = jnp.where(lane == i, 2.0 * aniso_ref[i], table_a)
        table_d = jnp.where(lane == i, damp_ref[i], table_d)
    info_ref[0] = table_a
    info_ref[1] = table_d
    info_ref[2] = -time_step / (1.0 + table_d * table_d)
    share = share_ref[...]
    spot = lax.broadcasted_iota(jnp.int32, share.shape, 1)
    target = jnp.sum(jnp.where(spot < here, share, 0.0), axis=1, keepdims=True) / jnp.sum(
        share, axis=1, keepdims=True
    )
    info_ref[3] = jnp.broadcast_to(target, (SUB, LANES))
    info_ref[4] = jnp.full((SUB, LANES), lower_ref[here].astype(jnp.float32))


def sort_kernel(both_ref, both_p_ref, left_ref, right_ref):
    for g, ref in enumerate((both_ref, both_p_ref)):
        left_ref[g] = ref[0]
        right_ref[g] = ref[1]


def merge_kernel(info_ref, left_ref, right_ref, out_ref, info_out_ref):
    info_out_ref[...] = info_ref[...]
    for g in range(2):
        out_ref[0, g] = left_ref[g, :COMPS]
        out_ref[1, g] = right_ref[g, :COMPS]


def take_first(info_ref, here):
    odd = (here & 1) == 1
    below = info_ref[4] < here.astype(jnp.float32)
    return jnp.where(below, jnp.where(odd, 1, 0), jnp.where(odd, 0, 1)) == 1, odd


def gather_kernel(info_ref, m_ref, first_ref, second_ref, part_ref, near_ref):
    here = lax.axis_index("img")
    pick, odd = take_first(info_ref, here)
    chunks = 4

    def squares(i, sums):
        sums = list(sums)
        done = []
        for u in range(chunks):
            rows = pl.ds(pl.multiple_of((chunks * i + u) * SUB, SUB), SUB)
            for c in range(COMPS):
                one = first_ref[c, rows, :]
                two = second_ref[c, rows, :]
                done.append((c, rows, jnp.where(pick, one, two)))
                diff = m_ref[c, rows, :] - jnp.where(odd, one, two)
                sums[c + COMPS * u] = sums[c + COMPS * u] + diff * diff
        for c, rows, cells in done:
            near_ref[c, rows, :] = cells
        return tuple(sums)

    zero = jnp.zeros((SUB, LANES), jnp.float32)
    sums = lax.fori_loop(0, m_ref.shape[1] // (chunks * SUB), squares, (zero,) * (chunks * COMPS))
    total = jnp.sum(functools.reduce(jnp.add, sums), axis=(0, 1), keepdims=True)
    slot = lax.broadcasted_iota(jnp.int32, part_ref.shape, 1)
    part_ref[...] = jnp.where((slot == here) & (here > 0), total, 0.0)


def turn(m, h, a2, b, sc):
    mx, my, mz = m
    hx, hy, hz = h
    hz = hz + a2 * mz
    gx = hx + b * (my * hz - mz * hy)
    gy = hy + b * (mz * hx - mx * hz)
    gz = hz + b * (mx * hy - my * hx)
    return (
        sc * (my * gz - mz * gy),
        sc * (mz * gx - mx * gz),
        sc * (mx * gy - my * gx),
    )


def normal(v):
    scale = lax.rsqrt(v[0] * v[0] + v[1] * v[1] + v[2] * v[2])
    return tuple(x * scale for x in v)


def evolve_kernel(
    ny,
    tiles,
    images,
    info_ref,
    sq_ref,
    m_ref,
    mp_ref,
    n_ref,
    np_ref,
    reg_ref,
    regp_ref,
    left_ref,
    right_ref,
    first_ref,
    second_ref,
    out_ref,
    main0,
    main1,
    strip0,
    strip1,
    edge,
    seam0,
    seam1,
    par,
    spar,
):
    main, strip, seam = (main0, main1), (strip0, strip1), (seam0, seam1)
    window = ny + 2 * DEPTH
    here = lax.axis_index("img")
    lane = lane_iota()
    sub = sub_iota()
    block = lane // DEPTH
    first_lane = lane == 0
    last_lane = lane == LANES - 1
    head_lane = lane % DEPTH == 0
    tail_lane = lane % DEPTH == DEPTH - 1
    top = sub == SUB - 1
    bottom = sub == 0

    pick, _ = take_first(info_ref, here)
    lo = info_ref[4]
    slot = lane.astype(jnp.float32)
    squares = jnp.broadcast_to(jnp.sum(sq_ref[...], axis=0, keepdims=True), (SUB, LANES))
    lengths = jnp.where((lane >= 1) & (lane < images), jnp.sqrt(squares + eps), 0.0)
    total = jnp.sum(lengths, axis=1, keepdims=True)
    arc = jnp.sum(jnp.where(slot <= lo, lengths, 0.0), axis=1, keepdims=True)
    gap = jnp.sum(jnp.where(slot == lo + 1.0, lengths, 0.0), axis=1, keepdims=True)
    weight = jnp.clip((info_ref[3] * total - arc) / gap, -0.5, 1.5)
    below = lo < here.astype(jnp.float32)
    w_own = jnp.where(below, weight, 1.0 - weight)
    w_near = jnp.where(below, 1.0 - weight, weight)

    tables = (info_ref[0], info_ref[1], info_ref[2])

    def params(region):
        return [jnp.take_along_axis(table, region, axis=1) for table in tables]

    def ends_of(k, new):
        shift = (DEPTH * (k + 1)) & (LANES - 1)
        return [pltpu.roll(new[c], shift, 1) for c in range(COMPS)]

    def fill(k, carry):
        done = []
        for g, (own, near, reg) in enumerate(((m_ref, n_ref, reg_ref), (mp_ref, np_ref, regp_ref))):
            for t in range(tiles):
                rows = rows_at(ny, tiles, k, t)
                v = normal(
                    [w_own * own[c, rows, :] + w_near * near[c, rows, :] for c in range(COMPS)]
                )
                done.append((g * ny + k, t, v, params(reg[rows, :])))
        for r, t, v, p in done:
            for c in range(COMPS):
                main0[c, r, t] = v[c]
            for i in range(3):
                par[i, r, t] = p[i]
        return carry

    lax.fori_loop(0, ny, fill, 0)

    def seam_of(left, right):
        return jnp.where(head_lane, pltpu.roll(left, 1, 1), pltpu.roll(right, LANES - 1, 1))

    def fill_strips(t, carry):
        done = []
        for g in range(2):
            for side, cells in enumerate((left_ref, right_ref)):
                near = [
                    jnp.where(pick, first_ref[side, g, c, t], second_ref[side, g, c, t])
                    for c in range(COMPS)
                ]
                v = normal([w_own * cells[g, c, t] + w_near * near[c] for c in range(COMPS)])
                done.append((side, g, v, params(cells[g, COMPS, t].astype(jnp.int32))))
        for side, g, v, p in done:
            for c in range(COMPS):
                strip0[c, side, g, t] = v[c]
            for i in range(3):
                spar[i, side, g, t] = p[i]
        for g in range(2):
            left, right = (v for _, h, v, _ in done if h == g)
            for c in range(COMPS):
                seam0[c, g, t] = seam_of(left[c], right[c])
        return carry

    lax.fori_loop(0, tiles, fill_strips, 0)

    def around_z(cells, t):
        if t + 1 < tiles:
            above = cells[t + 1]
        else:
            above = jnp.where(top, 0.0, pltpu.roll(cells[0], SUB - 1, 0))
        if t > 0:
            under = cells[t - 1]
        else:
            under = jnp.where(bottom, 0.0, pltpu.roll(cells[tiles - 1], 1, 0))
        return above + under

    def main_row(state, r):
        g = r // ny
        k = r & (ny - 1)
        after = (r + 1) & (window - 1)
        before = (r - 1) & (window - 1)
        shift = (LANES - DEPTH * (k + 1)) & (LANES - 1)
        center = [[main[state][c, r, t] for t in range(tiles)] for c in range(COMPS)]
        done = []
        for t in range(tiles):
            h = []
            for c in range(COMPS):
                cells = center[c][t]
                ends = pltpu.roll(seam[state][c, g, t], shift, 1)
                s = jnp.where(first_lane, ends, pltpu.roll(cells, 1, 1))
                s = s + jnp.where(last_lane, ends, pltpu.roll(cells, LANES - 1, 1))
                s = s + (main[state][c, after, t] + main[state][c, before, t])
                h.append(s + around_z(center[c], t))
            m = [center[c][t] for c in range(COMPS)]
            rate = turn(m, h, par[0, r, t], par[1, r, t], par[2, r, t])
            if state == 0:
                new = [m[c] + rate[c] for c in range(COMPS)]
            else:
                new = normal([main[0][c, r, t] + (m[c] + rate[c]) for c in range(COMPS)])
            done.append((r, t, new, ends_of(k, m)))
        return done

    def strip_rows(state):
        done = []
        for g in range(2):
            for side in range(2):
                start = block == side
                stop = block == (side + ny - 1) % ny
                center = [[strip[state][c, side, g, t] for t in range(tiles)] for c in range(COMPS)]
                for t in range(tiles):
                    h = []
                    for c in range(COMPS):
                        cells = center[c][t]
                        inner = edge[c, g, t]
                        other = strip[state][c, side, 1 - g, t]
                        if side == 0:
                            s = pltpu.roll(cells, 1, 1)
                            s = s + pltpu.roll(jnp.where(head_lane, inner, cells), LANES - 1, 1)
                        else:
                            s = pltpu.roll(jnp.where(tail_lane, inner, cells), 1, 1)
                            s = s + pltpu.roll(cells, LANES - 1, 1)
                        s = s + pltpu.roll(jnp.where(start, other, cells), LANES - DEPTH, 1)
                        s = s + pltpu.roll(jnp.where(stop, other, cells), DEPTH, 1)
                        h.append(s + around_z(center[c], t))
                    m = [center[c][t] for c in range(COMPS)]
                    rate = turn(
                        m, h, spar[0, side, g, t], spar[1, side, g, t], spar[2, side, g, t]
                    )
                    if state == 0:
                        new = [m[c] + rate[c] for c in range(COMPS)]
                    else:
                        new = normal(
                            [strip[0][c, side, g, t] + (m[c] + rate[c]) for c in range(COMPS)]
                        )
                    done.append((side, g, t, new))
        for side, g, t, new in done:
            for c in range(COMPS):
                strip[1 - state][c, side, g, t] = new[c]
        for g in range(2):
            for t in range(tiles):
                left, right = (new for _, h, u, new in done if (h, u) == (g, t))
                for c in range(COMPS):
                    seam[1 - state][c, g, t] = seam_of(left[c], right[c])

    def main_rows(state, first, count):
        def rows(i, carry):
            done = []
            for u in range(ROWS):
                done += main_row(state, (first + ROWS * i + u) & (window - 1))
            for r, t, new, ends in done:
                k = r & (ny - 1)
                mask = ((lane - (DEPTH * k + DEPTH - 1)) & (LANES - 1)) < 2
                for c in range(COMPS):
                    main[1 - state][c, r, t] = new[c]
                    pltpu.store(edge.at[c, r // ny, t], ends[c], mask=mask)
            return carry

        lax.fori_loop(0, count // ROWS, rows, 0)

    def step(i, carry):
        for state in range(2):
            margin = DEPTH - 2 * state - 2 * i
            main_rows(state, -margin, ny + 2 * margin)
            strip_rows(state)
        return carry

    lax.fori_loop(0, STEPS, step, 0)

    def hand_out(k, carry):
        for t in range(tiles):
            for c in range(COMPS):
                out_ref[c, rows_at(ny, tiles, k, t), :] = main[0][c, k, t]
        return carry

    lax.fori_loop(0, ny, hand_out, 0)


def shifted(cells, axis, step, closed):
    count = lax.axis_size(axis)
    pairs = [(i, (i + step) % count) for i in range(count) if closed or 0 <= i + step < count]
    return lax.ppermute(cells, axis, pairs)


def swapped(cells, axis, first):
    count = lax.axis_size(axis)
    pairs = [(i, i + 1) for i in range(first, count - 1, 2)]
    return lax.ppermute(cells, axis, pairs + [(j, i) for i, j in pairs])


def around(cells, dim):
    ny = cells.shape[dim]
    if lax.axis_size("gy") == 2:
        return shifted(cells, "gy", 1, True)
    head = lax.slice_in_dim(cells, 0, DEPTH, axis=dim)
    tail = lax.slice_in_dim(cells, ny - DEPTH, ny, axis=dim)
    return jnp.concatenate([shifted(head, "gy", -1, True), shifted(tail, "gy", 1, True)], axis=dim)


def around_strips(both):
    if lax.axis_size("gy") == 2:
        return shifted(both, "gy", 1, True)
    block = lax.broadcasted_iota(jnp.int32, both.shape, both.ndim - 1) // DEPTH
    side = lax.broadcasted_iota(jnp.int32, both.shape, 0)
    head = (block + side - 1) % (LANES // DEPTH) < DEPTH
    return jnp.where(head, shifted(both, "gy", -1, True), shifted(both, "gy", 1, True))


def body(magnetization, lower_image, image_weights, regions, anisotropy, damping):
    local, comps, nz, ny, nx = magnetization.shape
    images = local * lax.axis_size("img")
    tiles = nz // SUB
    devices = lax.axis_size(("img", "gx", "gy"))
    assert local == 1 and comps == COMPS and nx == LANES
    assert ny == 2 * DEPTH and ny * DEPTH == LANES and tiles >= 2
    flat = (comps, nz * ny, nx)
    own = magnetization[0]
    first = swapped(own, "img", 0)
    second = swapped(own, "img", 1)
    own_p = around(own, 2)

    smem = pl.BlockSpec(memory_space=pltpu.SMEM)
    vmem = pl.BlockSpec(memory_space=pltpu.VMEM)
    f32 = jnp.float32
    limit = pltpu.CompilerParams(vmem_limit_bytes=32 * 1024 * 1024)
    vreg = (SUB, LANES)
    both, info = pl.pallas_call(
        functools.partial(pack_kernel, ny, tiles, anisotropy.shape[0]),
        out_shape=(
            jax.ShapeDtypeStruct((2, comps + 1, tiles) + vreg, f32),
            jax.ShapeDtypeStruct((5,) + vreg, f32),
        ),
        in_specs=[smem] * 3 + [vmem] * 3,
        out_specs=(vmem,) * 2,
        compiler_params=limit,
        name="pack_strips",
    )(
        lower_image,
        anisotropy,
        damping,
        image_weights.reshape(1, -1),
        own.reshape(flat),
        regions.reshape(flat[1:]),
    )
    left, right = pl.pallas_call(
        sort_kernel,
        out_shape=(jax.ShapeDtypeStruct((2, comps + 1, tiles) + vreg, f32),) * 2,
        in_specs=[vmem] * 2,
        out_specs=(vmem,) * 2,
        compiler_params=limit,
        name="sort_strips",
    )(both, around_strips(both))
    strips = (shifted(right, "gx", 1, True), shifted(left, "gx", -1, True))
    strips_all, info = pl.pallas_call(
        merge_kernel,
        out_shape=(
            jax.ShapeDtypeStruct((2, 2, comps, tiles) + vreg, f32),
            jax.ShapeDtypeStruct(info.shape, f32),
        ),
        in_specs=[vmem] * 3,
        out_specs=(vmem,) * 2,
        compiler_params=limit,
        name="merge_strips",
    )(info, *strips)
    strips_first = swapped(strips_all, "img", 0)
    strips_second = swapped(strips_all, "img", 1)
    reg_p = around(regions, 1)

    info, own_p = lax.optimization_barrier((info, own_p))
    part, near = pl.pallas_call(
        gather_kernel,
        out_shape=(jax.ShapeDtypeStruct((devices, LANES), f32), jax.ShapeDtypeStruct(flat, f32)),
        in_specs=[vmem] * 4,
        out_specs=(vmem,) * 2,
        compiler_params=limit,
        name="gather_images",
    )(info, own.reshape(flat), first.reshape(flat), second.reshape(flat))
    near_p = around(near.reshape(own.shape), 2)
    squares = lax.all_to_all(part, ("img", "gx", "gy"), 0, 0, tiled=True)

    window = ny + 2 * DEPTH
    out = pl.pallas_call(
        functools.partial(evolve_kernel, ny, tiles, images),
        out_shape=jax.ShapeDtypeStruct(flat, f32),
        in_specs=[vmem] * 12,
        out_specs=vmem,
        scratch_shapes=[
            pltpu.VMEM((comps, window, tiles) + vreg, f32),
            pltpu.VMEM((comps, window, tiles) + vreg, f32),
            pltpu.VMEM((comps, 2, 2, tiles) + vreg, f32),
            pltpu.VMEM((comps, 2, 2, tiles) + vreg, f32),
            pltpu.VMEM((comps, 2, tiles) + vreg, f32),
            pltpu.VMEM((comps, 2, tiles) + vreg, f32),
            pltpu.VMEM((comps, 2, tiles) + vreg, f32),
            pltpu.VMEM((3, window, tiles) + vreg, f32),
            pltpu.VMEM((3, 2, 2, tiles) + vreg, f32),
        ],
        compiler_params=limit,
        name="evolve",
    )(
        info,
        squares,
        own.reshape(flat),
        own_p.reshape(flat),
        near,
        near_p.reshape(flat),
        regions.reshape(flat[1:]),
        reg_p.reshape(flat[1:]),
        *strips,
        strips_first,
        strips_second,
    )
    return out.reshape(magnetization.shape)


def solution(mesh):
    placed = (P("img", None, None, "gy", "gx"), P(), P(), P(None, "gy", "gx"), P(), P())
    return jax.shard_map(
        body,
        mesh=mesh,
        in_specs=placed,
        out_specs=P("img", None, None, "gy", "gx"),
        check_vma=False,
    )
```

```python
import functools

import jax
import jax.numpy as jnp
from jax import lax
from jax.experimental import pallas as pl
from jax.experimental.pallas import tpu as pltpu
from jax.sharding import PartitionSpec as P

STEPS = 4
DEPTH = 2 * STEPS

eps = 1e-06
time_step = 0.05

SUB = 8
LANES = 128
COMPS = 3
ROWS = 4


def lane_iota():
    return lax.broadcasted_iota(jnp.int32, (SUB, LANES), 1)


def sub_iota():
    return lax.broadcasted_iota(jnp.int32, (SUB, LANES), 0)


def rows_at(ny, tiles, y, t):
    return pl.ds(y + ny * t, SUB, stride=ny * tiles)


def pack_kernel(
    ny, tiles, regions, lower_ref, aniso_ref, damp_ref, share_ref, m_ref, reg_ref, both_ref, info_ref
):
    here = lax.axis_index("img")
    lane = lane_iota()
    block = lane // DEPTH

    def pack(i, carry):
        done = []
        for u in range(2):
            y = 2 * i + u
            shift = (DEPTH * (y + 1)) & (LANES - 1)
            left = block == ((y + 1) & (ny - 1))
            right = block == y
            for t in range(tiles):
                rows = rows_at(ny, tiles, y, t)
                for c in range(COMPS + 1):
                    cells = m_ref[c, rows, :] if c < COMPS else reg_ref[rows, :].astype(jnp.float32)
                    done.append((c, t, left, right, pltpu.roll(cells, shift, 1)))
        for c, t, left, right, cells in done:
            pltpu.store(both_ref.at[0, c, t], cells, mask=left)
            pltpu.store(both_ref.at[1, c, t], cells, mask=right)
        return carry

    lax.fori_loop(0, ny // 2, pack, 0)

    table_a = jnp.zeros((SUB, LANES), jnp.float32)
    table_d = jnp.zeros((SUB, LANES), jnp.float32)
    for i in range(regions):
        table_a = jnp.where(lane == i, 2.0 * aniso_ref[i], table_a)
        table_d = jnp.where(lane == i, damp_ref[i], table_d)
    info_ref[0] = table_a
    info_ref[1] = table_d
    info_ref[2] = -time_step / (1.0 + table_d * table_d)
    share = share_ref[...]
    spot = lax.broadcasted_iota(jnp.int32, share.shape, 1)
    target = jnp.sum(jnp.where(spot < here, share, 0.0), axis=1, keepdims=True) / jnp.sum(
        share, axis=1, keepdims=True
    )
    info_ref[3] = jnp.broadcast_to(target, (SUB, LANES))
    info_ref[4] = jnp.full((SUB, LANES), lower_ref[here].astype(jnp.float32))


def sort_kernel(both_ref, both_p_ref, left_ref, right_ref):
    for g, ref in enumerate((both_ref, both_p_ref)):
        left_ref[g] = ref[0]
        right_ref[g] = ref[1]


def merge_kernel(left_ref, right_ref, out_ref):
    for g in range(2):
        out_ref[0, g] = left_ref[g, :COMPS]
        out_ref[1, g] = right_ref[g, :COMPS]


def take_first(info_ref, here):
    odd = (here & 1) == 1
    below = info_ref[4] < here.astype(jnp.float32)
    return jnp.where(below, jnp.where(odd, 1, 0), jnp.where(odd, 0, 1)) == 1, odd


def gather_kernel(info_ref, m_ref, first_ref, second_ref, part_ref, near_ref):
    here = lax.axis_index("img")
    pick, odd = take_first(info_ref, here)
    chunks = 4

    def squares(i, sums):
        sums = list(sums)
        done = []
        for u in range(chunks):
            rows = pl.ds(pl.multiple_of((chunks * i + u) * SUB, SUB), SUB)
            for c in range(COMPS):
                one = first_ref[c, rows, :]
                two = second_ref[c, rows, :]
                done.append((c, rows, jnp.where(pick, one, two)))
                diff = m_ref[c, rows, :] - jnp.where(odd, one, two)
                sums[c + COMPS * u] = sums[c + COMPS * u] + diff * diff
        for c, rows, cells in done:
            near_ref[c, rows, :] = cells
        return tuple(sums)

    zero = jnp.zeros((SUB, LANES), jnp.float32)
    sums = lax.fori_loop(0, m_ref.shape[1] // (chunks * SUB), squares, (zero,) * (chunks * COMPS))
    total = jnp.sum(functools.reduce(jnp.add, sums), axis=(0, 1), keepdims=True)
    slot = lax.broadcasted_iota(jnp.int32, part_ref.shape, 1)
    part_ref[...] = jnp.where((slot == here) & (here > 0), total, 0.0)


def turn(m, h, a2, b, sc):
    mx, my, mz = m
    hx, hy, hz = h
    hz = hz + a2 * mz
    gx = hx + b * (my * hz - mz * hy)
    gy = hy + b * (mz * hx - mx * hz)
    gz = hz + b * (mx * hy - my * hx)
    return (
        sc * (my * gz - mz * gy),
        sc * (mz * gx - mx * gz),
        sc * (mx * gy - my * gx),
    )


def normal(v):
    scale = lax.rsqrt(v[0] * v[0] + v[1] * v[1] + v[2] * v[2])
    return tuple(x * scale for x in v)


def evolve_kernel(
    ny,
    tiles,
    images,
    info_ref,
    sq_ref,
    m_ref,
    mp_ref,
    n_ref,
    np_ref,
    reg_ref,
    regp_ref,
    left_ref,
    right_ref,
    first_ref,
    second_ref,
    out_ref,
    main0,
    main1,
    strip0,
    strip1,
    edge,
    seam0,
    seam1,
    par,
    spar,
):
    main, strip, seam = (main0, main1), (strip0, strip1), (seam0, seam1)
    window = ny + 2 * DEPTH
    here = lax.axis_index("img")
    lane = lane_iota()
    sub = sub_iota()
    block = lane // DEPTH
    first_lane = lane == 0
    last_lane = lane == LANES - 1
    head_lane = lane % DEPTH == 0
    tail_lane = lane % DEPTH == DEPTH - 1
    top = sub == SUB - 1
    bottom = sub == 0

    pick, _ = take_first(info_ref, here)
    lo = info_ref[4]
    slot = lane.astype(jnp.float32)
    squares = jnp.broadcast_to(jnp.sum(sq_ref[...], axis=0, keepdims=True), (SUB, LANES))
    lengths = jnp.where((lane >= 1) & (lane < images), jnp.sqrt(squares + eps), 0.0)
    total = jnp.sum(lengths, axis=1, keepdims=True)
    arc = jnp.sum(jnp.where(slot <= lo, lengths, 0.0), axis=1, keepdims=True)
    gap = jnp.sum(jnp.where(slot == lo + 1.0, lengths, 0.0), axis=1, keepdims=True)
    weight = jnp.clip((info_ref[3] * total - arc) / gap, -0.5, 1.5)
    below = lo < here.astype(jnp.float32)
    w_own = jnp.where(below, weight, 1.0 - weight)
    w_near = jnp.where(below, 1.0 - weight, weight)

    tables = (info_ref[0], info_ref[1], info_ref[2])

    def params(region):
        return [jnp.take_along_axis(table, region, axis=1) for table in tables]

    def ends_of(k, new):
        shift = (DEPTH * (k + 1)) & (LANES - 1)
        return [pltpu.roll(new[c], shift, 1) for c in range(COMPS)]

    def fill(k, carry):
        done = []
        for g, (own, near, reg) in enumerate(((m_ref, n_ref, reg_ref), (mp_ref, np_ref, regp_ref))):
            for t in range(tiles):
                rows = rows_at(ny, tiles, k, t)
                v = normal(
                    [w_own * own[c, rows, :] + w_near * near[c, rows, :] for c in range(COMPS)]
                )
                done.append((g * ny + k, t, v, params(reg[rows, :])))
        for r, t, v, p in done:
            for c in range(COMPS):
                main0[c, r, t] = v[c]
            for i in range(3):
                par[i, r, t] = p[i]
        return carry

    lax.fori_loop(0, ny, fill, 0)

    def seam_of(left, right):
        return jnp.where(head_lane, pltpu.roll(left, 1, 1), pltpu.roll(right, LANES - 1, 1))

    def fill_strips(t, carry):
        done = []
        for g in range(2):
            for side, cells in enumerate((left_ref, right_ref)):
                near = [
                    jnp.where(pick, first_ref[side, g, c, t], second_ref[side, g, c, t])
                    for c in range(COMPS)
                ]
                v = normal([w_own * cells[g, c, t] + w_near * near[c] for c in range(COMPS)])
                done.append((side, g, v, params(cells[g, COMPS, t].astype(jnp.int32))))
        for side, g, v, p in done:
            for c in range(COMPS):
                strip0[c, side, g, t] = v[c]
            for i in range(3):
                spar[i, side, g, t] = p[i]
        for g in range(2):
            left, right = (v for _, h, v, _ in done if h == g)
            for c in range(COMPS):
                seam0[c, g, t] = seam_of(left[c], right[c])
        return carry

    lax.fori_loop(0, tiles, fill_strips, 0)

    def around_z(cells, t):
        if t + 1 < tiles:
            above = cells[t + 1]
        else:
            above = jnp.where(top, 0.0, pltpu.roll(cells[0], SUB - 1, 0))
        if t > 0:
            under = cells[t - 1]
        else:
            under = jnp.where(bottom, 0.0, pltpu.roll(cells[tiles - 1], 1, 0))
        return above + under

    def main_row(state, r):
        g = r // ny
        k = r & (ny - 1)
        after = (r + 1) & (window - 1)
        before = (r - 1) & (window - 1)
        shift = (LANES - DEPTH * (k + 1)) & (LANES - 1)
        center = [[main[state][c, r, t] for t in range(tiles)] for c in range(COMPS)]
        done = []
        for t in range(tiles):
            h = []
            for c in range(COMPS):
                cells = center[c][t]
                ends = pltpu.roll(seam[state][c, g, t], shift, 1)
                s = jnp.where(first_lane, ends, pltpu.roll(cells, 1, 1))
                s = s + jnp.where(last_lane, ends, pltpu.roll(cells, LANES - 1, 1))
                s = s + (main[state][c, after, t] + main[state][c, before, t])
                h.append(s + around_z(center[c], t))
            m = [center[c][t] for c in range(COMPS)]
            rate = turn(m, h, par[0, r, t], par[1, r, t], par[2, r, t])
            if state == 0:
                new = [m[c] + rate[c] for c in range(COMPS)]
            else:
                new = normal([main[0][c, r, t] + (m[c] + rate[c]) for c in range(COMPS)])
            done.append((r, t, new, ends_of(k, m)))
        return done

    def strip_rows(state):
        done = []
        for g in range(2):
            for side in range(2):
                start = block == side
                stop = block == (side + ny - 1) % ny
                center = [[strip[state][c, side, g, t] for t in range(tiles)] for c in range(COMPS)]
                for t in range(tiles):
                    h = []
                    for c in range(COMPS):
                        cells = center[c][t]
                        inner = edge[c, g, t]
                        other = strip[state][c, side, 1 - g, t]
                        if side == 0:
                            s = pltpu.roll(cells, 1, 1)
                            s = s + pltpu.roll(jnp.where(head_lane, inner, cells), LANES - 1, 1)
                        else:
                            s = pltpu.roll(jnp.where(tail_lane, inner, cells), 1, 1)
                            s = s + pltpu.roll(cells, LANES - 1, 1)
                        s = s + pltpu.roll(jnp.where(start, other, cells), LANES - DEPTH, 1)
                        s = s + pltpu.roll(jnp.where(stop, other, cells), DEPTH, 1)
                        h.append(s + around_z(center[c], t))
                    m = [center[c][t] for c in range(COMPS)]
                    rate = turn(
                        m, h, spar[0, side, g, t], spar[1, side, g, t], spar[2, side, g, t]
                    )
                    if state == 0:
                        new = [m[c] + rate[c] for c in range(COMPS)]
                    else:
                        new = normal(
                            [strip[0][c, side, g, t] + (m[c] + rate[c]) for c in range(COMPS)]
                        )
                    done.append((side, g, t, new))
        for side, g, t, new in done:
            for c in range(COMPS):
                strip[1 - state][c, side, g, t] = new[c]
        for g in range(2):
            for t in range(tiles):
                left, right = (new for _, h, u, new in done if (h, u) == (g, t))
                for c in range(COMPS):
                    seam[1 - state][c, g, t] = seam_of(left[c], right[c])

    def main_rows(state, first, count):
        def rows(i, carry):
            done = []
            for u in range(ROWS):
                done += main_row(state, (first + ROWS * i + u) & (window - 1))
            for r, t, new, ends in done:
                k = r & (ny - 1)
                mask = ((lane - (DEPTH * k + DEPTH - 1)) & (LANES - 1)) < 2
                for c in range(COMPS):
                    main[1 - state][c, r, t] = new[c]
                    pltpu.store(edge.at[c, r // ny, t], ends[c], mask=mask)
            return carry

        lax.fori_loop(0, count // ROWS, rows, 0)

    def step(i, carry):
        for state in range(2):
            margin = DEPTH - 2 * state - 2 * i
            main_rows(state, -margin, ny + 2 * margin)
            strip_rows(state)
        return carry

    lax.fori_loop(0, STEPS, step, 0)

    def hand_out(k, carry):
        for t in range(tiles):
            for c in range(COMPS):
                out_ref[c, rows_at(ny, tiles, k, t), :] = main[0][c, k, t]
        return carry

    lax.fori_loop(0, ny, hand_out, 0)


def shifted(cells, axis, step, closed):
    count = lax.axis_size(axis)
    pairs = [(i, (i + step) % count) for i in range(count) if closed or 0 <= i + step < count]
    return lax.ppermute(cells, axis, pairs)


def swapped(cells, axis, first):
    count = lax.axis_size(axis)
    pairs = [(i, i + 1) for i in range(first, count - 1, 2)]
    return lax.ppermute(cells, axis, pairs + [(j, i) for i, j in pairs])


def around(cells, dim):
    ny = cells.shape[dim]
    if lax.axis_size("gy") == 2:
        return shifted(cells, "gy", 1, True)
    head = lax.slice_in_dim(cells, 0, DEPTH, axis=dim)
    tail = lax.slice_in_dim(cells, ny - DEPTH, ny, axis=dim)
    return jnp.concatenate([shifted(head, "gy", -1, True), shifted(tail, "gy", 1, True)], axis=dim)


def around_strips(both):
    if lax.axis_size("gy") == 2:
        return shifted(both, "gy", 1, True)
    block = lax.broadcasted_iota(jnp.int32, both.shape, both.ndim - 1) // DEPTH
    side = lax.broadcasted_iota(jnp.int32, both.shape, 0)
    head = (block + side - 1) % (LANES // DEPTH) < DEPTH
    return jnp.where(head, shifted(both, "gy", -1, True), shifted(both, "gy", 1, True))


def body(magnetization, lower_image, image_weights, regions, anisotropy, damping):
    local, comps, nz, ny, nx = magnetization.shape
    images = local * lax.axis_size("img")
    tiles = nz // SUB
    devices = lax.axis_size(("img", "gx", "gy"))
    assert local == 1 and comps == COMPS and nx == LANES
    assert ny == 2 * DEPTH and ny * DEPTH == LANES and tiles >= 2
    flat = (comps, nz * ny, nx)
    own = magnetization[0]
    first = swapped(own, "img", 0)
    second = swapped(own, "img", 1)
    own_p = around(own, 2)

    smem = pl.BlockSpec(memory_space=pltpu.SMEM)
    vmem = pl.BlockSpec(memory_space=pltpu.VMEM)
    f32 = jnp.float32
    small = pl.CostEstimate(flops=1000, bytes_accessed=1000, transcendentals=0)
    limit = pltpu.CompilerParams(vmem_limit_bytes=32 * 1024 * 1024)
    vreg = (SUB, LANES)
    both, info = pl.pallas_call(
        functools.partial(pack_kernel, ny, tiles, anisotropy.shape[0]),
        out_shape=(
            jax.ShapeDtypeStruct((2, comps + 1, tiles) + vreg, f32),
            jax.ShapeDtypeStruct((5,) + vreg, f32),
        ),
        in_specs=[smem] * 3 + [vmem] * 3,
        out_specs=(vmem,) * 2,
        compiler_params=limit,
        cost_estimate=small,
        name="pack_strips",
    )(
        lower_image,
        anisotropy,
        damping,
        image_weights.reshape(1, -1),
        own.reshape(flat),
        regions.reshape(flat[1:]),
    )
    both_p = around_strips(both)
    reg_p = around(regions, 1)
    left, right = pl.pallas_call(
        sort_kernel,
        out_shape=(jax.ShapeDtypeStruct((2, comps + 1, tiles) + vreg, f32),) * 2,
        in_specs=[vmem] * 2,
        out_specs=(vmem,) * 2,
        compiler_params=limit,
        cost_estimate=small,
        name="sort_strips",
    )(both, both_p)
    strips = (shifted(right, "gx", 1, True), shifted(left, "gx", -1, True))
    strips_all = pl.pallas_call(
        merge_kernel,
        out_shape=jax.ShapeDtypeStruct((2, 2, comps, tiles) + vreg, f32),
        in_specs=[vmem] * 2,
        out_specs=vmem,
        compiler_params=limit,
        cost_estimate=small,
        name="merge_strips",
    )(*strips)
    strips_first = swapped(strips_all, "img", 0)
    strips_second = swapped(strips_all, "img", 1)
    info, own_p, _ = lax.optimization_barrier((info, own_p, left))
    part, near = pl.pallas_call(
        gather_kernel,
        out_shape=(jax.ShapeDtypeStruct((devices, LANES), f32), jax.ShapeDtypeStruct(flat, f32)),
        in_specs=[vmem] * 4,
        out_specs=(vmem,) * 2,
        compiler_params=limit,
        cost_estimate=small,
        name="gather_images",
    )(info, own.reshape(flat), first.reshape(flat), second.reshape(flat))
    near_p = around(near.reshape(own.shape), 2)
    squares = lax.all_to_all(part, ("img", "gx", "gy"), 0, 0, tiled=True)

    window = ny + 2 * DEPTH
    out = pl.pallas_call(
        functools.partial(evolve_kernel, ny, tiles, images),
        out_shape=jax.ShapeDtypeStruct(flat, f32),
        in_specs=[vmem] * 12,
        out_specs=vmem,
        scratch_shapes=[
            pltpu.VMEM((comps, window, tiles) + vreg, f32),
            pltpu.VMEM((comps, window, tiles) + vreg, f32),
            pltpu.VMEM((comps, 2, 2, tiles) + vreg, f32),
            pltpu.VMEM((comps, 2, 2, tiles) + vreg, f32),
            pltpu.VMEM((comps, 2, tiles) + vreg, f32),
            pltpu.VMEM((comps, 2, tiles) + vreg, f32),
            pltpu.VMEM((comps, 2, tiles) + vreg, f32),
            pltpu.VMEM((3, window, tiles) + vreg, f32),
            pltpu.VMEM((3, 2, 2, tiles) + vreg, f32),
        ],
        compiler_params=limit,
        name="evolve",
    )(
        info,
        squares,
        own.reshape(flat),
        own_p.reshape(flat),
        near,
        near_p.reshape(flat),
        regions.reshape(flat[1:]),
        reg_p.reshape(flat[1:]),
        *strips,
        strips_first,
        strips_second,
    )
    return out.reshape(magnetization.shape)


def solution(mesh):
    placed = (P("img", None, None, "gy", "gx"), P(), P(), P(None, "gy", "gx"), P(), P())
    return jax.shard_map(
        body,
        mesh=mesh,
        in_specs=placed,
        out_specs=P("img", None, None, "gy", "gx"),
        check_vma=False,
    )
```

```python
import functools

import jax
import jax.numpy as jnp
from jax import lax
from jax.experimental import pallas as pl
from jax.experimental.pallas import tpu as pltpu
from jax.sharding import PartitionSpec as P

STEPS = 4
DEPTH = 2 * STEPS

eps = 1e-06
time_step = 0.05

SUB = 8
LANES = 128
COMPS = 3
ROWS = 4


def lane_iota():
    return lax.broadcasted_iota(jnp.int32, (SUB, LANES), 1)


def sub_iota():
    return lax.broadcasted_iota(jnp.int32, (SUB, LANES), 0)


def rows_at(ny, tiles, y, t):
    return pl.ds(y + ny * t, SUB, stride=ny * tiles)


def pack_kernel(
    ny, tiles, regions, lower_ref, aniso_ref, damp_ref, share_ref, m_ref, reg_ref, both_ref, info_ref
):
    here = lax.axis_index("img")
    lane = lane_iota()
    block = lane // DEPTH
    def pack(i, carry):
        done = []
        for u in range(2):
            y = 2 * i + u
            shift = (DEPTH * (y + 1)) & (LANES - 1)
            left = block == ((y + 1) & (ny - 1))
            right = block == y
            for t in range(tiles):
                rows = rows_at(ny, tiles, y, t)
                for c in range(COMPS + 1):
                    cells = m_ref[c, rows, :] if c < COMPS else reg_ref[rows, :].astype(jnp.float32)
                    done.append((c, t, left, right, pltpu.roll(cells, shift, 1)))
        for c, t, left, right, cells in done:
            pltpu.store(both_ref.at[0, c, t], cells, mask=left)
            pltpu.store(both_ref.at[1, c, t], cells, mask=right)
        return carry

    table_a = jnp.zeros((SUB, LANES), jnp.float32)
    table_d = jnp.zeros((SUB, LANES), jnp.float32)
    for i in range(regions):
        table_a = jnp.where(lane == i, 2.0 * aniso_ref[i], table_a)
        table_d = jnp.where(lane == i, damp_ref[i], table_d)
    info_ref[0] = table_a
    info_ref[1] = table_d
    info_ref[2] = -time_step / (1.0 + table_d * table_d)
    share = share_ref[...]
    spot = lax.broadcasted_iota(jnp.int32, share.shape, 1)
    target = jnp.sum(jnp.where(spot < here, share, 0.0), axis=1, keepdims=True) / jnp.sum(
        share, axis=1, keepdims=True
    )
    info_ref[3] = jnp.broadcast_to(target, (SUB, LANES))
    info_ref[4] = jnp.full((SUB, LANES), lower_ref[here].astype(jnp.float32))

    lax.fori_loop(0, ny // 2, pack, 0)


def sort_kernel(both_ref, both_p_ref, left_ref, right_ref):
    for g, ref in enumerate((both_ref, both_p_ref)):
        left_ref[g] = ref[0]
        right_ref[g] = ref[1]


def merge_kernel(info_ref, left_ref, right_ref, out_ref, info_out_ref):
    info_out_ref[...] = info_ref[...]
    for g in range(2):
        out_ref[0, g] = left_ref[g, :COMPS]
        out_ref[1, g] = right_ref[g, :COMPS]


def take_first(info_ref, here):
    odd = (here & 1) == 1
    below = info_ref[4] < here.astype(jnp.float32)
    return jnp.where(below, jnp.where(odd, 1, 0), jnp.where(odd, 0, 1)) == 1, odd


def gather_kernel(info_ref, m_ref, first_ref, second_ref, part_ref, near_ref):
    here = lax.axis_index("img")
    pick, odd = take_first(info_ref, here)
    chunks = 4

    def squares(i, sums):
        sums = list(sums)
        done = []
        for u in range(chunks):
            rows = pl.ds(pl.multiple_of((chunks * i + u) * SUB, SUB), SUB)
            for c in range(COMPS):
                one = first_ref[c, rows, :]
                two = second_ref[c, rows, :]
                done.append((c, rows, jnp.where(pick, one, two)))
                diff = m_ref[c, rows, :] - jnp.where(odd, one, two)
                sums[c + COMPS * u] = sums[c + COMPS * u] + diff * diff
        for c, rows, cells in done:
            near_ref[c, rows, :] = cells
        return tuple(sums)

    zero = jnp.zeros((SUB, LANES), jnp.float32)
    sums = lax.fori_loop(0, m_ref.shape[1] // (chunks * SUB), squares, (zero,) * (chunks * COMPS))
    total = jnp.sum(functools.reduce(jnp.add, sums), axis=(0, 1), keepdims=True)
    slot = lax.broadcasted_iota(jnp.int32, part_ref.shape, 1)
    part_ref[...] = jnp.where((slot == here) & (here > 0), total, 0.0)


def turn(m, h, a2, b, sc):
    mx, my, mz = m
    hx, hy, hz = h
    hz = hz + a2 * mz
    gx = hx + b * (my * hz - mz * hy)
    gy = hy + b * (mz * hx - mx * hz)
    gz = hz + b * (mx * hy - my * hx)
    return (
        sc * (my * gz - mz * gy),
        sc * (mz * gx - mx * gz),
        sc * (mx * gy - my * gx),
    )


def normal(v):
    scale = lax.rsqrt(v[0] * v[0] + v[1] * v[1] + v[2] * v[2])
    return tuple(x * scale for x in v)


def evolve_kernel(
    ny,
    tiles,
    images,
    info_ref,
    sq_ref,
    m_ref,
    mp_ref,
    n_ref,
    np_ref,
    reg_ref,
    regp_ref,
    left_ref,
    right_ref,
    first_ref,
    second_ref,
    out_ref,
    main0,
    main1,
    strip0,
    strip1,
    edge,
    seam0,
    seam1,
    par,
    spar,
):
    main, strip, seam = (main0, main1), (strip0, strip1), (seam0, seam1)
    window = ny + 2 * DEPTH
    here = lax.axis_index("img")
    lane = lane_iota()
    sub = sub_iota()
    block = lane // DEPTH
    first_lane = lane == 0
    last_lane = lane == LANES - 1
    head_lane = lane % DEPTH == 0
    tail_lane = lane % DEPTH == DEPTH - 1
    top = sub == SUB - 1
    bottom = sub == 0

    pick, _ = take_first(info_ref, here)
    lo = info_ref[4]
    slot = lane.astype(jnp.float32)
    squares = jnp.broadcast_to(jnp.sum(sq_ref[...], axis=0, keepdims=True), (SUB, LANES))
    lengths = jnp.where((lane >= 1) & (lane < images), jnp.sqrt(squares + eps), 0.0)
    total = jnp.sum(lengths, axis=1, keepdims=True)
    arc = jnp.sum(jnp.where(slot <= lo, lengths, 0.0), axis=1, keepdims=True)
    gap = jnp.sum(jnp.where(slot == lo + 1.0, lengths, 0.0), axis=1, keepdims=True)
    weight = jnp.clip((info_ref[3] * total - arc) / gap, -0.5, 1.5)
    below = lo < here.astype(jnp.float32)
    w_own = jnp.where(below, weight, 1.0 - weight)
    w_near = jnp.where(below, 1.0 - weight, weight)

    tables = (info_ref[0], info_ref[1], info_ref[2])

    def params(region):
        return [jnp.take_along_axis(table, region, axis=1) for table in tables]

    def ends_of(k, new):
        shift = (DEPTH * (k + 1)) & (LANES - 1)
        return [pltpu.roll(new[c], shift, 1) for c in range(COMPS)]

    def fill(k, carry):
        done = []
        for g, (own, near, reg) in enumerate(((m_ref, n_ref, reg_ref), (mp_ref, np_ref, regp_ref))):
            for t in range(tiles):
                rows = rows_at(ny, tiles, k, t)
                v = normal(
                    [w_own * own[c, rows, :] + w_near * near[c, rows, :] for c in range(COMPS)]
                )
                done.append((g * ny + k, t, v, params(reg[rows, :])))
        for r, t, v, p in done:
            for c in range(COMPS):
                main0[c, r, t] = v[c]
            for i in range(3):
                par[i, r, t] = p[i]
        return carry

    lax.fori_loop(0, ny, fill, 0)

    def seam_of(left, right):
        return jnp.where(head_lane, pltpu.roll(left, 1, 1), pltpu.roll(right, LANES - 1, 1))

    def fill_strips(t, carry):
        done = []
        for g in range(2):
            for side, cells in enumerate((left_ref, right_ref)):
                near = [
                    jnp.where(pick, first_ref[side, g, c, t], second_ref[side, g, c, t])
                    for c in range(COMPS)
                ]
                v = normal([w_own * cells[g, c, t] + w_near * near[c] for c in range(COMPS)])
                done.append((side, g, v, params(cells[g, COMPS, t].astype(jnp.int32))))
        for side, g, v, p in done:
            for c in range(COMPS):
                strip0[c, side, g, t] = v[c]
            for i in range(3):
                spar[i, side, g, t] = p[i]
        for g in range(2):
            left, right = (v for _, h, v, _ in done if h == g)
            for c in range(COMPS):
                seam0[c, g, t] = seam_of(left[c], right[c])
        return carry

    lax.fori_loop(0, tiles, fill_strips, 0)

    def around_z(cells, t):
        if t + 1 < tiles:
            above = cells[t + 1]
        else:
            above = jnp.where(top, 0.0, pltpu.roll(cells[0], SUB - 1, 0))
        if t > 0:
            under = cells[t - 1]
        else:
            under = jnp.where(bottom, 0.0, pltpu.roll(cells[tiles - 1], 1, 0))
        return above + under

    def main_row(state, r):
        g = r // ny
        k = r & (ny - 1)
        after = (r + 1) & (window - 1)
        before = (r - 1) & (window - 1)
        shift = (LANES - DEPTH * (k + 1)) & (LANES - 1)
        center = [[main[state][c, r, t] for t in range(tiles)] for c in range(COMPS)]
        done = []
        for t in range(tiles):
            h = []
            for c in range(COMPS):
                cells = center[c][t]
                ends = pltpu.roll(seam[state][c, g, t], shift, 1)
                s = jnp.where(first_lane, ends, pltpu.roll(cells, 1, 1))
                s = s + jnp.where(last_lane, ends, pltpu.roll(cells, LANES - 1, 1))
                s = s + (main[state][c, after, t] + main[state][c, before, t])
                h.append(s + around_z(center[c], t))
            m = [center[c][t] for c in range(COMPS)]
            rate = turn(m, h, par[0, r, t], par[1, r, t], par[2, r, t])
            if state == 0:
                new = [m[c] + rate[c] for c in range(COMPS)]
            else:
                new = normal([main[0][c, r, t] + (m[c] + rate[c]) for c in range(COMPS)])
            done.append((r, t, new, ends_of(k, m)))
        return done

    def strip_rows(state):
        done = []
        for g in range(2):
            for side in range(2):
                start = block == side
                stop = block == (side + ny - 1) % ny
                center = [[strip[state][c, side, g, t] for t in range(tiles)] for c in range(COMPS)]
                for t in range(tiles):
                    h = []
                    for c in range(COMPS):
                        cells = center[c][t]
                        inner = edge[c, g, t]
                        other = strip[state][c, side, 1 - g, t]
                        if side == 0:
                            s = pltpu.roll(cells, 1, 1)
                            s = s + pltpu.roll(jnp.where(head_lane, inner, cells), LANES - 1, 1)
                        else:
                            s = pltpu.roll(jnp.where(tail_lane, inner, cells), 1, 1)
                            s = s + pltpu.roll(cells, LANES - 1, 1)
                        s = s + pltpu.roll(jnp.where(start, other, cells), LANES - DEPTH, 1)
                        s = s + pltpu.roll(jnp.where(stop, other, cells), DEPTH, 1)
                        h.append(s + around_z(center[c], t))
                    m = [center[c][t] for c in range(COMPS)]
                    rate = turn(
                        m, h, spar[0, side, g, t], spar[1, side, g, t], spar[2, side, g, t]
                    )
                    if state == 0:
                        new = [m[c] + rate[c] for c in range(COMPS)]
                    else:
                        new = normal(
                            [strip[0][c, side, g, t] + (m[c] + rate[c]) for c in range(COMPS)]
                        )
                    done.append((side, g, t, new))
        for side, g, t, new in done:
            for c in range(COMPS):
                strip[1 - state][c, side, g, t] = new[c]
        for g in range(2):
            for t in range(tiles):
                left, right = (new for _, h, u, new in done if (h, u) == (g, t))
                for c in range(COMPS):
                    seam[1 - state][c, g, t] = seam_of(left[c], right[c])

    def main_rows(state, first, count):
        def rows(i, carry):
            done = []
            for u in range(ROWS):
                done += main_row(state, (first + ROWS * i + u) & (window - 1))
            for r, t, new, ends in done:
                k = r & (ny - 1)
                mask = ((lane - (DEPTH * k + DEPTH - 1)) & (LANES - 1)) < 2
                for c in range(COMPS):
                    main[1 - state][c, r, t] = new[c]
                    pltpu.store(edge.at[c, r // ny, t], ends[c], mask=mask)
            return carry

        lax.fori_loop(0, count // ROWS, rows, 0)

    def step(i, carry):
        for state in range(2):
            margin = DEPTH - 2 * state - 2 * i
            main_rows(state, -margin, ny + 2 * margin)
            strip_rows(state)
        return carry

    lax.fori_loop(0, STEPS, step, 0)

    def hand_out(k, carry):
        for t in range(tiles):
            for c in range(COMPS):
                out_ref[c, rows_at(ny, tiles, k, t), :] = main[0][c, k, t]
        return carry

    lax.fori_loop(0, ny, hand_out, 0)


def shifted(cells, axis, step, closed):
    count = lax.axis_size(axis)
    pairs = [(i, (i + step) % count) for i in range(count) if closed or 0 <= i + step < count]
    return lax.ppermute(cells, axis, pairs)


def swapped(cells, axis, first):
    count = lax.axis_size(axis)
    pairs = [(i, i + 1) for i in range(first, count - 1, 2)]
    return lax.ppermute(cells, axis, pairs + [(j, i) for i, j in pairs])


def around(cells, dim):
    ny = cells.shape[dim]
    if lax.axis_size("gy") == 2:
        return shifted(cells, "gy", 1, True)
    head = lax.slice_in_dim(cells, 0, DEPTH, axis=dim)
    tail = lax.slice_in_dim(cells, ny - DEPTH, ny, axis=dim)
    return jnp.concatenate([shifted(head, "gy", -1, True), shifted(tail, "gy", 1, True)], axis=dim)


def around_strips(both):
    if lax.axis_size("gy") == 2:
        return shifted(both, "gy", 1, True)
    block = lax.broadcasted_iota(jnp.int32, both.shape, both.ndim - 1) // DEPTH
    side = lax.broadcasted_iota(jnp.int32, both.shape, 0)
    head = (block + side - 1) % (LANES // DEPTH) < DEPTH
    return jnp.where(head, shifted(both, "gy", -1, True), shifted(both, "gy", 1, True))


def body(magnetization, lower_image, image_weights, regions, anisotropy, damping):
    local, comps, nz, ny, nx = magnetization.shape
    images = local * lax.axis_size("img")
    tiles = nz // SUB
    devices = lax.axis_size(("img", "gx", "gy"))
    assert local == 1 and comps == COMPS and nx == LANES
    assert ny == 2 * DEPTH and ny * DEPTH == LANES and tiles >= 2
    flat = (comps, nz * ny, nx)
    own = magnetization[0]
    first = swapped(own, "img", 0)
    second = swapped(own, "img", 1)
    reg_p = around(regions, 1)

    smem = pl.BlockSpec(memory_space=pltpu.SMEM)
    vmem = pl.BlockSpec(memory_space=pltpu.VMEM)
    f32 = jnp.float32
    limit = pltpu.CompilerParams(vmem_limit_bytes=32 * 1024 * 1024)
    vreg = (SUB, LANES)
    both, info = pl.pallas_call(
        functools.partial(pack_kernel, ny, tiles, anisotropy.shape[0]),
        out_shape=(
            jax.ShapeDtypeStruct((2, comps + 1, tiles) + vreg, f32),
            jax.ShapeDtypeStruct((5,) + vreg, f32),
        ),
        in_specs=[smem] * 3 + [vmem] * 3,
        out_specs=(vmem,) * 2,
        compiler_params=limit,
        name="pack_strips",
    )(
        lower_image,
        anisotropy,
        damping,
        image_weights.reshape(1, -1),
        own.reshape(flat),
        regions.reshape(flat[1:]),
    )
    both_p = around_strips(both)
    own_p = around(lax.optimization_barrier((own, both))[0], 2)
    both_p, reg_p = lax.optimization_barrier((both_p, reg_p))
    left, right = pl.pallas_call(
        sort_kernel,
        out_shape=(jax.ShapeDtypeStruct((2, comps + 1, tiles) + vreg, f32),) * 2,
        in_specs=[vmem] * 2,
        out_specs=(vmem,) * 2,
        compiler_params=limit,
        name="sort_strips",
    )(both, both_p)
    strips = (shifted(right, "gx", 1, True), shifted(left, "gx", -1, True))
    strips_all, info = pl.pallas_call(
        merge_kernel,
        out_shape=(
            jax.ShapeDtypeStruct((2, 2, comps, tiles) + vreg, f32),
            jax.ShapeDtypeStruct(info.shape, f32),
        ),
        in_specs=[vmem] * 3,
        out_specs=(vmem,) * 2,
        compiler_params=limit,
        name="merge_strips",
    )(info, *strips)
    strips_first = swapped(strips_all, "img", 0)
    strips_second = swapped(strips_all, "img", 1)
    part, near = pl.pallas_call(
        gather_kernel,
        out_shape=(jax.ShapeDtypeStruct((devices, LANES), f32), jax.ShapeDtypeStruct(flat, f32)),
        in_specs=[vmem] * 4,
        out_specs=(vmem,) * 2,
        compiler_params=limit,
        name="gather_images",
    )(info, own.reshape(flat), first.reshape(flat), second.reshape(flat))
    near_p = around(near.reshape(own.shape), 2)
    squares = lax.all_to_all(part, ("img", "gx", "gy"), 0, 0, tiled=True)

    window = ny + 2 * DEPTH
    out = pl.pallas_call(
        functools.partial(evolve_kernel, ny, tiles, images),
        out_shape=jax.ShapeDtypeStruct(flat, f32),
        in_specs=[vmem] * 12,
        out_specs=vmem,
        scratch_shapes=[
            pltpu.VMEM((comps, window, tiles) + vreg, f32),
            pltpu.VMEM((comps, window, tiles) + vreg, f32),
            pltpu.VMEM((comps, 2, 2, tiles) + vreg, f32),
            pltpu.VMEM((comps, 2, 2, tiles) + vreg, f32),
            pltpu.VMEM((comps, 2, tiles) + vreg, f32),
            pltpu.VMEM((comps, 2, tiles) + vreg, f32),
            pltpu.VMEM((comps, 2, tiles) + vreg, f32),
            pltpu.VMEM((3, window, tiles) + vreg, f32),
            pltpu.VMEM((3, 2, 2, tiles) + vreg, f32),
        ],
        compiler_params=limit,
        name="evolve",
    )(
        info,
        squares,
        own.reshape(flat),
        own_p.reshape(flat),
        near,
        near_p.reshape(flat),
        regions.reshape(flat[1:]),
        reg_p.reshape(flat[1:]),
        *strips,
        strips_first,
        strips_second,
    )
    return out.reshape(magnetization.shape)


def solution(mesh):
    placed = (P("img", None, None, "gy", "gx"), P(), P(), P(None, "gy", "gx"), P(), P())
    return jax.shard_map(
        body,
        mesh=mesh,
        in_specs=placed,
        out_specs=P("img", None, None, "gy", "gx"),
        check_vma=False,
    )
```

```python
import functools

import jax
import jax.numpy as jnp
from jax import lax
from jax.experimental import pallas as pl
from jax.experimental.pallas import tpu as pltpu
from jax.sharding import PartitionSpec as P

STEPS = 4
DEPTH = 2 * STEPS

eps = 1e-06
time_step = 0.05

SUB = 8
LANES = 128
COMPS = 3
ROWS = 4


def lane_iota():
    return lax.broadcasted_iota(jnp.int32, (SUB, LANES), 1)


def sub_iota():
    return lax.broadcasted_iota(jnp.int32, (SUB, LANES), 0)


def rows_at(ny, tiles, y, t, first=0):
    return pl.ds(first + y + ny * t, SUB, stride=ny * tiles)


def pack_kernel(
    ny, tiles, regions, lower_ref, aniso_ref, damp_ref, share_ref, m_ref, reg_ref, left_ref, right_ref, info_ref
):
    here = lax.axis_index("img")
    lane = lane_iota()
    block = lane // DEPTH
    def pack(i, carry):
        done = []
        for u in range(2):
            y = 2 * i + u
            shift = (DEPTH * (y + 1)) & (LANES - 1)
            left = block == ((y + 1) & (ny - 1))
            right = block == y
            for t in range(tiles):
                rows = rows_at(ny, tiles, y, t)
                for c in range(COMPS + 1):
                    cells = m_ref[c, rows, :] if c < COMPS else reg_ref[rows, :].astype(jnp.float32)
                    done.append((c, t, left, right, pltpu.roll(cells, shift, 1)))
        for c, t, left, right, cells in done:
            pltpu.store(left_ref.at[c, t], cells, mask=left)
            pltpu.store(right_ref.at[c, t], cells, mask=right)
        return carry

    table_a = jnp.zeros((SUB, LANES), jnp.float32)
    table_d = jnp.zeros((SUB, LANES), jnp.float32)
    for i in range(regions):
        table_a = jnp.where(lane == i, 2.0 * aniso_ref[i], table_a)
        table_d = jnp.where(lane == i, damp_ref[i], table_d)
    info_ref[0] = table_a
    info_ref[1] = table_d
    info_ref[2] = -time_step / (1.0 + table_d * table_d)
    share = share_ref[...]
    spot = lax.broadcasted_iota(jnp.int32, share.shape, 1)
    target = jnp.sum(jnp.where(spot < here, share, 0.0), axis=1, keepdims=True) / jnp.sum(
        share, axis=1, keepdims=True
    )
    info_ref[3] = jnp.broadcast_to(target, (SUB, LANES))
    info_ref[4] = jnp.full((SUB, LANES), lower_ref[here].astype(jnp.float32))

    lax.fori_loop(0, ny // 2, pack, 0)


def merge_kernel(info_ref, left_ref, right_ref, out_ref, info_out_ref):
    info_out_ref[...] = info_ref[...]
    out_ref[0] = left_ref[...]
    out_ref[1] = right_ref[...]


def take_first(info_ref, here):
    odd = (here & 1) == 1
    below = info_ref[4] < here.astype(jnp.float32)
    return jnp.where(below, jnp.where(odd, 1, 0), jnp.where(odd, 0, 1)) == 1, odd


def strip_rows_at(cells, tiles, part, c, t):
    row = cells + ((part * (COMPS + 1) + c) * tiles + t) * SUB
    return pl.ds(row if isinstance(t, int) else pl.multiple_of(row, SUB), SUB)


def gather_kernel(
    tiles, info_ref, m_ref, first_ref, second_ref, strips_ref, strips1_ref, strips2_ref, part_ref, near_ref
):
    here = lax.axis_index("img")
    pick, odd = take_first(info_ref, here)
    chunks = 4
    depth = m_ref.shape[1]

    def squares(i, sums):
        sums = list(sums)
        done = []
        for u in range(chunks):
            start = pl.multiple_of((chunks * i + u) * SUB, SUB)
            for c in range(COMPS):
                one = first_ref[c, pl.ds(start, SUB), :]
                two = second_ref[c, pl.ds(start, SUB), :]
                done.append((c * depth + start, jnp.where(pick, one, two)))
                diff = m_ref[c, pl.ds(start, SUB), :] - jnp.where(odd, one, two)
                sums[c + COMPS * u] = sums[c + COMPS * u] + diff * diff
        for start, cells in done:
            near_ref[pl.ds(pl.multiple_of(start, SUB), SUB), :] = cells
        return tuple(sums)

    zero = jnp.zeros((SUB, LANES), jnp.float32)
    sums = lax.fori_loop(0, depth // (chunks * SUB), squares, (zero,) * (chunks * COMPS))
    total = jnp.sum(functools.reduce(jnp.add, sums), axis=(0, 1), keepdims=True)
    slot = lax.broadcasted_iota(jnp.int32, part_ref.shape, 1)
    part_ref[...] = jnp.where((slot == here) & (here > 0), total, 0.0)
    for side in range(2):
        for c in range(COMPS + 1):
            for t in range(tiles):
                near_ref[strip_rows_at(COMPS * depth, tiles, side, c, t), :] = jnp.where(
                    pick, strips1_ref[side, c, t], strips2_ref[side, c, t]
                )
                near_ref[strip_rows_at(COMPS * depth, tiles, 2 + side, c, t), :] = strips_ref[side, c, t]


def turn(m, h, a2, b, sc):
    mx, my, mz = m
    hx, hy, hz = h
    hz = hz + a2 * mz
    gx = hx + b * (my * hz - mz * hy)
    gy = hy + b * (mz * hx - mx * hz)
    gz = hz + b * (mx * hy - my * hx)
    return (
        sc * (my * gz - mz * gy),
        sc * (mz * gx - mx * gz),
        sc * (mx * gy - my * gx),
    )


def normal(v):
    scale = lax.rsqrt(v[0] * v[0] + v[1] * v[1] + v[2] * v[2])
    return tuple(x * scale for x in v)


def evolve_kernel(
    ny,
    tiles,
    images,
    info_ref,
    sq_ref,
    m_ref,
    mp_ref,
    n_ref,
    np_ref,
    reg_ref,
    regp_ref,
    out_ref,
    main0,
    main1,
    strip0,
    strip1,
    edge,
    seam0,
    seam1,
    par,
    spar,
):
    main, strip, seam = (main0, main1), (strip0, strip1), (seam0, seam1)
    window = ny + 2 * DEPTH
    here = lax.axis_index("img")
    lane = lane_iota()
    sub = sub_iota()
    block = lane // DEPTH
    first_lane = lane == 0
    last_lane = lane == LANES - 1
    head_lane = lane % DEPTH == 0
    tail_lane = lane % DEPTH == DEPTH - 1
    top = sub == SUB - 1
    bottom = sub == 0

    lo = info_ref[4]
    slot = lane.astype(jnp.float32)
    squares = jnp.broadcast_to(jnp.sum(sq_ref[...], axis=0, keepdims=True), (SUB, LANES))
    lengths = jnp.where((lane >= 1) & (lane < images), jnp.sqrt(squares + eps), 0.0)
    total = jnp.sum(lengths, axis=1, keepdims=True)
    arc = jnp.sum(jnp.where(slot <= lo, lengths, 0.0), axis=1, keepdims=True)
    gap = jnp.sum(jnp.where(slot == lo + 1.0, lengths, 0.0), axis=1, keepdims=True)
    weight = jnp.clip((info_ref[3] * total - arc) / gap, -0.5, 1.5)
    below = lo < here.astype(jnp.float32)
    w_own = jnp.where(below, weight, 1.0 - weight)
    w_near = jnp.where(below, 1.0 - weight, weight)

    tables = (info_ref[0], info_ref[1], info_ref[2])

    def params(region):
        return [jnp.take_along_axis(table, region, axis=1) for table in tables]

    def ends_of(k, new):
        shift = (DEPTH * (k + 1)) & (LANES - 1)
        return [pltpu.roll(new[c], shift, 1) for c in range(COMPS)]

    depth = m_ref.shape[1]

    def fill(k, carry):
        done = []
        for g, (own, near, reg) in enumerate(((m_ref, n_ref, reg_ref), (mp_ref, np_ref, regp_ref))):
            for t in range(tiles):
                rows = rows_at(ny, tiles, k, t)
                v = normal(
                    [
                        w_own * own[c, rows, :] + w_near * near[rows_at(ny, tiles, k, t, c * depth), :]
                        for c in range(COMPS)
                    ]
                )
                done.append((g * ny + k, t, v, params(reg[rows, :])))
        for r, t, v, p in done:
            for c in range(COMPS):
                main0[c, r, t] = v[c]
            for i in range(3):
                par[i, r, t] = p[i]
        return carry

    lax.fori_loop(0, ny, fill, 0)

    def seam_of(left, right):
        return jnp.where(head_lane, pltpu.roll(left, 1, 1), pltpu.roll(right, LANES - 1, 1))

    def fill_strips(t, carry):
        done = []
        for g, cells in enumerate((n_ref, np_ref)):
            for side in range(2):
                near, own = (
                    [
                        cells[strip_rows_at(COMPS * depth, tiles, part, c, t), :]
                        for c in range(COMPS + 1)
                    ]
                    for part in (side, 2 + side)
                )
                v = normal([w_own * own[c] + w_near * near[c] for c in range(COMPS)])
                done.append((side, g, v, params(own[COMPS].astype(jnp.int32))))
        for side, g, v, p in done:
            for c in range(COMPS):
                strip0[c, side, g, t] = v[c]
            for i in range(3):
                spar[i, side, g, t] = p[i]
        for g in range(2):
            left, right = (v for _, h, v, _ in done if h == g)
            for c in range(COMPS):
                seam0[c, g, t] = seam_of(left[c], right[c])
        return carry

    lax.fori_loop(0, tiles, fill_strips, 0)

    def around_z(cells, t):
        if t + 1 < tiles:
            above = cells[t + 1]
        else:
            above = jnp.where(top, 0.0, pltpu.roll(cells[0], SUB - 1, 0))
        if t > 0:
            under = cells[t - 1]
        else:
            under = jnp.where(bottom, 0.0, pltpu.roll(cells[tiles - 1], 1, 0))
        return above + under

    def main_row(state, r):
        g = r // ny
        k = r & (ny - 1)
        after = (r + 1) & (window - 1)
        before = (r - 1) & (window - 1)
        shift = (LANES - DEPTH * (k + 1)) & (LANES - 1)
        center = [[main[state][c, r, t] for t in range(tiles)] for c in range(COMPS)]
        done = []
        for t in range(tiles):
            h = []
            for c in range(COMPS):
                cells = center[c][t]
                ends = pltpu.roll(seam[state][c, g, t], shift, 1)
                s = jnp.where(first_lane, ends, pltpu.roll(cells, 1, 1))
                s = s + jnp.where(last_lane, ends, pltpu.roll(cells, LANES - 1, 1))
                s = s + (main[state][c, after, t] + main[state][c, before, t])
                h.append(s + around_z(center[c], t))
            m = [center[c][t] for c in range(COMPS)]
            rate = turn(m, h, par[0, r, t], par[1, r, t], par[2, r, t])
            if state == 0:
                new = [m[c] + rate[c] for c in range(COMPS)]
            else:
                new = normal([main[0][c, r, t] + (m[c] + rate[c]) for c in range(COMPS)])
            done.append((r, t, new, ends_of(k, m)))
        return done

    def strip_rows(state):
        done = []
        for g in range(2):
            for side in range(2):
                start = block == side
                stop = block == (side + ny - 1) % ny
                center = [[strip[state][c, side, g, t] for t in range(tiles)] for c in range(COMPS)]
                for t in range(tiles):
                    h = []
                    for c in range(COMPS):
                        cells = center[c][t]
                        inner = edge[c, g, t]
                        other = strip[state][c, side, 1 - g, t]
                        if side == 0:
                            s = pltpu.roll(cells, 1, 1)
                            s = s + pltpu.roll(jnp.where(head_lane, inner, cells), LANES - 1, 1)
                        else:
                            s = pltpu.roll(jnp.where(tail_lane, inner, cells), 1, 1)
                            s = s + pltpu.roll(cells, LANES - 1, 1)
                        s = s + pltpu.roll(jnp.where(start, other, cells), LANES - DEPTH, 1)
                        s = s + pltpu.roll(jnp.where(stop, other, cells), DEPTH, 1)
                        h.append(s + around_z(center[c], t))
                    m = [center[c][t] for c in range(COMPS)]
                    rate = turn(
                        m, h, spar[0, side, g, t], spar[1, side, g, t], spar[2, side, g, t]
                    )
                    if state == 0:
                        new = [m[c] + rate[c] for c in range(COMPS)]
                    else:
                        new = normal(
                            [strip[0][c, side, g, t] + (m[c] + rate[c]) for c in range(COMPS)]
                        )
                    done.append((side, g, t, new))
        for side, g, t, new in done:
            for c in range(COMPS):
                strip[1 - state][c, side, g, t] = new[c]
        for g in range(2):
            for t in range(tiles):
                left, right = (new for _, h, u, new in done if (h, u) == (g, t))
                for c in range(COMPS):
                    seam[1 - state][c, g, t] = seam_of(left[c], right[c])

    def main_rows(state, first, count):
        def rows(i, carry):
            done = []
            for u in range(ROWS):
                done += main_row(state, (first + ROWS * i + u) & (window - 1))
            for r, t, new, ends in done:
                k = r & (ny - 1)
                mask = ((lane - (DEPTH * k + DEPTH - 1)) & (LANES - 1)) < 2
                for c in range(COMPS):
                    main[1 - state][c, r, t] = new[c]
                    pltpu.store(edge.at[c, r // ny, t], ends[c], mask=mask)
            return carry

        lax.fori_loop(0, count // ROWS, rows, 0)

    def step(i, carry):
        for state in range(2):
            margin = DEPTH - 2 * state - 2 * i
            main_rows(state, -margin, ny + 2 * margin)
            strip_rows(state)
        return carry

    lax.fori_loop(0, STEPS, step, 0)

    def hand_out(k, carry):
        for t in range(tiles):
            for c in range(COMPS):
                out_ref[c, rows_at(ny, tiles, k, t), :] = main[0][c, k, t]
        return carry

    lax.fori_loop(0, ny, hand_out, 0)


def shifted(cells, axis, step, closed):
    count = lax.axis_size(axis)
    pairs = [(i, (i + step) % count) for i in range(count) if closed or 0 <= i + step < count]
    return lax.ppermute(cells, axis, pairs)


def swapped(cells, axis, first):
    count = lax.axis_size(axis)
    pairs = [(i, i + 1) for i in range(first, count - 1, 2)]
    return lax.ppermute(cells, axis, pairs + [(j, i) for i, j in pairs])


def around(cells, dim):
    ny = cells.shape[dim]
    if lax.axis_size("gy") == 2:
        return shifted(cells, "gy", 1, True)
    head = lax.slice_in_dim(cells, 0, DEPTH, axis=dim)
    tail = lax.slice_in_dim(cells, ny - DEPTH, ny, axis=dim)
    return jnp.concatenate([shifted(head, "gy", -1, True), shifted(tail, "gy", 1, True)], axis=dim)


def around_strips(both):
    if lax.axis_size("gy") == 2:
        return shifted(both, "gy", 1, True)
    block = lax.broadcasted_iota(jnp.int32, both.shape, both.ndim - 1) // DEPTH
    side = lax.broadcasted_iota(jnp.int32, both.shape, 1)
    head = (block + side - 1) % (LANES // DEPTH) < DEPTH
    return jnp.where(head, shifted(both, "gy", -1, True), shifted(both, "gy", 1, True))


def body(magnetization, lower_image, image_weights, regions, anisotropy, damping):
    local, comps, nz, ny, nx = magnetization.shape
    images = local * lax.axis_size("img")
    tiles = nz // SUB
    devices = lax.axis_size(("img", "gx", "gy"))
    assert local == 1 and comps == COMPS and nx == LANES
    assert ny == 2 * DEPTH and ny * DEPTH == LANES and tiles >= 2
    flat = (comps, nz * ny, nx)
    own = magnetization[0]
    own_p = around(own, 2)
    first = swapped(own, "img", 0)
    second = swapped(own, "img", 1)

    smem = pl.BlockSpec(memory_space=pltpu.SMEM)
    vmem = pl.BlockSpec(memory_space=pltpu.VMEM)
    f32 = jnp.float32
    limit = pltpu.CompilerParams(vmem_limit_bytes=32 * 1024 * 1024)
    vreg = (SUB, LANES)
    packed = jax.ShapeDtypeStruct((comps + 1, tiles) + vreg, f32)
    left, right, info = pl.pallas_call(
        functools.partial(pack_kernel, ny, tiles, anisotropy.shape[0]),
        out_shape=(packed, packed, jax.ShapeDtypeStruct((5,) + vreg, f32)),
        in_specs=[smem] * 3 + [vmem] * 3,
        out_specs=(vmem,) * 3,
        compiler_params=limit,
        name="pack_strips",
    )(
        lower_image,
        anisotropy,
        damping,
        image_weights.reshape(1, -1),
        own.reshape(flat),
        regions.reshape(flat[1:]),
    )
    strip_l = shifted(right, "gx", 1, True)
    strip_r = shifted(left, "gx", -1, True)
    strips, info = pl.pallas_call(
        merge_kernel,
        out_shape=(
            jax.ShapeDtypeStruct((2,) + packed.shape, f32),
            jax.ShapeDtypeStruct(info.shape, f32),
        ),
        in_specs=[vmem] * 3,
        out_specs=(vmem,) * 2,
        compiler_params=limit,
        name="merge_strips",
    )(info, strip_l, strip_r)
    strips_first = swapped(strips, "img", 0)
    strips_second = swapped(strips, "img", 1)

    late_regions, own_p, info = lax.optimization_barrier((regions, own_p, info))
    reg_p = around(late_regions, 1)
    info, reg_p = lax.optimization_barrier((info, reg_p))
    cells = comps * nz * ny
    rows = cells + 4 * (comps + 1) * tiles * SUB
    part, near = pl.pallas_call(
        functools.partial(gather_kernel, tiles),
        out_shape=(
            jax.ShapeDtypeStruct((devices, LANES), f32),
            jax.ShapeDtypeStruct((rows, LANES), f32),
        ),
        in_specs=[vmem] * 7,
        out_specs=(vmem,) * 2,
        compiler_params=limit,
        name="gather_images",
    )(info, own.reshape(flat), first.reshape(flat), second.reshape(flat), strips, strips_first, strips_second)
    if lax.axis_size("gy") == 2:
        near_p = shifted(near, "gy", 1, True)
    else:
        tile_p = around(near[:cells].reshape(own.shape), 2).reshape(cells, LANES)
        rims_p = around_strips(near[cells:].reshape((2, 2, comps + 1, tiles) + vreg)).reshape(-1, LANES)
        near_p = jnp.concatenate([tile_p, rims_p])
    squares = lax.all_to_all(part, ("img", "gx", "gy"), 0, 0, tiled=True)

    window = ny + 2 * DEPTH
    out = pl.pallas_call(
        functools.partial(evolve_kernel, ny, tiles, images),
        out_shape=jax.ShapeDtypeStruct(flat, f32),
        in_specs=[vmem] * 8,
        out_specs=vmem,
        scratch_shapes=[
            pltpu.VMEM((comps, window, tiles) + vreg, f32),
            pltpu.VMEM((comps, window, tiles) + vreg, f32),
            pltpu.VMEM((comps, 2, 2, tiles) + vreg, f32),
            pltpu.VMEM((comps, 2, 2, tiles) + vreg, f32),
            pltpu.VMEM((comps, 2, tiles) + vreg, f32),
            pltpu.VMEM((comps, 2, tiles) + vreg, f32),
            pltpu.VMEM((comps, 2, tiles) + vreg, f32),
            pltpu.VMEM((3, window, tiles) + vreg, f32),
            pltpu.VMEM((3, 2, 2, tiles) + vreg, f32),
        ],
        compiler_params=limit,
        name="evolve",
    )(
        info,
        squares,
        own.reshape(flat),
        own_p.reshape(flat),
        near,
        near_p,
        regions.reshape(flat[1:]),
        reg_p.reshape(flat[1:]),
    )
    return out.reshape(magnetization.shape)


def solution(mesh):
    placed = (P("img", None, None, "gy", "gx"), P(), P(), P(None, "gy", "gx"), P(), P())
    return jax.shard_map(
        body,
        mesh=mesh,
        in_specs=placed,
        out_specs=P("img", None, None, "gy", "gx"),
        check_vma=False,
    )
```

```python
import functools

import jax
import jax.numpy as jnp
from jax import lax
from jax.experimental import pallas as pl
from jax.experimental.pallas import tpu as pltpu
from jax.sharding import PartitionSpec as P

STEPS = 4
DEPTH = 2 * STEPS

eps = 1e-06
time_step = 0.05

SUB = 8
LANES = 128
COMPS = 3
ROWS = 4


def lane_iota():
    return lax.broadcasted_iota(jnp.int32, (SUB, LANES), 1)


def sub_iota():
    return lax.broadcasted_iota(jnp.int32, (SUB, LANES), 0)


def rows_at(ny, tiles, y, t):
    return pl.ds(y + ny * t, SUB, stride=ny * tiles)


def pack_kernel(
    ny, tiles, regions, lower_ref, aniso_ref, damp_ref, share_ref, m_ref, reg_ref, left_ref, right_ref, info_ref
):
    here = lax.axis_index("img")
    lane = lane_iota()
    block = lane // DEPTH
    def pack(i, carry):
        done = []
        for u in range(2):
            y = 2 * i + u
            shift = (DEPTH * (y + 1)) & (LANES - 1)
            left = block == ((y + 1) & (ny - 1))
            right = block == y
            for t in range(tiles):
                rows = rows_at(ny, tiles, y, t)
                for c in range(COMPS + 1):
                    cells = m_ref[c, rows, :] if c < COMPS else reg_ref[rows, :].astype(jnp.float32)
                    done.append((c, t, left, right, pltpu.roll(cells, shift, 1)))
        for c, t, left, right, cells in done:
            pltpu.store(left_ref.at[c, t], cells, mask=left)
            pltpu.store(right_ref.at[c, t], cells, mask=right)
        return carry

    table_a = jnp.zeros((SUB, LANES), jnp.float32)
    table_d = jnp.zeros((SUB, LANES), jnp.float32)
    for i in range(regions):
        table_a = jnp.where(lane == i, 2.0 * aniso_ref[i], table_a)
        table_d = jnp.where(lane == i, damp_ref[i], table_d)
    info_ref[0] = table_a
    info_ref[1] = table_d
    info_ref[2] = -time_step / (1.0 + table_d * table_d)
    share = share_ref[...]
    spot = lax.broadcasted_iota(jnp.int32, share.shape, 1)
    target = jnp.sum(jnp.where(spot < here, share, 0.0), axis=1, keepdims=True) / jnp.sum(
        share, axis=1, keepdims=True
    )
    info_ref[3] = jnp.broadcast_to(target, (SUB, LANES))
    info_ref[4] = jnp.full((SUB, LANES), lower_ref[here].astype(jnp.float32))

    lax.fori_loop(0, ny // 2, pack, 0)


def merge_kernel(left_ref, right_ref, out_ref):
    out_ref[0] = left_ref[...]
    out_ref[1] = right_ref[...]


def take_first(info_ref, here):
    odd = (here & 1) == 1
    below = info_ref[4] < here.astype(jnp.float32)
    return jnp.where(below, jnp.where(odd, 1, 0), jnp.where(odd, 0, 1)) == 1, odd


def gather_kernel(
    ny, tiles, info_ref, m_ref, first_ref, second_ref, own_left_ref, own_right_ref, part_ref, near_ref, left_ref, right_ref
):
    here = lax.axis_index("img")
    pick, odd = take_first(info_ref, here)
    chunks = 4
    depth = m_ref.shape[1]

    def squares(i, sums):
        sums = list(sums)
        done = []
        for u in range(chunks):
            start = pl.multiple_of((chunks * i + u) * SUB, SUB)
            for c in range(COMPS):
                one = first_ref[c, pl.ds(start, SUB), :]
                two = second_ref[c, pl.ds(start, SUB), :]
                done.append((c, start, jnp.where(pick, one, two)))
                diff = m_ref[c, pl.ds(start, SUB), :] - jnp.where(odd, one, two)
                sums[c + COMPS * u] = sums[c + COMPS * u] + diff * diff
        for c, start, cells in done:
            near_ref[c, pl.ds(start, SUB), :] = cells
        return tuple(sums)

    zero = jnp.zeros((SUB, LANES), jnp.float32)
    sums = lax.fori_loop(0, depth // (chunks * SUB), squares, (zero,) * (chunks * COMPS))
    total = jnp.sum(functools.reduce(jnp.add, sums), axis=(0, 1), keepdims=True)
    slot = lax.broadcasted_iota(jnp.int32, part_ref.shape, 1)
    part_ref[...] = jnp.where((slot == here) & (here > 0), total, 0.0)
    left_ref[COMPS:] = own_left_ref[...]
    right_ref[COMPS:] = own_right_ref[...]
    block = lane_iota() // DEPTH

    def pack(i, carry):
        done = []
        for u in range(2):
            y = 2 * i + u
            left = block == ((y + 1) & (ny - 1))
            right = block == y
            shift = (DEPTH * (y + 1)) & (LANES - 1)
            for t in range(tiles):
                for c in range(COMPS):
                    cells = pltpu.roll(near_ref[c, rows_at(ny, tiles, y, t), :], shift, 1)
                    done.append((c, t, left, right, cells))
        for c, t, left, right, cells in done:
            pltpu.store(left_ref.at[c, t], cells, mask=left)
            pltpu.store(right_ref.at[c, t], cells, mask=right)
        return carry

    lax.fori_loop(0, ny // 2, pack, 0)


def turn(m, h, a2, b, sc):
    mx, my, mz = m
    hx, hy, hz = h
    hz = hz + a2 * mz
    gx = hx + b * (my * hz - mz * hy)
    gy = hy + b * (mz * hx - mx * hz)
    gz = hz + b * (mx * hy - my * hx)
    return (
        sc * (my * gz - mz * gy),
        sc * (mz * gx - mx * gz),
        sc * (mx * gy - my * gx),
    )


def normal(v):
    scale = lax.rsqrt(v[0] * v[0] + v[1] * v[1] + v[2] * v[2])
    return tuple(x * scale for x in v)


def evolve_kernel(
    ny,
    tiles,
    images,
    info_ref,
    sq_ref,
    m_ref,
    mp_ref,
    n_ref,
    np_ref,
    reg_ref,
    regp_ref,
    strips_ref,
    stripsp_ref,
    out_ref,
    main0,
    main1,
    strip0,
    strip1,
    edge,
    seam0,
    seam1,
    par,
    spar,
):
    main, strip, seam = (main0, main1), (strip0, strip1), (seam0, seam1)
    window = ny + 2 * DEPTH
    here = lax.axis_index("img")
    lane = lane_iota()
    sub = sub_iota()
    block = lane // DEPTH
    first_lane = lane == 0
    last_lane = lane == LANES - 1
    head_lane = lane % DEPTH == 0
    tail_lane = lane % DEPTH == DEPTH - 1
    top = sub == SUB - 1
    bottom = sub == 0

    lo = info_ref[4]
    slot = lane.astype(jnp.float32)
    squares = jnp.broadcast_to(jnp.sum(sq_ref[...], axis=0, keepdims=True), (SUB, LANES))
    lengths = jnp.where((lane >= 1) & (lane < images), jnp.sqrt(squares + eps), 0.0)
    total = jnp.sum(lengths, axis=1, keepdims=True)
    arc = jnp.sum(jnp.where(slot <= lo, lengths, 0.0), axis=1, keepdims=True)
    gap = jnp.sum(jnp.where(slot == lo + 1.0, lengths, 0.0), axis=1, keepdims=True)
    weight = jnp.clip((info_ref[3] * total - arc) / gap, -0.5, 1.5)
    below = lo < here.astype(jnp.float32)
    w_own = jnp.where(below, weight, 1.0 - weight)
    w_near = jnp.where(below, 1.0 - weight, weight)

    tables = (info_ref[0], info_ref[1], info_ref[2])

    def params(region):
        return [jnp.take_along_axis(table, region, axis=1) for table in tables]

    def ends_of(k, new):
        shift = (DEPTH * (k + 1)) & (LANES - 1)
        return [pltpu.roll(new[c], shift, 1) for c in range(COMPS)]

    def fill(k, carry):
        done = []
        for g, (own, near, reg) in enumerate(((m_ref, n_ref, reg_ref), (mp_ref, np_ref, regp_ref))):
            for t in range(tiles):
                rows = rows_at(ny, tiles, k, t)
                v = normal(
                    [
                        w_own * own[c, rows, :] + w_near * near[c, rows, :]
                        for c in range(COMPS)
                    ]
                )
                done.append((g * ny + k, t, v, params(reg[rows, :])))
        for r, t, v, p in done:
            for c in range(COMPS):
                main0[c, r, t] = v[c]
            for i in range(3):
                par[i, r, t] = p[i]
        return carry

    lax.fori_loop(0, ny, fill, 0)

    def seam_of(left, right):
        return jnp.where(head_lane, pltpu.roll(left, 1, 1), pltpu.roll(right, LANES - 1, 1))

    def fill_strips(t, carry):
        done = []
        for g, cells in enumerate((strips_ref, stripsp_ref)):
            for side in range(2):
                v = normal(
                    [w_own * cells[side, COMPS + c, t] + w_near * cells[side, c, t] for c in range(COMPS)]
                )
                done.append((side, g, v, params(cells[side, 2 * COMPS, t].astype(jnp.int32))))
        for side, g, v, p in done:
            for c in range(COMPS):
                strip0[c, side, g, t] = v[c]
            for i in range(3):
                spar[i, side, g, t] = p[i]
        for g in range(2):
            left, right = (v for _, h, v, _ in done if h == g)
            for c in range(COMPS):
                seam0[c, g, t] = seam_of(left[c], right[c])
        return carry

    lax.fori_loop(0, tiles, fill_strips, 0)

    def around_z(cells, t):
        if t + 1 < tiles:
            above = cells[t + 1]
        else:
            above = jnp.where(top, 0.0, pltpu.roll(cells[0], SUB - 1, 0))
        if t > 0:
            under = cells[t - 1]
        else:
            under = jnp.where(bottom, 0.0, pltpu.roll(cells[tiles - 1], 1, 0))
        return above + under

    def main_row(state, r):
        g = r // ny
        k = r & (ny - 1)
        after = (r + 1) & (window - 1)
        before = (r - 1) & (window - 1)
        shift = (LANES - DEPTH * (k + 1)) & (LANES - 1)
        center = [[main[state][c, r, t] for t in range(tiles)] for c in range(COMPS)]
        done = []
        for t in range(tiles):
            h = []
            for c in range(COMPS):
                cells = center[c][t]
                ends = pltpu.roll(seam[state][c, g, t], shift, 1)
                s = jnp.where(first_lane, ends, pltpu.roll(cells, 1, 1))
                s = s + jnp.where(last_lane, ends, pltpu.roll(cells, LANES - 1, 1))
                s = s + (main[state][c, after, t] + main[state][c, before, t])
                h.append(s + around_z(center[c], t))
            m = [center[c][t] for c in range(COMPS)]
            rate = turn(m, h, par[0, r, t], par[1, r, t], par[2, r, t])
            if state == 0:
                new = [m[c] + rate[c] for c in range(COMPS)]
            else:
                new = normal([main[0][c, r, t] + (m[c] + rate[c]) for c in range(COMPS)])
            done.append((r, t, new, ends_of(k, m)))
        return done

    def strip_rows(state):
        done = []
        for g in range(2):
            for side in range(2):
                start = block == side
                stop = block == (side + ny - 1) % ny
                center = [[strip[state][c, side, g, t] for t in range(tiles)] for c in range(COMPS)]
                for t in range(tiles):
                    h = []
                    for c in range(COMPS):
                        cells = center[c][t]
                        inner = edge[c, g, t]
                        other = strip[state][c, side, 1 - g, t]
                        if side == 0:
                            s = pltpu.roll(cells, 1, 1)
                            s = s + pltpu.roll(jnp.where(head_lane, inner, cells), LANES - 1, 1)
                        else:
                            s = pltpu.roll(jnp.where(tail_lane, inner, cells), 1, 1)
                            s = s + pltpu.roll(cells, LANES - 1, 1)
                        s = s + pltpu.roll(jnp.where(start, other, cells), LANES - DEPTH, 1)
                        s = s + pltpu.roll(jnp.where(stop, other, cells), DEPTH, 1)
                        h.append(s + around_z(center[c], t))
                    m = [center[c][t] for c in range(COMPS)]
                    rate = turn(
                        m, h, spar[0, side, g, t], spar[1, side, g, t], spar[2, side, g, t]
                    )
                    if state == 0:
                        new = [m[c] + rate[c] for c in range(COMPS)]
                    else:
                        new = normal(
                            [strip[0][c, side, g, t] + (m[c] + rate[c]) for c in range(COMPS)]
                        )
                    done.append((side, g, t, new))
        for side, g, t, new in done:
            for c in range(COMPS):
                strip[1 - state][c, side, g, t] = new[c]
        for g in range(2):
            for t in range(tiles):
                left, right = (new for _, h, u, new in done if (h, u) == (g, t))
                for c in range(COMPS):
                    seam[1 - state][c, g, t] = seam_of(left[c], right[c])

    def main_rows(state, first, count):
        def rows(i, carry):
            done = []
            for u in range(ROWS):
                done += main_row(state, (first + ROWS * i + u) & (window - 1))
            for r, t, new, ends in done:
                k = r & (ny - 1)
                mask = ((lane - (DEPTH * k + DEPTH - 1)) & (LANES - 1)) < 2
                for c in range(COMPS):
                    main[1 - state][c, r, t] = new[c]
                    pltpu.store(edge.at[c, r // ny, t], ends[c], mask=mask)
            return carry

        lax.fori_loop(0, count // ROWS, rows, 0)

    def step(i, carry):
        for state in range(2):
            margin = DEPTH - 2 * state - 2 * i
            main_rows(state, -margin, ny + 2 * margin)
            strip_rows(state)
        return carry

    lax.fori_loop(0, STEPS, step, 0)

    def hand_out(k, carry):
        for t in range(tiles):
            for c in range(COMPS):
                out_ref[c, rows_at(ny, tiles, k, t), :] = main[0][c, k, t]
        return carry

    lax.fori_loop(0, ny, hand_out, 0)


def shifted(cells, axis, step, closed):
    count = lax.axis_size(axis)
    pairs = [(i, (i + step) % count) for i in range(count) if closed or 0 <= i + step < count]
    return lax.ppermute(cells, axis, pairs)


def swapped(cells, axis, first):
    count = lax.axis_size(axis)
    pairs = [(i, i + 1) for i in range(first, count - 1, 2)]
    return lax.ppermute(cells, axis, pairs + [(j, i) for i, j in pairs])


def around(cells, dim):
    ny = cells.shape[dim]
    if lax.axis_size("gy") == 2:
        return shifted(cells, "gy", 1, True)
    head = lax.slice_in_dim(cells, 0, DEPTH, axis=dim)
    tail = lax.slice_in_dim(cells, ny - DEPTH, ny, axis=dim)
    return jnp.concatenate([shifted(head, "gy", -1, True), shifted(tail, "gy", 1, True)], axis=dim)


def around_strips(both):
    if lax.axis_size("gy") == 2:
        return shifted(both, "gy", 1, True)
    block = lax.broadcasted_iota(jnp.int32, both.shape, both.ndim - 1) // DEPTH
    side = lax.broadcasted_iota(jnp.int32, both.shape, 0)
    head = (block + side - 1) % (LANES // DEPTH) < DEPTH
    return jnp.where(head, shifted(both, "gy", -1, True), shifted(both, "gy", 1, True))


def body(magnetization, lower_image, image_weights, regions, anisotropy, damping):
    local, comps, nz, ny, nx = magnetization.shape
    images = local * lax.axis_size("img")
    tiles = nz // SUB
    devices = lax.axis_size(("img", "gx", "gy"))
    assert local == 1 and comps == COMPS and nx == LANES
    assert ny == 2 * DEPTH and ny * DEPTH == LANES and tiles >= 2
    flat = (comps, nz * ny, nx)
    own = magnetization[0]
    own_p = around(own, 2)
    first = swapped(own, "img", 0)
    second = swapped(own, "img", 1)

    smem = pl.BlockSpec(memory_space=pltpu.SMEM)
    vmem = pl.BlockSpec(memory_space=pltpu.VMEM)
    f32 = jnp.float32
    limit = pltpu.CompilerParams(vmem_limit_bytes=32 * 1024 * 1024)
    vreg = (SUB, LANES)
    packed = jax.ShapeDtypeStruct((comps + 1, tiles) + vreg, f32)
    left, right, info = pl.pallas_call(
        functools.partial(pack_kernel, ny, tiles, anisotropy.shape[0]),
        out_shape=(packed, packed, jax.ShapeDtypeStruct((5,) + vreg, f32)),
        in_specs=[smem] * 3 + [vmem] * 3,
        out_specs=(vmem,) * 3,
        compiler_params=limit,
        name="pack_strips",
    )(
        lower_image,
        anisotropy,
        damping,
        image_weights.reshape(1, -1),
        own.reshape(flat),
        regions.reshape(flat[1:]),
    )
    late_regions, own_p, info = lax.optimization_barrier((regions, own_p, info))
    reg_p = around(late_regions, 1)
    info, reg_p = lax.optimization_barrier((info, reg_p))
    packed = jax.ShapeDtypeStruct((2 * comps + 1, tiles) + vreg, f32)
    part, near, left, right = pl.pallas_call(
        functools.partial(gather_kernel, ny, tiles),
        out_shape=(
            jax.ShapeDtypeStruct((devices, LANES), f32),
            jax.ShapeDtypeStruct(flat, f32),
            packed,
            packed,
        ),
        in_specs=[vmem] * 6,
        out_specs=(vmem,) * 4,
        compiler_params=limit,
        name="gather_images",
    )(info, own.reshape(flat), first.reshape(flat), second.reshape(flat), left, right)
    near_p = around(near.reshape(own.shape), 2)
    strip_l = shifted(right, "gx", 1, True)
    strip_r = shifted(left, "gx", -1, True)
    strips = pl.pallas_call(
        merge_kernel,
        out_shape=jax.ShapeDtypeStruct((2,) + packed.shape, f32),
        in_specs=[vmem] * 2,
        out_specs=vmem,
        compiler_params=limit,
        name="merge_strips",
    )(strip_l, strip_r)
    strips_p = around_strips(strips)
    squares = lax.all_to_all(part, ("img", "gx", "gy"), 0, 0, tiled=True)

    window = ny + 2 * DEPTH
    out = pl.pallas_call(
        functools.partial(evolve_kernel, ny, tiles, images),
        out_shape=jax.ShapeDtypeStruct(flat, f32),
        in_specs=[vmem] * 10,
        out_specs=vmem,
        scratch_shapes=[
            pltpu.VMEM((comps, window, tiles) + vreg, f32),
            pltpu.VMEM((comps, window, tiles) + vreg, f32),
            pltpu.VMEM((comps, 2, 2, tiles) + vreg, f32),
            pltpu.VMEM((comps, 2, 2, tiles) + vreg, f32),
            pltpu.VMEM((comps, 2, tiles) + vreg, f32),
            pltpu.VMEM((comps, 2, tiles) + vreg, f32),
            pltpu.VMEM((comps, 2, tiles) + vreg, f32),
            pltpu.VMEM((3, window, tiles) + vreg, f32),
            pltpu.VMEM((3, 2, 2, tiles) + vreg, f32),
        ],
        compiler_params=limit,
        name="evolve",
    )(
        info,
        squares,
        own.reshape(flat),
        own_p.reshape(flat),
        near,
        near_p.reshape(flat),
        regions.reshape(flat[1:]),
        reg_p.reshape(flat[1:]),
        strips,
        strips_p,
    )
    return out.reshape(magnetization.shape)


def solution(mesh):
    placed = (P("img", None, None, "gy", "gx"), P(), P(), P(None, "gy", "gx"), P(), P())
    return jax.shard_map(
        body,
        mesh=mesh,
        in_specs=placed,
        out_specs=P("img", None, None, "gy", "gx"),
        check_vma=False,
    )
```

```python
import functools

import jax
import jax.numpy as jnp
from jax import lax
from jax.experimental import pallas as pl
from jax.experimental.pallas import tpu as pltpu
from jax.sharding import PartitionSpec as P

STEPS = 4
DEPTH = 2 * STEPS

eps = 1e-06
time_step = 0.05

SUB = 8
LANES = 128
COMPS = 3
ROWS = 4


def lane_iota():
    return lax.broadcasted_iota(jnp.int32, (SUB, LANES), 1)


def sub_iota():
    return lax.broadcasted_iota(jnp.int32, (SUB, LANES), 0)


def rows_at(ny, tiles, y, t):
    return pl.ds(y + ny * t, SUB, stride=ny * tiles)


def pack_kernel(
    ny, tiles, regions, lower_ref, aniso_ref, damp_ref, share_ref, m_ref, reg_ref, left_ref, right_ref, info_ref
):
    here = lax.axis_index("img")
    lane = lane_iota()
    block = lane // DEPTH
    def pack(i, carry):
        done = []
        for u in range(2):
            y = 2 * i + u
            shift = (DEPTH * (y + 1)) & (LANES - 1)
            left = block == ((y + 1) & (ny - 1))
            right = block == y
            for t in range(tiles):
                rows = rows_at(ny, tiles, y, t)
                for c in range(COMPS + 1):
                    cells = m_ref[c, rows, :] if c < COMPS else reg_ref[rows, :].astype(jnp.float32)
                    done.append((c, t, left, right, pltpu.roll(cells, shift, 1)))
        for c, t, left, right, cells in done:
            pltpu.store(left_ref.at[c, t], cells, mask=left)
            pltpu.store(right_ref.at[c, t], cells, mask=right)
        return carry

    table_a = jnp.zeros((SUB, LANES), jnp.float32)
    table_d = jnp.zeros((SUB, LANES), jnp.float32)
    for i in range(regions):
        table_a = jnp.where(lane == i, 2.0 * aniso_ref[i], table_a)
        table_d = jnp.where(lane == i, damp_ref[i], table_d)
    info_ref[0] = table_a
    info_ref[1] = table_d
    info_ref[2] = -time_step / (1.0 + table_d * table_d)
    share = share_ref[...]
    spot = lax.broadcasted_iota(jnp.int32, share.shape, 1)
    target = jnp.sum(jnp.where(spot < here, share, 0.0), axis=1, keepdims=True) / jnp.sum(
        share, axis=1, keepdims=True
    )
    info_ref[3] = jnp.broadcast_to(target, (SUB, LANES))
    info_ref[4] = jnp.full((SUB, LANES), lower_ref[here].astype(jnp.float32))

    lax.fori_loop(0, ny // 2, pack, 0)


def merge_kernel(one_ref, two_ref, out_ref):
    turned = (lax.axis_index("gx") & 1) == 1
    one, two = one_ref[...], two_ref[...]
    out_ref[0] = jnp.where(turned, one, two)
    out_ref[1] = jnp.where(turned, two, one)


def take_first(info_ref, here):
    odd = (here & 1) == 1
    below = info_ref[4] < here.astype(jnp.float32)
    return jnp.where(below, jnp.where(odd, 1, 0), jnp.where(odd, 0, 1)) == 1, odd


def gather_kernel(
    ny, tiles, info_ref, m_ref, first_ref, second_ref, own_left_ref, own_right_ref, part_ref, near_ref, one_ref, two_ref
):
    here = lax.axis_index("img")
    pick, odd = take_first(info_ref, here)
    chunks = 4
    depth = m_ref.shape[1]

    def squares(i, sums):
        sums = list(sums)
        done = []
        for u in range(chunks):
            start = pl.multiple_of((chunks * i + u) * SUB, SUB)
            for c in range(COMPS):
                one = first_ref[c, pl.ds(start, SUB), :]
                two = second_ref[c, pl.ds(start, SUB), :]
                done.append((c, start, jnp.where(pick, one, two)))
                diff = m_ref[c, pl.ds(start, SUB), :] - jnp.where(odd, one, two)
                sums[c + COMPS * u] = sums[c + COMPS * u] + diff * diff
        for c, start, cells in done:
            near_ref[c, pl.ds(start, SUB), :] = cells
        return tuple(sums)

    zero = jnp.zeros((SUB, LANES), jnp.float32)
    sums = lax.fori_loop(0, depth // (chunks * SUB), squares, (zero,) * (chunks * COMPS))
    total = jnp.sum(functools.reduce(jnp.add, sums), axis=(0, 1), keepdims=True)
    slot = lax.broadcasted_iota(jnp.int32, part_ref.shape, 1)
    part_ref[...] = jnp.where((slot == here) & (here > 0), total, 0.0)
    turned = (lax.axis_index("gx") & 1) == 1
    one_ref[COMPS:] = jnp.where(turned, own_left_ref[...], own_right_ref[...])
    two_ref[COMPS:] = jnp.where(turned, own_right_ref[...], own_left_ref[...])
    block = lane_iota() // DEPTH

    def pack(i, carry):
        done = []
        for u in range(2):
            y = 2 * i + u
            after = (y + 1) & (ny - 1)
            one = block == jnp.where(turned, after, y)
            two = block == jnp.where(turned, y, after)
            shift = (DEPTH * (y + 1)) & (LANES - 1)
            for t in range(tiles):
                for c in range(COMPS):
                    cells = pltpu.roll(near_ref[c, rows_at(ny, tiles, y, t), :], shift, 1)
                    done.append((c, t, one, two, cells))
        for c, t, one, two, cells in done:
            pltpu.store(one_ref.at[c, t], cells, mask=one)
            pltpu.store(two_ref.at[c, t], cells, mask=two)
        return carry

    lax.fori_loop(0, ny // 2, pack, 0)


def turn(m, h, a2, b, sc):
    mx, my, mz = m
    hx, hy, hz = h
    hz = hz + a2 * mz
    gx = hx + b * (my * hz - mz * hy)
    gy = hy + b * (mz * hx - mx * hz)
    gz = hz + b * (mx * hy - my * hx)
    return (
        sc * (my * gz - mz * gy),
        sc * (mz * gx - mx * gz),
        sc * (mx * gy - my * gx),
    )


def normal(v):
    scale = lax.rsqrt(v[0] * v[0] + v[1] * v[1] + v[2] * v[2])
    return tuple(x * scale for x in v)


def evolve_kernel(
    ny,
    tiles,
    images,
    info_ref,
    sq_ref,
    m_ref,
    mp_ref,
    n_ref,
    np_ref,
    reg_ref,
    regp_ref,
    strips_ref,
    stripsp_ref,
    out_ref,
    main0,
    main1,
    strip0,
    strip1,
    edge,
    seam0,
    seam1,
    par,
    spar,
):
    main, strip, seam = (main0, main1), (strip0, strip1), (seam0, seam1)
    window = ny + 2 * DEPTH
    here = lax.axis_index("img")
    lane = lane_iota()
    sub = sub_iota()
    block = lane // DEPTH
    first_lane = lane == 0
    last_lane = lane == LANES - 1
    head_lane = lane % DEPTH == 0
    tail_lane = lane % DEPTH == DEPTH - 1
    top = sub == SUB - 1
    bottom = sub == 0

    lo = info_ref[4]
    slot = lane.astype(jnp.float32)
    squares = jnp.broadcast_to(jnp.sum(sq_ref[...], axis=0, keepdims=True), (SUB, LANES))
    lengths = jnp.where((lane >= 1) & (lane < images), jnp.sqrt(squares + eps), 0.0)
    total = jnp.sum(lengths, axis=1, keepdims=True)
    arc = jnp.sum(jnp.where(slot <= lo, lengths, 0.0), axis=1, keepdims=True)
    gap = jnp.sum(jnp.where(slot == lo + 1.0, lengths, 0.0), axis=1, keepdims=True)
    weight = jnp.clip((info_ref[3] * total - arc) / gap, -0.5, 1.5)
    below = lo < here.astype(jnp.float32)
    w_own = jnp.where(below, weight, 1.0 - weight)
    w_near = jnp.where(below, 1.0 - weight, weight)

    tables = (info_ref[0], info_ref[1], info_ref[2])

    def params(region):
        return [jnp.take_along_axis(table, region, axis=1) for table in tables]

    def ends_of(k, new):
        shift = (DEPTH * (k + 1)) & (LANES - 1)
        return [pltpu.roll(new[c], shift, 1) for c in range(COMPS)]

    def fill(k, carry):
        done = []
        for g, (own, near, reg) in enumerate(((m_ref, n_ref, reg_ref), (mp_ref, np_ref, regp_ref))):
            for t in range(tiles):
                rows = rows_at(ny, tiles, k, t)
                v = normal(
                    [
                        w_own * own[c, rows, :] + w_near * near[c, rows, :]
                        for c in range(COMPS)
                    ]
                )
                done.append((g * ny + k, t, v, params(reg[rows, :])))
        for r, t, v, p in done:
            for c in range(COMPS):
                main0[c, r, t] = v[c]
            for i in range(3):
                par[i, r, t] = p[i]
        return carry

    lax.fori_loop(0, ny, fill, 0)

    def seam_of(left, right):
        return jnp.where(head_lane, pltpu.roll(left, 1, 1), pltpu.roll(right, LANES - 1, 1))

    def fill_strips(t, carry):
        done = []
        for g, cells in enumerate((strips_ref, stripsp_ref)):
            for side in range(2):
                v = normal(
                    [w_own * cells[side, COMPS + c, t] + w_near * cells[side, c, t] for c in range(COMPS)]
                )
                done.append((side, g, v, params(cells[side, 2 * COMPS, t].astype(jnp.int32))))
        for side, g, v, p in done:
            for c in range(COMPS):
                strip0[c, side, g, t] = v[c]
            for i in range(3):
                spar[i, side, g, t] = p[i]
        for g in range(2):
            left, right = (v for _, h, v, _ in done if h == g)
            for c in range(COMPS):
                seam0[c, g, t] = seam_of(left[c], right[c])
        return carry

    lax.fori_loop(0, tiles, fill_strips, 0)

    def around_z(cells, t):
        if t + 1 < tiles:
            above = cells[t + 1]
        else:
            above = jnp.where(top, 0.0, pltpu.roll(cells[0], SUB - 1, 0))
        if t > 0:
            under = cells[t - 1]
        else:
            under = jnp.where(bottom, 0.0, pltpu.roll(cells[tiles - 1], 1, 0))
        return above + under

    def main_row(state, r):
        g = r // ny
        k = r & (ny - 1)
        after = (r + 1) & (window - 1)
        before = (r - 1) & (window - 1)
        shift = (LANES - DEPTH * (k + 1)) & (LANES - 1)
        center = [[main[state][c, r, t] for t in range(tiles)] for c in range(COMPS)]
        done = []
        for t in range(tiles):
            h = []
            for c in range(COMPS):
                cells = center[c][t]
                ends = pltpu.roll(seam[state][c, g, t], shift, 1)
                s = jnp.where(first_lane, ends, pltpu.roll(cells, 1, 1))
                s = s + jnp.where(last_lane, ends, pltpu.roll(cells, LANES - 1, 1))
                s = s + (main[state][c, after, t] + main[state][c, before, t])
                h.append(s + around_z(center[c], t))
            m = [center[c][t] for c in range(COMPS)]
            rate = turn(m, h, par[0, r, t], par[1, r, t], par[2, r, t])
            if state == 0:
                new = [m[c] + rate[c] for c in range(COMPS)]
            else:
                new = normal([main[0][c, r, t] + (m[c] + rate[c]) for c in range(COMPS)])
            done.append((r, t, new, ends_of(k, m)))
        return done

    def strip_rows(state):
        done = []
        for g in range(2):
            for side in range(2):
                start = block == side
                stop = block == (side + ny - 1) % ny
                center = [[strip[state][c, side, g, t] for t in range(tiles)] for c in range(COMPS)]
                for t in range(tiles):
                    h = []
                    for c in range(COMPS):
                        cells = center[c][t]
                        inner = edge[c, g, t]
                        other = strip[state][c, side, 1 - g, t]
                        if side == 0:
                            s = pltpu.roll(cells, 1, 1)
                            s = s + pltpu.roll(jnp.where(head_lane, inner, cells), LANES - 1, 1)
                        else:
                            s = pltpu.roll(jnp.where(tail_lane, inner, cells), 1, 1)
                            s = s + pltpu.roll(cells, LANES - 1, 1)
                        s = s + pltpu.roll(jnp.where(start, other, cells), LANES - DEPTH, 1)
                        s = s + pltpu.roll(jnp.where(stop, other, cells), DEPTH, 1)
                        h.append(s + around_z(center[c], t))
                    m = [center[c][t] for c in range(COMPS)]
                    rate = turn(
                        m, h, spar[0, side, g, t], spar[1, side, g, t], spar[2, side, g, t]
                    )
                    if state == 0:
                        new = [m[c] + rate[c] for c in range(COMPS)]
                    else:
                        new = normal(
                            [strip[0][c, side, g, t] + (m[c] + rate[c]) for c in range(COMPS)]
                        )
                    done.append((side, g, t, new))
        for side, g, t, new in done:
            for c in range(COMPS):
                strip[1 - state][c, side, g, t] = new[c]
        for g in range(2):
            for t in range(tiles):
                left, right = (new for _, h, u, new in done if (h, u) == (g, t))
                for c in range(COMPS):
                    seam[1 - state][c, g, t] = seam_of(left[c], right[c])

    def main_rows(state, first, count):
        def rows(i, carry):
            done = []
            for u in range(ROWS):
                done += main_row(state, (first + ROWS * i + u) & (window - 1))
            for r, t, new, ends in done:
                k = r & (ny - 1)
                mask = ((lane - (DEPTH * k + DEPTH - 1)) & (LANES - 1)) < 2
                for c in range(COMPS):
                    main[1 - state][c, r, t] = new[c]
                    pltpu.store(edge.at[c, r // ny, t], ends[c], mask=mask)
            return carry

        lax.fori_loop(0, count // ROWS, rows, 0)

    def step(i, carry):
        for state in range(2):
            margin = DEPTH - 2 * state - 2 * i
            main_rows(state, -margin, ny + 2 * margin)
            strip_rows(state)
        return carry

    lax.fori_loop(0, STEPS, step, 0)

    def hand_out(k, carry):
        for t in range(tiles):
            for c in range(COMPS):
                out_ref[c, rows_at(ny, tiles, k, t), :] = main[0][c, k, t]
        return carry

    lax.fori_loop(0, ny, hand_out, 0)


def shifted(cells, axis, step, closed):
    count = lax.axis_size(axis)
    pairs = [(i, (i + step) % count) for i in range(count) if closed or 0 <= i + step < count]
    return lax.ppermute(cells, axis, pairs)


def swapped(cells, axis, first, closed):
    count = lax.axis_size(axis)
    pairs = [(i, (i + 1) % count) for i in range(first, count if closed else count - 1, 2)]
    return lax.ppermute(cells, axis, pairs + [(j, i) for i, j in pairs])


def around(cells, dim):
    ny = cells.shape[dim]
    if lax.axis_size("gy") == 2:
        return shifted(cells, "gy", 1, True)
    head = lax.slice_in_dim(cells, 0, DEPTH, axis=dim)
    tail = lax.slice_in_dim(cells, ny - DEPTH, ny, axis=dim)
    return jnp.concatenate([shifted(head, "gy", -1, True), shifted(tail, "gy", 1, True)], axis=dim)


def around_strips(both):
    if lax.axis_size("gy") == 2:
        return shifted(both, "gy", 1, True)
    block = lax.broadcasted_iota(jnp.int32, both.shape, both.ndim - 1) // DEPTH
    side = lax.broadcasted_iota(jnp.int32, both.shape, 0)
    head = (block + side - 1) % (LANES // DEPTH) < DEPTH
    return jnp.where(head, shifted(both, "gy", -1, True), shifted(both, "gy", 1, True))


def body(magnetization, lower_image, image_weights, regions, anisotropy, damping):
    local, comps, nz, ny, nx = magnetization.shape
    images = local * lax.axis_size("img")
    tiles = nz // SUB
    devices = lax.axis_size(("img", "gx", "gy"))
    assert lax.axis_size("gx") % 2 == 0
    assert local == 1 and comps == COMPS and nx == LANES
    assert ny == 2 * DEPTH and ny * DEPTH == LANES and tiles >= 2
    flat = (comps, nz * ny, nx)
    own = magnetization[0]
    own_p = around(own, 2)
    first = swapped(own, "img", 0, False)
    second = swapped(own, "img", 1, False)

    smem = pl.BlockSpec(memory_space=pltpu.SMEM)
    vmem = pl.BlockSpec(memory_space=pltpu.VMEM)
    f32 = jnp.float32
    limit = pltpu.CompilerParams(vmem_limit_bytes=32 * 1024 * 1024)
    vreg = (SUB, LANES)
    packed = jax.ShapeDtypeStruct((comps + 1, tiles) + vreg, f32)
    left, right, info = pl.pallas_call(
        functools.partial(pack_kernel, ny, tiles, anisotropy.shape[0]),
        out_shape=(packed, packed, jax.ShapeDtypeStruct((5,) + vreg, f32)),
        in_specs=[smem] * 3 + [vmem] * 3,
        out_specs=(vmem,) * 3,
        compiler_params=limit,
        name="pack_strips",
    )(
        lower_image,
        anisotropy,
        damping,
        image_weights.reshape(1, -1),
        own.reshape(flat),
        regions.reshape(flat[1:]),
    )
    late_regions, info = lax.optimization_barrier((regions, info))
    reg_p = around(late_regions, 1)
    info, own_p, reg_p = lax.optimization_barrier((info, own_p, reg_p))
    packed = jax.ShapeDtypeStruct((2 * comps + 1, tiles) + vreg, f32)
    part, near, one, two = pl.pallas_call(
        functools.partial(gather_kernel, ny, tiles),
        out_shape=(
            jax.ShapeDtypeStruct((devices, LANES), f32),
            jax.ShapeDtypeStruct(flat, f32),
            packed,
            packed,
        ),
        in_specs=[vmem] * 6,
        out_specs=(vmem,) * 4,
        compiler_params=limit,
        name="gather_images",
    )(info, own.reshape(flat), first.reshape(flat), second.reshape(flat), left, right)
    near_p = around(near.reshape(own.shape), 2)
    one = swapped(one, "gx", 0, True)
    two = swapped(two, "gx", 1, True)
    strips = pl.pallas_call(
        merge_kernel,
        out_shape=jax.ShapeDtypeStruct((2,) + packed.shape, f32),
        in_specs=[vmem] * 2,
        out_specs=vmem,
        compiler_params=limit,
        name="merge_strips",
    )(one, two)
    strips_p = around_strips(strips)
    squares = lax.all_to_all(part, ("img", "gx", "gy"), 0, 0, tiled=True)

    window = ny + 2 * DEPTH
    out = pl.pallas_call(
        functools.partial(evolve_kernel, ny, tiles, images),
        out_shape=jax.ShapeDtypeStruct(flat, f32),
        in_specs=[vmem] * 10,
        out_specs=vmem,
        scratch_shapes=[
            pltpu.VMEM((comps, window, tiles) + vreg, f32),
            pltpu.VMEM((comps, window, tiles) + vreg, f32),
            pltpu.VMEM((comps, 2, 2, tiles) + vreg, f32),
            pltpu.VMEM((comps, 2, 2, tiles) + vreg, f32),
            pltpu.VMEM((comps, 2, tiles) + vreg, f32),
            pltpu.VMEM((comps, 2, tiles) + vreg, f32),
            pltpu.VMEM((comps, 2, tiles) + vreg, f32),
            pltpu.VMEM((3, window, tiles) + vreg, f32),
            pltpu.VMEM((3, 2, 2, tiles) + vreg, f32),
        ],
        compiler_params=limit,
        name="evolve",
    )(
        info,
        squares,
        own.reshape(flat),
        own_p.reshape(flat),
        near,
        near_p.reshape(flat),
        regions.reshape(flat[1:]),
        reg_p.reshape(flat[1:]),
        strips,
        strips_p,
    )
    return out.reshape(magnetization.shape)


def solution(mesh):
    placed = (P("img", None, None, "gy", "gx"), P(), P(), P(None, "gy", "gx"), P(), P())
    return jax.shard_map(
        body,
        mesh=mesh,
        in_specs=placed,
        out_specs=P("img", None, None, "gy", "gx"),
        check_vma=False,
    )
```

```python
import functools

import jax
import jax.numpy as jnp
from jax import lax
from jax.experimental import pallas as pl
from jax.experimental.pallas import tpu as pltpu
from jax.sharding import PartitionSpec as P

STEPS = 4
DEPTH = 2 * STEPS

eps = 1e-06
time_step = 0.05

SUB = 8
LANES = 128
COMPS = 3
ROWS = 4


def lane_iota():
    return lax.broadcasted_iota(jnp.int32, (SUB, LANES), 1)


def sub_iota():
    return lax.broadcasted_iota(jnp.int32, (SUB, LANES), 0)


def rows_at(ny, tiles, y, t):
    return pl.ds(y + ny * t, SUB, stride=ny * tiles)


def pack_kernel(
    ny, tiles, regions, lower_ref, aniso_ref, damp_ref, share_ref, m_ref, reg_ref, left_ref, right_ref, info_ref
):
    here = lax.axis_index("img")
    lane = lane_iota()
    block = lane // DEPTH
    def pack(i, carry):
        done = []
        for u in range(2):
            y = 2 * i + u
            shift = (DEPTH * (y + 1)) & (LANES - 1)
            left = block == ((y + 1) & (ny - 1))
            right = block == y
            for t in range(tiles):
                rows = rows_at(ny, tiles, y, t)
                for c in range(COMPS + 1):
                    cells = m_ref[c, rows, :] if c < COMPS else reg_ref[rows, :].astype(jnp.float32)
                    done.append((c, t, left, right, pltpu.roll(cells, shift, 1)))
        for c, t, left, right, cells in done:
            pltpu.store(left_ref.at[c, t], cells, mask=left)
            pltpu.store(right_ref.at[c, t], cells, mask=right)
        return carry

    table_a = jnp.zeros((SUB, LANES), jnp.float32)
    table_d = jnp.zeros((SUB, LANES), jnp.float32)
    for i in range(regions):
        table_a = jnp.where(lane == i, 2.0 * aniso_ref[i], table_a)
        table_d = jnp.where(lane == i, damp_ref[i], table_d)
    info_ref[0] = table_a
    info_ref[1] = table_d
    info_ref[2] = -time_step / (1.0 + table_d * table_d)
    share = share_ref[...]
    spot = lax.broadcasted_iota(jnp.int32, share.shape, 1)
    target = jnp.sum(jnp.where(spot < here, share, 0.0), axis=1, keepdims=True) / jnp.sum(
        share, axis=1, keepdims=True
    )
    info_ref[3] = jnp.broadcast_to(target, (SUB, LANES))
    info_ref[4] = jnp.full((SUB, LANES), lower_ref[here].astype(jnp.float32))

    lax.fori_loop(0, ny // 2, pack, 0)


def merge_kernel(one_ref, two_ref, out_ref):
    turned = (lax.axis_index("gx") & 1) == 1
    one, two = one_ref[...], two_ref[...]
    out_ref[0] = jnp.where(turned, one, two)
    out_ref[1] = jnp.where(turned, two, one)


def take_first(info_ref, here):
    odd = (here & 1) == 1
    below = info_ref[4] < here.astype(jnp.float32)
    return jnp.where(below, jnp.where(odd, 1, 0), jnp.where(odd, 0, 1)) == 1, odd


def gather_kernel(
    ny, tiles, info_ref, m_ref, first_ref, second_ref, own_left_ref, own_right_ref, part_ref, near_ref, one_ref, two_ref
):
    here = lax.axis_index("img")
    pick, odd = take_first(info_ref, here)
    chunks = 4
    depth = m_ref.shape[1]

    def squares(i, sums):
        sums = list(sums)
        done = []
        for u in range(chunks):
            start = pl.multiple_of((chunks * i + u) * SUB, SUB)
            for c in range(COMPS):
                one = first_ref[c, pl.ds(start, SUB), :]
                two = second_ref[c, pl.ds(start, SUB), :]
                done.append((c, start, jnp.where(pick, one, two)))
                diff = m_ref[c, pl.ds(start, SUB), :] - jnp.where(odd, one, two)
                sums[c + COMPS * u] = sums[c + COMPS * u] + diff * diff
        for c, start, cells in done:
            near_ref[c, pl.ds(start, SUB), :] = cells
        return tuple(sums)

    zero = jnp.zeros((SUB, LANES), jnp.float32)
    sums = lax.fori_loop(0, depth // (chunks * SUB), squares, (zero,) * (chunks * COMPS))
    total = jnp.sum(functools.reduce(jnp.add, sums), axis=(0, 1), keepdims=True)
    slot = lax.broadcasted_iota(jnp.int32, part_ref.shape, 1)
    part_ref[...] = jnp.where((slot == here) & (here > 0), total, 0.0)
    turned = (lax.axis_index("gx") & 1) == 1
    one_ref[COMPS:] = jnp.where(turned, own_left_ref[...], own_right_ref[...])
    two_ref[COMPS:] = jnp.where(turned, own_right_ref[...], own_left_ref[...])
    block = lane_iota() // DEPTH

    def pack(i, carry):
        done = []
        for u in range(2):
            y = 2 * i + u
            after = (y + 1) & (ny - 1)
            one = block == jnp.where(turned, after, y)
            two = block == jnp.where(turned, y, after)
            shift = (DEPTH * (y + 1)) & (LANES - 1)
            for t in range(tiles):
                for c in range(COMPS):
                    cells = pltpu.roll(near_ref[c, rows_at(ny, tiles, y, t), :], shift, 1)
                    done.append((c, t, one, two, cells))
        for c, t, one, two, cells in done:
            pltpu.store(one_ref.at[c, t], cells, mask=one)
            pltpu.store(two_ref.at[c, t], cells, mask=two)
        return carry

    lax.fori_loop(0, ny // 2, pack, 0)


def turn(m, h, a2, b, sc):
    mx, my, mz = m
    hx, hy, hz = h
    hz = hz + a2 * mz
    gx = hx + b * (my * hz - mz * hy)
    gy = hy + b * (mz * hx - mx * hz)
    gz = hz + b * (mx * hy - my * hx)
    return (
        sc * (my * gz - mz * gy),
        sc * (mz * gx - mx * gz),
        sc * (mx * gy - my * gx),
    )


def normal(v):
    scale = lax.rsqrt(v[0] * v[0] + v[1] * v[1] + v[2] * v[2])
    return tuple(x * scale for x in v)


def evolve_kernel(
    ny,
    tiles,
    images,
    info_ref,
    sq_ref,
    m_ref,
    mp_ref,
    n_ref,
    np_ref,
    reg_ref,
    regp_ref,
    strips_ref,
    stripsp_ref,
    out_ref,
    main0,
    main1,
    strip0,
    strip1,
    edge,
    seam0,
    seam1,
    par,
    spar,
):
    main, strip, seam = (main0, main1), (strip0, strip1), (seam0, seam1)
    window = ny + 2 * DEPTH
    here = lax.axis_index("img")
    lane = lane_iota()
    sub = sub_iota()
    block = lane // DEPTH
    first_lane = lane == 0
    last_lane = lane == LANES - 1
    head_lane = lane % DEPTH == 0
    tail_lane = lane % DEPTH == DEPTH - 1
    top = sub == SUB - 1
    bottom = sub == 0

    lo = info_ref[4]
    slot = lane.astype(jnp.float32)
    squares = jnp.broadcast_to(jnp.sum(sq_ref[...], axis=0, keepdims=True), (SUB, LANES))
    lengths = jnp.where((lane >= 1) & (lane < images), jnp.sqrt(squares + eps), 0.0)
    total = jnp.sum(lengths, axis=1, keepdims=True)
    arc = jnp.sum(jnp.where(slot <= lo, lengths, 0.0), axis=1, keepdims=True)
    gap = jnp.sum(jnp.where(slot == lo + 1.0, lengths, 0.0), axis=1, keepdims=True)
    weight = jnp.clip((info_ref[3] * total - arc) / gap, -0.5, 1.5)
    below = lo < here.astype(jnp.float32)
    w_own = jnp.where(below, weight, 1.0 - weight)
    w_near = jnp.where(below, 1.0 - weight, weight)

    tables = (info_ref[0], info_ref[1], info_ref[2])

    def params(region):
        return [jnp.take_along_axis(table, region, axis=1) for table in tables]

    def ends_of(k, new):
        shift = (DEPTH * (k + 1)) & (LANES - 1)
        return [pltpu.roll(new[c], shift, 1) for c in range(COMPS)]

    def fill(i, carry):
        done = []
        for k in (2 * i, 2 * i + 1):
            for g, (own, near, reg) in enumerate(((m_ref, n_ref, reg_ref), (mp_ref, np_ref, regp_ref))):
                for t in range(tiles):
                    rows = rows_at(ny, tiles, k, t)
                    v = normal(
                        [w_own * own[c, rows, :] + w_near * near[c, rows, :] for c in range(COMPS)]
                    )
                    done.append((g * ny + k, t, v, params(reg[rows, :])))
        for r, t, v, p in done:
            for c in range(COMPS):
                main0[c, r, t] = v[c]
            for i in range(3):
                par[i, r, t] = p[i]
        return carry

    lax.fori_loop(0, ny // 2, fill, 0)

    def seam_of(left, right):
        return jnp.where(head_lane, pltpu.roll(left, 1, 1), pltpu.roll(right, LANES - 1, 1))

    def fill_strips(t, carry):
        done = []
        for g, cells in enumerate((strips_ref, stripsp_ref)):
            for side in range(2):
                v = normal(
                    [w_own * cells[side, COMPS + c, t] + w_near * cells[side, c, t] for c in range(COMPS)]
                )
                done.append((side, g, v, params(cells[side, 2 * COMPS, t].astype(jnp.int32))))
        for side, g, v, p in done:
            for c in range(COMPS):
                strip0[c, side, g, t] = v[c]
            for i in range(3):
                spar[i, side, g, t] = p[i]
        for g in range(2):
            left, right = (v for _, h, v, _ in done if h == g)
            for c in range(COMPS):
                seam0[c, g, t] = seam_of(left[c], right[c])
        return carry

    lax.fori_loop(0, tiles, fill_strips, 0)

    def around_z(cells, t):
        if t + 1 < tiles:
            above = cells[t + 1]
        else:
            above = jnp.where(top, 0.0, pltpu.roll(cells[0], SUB - 1, 0))
        if t > 0:
            under = cells[t - 1]
        else:
            under = jnp.where(bottom, 0.0, pltpu.roll(cells[tiles - 1], 1, 0))
        return above + under

    def main_sums(state, r):
        g = r // ny
        k = r & (ny - 1)
        after = (r + 1) & (window - 1)
        before = (r - 1) & (window - 1)
        shift = (LANES - DEPTH * (k + 1)) & (LANES - 1)
        center = [[main[state][c, r, t] for t in range(tiles)] for c in range(COMPS)]
        sums, ends = [], []
        for t in range(tiles):
            for c in range(COMPS):
                cells = center[c][t]
                rim = pltpu.roll(seam[state][c, g, t], shift, 1)
                s = jnp.where(first_lane, rim, pltpu.roll(cells, 1, 1))
                s = s + jnp.where(last_lane, rim, pltpu.roll(cells, LANES - 1, 1))
                s = s + (main[state][c, after, t] + main[state][c, before, t])
                sums.append(s + around_z(center[c], t))
            ends.append((r, t, ends_of(k, [center[c][t] for c in range(COMPS)])))
        return sums, ends

    def main_turn(state, r, sums):
        done = []
        for t in range(tiles):
            m = [main[state][c, r, t] for c in range(COMPS)]
            h = sums[COMPS * t : COMPS * (t + 1)]
            rate = turn(m, h, par[0, r, t], par[1, r, t], par[2, r, t])
            if state == 0:
                new = [m[c] + rate[c] for c in range(COMPS)]
            else:
                new = normal([main[0][c, r, t] + (m[c] + rate[c]) for c in range(COMPS)])
            done.append((r, t, new))
        return done

    def strip_rows(state):
        done = []
        for g in range(2):
            for side in range(2):
                start = block == side
                stop = block == (side + ny - 1) % ny
                center = [[strip[state][c, side, g, t] for t in range(tiles)] for c in range(COMPS)]
                for t in range(tiles):
                    h = []
                    for c in range(COMPS):
                        cells = center[c][t]
                        inner = edge[c, g, t]
                        other = strip[state][c, side, 1 - g, t]
                        if side == 0:
                            s = pltpu.roll(cells, 1, 1)
                            s = s + pltpu.roll(jnp.where(head_lane, inner, cells), LANES - 1, 1)
                        else:
                            s = pltpu.roll(jnp.where(tail_lane, inner, cells), 1, 1)
                            s = s + pltpu.roll(cells, LANES - 1, 1)
                        s = s + pltpu.roll(jnp.where(start, other, cells), LANES - DEPTH, 1)
                        s = s + pltpu.roll(jnp.where(stop, other, cells), DEPTH, 1)
                        h.append(s + around_z(center[c], t))
                    m = [center[c][t] for c in range(COMPS)]
                    rate = turn(
                        m, h, spar[0, side, g, t], spar[1, side, g, t], spar[2, side, g, t]
                    )
                    if state == 0:
                        new = [m[c] + rate[c] for c in range(COMPS)]
                    else:
                        new = normal(
                            [strip[0][c, side, g, t] + (m[c] + rate[c]) for c in range(COMPS)]
                        )
                    done.append((side, g, t, new))
        for side, g, t, new in done:
            for c in range(COMPS):
                strip[1 - state][c, side, g, t] = new[c]
        for g in range(2):
            for t in range(tiles):
                left, right = (new for _, h, u, new in done if (h, u) == (g, t))
                for c in range(COMPS):
                    seam[1 - state][c, g, t] = seam_of(left[c], right[c])

    def main_rows(state, first, count):
        def rows(i, sums):
            done, ends, later = [], [], []
            each = COMPS * tiles
            for u in range(ROWS):
                r = (first + ROWS * (i - 1) + u) & (window - 1)
                done += main_turn(state, r, sums[each * u : each * (u + 1)])
            for u in range(ROWS):
                found, row_ends = main_sums(state, (first + ROWS * i + u) & (window - 1))
                later += found
                ends += row_ends
            for r, t, new in done:
                for c in range(COMPS):
                    main[1 - state][c, r, t] = new[c]
            for r, t, row_ends in ends:
                k = r & (ny - 1)
                mask = ((lane - (DEPTH * k + DEPTH - 1)) & (LANES - 1)) < 2
                for c in range(COMPS):
                    pltpu.store(edge.at[c, r // ny, t], row_ends[c], mask=mask)
            return tuple(later)

        zero = jnp.zeros((SUB, LANES), jnp.float32)
        lax.fori_loop(0, count // ROWS + 1, rows, (zero,) * (COMPS * tiles * ROWS))

    def step(i, carry):
        for state in range(2):
            margin = DEPTH - 2 * state - 2 * i
            main_rows(state, -margin, ny + 2 * margin)
            strip_rows(state)
        return carry

    lax.fori_loop(0, STEPS, step, 0)

    def hand_out(i, carry):
        for k in (2 * i, 2 * i + 1):
            for t in range(tiles):
                for c in range(COMPS):
                    out_ref[c, rows_at(ny, tiles, k, t), :] = main0[c, k, t]
        return carry

    lax.fori_loop(0, ny // 2, hand_out, 0)


def shifted(cells, axis, step, closed):
    count = lax.axis_size(axis)
    pairs = [(i, (i + step) % count) for i in range(count) if closed or 0 <= i + step < count]
    return lax.ppermute(cells, axis, pairs)


def swapped(cells, axis, first, closed):
    count = lax.axis_size(axis)
    pairs = [(i, (i + 1) % count) for i in range(first, count if closed else count - 1, 2)]
    return lax.ppermute(cells, axis, pairs + [(j, i) for i, j in pairs])


def around(cells, dim):
    ny = cells.shape[dim]
    if lax.axis_size("gy") == 2:
        return shifted(cells, "gy", 1, True)
    head = lax.slice_in_dim(cells, 0, DEPTH, axis=dim)
    tail = lax.slice_in_dim(cells, ny - DEPTH, ny, axis=dim)
    return jnp.concatenate([shifted(head, "gy", -1, True), shifted(tail, "gy", 1, True)], axis=dim)


def around_strips(both):
    if lax.axis_size("gy") == 2:
        return shifted(both, "gy", 1, True)
    block = lax.broadcasted_iota(jnp.int32, both.shape, both.ndim - 1) // DEPTH
    side = lax.broadcasted_iota(jnp.int32, both.shape, 0)
    head = (block + side - 1) % (LANES // DEPTH) < DEPTH
    return jnp.where(head, shifted(both, "gy", -1, True), shifted(both, "gy", 1, True))


def body(magnetization, lower_image, image_weights, regions, anisotropy, damping):
    local, comps, nz, ny, nx = magnetization.shape
    images = local * lax.axis_size("img")
    tiles = nz // SUB
    devices = lax.axis_size(("img", "gx", "gy"))
    assert lax.axis_size("gx") % 2 == 0
    assert local == 1 and comps == COMPS and nx == LANES
    assert ny == 2 * DEPTH and ny * DEPTH == LANES and tiles >= 2
    flat = (comps, nz * ny, nx)
    own = magnetization[0]
    own_p = around(own, 2)
    first = swapped(own, "img", 0, False)
    second = swapped(own, "img", 1, False)

    smem = pl.BlockSpec(memory_space=pltpu.SMEM)
    vmem = pl.BlockSpec(memory_space=pltpu.VMEM)
    f32 = jnp.float32
    limit = pltpu.CompilerParams(vmem_limit_bytes=32 * 1024 * 1024)
    vreg = (SUB, LANES)
    packed = jax.ShapeDtypeStruct((comps + 1, tiles) + vreg, f32)
    left, right, info = pl.pallas_call(
        functools.partial(pack_kernel, ny, tiles, anisotropy.shape[0]),
        out_shape=(packed, packed, jax.ShapeDtypeStruct((5,) + vreg, f32)),
        in_specs=[smem] * 3 + [vmem] * 3,
        out_specs=(vmem,) * 3,
        compiler_params=limit,
        name="pack_strips",
    )(
        lower_image,
        anisotropy,
        damping,
        image_weights.reshape(1, -1),
        own.reshape(flat),
        regions.reshape(flat[1:]),
    )
    late_regions, info = lax.optimization_barrier((regions, info))
    reg_p = around(late_regions, 1)
    info, own_p, reg_p = lax.optimization_barrier((info, own_p, reg_p))
    packed = jax.ShapeDtypeStruct((2 * comps + 1, tiles) + vreg, f32)
    part, near, one, two = pl.pallas_call(
        functools.partial(gather_kernel, ny, tiles),
        out_shape=(
            jax.ShapeDtypeStruct((devices, LANES), f32),
            jax.ShapeDtypeStruct(flat, f32),
            packed,
            packed,
        ),
        in_specs=[vmem] * 6,
        out_specs=(vmem,) * 4,
        compiler_params=limit,
        name="gather_images",
    )(info, own.reshape(flat), first.reshape(flat), second.reshape(flat), left, right)
    near_p = around(near.reshape(own.shape), 2)
    one = swapped(one, "gx", 0, True)
    two = swapped(two, "gx", 1, True)
    strips = pl.pallas_call(
        merge_kernel,
        out_shape=jax.ShapeDtypeStruct((2,) + packed.shape, f32),
        in_specs=[vmem] * 2,
        out_specs=vmem,
        compiler_params=limit,
        name="merge_strips",
    )(one, two)
    strips_p = around_strips(strips)
    squares = lax.all_to_all(part, ("img", "gx", "gy"), 0, 0, tiled=True)

    window = ny + 2 * DEPTH
    out = pl.pallas_call(
        functools.partial(evolve_kernel, ny, tiles, images),
        out_shape=jax.ShapeDtypeStruct(flat, f32),
        in_specs=[vmem] * 10,
        out_specs=vmem,
        scratch_shapes=[
            pltpu.VMEM((comps, window, tiles) + vreg, f32),
            pltpu.VMEM((comps, window, tiles) + vreg, f32),
            pltpu.VMEM((comps, 2, 2, tiles) + vreg, f32),
            pltpu.VMEM((comps, 2, 2, tiles) + vreg, f32),
            pltpu.VMEM((comps, 2, tiles) + vreg, f32),
            pltpu.VMEM((comps, 2, tiles) + vreg, f32),
            pltpu.VMEM((comps, 2, tiles) + vreg, f32),
            pltpu.VMEM((3, window, tiles) + vreg, f32),
            pltpu.VMEM((3, 2, 2, tiles) + vreg, f32),
        ],
        compiler_params=limit,
        name="evolve",
    )(
        info,
        squares,
        own.reshape(flat),
        own_p.reshape(flat),
        near,
        near_p.reshape(flat),
        regions.reshape(flat[1:]),
        reg_p.reshape(flat[1:]),
        strips,
        strips_p,
    )
    return out.reshape(magnetization.shape)


def solution(mesh):
    placed = (P("img", None, None, "gy", "gx"), P(), P(), P(None, "gy", "gx"), P(), P())
    return jax.shard_map(
        body,
        mesh=mesh,
        in_specs=placed,
        out_specs=P("img", None, None, "gy", "gx"),
        check_vma=False,
    )
```

```python
import functools

import jax
import jax.numpy as jnp
from jax import lax
from jax.experimental import pallas as pl
from jax.experimental.pallas import tpu as pltpu
from jax.sharding import PartitionSpec as P

STEPS = 4
DEPTH = 2 * STEPS

eps = 1e-06
time_step = 0.05

SUB = 8
LANES = 128
COMPS = 3
ROWS = 4


def lane_iota():
    return lax.broadcasted_iota(jnp.int32, (SUB, LANES), 1)


def sub_iota():
    return lax.broadcasted_iota(jnp.int32, (SUB, LANES), 0)


def rows_at(ny, tiles, y, t):
    return pl.ds(y + ny * t, SUB, stride=ny * tiles)


def pack_kernel(
    ny, tiles, regions, lower_ref, aniso_ref, damp_ref, share_ref, m_ref, reg_ref, left_ref, right_ref, info_ref
):
    here = lax.axis_index("img")
    lane = lane_iota()
    block = lane // DEPTH
    def pack(i, carry):
        done = []
        for u in range(2):
            y = 2 * i + u
            shift = (DEPTH * (y + 1)) & (LANES - 1)
            left = block == ((y + 1) & (ny - 1))
            right = block == y
            for t in range(tiles):
                rows = rows_at(ny, tiles, y, t)
                for c in range(COMPS + 1):
                    cells = m_ref[c, rows, :] if c < COMPS else reg_ref[rows, :].astype(jnp.float32)
                    done.append((c, t, left, right, pltpu.roll(cells, shift, 1)))
        for c, t, left, right, cells in done:
            pltpu.store(left_ref.at[c, t], cells, mask=left)
            pltpu.store(right_ref.at[c, t], cells, mask=right)
        return carry

    table_a = jnp.zeros((SUB, LANES), jnp.float32)
    table_d = jnp.zeros((SUB, LANES), jnp.float32)
    for i in range(regions):
        table_a = jnp.where(lane == i, 2.0 * aniso_ref[i], table_a)
        table_d = jnp.where(lane == i, damp_ref[i], table_d)
    info_ref[0] = table_a
    info_ref[1] = table_d
    info_ref[2] = -time_step / (1.0 + table_d * table_d)
    share = share_ref[...]
    spot = lax.broadcasted_iota(jnp.int32, share.shape, 1)
    target = jnp.sum(jnp.where(spot < here, share, 0.0), axis=1, keepdims=True) / jnp.sum(
        share, axis=1, keepdims=True
    )
    info_ref[3] = jnp.broadcast_to(target, (SUB, LANES))
    info_ref[4] = jnp.full((SUB, LANES), lower_ref[here].astype(jnp.float32))

    lax.fori_loop(0, ny // 2, pack, 0)


def merge_kernel(one_ref, two_ref, out_ref):
    turned = (lax.axis_index("gx") & 1) == 1
    one, two = one_ref[...], two_ref[...]
    out_ref[0] = jnp.where(turned, one, two)
    out_ref[1] = jnp.where(turned, two, one)


def take_first(info_ref, here):
    odd = (here & 1) == 1
    below = info_ref[4] < here.astype(jnp.float32)
    return jnp.where(below, jnp.where(odd, 1, 0), jnp.where(odd, 0, 1)) == 1, odd


def gather_kernel(
    ny, tiles, info_ref, m_ref, first_ref, second_ref, own_left_ref, own_right_ref, part_ref, near_ref, one_ref, two_ref
):
    here = lax.axis_index("img")
    pick, odd = take_first(info_ref, here)
    chunks = 4
    depth = m_ref.shape[1]

    def squares(i, sums):
        sums = list(sums)
        done = []
        for u in range(chunks):
            start = pl.multiple_of((chunks * i + u) * SUB, SUB)
            for c in range(COMPS):
                one = first_ref[c, pl.ds(start, SUB), :]
                two = second_ref[c, pl.ds(start, SUB), :]
                done.append((c, start, jnp.where(pick, one, two)))
                diff = m_ref[c, pl.ds(start, SUB), :] - jnp.where(odd, one, two)
                sums[c + COMPS * u] = sums[c + COMPS * u] + diff * diff
        for c, start, cells in done:
            near_ref[c, pl.ds(start, SUB), :] = cells
        return tuple(sums)

    zero = jnp.zeros((SUB, LANES), jnp.float32)
    sums = lax.fori_loop(0, depth // (chunks * SUB), squares, (zero,) * (chunks * COMPS))
    total = jnp.sum(functools.reduce(jnp.add, sums), axis=(0, 1), keepdims=True)
    slot = lax.broadcasted_iota(jnp.int32, part_ref.shape, 1)
    part_ref[...] = jnp.where((slot == here) & (here > 0), total, 0.0)
    turned = (lax.axis_index("gx") & 1) == 1
    one_ref[COMPS:] = jnp.where(turned, own_left_ref[...], own_right_ref[...])
    two_ref[COMPS:] = jnp.where(turned, own_right_ref[...], own_left_ref[...])
    block = lane_iota() // DEPTH

    def pack(i, carry):
        done = []
        for u in range(2):
            y = 2 * i + u
            after = (y + 1) & (ny - 1)
            one = block == jnp.where(turned, after, y)
            two = block == jnp.where(turned, y, after)
            shift = (DEPTH * (y + 1)) & (LANES - 1)
            for t in range(tiles):
                for c in range(COMPS):
                    cells = pltpu.roll(near_ref[c, rows_at(ny, tiles, y, t), :], shift, 1)
                    done.append((c, t, one, two, cells))
        for c, t, one, two, cells in done:
            pltpu.store(one_ref.at[c, t], cells, mask=one)
            pltpu.store(two_ref.at[c, t], cells, mask=two)
        return carry

    lax.fori_loop(0, ny // 2, pack, 0)


def turn(m, h, a2, b, sc):
    mx, my, mz = m
    hx, hy, hz = h
    hz = hz + a2 * mz
    gx = hx + b * (my * hz - mz * hy)
    gy = hy + b * (mz * hx - mx * hz)
    gz = hz + b * (mx * hy - my * hx)
    return (
        sc * (my * gz - mz * gy),
        sc * (mz * gx - mx * gz),
        sc * (mx * gy - my * gx),
    )


def normal(v):
    scale = lax.rsqrt(v[0] * v[0] + v[1] * v[1] + v[2] * v[2])
    return tuple(x * scale for x in v)


def evolve_kernel(
    ny,
    tiles,
    images,
    info_ref,
    sq_ref,
    m_ref,
    mp_ref,
    n_ref,
    np_ref,
    reg_ref,
    regp_ref,
    strips_ref,
    stripsp_ref,
    out_ref,
    main0,
    main1,
    strip0,
    strip1,
    edge,
    seam0,
    seam1,
    par,
    spar,
):
    main, strip, seam = (main0, main1), (strip0, strip1), (seam0, seam1)
    window = ny + 2 * DEPTH
    here = lax.axis_index("img")
    lane = lane_iota()
    sub = sub_iota()
    block = lane // DEPTH
    first_lane = lane == 0
    last_lane = lane == LANES - 1
    head_lane = lane % DEPTH == 0
    tail_lane = lane % DEPTH == DEPTH - 1
    top = sub == SUB - 1
    bottom = sub == 0

    lo = info_ref[4]
    slot = lane.astype(jnp.float32)
    squares = jnp.broadcast_to(jnp.sum(sq_ref[...], axis=0, keepdims=True), (SUB, LANES))
    lengths = jnp.where((lane >= 1) & (lane < images), jnp.sqrt(squares + eps), 0.0)
    total = jnp.sum(lengths, axis=1, keepdims=True)
    arc = jnp.sum(jnp.where(slot <= lo, lengths, 0.0), axis=1, keepdims=True)
    gap = jnp.sum(jnp.where(slot == lo + 1.0, lengths, 0.0), axis=1, keepdims=True)
    weight = jnp.clip((info_ref[3] * total - arc) / gap, -0.5, 1.5)
    below = lo < here.astype(jnp.float32)
    w_own = jnp.where(below, weight, 1.0 - weight)
    w_near = jnp.where(below, 1.0 - weight, weight)

    tables = (info_ref[0], info_ref[1], info_ref[2])

    def params(region):
        return [jnp.take_along_axis(table, region, axis=1) for table in tables]

    def ends_of(k, new):
        shift = (DEPTH * (k + 1)) & (LANES - 1)
        return [pltpu.roll(new[c], shift, 1) for c in range(COMPS)]

    def place(r, t, offset=0):
        row = (tiles + 1) * SUB * r + SUB * (0 if t == 0 else 2 if t == tiles - 1 else t + 2)
        return pl.ds(row + offset if offset else pl.multiple_of(row, SUB), SUB)

    zero = jnp.zeros((SUB, LANES), jnp.float32)

    def fill(i, carry):
        done = []
        for k in (2 * i, 2 * i + 1):
            for g, (own, near, reg) in enumerate(((m_ref, n_ref, reg_ref), (mp_ref, np_ref, regp_ref))):
                for t in range(tiles):
                    rows = rows_at(ny, tiles, k, t)
                    v = normal(
                        [w_own * own[c, rows, :] + w_near * near[c, rows, :] for c in range(COMPS)]
                    )
                    done.append((g * ny + k, t, v, params(reg[rows, :])))
        for r, t, v, p in done:
            for c in range(COMPS):
                main0[c, place(r, t), :] = v[c]
                if t == 0:
                    main0[c, place(r, t, SUB), :] = zero
                    main1[c, place(r, t, SUB), :] = zero
            for i in range(3):
                par[i, r, t] = p[i]
        return carry

    lax.fori_loop(0, ny // 2, fill, 0)

    def seam_of(left, right):
        return jnp.where(head_lane, pltpu.roll(left, 1, 1), pltpu.roll(right, LANES - 1, 1))

    def fill_strips(t, carry):
        done = []
        for g, cells in enumerate((strips_ref, stripsp_ref)):
            for side in range(2):
                v = normal(
                    [w_own * cells[side, COMPS + c, t] + w_near * cells[side, c, t] for c in range(COMPS)]
                )
                done.append((side, g, v, params(cells[side, 2 * COMPS, t].astype(jnp.int32))))
        for side, g, v, p in done:
            for c in range(COMPS):
                strip0[c, side, g, t] = v[c]
            for i in range(3):
                spar[i, side, g, t] = p[i]
        for g in range(2):
            left, right = (v for _, h, v, _ in done if h == g)
            for c in range(COMPS):
                seam0[c, g, t] = seam_of(left[c], right[c])
        return carry

    lax.fori_loop(0, tiles, fill_strips, 0)

    def around_z(cells, t):
        if t + 1 < tiles:
            above = cells[t + 1]
        else:
            above = jnp.where(top, 0.0, pltpu.roll(cells[0], SUB - 1, 0))
        if t > 0:
            under = cells[t - 1]
        else:
            under = jnp.where(bottom, 0.0, pltpu.roll(cells[tiles - 1], 1, 0))
        return above + under

    def main_row(state, r):
        g = r // ny
        k = r & (ny - 1)
        after = (r + 1) & (window - 1)
        before = (r - 1) & (window - 1)
        shift = (LANES - DEPTH * (k + 1)) & (LANES - 1)
        done = []
        for t in range(tiles):
            m, h = [], []
            for c in range(COMPS):
                cells = main[state][c, place(r, t), :]
                ends = pltpu.roll(seam[state][c, g, t], shift, 1)
                s = jnp.where(first_lane, ends, pltpu.roll(cells, 1, 1))
                s = s + jnp.where(last_lane, ends, pltpu.roll(cells, LANES - 1, 1))
                s = s + (main[state][c, place(after, t), :] + main[state][c, place(before, t), :])
                if t + 1 < tiles:
                    above = main[state][c, place(r, t + 1), :]
                else:
                    above = main[state][c, place(r, 0, 1), :]
                if t > 0:
                    under = main[state][c, place(r, t - 1), :]
                else:
                    under = main[state][c, place(r, tiles - 1, -1), :]
                h.append(s + (above + under))
                m.append(cells)
            rate = turn(m, h, par[0, r, t], par[1, r, t], par[2, r, t])
            if state == 0:
                new = [m[c] + rate[c] for c in range(COMPS)]
            else:
                new = normal([main[0][c, place(r, t), :] + (m[c] + rate[c]) for c in range(COMPS)])
            done.append((r, t, new, ends_of(k, m)))
        return done

    def strip_rows(state):
        done = []
        for g in range(2):
            for side in range(2):
                start = block == side
                stop = block == (side + ny - 1) % ny
                center = [[strip[state][c, side, g, t] for t in range(tiles)] for c in range(COMPS)]
                for t in range(tiles):
                    h = []
                    for c in range(COMPS):
                        cells = center[c][t]
                        inner = edge[c, g, t]
                        other = strip[state][c, side, 1 - g, t]
                        if side == 0:
                            s = pltpu.roll(cells, 1, 1)
                            s = s + pltpu.roll(jnp.where(head_lane, inner, cells), LANES - 1, 1)
                        else:
                            s = pltpu.roll(jnp.where(tail_lane, inner, cells), 1, 1)
                            s = s + pltpu.roll(cells, LANES - 1, 1)
                        s = s + pltpu.roll(jnp.where(start, other, cells), LANES - DEPTH, 1)
                        s = s + pltpu.roll(jnp.where(stop, other, cells), DEPTH, 1)
                        h.append(s + around_z(center[c], t))
                    m = [center[c][t] for c in range(COMPS)]
                    rate = turn(
                        m, h, spar[0, side, g, t], spar[1, side, g, t], spar[2, side, g, t]
                    )
                    if state == 0:
                        new = [m[c] + rate[c] for c in range(COMPS)]
                    else:
                        new = normal(
                            [strip[0][c, side, g, t] + (m[c] + rate[c]) for c in range(COMPS)]
                        )
                    done.append((side, g, t, new))
        for side, g, t, new in done:
            for c in range(COMPS):
                strip[1 - state][c, side, g, t] = new[c]
        for g in range(2):
            for t in range(tiles):
                left, right = (new for _, h, u, new in done if (h, u) == (g, t))
                for c in range(COMPS):
                    seam[1 - state][c, g, t] = seam_of(left[c], right[c])

    def main_rows(state, first, count):
        def rows(i, carry):
            done = []
            for u in range(ROWS):
                done += main_row(state, (first + ROWS * i + u) & (window - 1))
            for r, t, new, ends in done:
                k = r & (ny - 1)
                mask = ((lane - (DEPTH * k + DEPTH - 1)) & (LANES - 1)) < 2
                for c in range(COMPS):
                    main[1 - state][c, place(r, t), :] = new[c]
                    pltpu.store(edge.at[c, r // ny, t], ends[c], mask=mask)
            return carry

        lax.fori_loop(0, count // ROWS, rows, 0)

    def step(i, carry):
        for state in range(2):
            margin = DEPTH - 2 * state - 2 * i
            main_rows(state, -margin, ny + 2 * margin)
            strip_rows(state)
        return carry

    lax.fori_loop(0, STEPS, step, 0)

    def hand_out(i, carry):
        for k in (2 * i, 2 * i + 1):
            for t in range(tiles):
                for c in range(COMPS):
                    out_ref[c, rows_at(ny, tiles, k, t), :] = main0[c, place(k, t), :]
        return carry

    lax.fori_loop(0, ny // 2, hand_out, 0)


def shifted(cells, axis, step, closed):
    count = lax.axis_size(axis)
    pairs = [(i, (i + step) % count) for i in range(count) if closed or 0 <= i + step < count]
    return lax.ppermute(cells, axis, pairs)


def swapped(cells, axis, first, closed):
    count = lax.axis_size(axis)
    pairs = [(i, (i + 1) % count) for i in range(first, count if closed else count - 1, 2)]
    return lax.ppermute(cells, axis, pairs + [(j, i) for i, j in pairs])


def around(cells, dim):
    ny = cells.shape[dim]
    if lax.axis_size("gy") == 2:
        return shifted(cells, "gy", 1, True)
    head = lax.slice_in_dim(cells, 0, DEPTH, axis=dim)
    tail = lax.slice_in_dim(cells, ny - DEPTH, ny, axis=dim)
    return jnp.concatenate([shifted(head, "gy", -1, True), shifted(tail, "gy", 1, True)], axis=dim)


def around_strips(both):
    if lax.axis_size("gy") == 2:
        return shifted(both, "gy", 1, True)
    block = lax.broadcasted_iota(jnp.int32, both.shape, both.ndim - 1) // DEPTH
    side = lax.broadcasted_iota(jnp.int32, both.shape, 0)
    head = (block + side - 1) % (LANES // DEPTH) < DEPTH
    return jnp.where(head, shifted(both, "gy", -1, True), shifted(both, "gy", 1, True))


def body(magnetization, lower_image, image_weights, regions, anisotropy, damping):
    local, comps, nz, ny, nx = magnetization.shape
    images = local * lax.axis_size("img")
    tiles = nz // SUB
    devices = lax.axis_size(("img", "gx", "gy"))
    assert lax.axis_size("gx") % 2 == 0
    assert local == 1 and comps == COMPS and nx == LANES
    assert ny == 2 * DEPTH and ny * DEPTH == LANES and tiles >= 2
    flat = (comps, nz * ny, nx)
    own = magnetization[0]
    own_p = around(own, 2)
    first = swapped(own, "img", 0, False)
    second = swapped(own, "img", 1, False)

    smem = pl.BlockSpec(memory_space=pltpu.SMEM)
    vmem = pl.BlockSpec(memory_space=pltpu.VMEM)
    f32 = jnp.float32
    limit = pltpu.CompilerParams(vmem_limit_bytes=32 * 1024 * 1024)
    vreg = (SUB, LANES)
    packed = jax.ShapeDtypeStruct((comps + 1, tiles) + vreg, f32)
    left, right, info = pl.pallas_call(
        functools.partial(pack_kernel, ny, tiles, anisotropy.shape[0]),
        out_shape=(packed, packed, jax.ShapeDtypeStruct((5,) + vreg, f32)),
        in_specs=[smem] * 3 + [vmem] * 3,
        out_specs=(vmem,) * 3,
        compiler_params=limit,
        name="pack_strips",
    )(
        lower_image,
        anisotropy,
        damping,
        image_weights.reshape(1, -1),
        own.reshape(flat),
        regions.reshape(flat[1:]),
    )
    late_regions, info = lax.optimization_barrier((regions, info))
    reg_p = around(late_regions, 1)
    info, own_p, reg_p = lax.optimization_barrier((info, own_p, reg_p))
    packed = jax.ShapeDtypeStruct((2 * comps + 1, tiles) + vreg, f32)
    part, near, one, two = pl.pallas_call(
        functools.partial(gather_kernel, ny, tiles),
        out_shape=(
            jax.ShapeDtypeStruct((devices, LANES), f32),
            jax.ShapeDtypeStruct(flat, f32),
            packed,
            packed,
        ),
        in_specs=[vmem] * 6,
        out_specs=(vmem,) * 4,
        compiler_params=limit,
        name="gather_images",
    )(info, own.reshape(flat), first.reshape(flat), second.reshape(flat), left, right)
    near_p = around(near.reshape(own.shape), 2)
    one = swapped(one, "gx", 0, True)
    two = swapped(two, "gx", 1, True)
    strips = pl.pallas_call(
        merge_kernel,
        out_shape=jax.ShapeDtypeStruct((2,) + packed.shape, f32),
        in_specs=[vmem] * 2,
        out_specs=vmem,
        compiler_params=limit,
        name="merge_strips",
    )(one, two)
    strips_p = around_strips(strips)
    squares = lax.all_to_all(part, ("img", "gx", "gy"), 0, 0, tiled=True)

    window = ny + 2 * DEPTH
    out = pl.pallas_call(
        functools.partial(evolve_kernel, ny, tiles, images),
        out_shape=jax.ShapeDtypeStruct(flat, f32),
        in_specs=[vmem] * 10,
        out_specs=vmem,
        scratch_shapes=[
            pltpu.VMEM((comps, window * (tiles + 1) * SUB, LANES), f32),
            pltpu.VMEM((comps, window * (tiles + 1) * SUB, LANES), f32),
            pltpu.VMEM((comps, 2, 2, tiles) + vreg, f32),
            pltpu.VMEM((comps, 2, 2, tiles) + vreg, f32),
            pltpu.VMEM((comps, 2, tiles) + vreg, f32),
            pltpu.VMEM((comps, 2, tiles) + vreg, f32),
            pltpu.VMEM((comps, 2, tiles) + vreg, f32),
            pltpu.VMEM((3, window, tiles) + vreg, f32),
            pltpu.VMEM((3, 2, 2, tiles) + vreg, f32),
        ],
        compiler_params=limit,
        name="evolve",
    )(
        info,
        squares,
        own.reshape(flat),
        own_p.reshape(flat),
        near,
        near_p.reshape(flat),
        regions.reshape(flat[1:]),
        reg_p.reshape(flat[1:]),
        strips,
        strips_p,
    )
    return out.reshape(magnetization.shape)


def solution(mesh):
    placed = (P("img", None, None, "gy", "gx"), P(), P(), P(None, "gy", "gx"), P(), P())
    return jax.shard_map(
        body,
        mesh=mesh,
        in_specs=placed,
        out_specs=P("img", None, None, "gy", "gx"),
        check_vma=False,
    )
```

```python
import functools

import jax
import jax.numpy as jnp
from jax import lax
from jax.experimental import pallas as pl
from jax.experimental.pallas import tpu as pltpu
from jax.sharding import PartitionSpec as P

STEPS = 4
DEPTH = 2 * STEPS

eps = 1e-06
time_step = 0.05

SUB = 8
LANES = 128
COMPS = 3
ROWS = 4


def lane_iota():
    return lax.broadcasted_iota(jnp.int32, (SUB, LANES), 1)


def sub_iota():
    return lax.broadcasted_iota(jnp.int32, (SUB, LANES), 0)


def rows_at(ny, tiles, y, t):
    return pl.ds(y + ny * t, SUB, stride=ny * tiles)


def pack_kernel(
    ny, tiles, regions, lower_ref, aniso_ref, damp_ref, share_ref, m_ref, reg_ref, left_ref, right_ref, info_ref
):
    here = lax.axis_index("img")
    lane = lane_iota()
    block = lane // DEPTH
    def pack(i, carry):
        done = []
        for u in range(2):
            y = 2 * i + u
            shift = (DEPTH * (y + 1)) & (LANES - 1)
            left = block == ((y + 1) & (ny - 1))
            right = block == y
            for t in range(tiles):
                rows = rows_at(ny, tiles, y, t)
                for c in range(COMPS + 1):
                    cells = m_ref[c, rows, :] if c < COMPS else reg_ref[rows, :].astype(jnp.float32)
                    done.append((c, t, left, right, pltpu.roll(cells, shift, 1)))
        for c, t, left, right, cells in done:
            pltpu.store(left_ref.at[c, t], cells, mask=left)
            pltpu.store(right_ref.at[c, t], cells, mask=right)
        return carry

    table_a = jnp.zeros((SUB, LANES), jnp.float32)
    table_d = jnp.zeros((SUB, LANES), jnp.float32)
    for i in range(regions):
        table_a = jnp.where(lane == i, 2.0 * aniso_ref[i], table_a)
        table_d = jnp.where(lane == i, damp_ref[i], table_d)
    info_ref[0] = table_a
    info_ref[1] = table_d
    info_ref[2] = -time_step / (1.0 + table_d * table_d)
    share = share_ref[...]
    spot = lax.broadcasted_iota(jnp.int32, share.shape, 1)
    target = jnp.sum(jnp.where(spot < here, share, 0.0), axis=1, keepdims=True) / jnp.sum(
        share, axis=1, keepdims=True
    )
    info_ref[3] = jnp.broadcast_to(target, (SUB, LANES))
    info_ref[4] = jnp.full((SUB, LANES), lower_ref[here].astype(jnp.float32))

    lax.fori_loop(0, ny // 2, pack, 0)


def merge_kernel(one_ref, two_ref, out_ref):
    turned = (lax.axis_index("gx") & 1) == 1
    one, two = one_ref[...], two_ref[...]
    out_ref[0] = jnp.where(turned, one, two)
    out_ref[1] = jnp.where(turned, two, one)


def take_first(info_ref, here):
    odd = (here & 1) == 1
    below = info_ref[4] < here.astype(jnp.float32)
    return jnp.where(below, jnp.where(odd, 1, 0), jnp.where(odd, 0, 1)) == 1, odd


def gather_kernel(
    ny, tiles, info_ref, m_ref, first_ref, second_ref, own_left_ref, own_right_ref, part_ref, near_ref, one_ref, two_ref
):
    here = lax.axis_index("img")
    pick, odd = take_first(info_ref, here)
    chunks = 4
    depth = m_ref.shape[1]

    def squares(i, sums):
        sums = list(sums)
        done = []
        for u in range(chunks):
            start = pl.multiple_of((chunks * i + u) * SUB, SUB)
            for c in range(COMPS):
                one = first_ref[c, pl.ds(start, SUB), :]
                two = second_ref[c, pl.ds(start, SUB), :]
                done.append((c, start, jnp.where(pick, one, two)))
                diff = m_ref[c, pl.ds(start, SUB), :] - jnp.where(odd, one, two)
                sums[c + COMPS * u] = sums[c + COMPS * u] + diff * diff
        for c, start, cells in done:
            near_ref[c, pl.ds(start, SUB), :] = cells
        return tuple(sums)

    zero = jnp.zeros((SUB, LANES), jnp.float32)
    sums = lax.fori_loop(0, depth // (chunks * SUB), squares, (zero,) * (chunks * COMPS))
    total = jnp.sum(functools.reduce(jnp.add, sums), axis=(0, 1), keepdims=True)
    slot = lane_iota()
    part_ref[...] = jnp.where((slot == here) & (here > 0), total, 0.0)
    turned = (lax.axis_index("gx") & 1) == 1
    one_ref[COMPS:] = jnp.where(turned, own_left_ref[...], own_right_ref[...])
    two_ref[COMPS:] = jnp.where(turned, own_right_ref[...], own_left_ref[...])
    block = lane_iota() // DEPTH

    def pack(i, carry):
        done = []
        for u in range(2):
            y = 2 * i + u
            after = (y + 1) & (ny - 1)
            one = block == jnp.where(turned, after, y)
            two = block == jnp.where(turned, y, after)
            shift = (DEPTH * (y + 1)) & (LANES - 1)
            for t in range(tiles):
                for c in range(COMPS):
                    cells = pltpu.roll(near_ref[c, rows_at(ny, tiles, y, t), :], shift, 1)
                    done.append((c, t, one, two, cells))
        for c, t, one, two, cells in done:
            pltpu.store(one_ref.at[c, t], cells, mask=one)
            pltpu.store(two_ref.at[c, t], cells, mask=two)
        return carry

    lax.fori_loop(0, ny // 2, pack, 0)


def turn(m, h, a2, b, sc):
    mx, my, mz = m
    hx, hy, hz = h
    hz = hz + a2 * mz
    gx = hx + b * (my * hz - mz * hy)
    gy = hy + b * (mz * hx - mx * hz)
    gz = hz + b * (mx * hy - my * hx)
    return (
        sc * (my * gz - mz * gy),
        sc * (mz * gx - mx * gz),
        sc * (mx * gy - my * gx),
    )


def normal(v):
    scale = lax.rsqrt(v[0] * v[0] + v[1] * v[1] + v[2] * v[2])
    return tuple(x * scale for x in v)


def evolve_kernel(
    ny,
    tiles,
    images,
    info_ref,
    m_ref,
    mp_ref,
    n_ref,
    np_ref,
    reg_ref,
    regp_ref,
    strips_ref,
    stripsp_ref,
    *refs,
):
    *sq_refs, out_ref = refs[:-9]
    main0, main1, strip0, strip1, edge, seam0, seam1, par, spar = refs[-9:]
    main, strip, seam = (main0, main1), (strip0, strip1), (seam0, seam1)
    window = ny + 2 * DEPTH
    here = lax.axis_index("img")
    lane = lane_iota()
    sub = sub_iota()
    block = lane // DEPTH
    first_lane = lane == 0
    last_lane = lane == LANES - 1
    head_lane = lane % DEPTH == 0
    tail_lane = lane % DEPTH == DEPTH - 1
    top = sub == SUB - 1
    bottom = sub == 0

    lo = info_ref[4]
    slot = lane.astype(jnp.float32)
    squares = functools.reduce(jnp.add, [ref[...] for ref in sq_refs])
    lengths = jnp.where((lane >= 1) & (lane < images), jnp.sqrt(squares + eps), 0.0)
    total = jnp.sum(lengths, axis=1, keepdims=True)
    arc = jnp.sum(jnp.where(slot <= lo, lengths, 0.0), axis=1, keepdims=True)
    gap = jnp.sum(jnp.where(slot == lo + 1.0, lengths, 0.0), axis=1, keepdims=True)
    weight = jnp.clip((info_ref[3] * total - arc) / gap, -0.5, 1.5)
    below = lo < here.astype(jnp.float32)
    w_own = jnp.where(below, weight, 1.0 - weight)
    w_near = jnp.where(below, 1.0 - weight, weight)

    tables = (info_ref[0], info_ref[1], info_ref[2])

    def params(region):
        return [jnp.take_along_axis(table, region, axis=1) for table in tables]

    def ends_of(k, new):
        shift = (DEPTH * (k + 1)) & (LANES - 1)
        return [pltpu.roll(new[c], shift, 1) for c in range(COMPS)]

    def fill(k, carry):
        done = []
        for g, (own, near, reg) in enumerate(((m_ref, n_ref, reg_ref), (mp_ref, np_ref, regp_ref))):
            for t in range(tiles):
                rows = rows_at(ny, tiles, k, t)
                v = normal(
                    [
                        w_own * own[c, rows, :] + w_near * near[c, rows, :]
                        for c in range(COMPS)
                    ]
                )
                done.append((g * ny + k, t, v, params(reg[rows, :])))
        for r, t, v, p in done:
            for c in range(COMPS):
                main0[c, r, t] = v[c]
            for i in range(3):
                par[i, r, t] = p[i]
        return carry

    lax.fori_loop(0, ny, fill, 0)

    def seam_of(left, right):
        return jnp.where(head_lane, pltpu.roll(left, 1, 1), pltpu.roll(right, LANES - 1, 1))

    def fill_strips(t, carry):
        done = []
        for g, cells in enumerate((strips_ref, stripsp_ref)):
            for side in range(2):
                v = normal(
                    [w_own * cells[side, COMPS + c, t] + w_near * cells[side, c, t] for c in range(COMPS)]
                )
                done.append((side, g, v, params(cells[side, 2 * COMPS, t].astype(jnp.int32))))
        for side, g, v, p in done:
            for c in range(COMPS):
                strip0[c, side, g, t] = v[c]
            for i in range(3):
                spar[i, side, g, t] = p[i]
        for g in range(2):
            left, right = (v for _, h, v, _ in done if h == g)
            for c in range(COMPS):
                seam0[c, g, t] = seam_of(left[c], right[c])
        return carry

    lax.fori_loop(0, tiles, fill_strips, 0)

    def around_z(cells, t):
        if t + 1 < tiles:
            above = cells[t + 1]
        else:
            above = jnp.where(top, 0.0, pltpu.roll(cells[0], SUB - 1, 0))
        if t > 0:
            under = cells[t - 1]
        else:
            under = jnp.where(bottom, 0.0, pltpu.roll(cells[tiles - 1], 1, 0))
        return above + under

    def main_row(state, r):
        g = r // ny
        k = r & (ny - 1)
        after = (r + 1) & (window - 1)
        before = (r - 1) & (window - 1)
        shift = (LANES - DEPTH * (k + 1)) & (LANES - 1)
        center = [[main[state][c, r, t] for t in range(tiles)] for c in range(COMPS)]
        done = []
        for t in range(tiles):
            h = []
            for c in range(COMPS):
                cells = center[c][t]
                ends = pltpu.roll(seam[state][c, g, t], shift, 1)
                s = jnp.where(first_lane, ends, pltpu.roll(cells, 1, 1))
                s = s + jnp.where(last_lane, ends, pltpu.roll(cells, LANES - 1, 1))
                s = s + (main[state][c, after, t] + main[state][c, before, t])
                h.append(s + around_z(center[c], t))
            m = [center[c][t] for c in range(COMPS)]
            rate = turn(m, h, par[0, r, t], par[1, r, t], par[2, r, t])
            if state == 0:
                new = [m[c] + rate[c] for c in range(COMPS)]
            else:
                new = normal([main[0][c, r, t] + (m[c] + rate[c]) for c in range(COMPS)])
            done.append((r, t, new, ends_of(k, m)))
        return done

    def strip_rows(state):
        done = []
        for g in range(2):
            for side in range(2):
                start = block == side
                stop = block == (side + ny - 1) % ny
                center = [[strip[state][c, side, g, t] for t in range(tiles)] for c in range(COMPS)]
                for t in range(tiles):
                    h = []
                    for c in range(COMPS):
                        cells = center[c][t]
                        inner = edge[c, g, t]
                        other = strip[state][c, side, 1 - g, t]
                        if side == 0:
                            s = pltpu.roll(cells, 1, 1)
                            s = s + pltpu.roll(jnp.where(head_lane, inner, cells), LANES - 1, 1)
                        else:
                            s = pltpu.roll(jnp.where(tail_lane, inner, cells), 1, 1)
                            s = s + pltpu.roll(cells, LANES - 1, 1)
                        s = s + pltpu.roll(jnp.where(start, other, cells), LANES - DEPTH, 1)
                        s = s + pltpu.roll(jnp.where(stop, other, cells), DEPTH, 1)
                        h.append(s + around_z(center[c], t))
                    m = [center[c][t] for c in range(COMPS)]
                    rate = turn(
                        m, h, spar[0, side, g, t], spar[1, side, g, t], spar[2, side, g, t]
                    )
                    if state == 0:
                        new = [m[c] + rate[c] for c in range(COMPS)]
                    else:
                        new = normal(
                            [strip[0][c, side, g, t] + (m[c] + rate[c]) for c in range(COMPS)]
                        )
                    done.append((side, g, t, new))
        for side, g, t, new in done:
            for c in range(COMPS):
                strip[1 - state][c, side, g, t] = new[c]
        for g in range(2):
            for t in range(tiles):
                left, right = (new for _, h, u, new in done if (h, u) == (g, t))
                for c in range(COMPS):
                    seam[1 - state][c, g, t] = seam_of(left[c], right[c])

    def main_rows(state, first, count):
        def rows(i, carry):
            done = []
            for u in range(ROWS):
                done += main_row(state, (first + ROWS * i + u) & (window - 1))
            for r, t, new, ends in done:
                k = r & (ny - 1)
                mask = ((lane - (DEPTH * k + DEPTH - 1)) & (LANES - 1)) < 2
                for c in range(COMPS):
                    main[1 - state][c, r, t] = new[c]
                    pltpu.store(edge.at[c, r // ny, t], ends[c], mask=mask)
            return carry

        lax.fori_loop(0, count // ROWS, rows, 0)

    def step(i, carry):
        for state in range(2):
            margin = DEPTH - 2 * state - 2 * i
            main_rows(state, -margin, ny + 2 * margin)
            strip_rows(state)
        return carry

    lax.fori_loop(0, STEPS, step, 0)

    def hand_out(k, carry):
        for t in range(tiles):
            for c in range(COMPS):
                out_ref[c, rows_at(ny, tiles, k, t), :] = main[0][c, k, t]
        return carry

    lax.fori_loop(0, ny, hand_out, 0)


def shifted(cells, axis, step, closed):
    count = lax.axis_size(axis)
    pairs = [(i, (i + step) % count) for i in range(count) if closed or 0 <= i + step < count]
    return lax.ppermute(cells, axis, pairs)


def swapped(cells, axis, first, closed):
    count = lax.axis_size(axis)
    pairs = [(i, (i + 1) % count) for i in range(first, count if closed else count - 1, 2)]
    return lax.ppermute(cells, axis, pairs + [(j, i) for i, j in pairs])


def paired(cells, axis, step):
    return lax.ppermute(cells, axis, [(i, i ^ step) for i in range(lax.axis_size(axis))])


def paired_sum(part, axis):
    step = 1
    while step < lax.axis_size(axis):
        part = part + paired(part, axis, step)
        step *= 2
    return part


def around(cells, dim):
    ny = cells.shape[dim]
    if lax.axis_size("gy") == 2:
        return shifted(cells, "gy", 1, True)
    head = lax.slice_in_dim(cells, 0, DEPTH, axis=dim)
    tail = lax.slice_in_dim(cells, ny - DEPTH, ny, axis=dim)
    return jnp.concatenate([shifted(head, "gy", -1, True), shifted(tail, "gy", 1, True)], axis=dim)


def around_strips(both):
    if lax.axis_size("gy") == 2:
        return shifted(both, "gy", 1, True)
    block = lax.broadcasted_iota(jnp.int32, both.shape, both.ndim - 1) // DEPTH
    side = lax.broadcasted_iota(jnp.int32, both.shape, 0)
    head = (block + side - 1) % (LANES // DEPTH) < DEPTH
    return jnp.where(head, shifted(both, "gy", -1, True), shifted(both, "gy", 1, True))


def body(magnetization, lower_image, image_weights, regions, anisotropy, damping):
    local, comps, nz, ny, nx = magnetization.shape
    images = local * lax.axis_size("img")
    tiles = nz // SUB
    assert lax.axis_size("gx") % 2 == 0
    assert local == 1 and comps == COMPS and nx == LANES
    assert ny == 2 * DEPTH and ny * DEPTH == LANES and tiles >= 2
    flat = (comps, nz * ny, nx)
    own = magnetization[0]
    own_p = around(own, 2)
    first = swapped(own, "img", 0, False)
    second = swapped(own, "img", 1, False)

    smem = pl.BlockSpec(memory_space=pltpu.SMEM)
    vmem = pl.BlockSpec(memory_space=pltpu.VMEM)
    f32 = jnp.float32
    limit = pltpu.CompilerParams(vmem_limit_bytes=32 * 1024 * 1024)
    vreg = (SUB, LANES)
    packed = jax.ShapeDtypeStruct((comps + 1, tiles) + vreg, f32)
    left, right, info = pl.pallas_call(
        functools.partial(pack_kernel, ny, tiles, anisotropy.shape[0]),
        out_shape=(packed, packed, jax.ShapeDtypeStruct((5,) + vreg, f32)),
        in_specs=[smem] * 3 + [vmem] * 3,
        out_specs=(vmem,) * 3,
        compiler_params=limit,
        name="pack_strips",
    )(
        lower_image,
        anisotropy,
        damping,
        image_weights.reshape(1, -1),
        own.reshape(flat),
        regions.reshape(flat[1:]),
    )
    late_regions, info = lax.optimization_barrier((regions, info))
    reg_p = around(late_regions, 1)
    info, own_p, reg_p = lax.optimization_barrier((info, own_p, reg_p))
    packed = jax.ShapeDtypeStruct((2 * comps + 1, tiles) + vreg, f32)
    part, near, one, two = pl.pallas_call(
        functools.partial(gather_kernel, ny, tiles),
        out_shape=(
            jax.ShapeDtypeStruct(vreg, f32),
            jax.ShapeDtypeStruct(flat, f32),
            packed,
            packed,
        ),
        in_specs=[vmem] * 6,
        out_specs=(vmem,) * 4,
        compiler_params=limit,
        name="gather_images",
    )(info, own.reshape(flat), first.reshape(flat), second.reshape(flat), left, right)
    near_p = around(near.reshape(own.shape), 2)
    one = swapped(one, "gx", 0, True)
    two = swapped(two, "gx", 1, True)
    pairs = [lax.axis_size(axis) for axis in ("img", "gx", "gy")] == [4, 4, 2]
    if pairs:
        part, one, two = lax.optimization_barrier((paired_sum(part, "img"), one, two))
    strips = pl.pallas_call(
        merge_kernel,
        out_shape=jax.ShapeDtypeStruct((2,) + packed.shape, f32),
        in_specs=[vmem] * 2,
        out_specs=vmem,
        compiler_params=limit,
        name="merge_strips",
    )(one, two)
    strips_p = around_strips(strips)
    if pairs:
        part, near_p = lax.optimization_barrier((paired_sum(part, "gx"), near_p))
        squares = [part, paired(part, "gy", 1)]
    else:
        squares = [lax.psum(part, ("img", "gx", "gy"))]

    window = ny + 2 * DEPTH
    out = pl.pallas_call(
        functools.partial(evolve_kernel, ny, tiles, images),
        out_shape=jax.ShapeDtypeStruct(flat, f32),
        in_specs=[vmem] * (9 + len(squares)),
        out_specs=vmem,
        scratch_shapes=[
            pltpu.VMEM((comps, window, tiles) + vreg, f32),
            pltpu.VMEM((comps, window, tiles) + vreg, f32),
            pltpu.VMEM((comps, 2, 2, tiles) + vreg, f32),
            pltpu.VMEM((comps, 2, 2, tiles) + vreg, f32),
            pltpu.VMEM((comps, 2, tiles) + vreg, f32),
            pltpu.VMEM((comps, 2, tiles) + vreg, f32),
            pltpu.VMEM((comps, 2, tiles) + vreg, f32),
            pltpu.VMEM((3, window, tiles) + vreg, f32),
            pltpu.VMEM((3, 2, 2, tiles) + vreg, f32),
        ],
        compiler_params=limit,
        name="evolve",
    )(
        info,
        own.reshape(flat),
        own_p.reshape(flat),
        near,
        near_p.reshape(flat),
        regions.reshape(flat[1:]),
        reg_p.reshape(flat[1:]),
        strips,
        strips_p,
        *squares,
    )
    return out.reshape(magnetization.shape)


def solution(mesh):
    placed = (P("img", None, None, "gy", "gx"), P(), P(), P(None, "gy", "gx"), P(), P())
    return jax.shard_map(
        body,
        mesh=mesh,
        in_specs=placed,
        out_specs=P("img", None, None, "gy", "gx"),
        check_vma=False,
    )
```

```python
import functools

import jax
import jax.numpy as jnp
from jax import lax
from jax.experimental import pallas as pl
from jax.experimental.pallas import tpu as pltpu
from jax.sharding import PartitionSpec as P

STEPS = 4
DEPTH = 2 * STEPS

eps = 1e-06
time_step = 0.05

SUB = 8
LANES = 128
COMPS = 3
ROWS = 4


def lane_iota():
    return lax.broadcasted_iota(jnp.int32, (SUB, LANES), 1)


def sub_iota():
    return lax.broadcasted_iota(jnp.int32, (SUB, LANES), 0)


def rows_at(ny, tiles, y, t):
    return pl.ds(y + ny * t, SUB, stride=ny * tiles)


def pack_kernel(
    ny, tiles, regions, lower_ref, aniso_ref, damp_ref, share_ref, m_ref, reg_ref, left_ref, right_ref, info_ref
):
    here = lax.axis_index("img")
    lane = lane_iota()
    block = lane // DEPTH
    def pack(i, carry):
        done = []
        for u in range(2):
            y = 2 * i + u
            shift = (DEPTH * (y + 1)) & (LANES - 1)
            left = block == ((y + 1) & (ny - 1))
            right = block == y
            for t in range(tiles):
                rows = rows_at(ny, tiles, y, t)
                for c in range(COMPS + 1):
                    cells = m_ref[c, rows, :] if c < COMPS else reg_ref[rows, :].astype(jnp.float32)
                    done.append((c, t, left, right, pltpu.roll(cells, shift, 1)))
        for c, t, left, right, cells in done:
            pltpu.store(left_ref.at[c, t], cells, mask=left)
            pltpu.store(right_ref.at[c, t], cells, mask=right)
        return carry

    table_a = jnp.zeros((SUB, LANES), jnp.float32)
    table_d = jnp.zeros((SUB, LANES), jnp.float32)
    for i in range(regions):
        table_a = jnp.where(lane == i, 2.0 * aniso_ref[i], table_a)
        table_d = jnp.where(lane == i, damp_ref[i], table_d)
    info_ref[0] = table_a
    info_ref[1] = table_d
    info_ref[2] = -time_step / (1.0 + table_d * table_d)
    share = share_ref[...]
    spot = lax.broadcasted_iota(jnp.int32, share.shape, 1)
    target = jnp.sum(jnp.where(spot < here, share, 0.0), axis=1, keepdims=True) / jnp.sum(
        share, axis=1, keepdims=True
    )
    info_ref[3] = jnp.broadcast_to(target, (SUB, LANES))
    info_ref[4] = jnp.full((SUB, LANES), lower_ref[here].astype(jnp.float32))

    lax.fori_loop(0, ny // 2, pack, 0)


def merge_kernel(one_ref, two_ref, out_ref):
    turned = (lax.axis_index("gx") & 1) == 1
    one, two = one_ref[...], two_ref[...]
    out_ref[0] = jnp.where(turned, one, two)
    out_ref[1] = jnp.where(turned, two, one)


def take_first(info_ref, here):
    odd = (here & 1) == 1
    below = info_ref[4] < here.astype(jnp.float32)
    return jnp.where(below, jnp.where(odd, 1, 0), jnp.where(odd, 0, 1)) == 1, odd


def gather_kernel(
    ny, tiles, info_ref, m_ref, first_ref, second_ref, own_left_ref, own_right_ref, part_ref, near_ref, one_ref, two_ref
):
    here = lax.axis_index("img")
    pick, odd = take_first(info_ref, here)
    chunks = 4
    depth = m_ref.shape[1]

    def squares(i, sums):
        sums = list(sums)
        done = []
        for u in range(chunks):
            start = pl.multiple_of((chunks * i + u) * SUB, SUB)
            for c in range(COMPS):
                one = first_ref[c, pl.ds(start, SUB), :]
                two = second_ref[c, pl.ds(start, SUB), :]
                done.append((c, start, jnp.where(pick, one, two)))
                diff = m_ref[c, pl.ds(start, SUB), :] - jnp.where(odd, one, two)
                sums[c + COMPS * u] = sums[c + COMPS * u] + diff * diff
        for c, start, cells in done:
            near_ref[c, pl.ds(start, SUB), :] = cells
        return tuple(sums)

    zero = jnp.zeros((SUB, LANES), jnp.float32)
    sums = lax.fori_loop(0, depth // (chunks * SUB), squares, (zero,) * (chunks * COMPS))
    total = jnp.sum(functools.reduce(jnp.add, sums), axis=(0, 1), keepdims=True)
    slot = lax.broadcasted_iota(jnp.int32, part_ref.shape, 1)
    part_ref[...] = jnp.where((slot == here) & (here > 0), total, 0.0)
    turned = (lax.axis_index("gx") & 1) == 1
    one_ref[COMPS:] = jnp.where(turned, own_left_ref[...], own_right_ref[...])
    two_ref[COMPS:] = jnp.where(turned, own_right_ref[...], own_left_ref[...])
    block = lane_iota() // DEPTH

    def pack(i, carry):
        done = []
        for u in range(2):
            y = 2 * i + u
            after = (y + 1) & (ny - 1)
            one = block == jnp.where(turned, after, y)
            two = block == jnp.where(turned, y, after)
            shift = (DEPTH * (y + 1)) & (LANES - 1)
            for t in range(tiles):
                for c in range(COMPS):
                    cells = pltpu.roll(near_ref[c, rows_at(ny, tiles, y, t), :], shift, 1)
                    done.append((c, t, one, two, cells))
        for c, t, one, two, cells in done:
            pltpu.store(one_ref.at[c, t], cells, mask=one)
            pltpu.store(two_ref.at[c, t], cells, mask=two)
        return carry

    lax.fori_loop(0, ny // 2, pack, 0)


def turn(m, h, a2, b, sc):
    mx, my, mz = m
    hx, hy, hz = h
    hz = hz + a2 * mz
    gx = hx + b * (my * hz - mz * hy)
    gy = hy + b * (mz * hx - mx * hz)
    gz = hz + b * (mx * hy - my * hx)
    return (
        sc * (my * gz - mz * gy),
        sc * (mz * gx - mx * gz),
        sc * (mx * gy - my * gx),
    )


def normal(v):
    scale = lax.rsqrt(v[0] * v[0] + v[1] * v[1] + v[2] * v[2])
    return tuple(x * scale for x in v)


def evolve_kernel(
    ny,
    tiles,
    images,
    info_ref,
    sq_ref,
    m_ref,
    mp_ref,
    n_ref,
    np1_ref,
    np2_ref,
    reg_ref,
    regp_ref,
    strips_ref,
    stripsp_ref,
    out_ref,
    main0,
    main1,
    strip0,
    strip1,
    edge,
    seam0,
    seam1,
    par,
    spar,
):
    main, strip, seam = (main0, main1), (strip0, strip1), (seam0, seam1)
    window = ny + 2 * DEPTH
    here = lax.axis_index("img")
    lane = lane_iota()
    sub = sub_iota()
    block = lane // DEPTH
    first_lane = lane == 0
    last_lane = lane == LANES - 1
    head_lane = lane % DEPTH == 0
    tail_lane = lane % DEPTH == DEPTH - 1
    top = sub == SUB - 1
    bottom = sub == 0

    pick, _ = take_first(info_ref, here)
    lo = info_ref[4]
    slot = lane.astype(jnp.float32)
    squares = jnp.broadcast_to(jnp.sum(sq_ref[...], axis=0, keepdims=True), (SUB, LANES))
    lengths = jnp.where((lane >= 1) & (lane < images), jnp.sqrt(squares + eps), 0.0)
    total = jnp.sum(lengths, axis=1, keepdims=True)
    arc = jnp.sum(jnp.where(slot <= lo, lengths, 0.0), axis=1, keepdims=True)
    gap = jnp.sum(jnp.where(slot == lo + 1.0, lengths, 0.0), axis=1, keepdims=True)
    weight = jnp.clip((info_ref[3] * total - arc) / gap, -0.5, 1.5)
    below = lo < here.astype(jnp.float32)
    w_own = jnp.where(below, weight, 1.0 - weight)
    w_near = jnp.where(below, 1.0 - weight, weight)

    tables = (info_ref[0], info_ref[1], info_ref[2])

    def params(region):
        return [jnp.take_along_axis(table, region, axis=1) for table in tables]

    def ends_of(k, new):
        shift = (DEPTH * (k + 1)) & (LANES - 1)
        return [pltpu.roll(new[c], shift, 1) for c in range(COMPS)]

    def fill(k, carry):
        done = []
        for g, (own, reg) in enumerate(((m_ref, reg_ref), (mp_ref, regp_ref))):
            for t in range(tiles):
                rows = rows_at(ny, tiles, k, t)
                if g == 0:
                    near = [n_ref[c, rows, :] for c in range(COMPS)]
                else:
                    near = [
                        jnp.where(pick, np1_ref[c, rows, :], np2_ref[c, rows, :]) for c in range(COMPS)
                    ]
                v = normal([w_own * own[c, rows, :] + w_near * near[c] for c in range(COMPS)])
                done.append((g * ny + k, t, v, params(reg[rows, :])))
        for r, t, v, p in done:
            for c in range(COMPS):
                main0[c, r, t] = v[c]
            for i in range(3):
                par[i, r, t] = p[i]
        return carry

    lax.fori_loop(0, ny, fill, 0)

    def seam_of(left, right):
        return jnp.where(head_lane, pltpu.roll(left, 1, 1), pltpu.roll(right, LANES - 1, 1))

    def fill_strips(t, carry):
        done = []
        for g, cells in enumerate((strips_ref, stripsp_ref)):
            for side in range(2):
                v = normal(
                    [w_own * cells[side, COMPS + c, t] + w_near * cells[side, c, t] for c in range(COMPS)]
                )
                done.append((side, g, v, params(cells[side, 2 * COMPS, t].astype(jnp.int32))))
        for side, g, v, p in done:
            for c in range(COMPS):
                strip0[c, side, g, t] = v[c]
            for i in range(3):
                spar[i, side, g, t] = p[i]
        for g in range(2):
            left, right = (v for _, h, v, _ in done if h == g)
            for c in range(COMPS):
                seam0[c, g, t] = seam_of(left[c], right[c])
        return carry

    lax.fori_loop(0, tiles, fill_strips, 0)

    def around_z(cells, t):
        if t + 1 < tiles:
            above = cells[t + 1]
        else:
            above = jnp.where(top, 0.0, pltpu.roll(cells[0], SUB - 1, 0))
        if t > 0:
            under = cells[t - 1]
        else:
            under = jnp.where(bottom, 0.0, pltpu.roll(cells[tiles - 1], 1, 0))
        return above + under

    def main_row(state, r):
        g = r // ny
        k = r & (ny - 1)
        after = (r + 1) & (window - 1)
        before = (r - 1) & (window - 1)
        shift = (LANES - DEPTH * (k + 1)) & (LANES - 1)
        center = [[main[state][c, r, t] for t in range(tiles)] for c in range(COMPS)]
        done = []
        for t in range(tiles):
            h = []
            for c in range(COMPS):
                cells = center[c][t]
                ends = pltpu.roll(seam[state][c, g, t], shift, 1)
                s = jnp.where(first_lane, ends, pltpu.roll(cells, 1, 1))
                s = s + jnp.where(last_lane, ends, pltpu.roll(cells, LANES - 1, 1))
                s = s + (main[state][c, after, t] + main[state][c, before, t])
                h.append(s + around_z(center[c], t))
            m = [center[c][t] for c in range(COMPS)]
            rate = turn(m, h, par[0, r, t], par[1, r, t], par[2, r, t])
            if state == 0:
                new = [m[c] + rate[c] for c in range(COMPS)]
            else:
                new = normal([main[0][c, r, t] + (m[c] + rate[c]) for c in range(COMPS)])
            done.append((r, t, new, ends_of(k, m)))
        return done

    def strip_rows(state):
        done = []
        for g in range(2):
            for side in range(2):
                start = block == side
                stop = block == (side + ny - 1) % ny
                center = [[strip[state][c, side, g, t] for t in range(tiles)] for c in range(COMPS)]
                for t in range(tiles):
                    h = []
                    for c in range(COMPS):
                        cells = center[c][t]
                        inner = edge[c, g, t]
                        other = strip[state][c, side, 1 - g, t]
                        if side == 0:
                            s = pltpu.roll(cells, 1, 1)
                            s = s + pltpu.roll(jnp.where(head_lane, inner, cells), LANES - 1, 1)
                        else:
                            s = pltpu.roll(jnp.where(tail_lane, inner, cells), 1, 1)
                            s = s + pltpu.roll(cells, LANES - 1, 1)
                        s = s + pltpu.roll(jnp.where(start, other, cells), LANES - DEPTH, 1)
                        s = s + pltpu.roll(jnp.where(stop, other, cells), DEPTH, 1)
                        h.append(s + around_z(center[c], t))
                    m = [center[c][t] for c in range(COMPS)]
                    rate = turn(
                        m, h, spar[0, side, g, t], spar[1, side, g, t], spar[2, side, g, t]
                    )
                    if state == 0:
                        new = [m[c] + rate[c] for c in range(COMPS)]
                    else:
                        new = normal(
                            [strip[0][c, side, g, t] + (m[c] + rate[c]) for c in range(COMPS)]
                        )
                    done.append((side, g, t, new))
        for side, g, t, new in done:
            for c in range(COMPS):
                strip[1 - state][c, side, g, t] = new[c]
        for g in range(2):
            for t in range(tiles):
                left, right = (new for _, h, u, new in done if (h, u) == (g, t))
                for c in range(COMPS):
                    seam[1 - state][c, g, t] = seam_of(left[c], right[c])

    def main_rows(state, first, count):
        def rows(i, carry):
            done = []
            for u in range(ROWS):
                done += main_row(state, (first + ROWS * i + u) & (window - 1))
            for r, t, new, ends in done:
                k = r & (ny - 1)
                mask = ((lane - (DEPTH * k + DEPTH - 1)) & (LANES - 1)) < 2
                for c in range(COMPS):
                    main[1 - state][c, r, t] = new[c]
                    pltpu.store(edge.at[c, r // ny, t], ends[c], mask=mask)
            return carry

        lax.fori_loop(0, count // ROWS, rows, 0)

    def step(i, carry):
        for state in range(2):
            margin = DEPTH - 2 * state - 2 * i
            main_rows(state, -margin, ny + 2 * margin)
            strip_rows(state)
        return carry

    lax.fori_loop(0, STEPS, step, 0)

    def hand_out(k, carry):
        for t in range(tiles):
            for c in range(COMPS):
                out_ref[c, rows_at(ny, tiles, k, t), :] = main[0][c, k, t]
        return carry

    lax.fori_loop(0, ny, hand_out, 0)


def shifted(cells, axis, step, closed):
    count = lax.axis_size(axis)
    pairs = [(i, (i + step) % count) for i in range(count) if closed or 0 <= i + step < count]
    return lax.ppermute(cells, axis, pairs)


def swapped(cells, axis, first, closed):
    count = lax.axis_size(axis)
    pairs = [(i, (i + 1) % count) for i in range(first, count if closed else count - 1, 2)]
    return lax.ppermute(cells, axis, pairs + [(j, i) for i, j in pairs])


def around(cells, dim):
    ny = cells.shape[dim]
    if lax.axis_size("gy") == 2:
        return shifted(cells, "gy", 1, True)
    head = lax.slice_in_dim(cells, 0, DEPTH, axis=dim)
    tail = lax.slice_in_dim(cells, ny - DEPTH, ny, axis=dim)
    return jnp.concatenate([shifted(head, "gy", -1, True), shifted(tail, "gy", 1, True)], axis=dim)


def around_strips(both):
    if lax.axis_size("gy") == 2:
        return shifted(both, "gy", 1, True)
    block = lax.broadcasted_iota(jnp.int32, both.shape, both.ndim - 1) // DEPTH
    side = lax.broadcasted_iota(jnp.int32, both.shape, 0)
    head = (block + side - 1) % (LANES // DEPTH) < DEPTH
    return jnp.where(head, shifted(both, "gy", -1, True), shifted(both, "gy", 1, True))


def body(magnetization, lower_image, image_weights, regions, anisotropy, damping):
    local, comps, nz, ny, nx = magnetization.shape
    images = local * lax.axis_size("img")
    tiles = nz // SUB
    devices = lax.axis_size(("img", "gx", "gy"))
    assert lax.axis_size("gx") % 2 == 0
    assert local == 1 and comps == COMPS and nx == LANES
    assert ny == 2 * DEPTH and ny * DEPTH == LANES and tiles >= 2
    flat = (comps, nz * ny, nx)
    own = magnetization[0]
    own_p = around(own, 2)
    first = swapped(own, "img", 0, False)
    second = swapped(own, "img", 1, False)

    smem = pl.BlockSpec(memory_space=pltpu.SMEM)
    vmem = pl.BlockSpec(memory_space=pltpu.VMEM)
    f32 = jnp.float32
    limit = pltpu.CompilerParams(vmem_limit_bytes=32 * 1024 * 1024)
    vreg = (SUB, LANES)
    packed = jax.ShapeDtypeStruct((comps + 1, tiles) + vreg, f32)
    left, right, info = pl.pallas_call(
        functools.partial(pack_kernel, ny, tiles, anisotropy.shape[0]),
        out_shape=(packed, packed, jax.ShapeDtypeStruct((5,) + vreg, f32)),
        in_specs=[smem] * 3 + [vmem] * 3,
        out_specs=(vmem,) * 3,
        compiler_params=limit,
        name="pack_strips",
    )(
        lower_image,
        anisotropy,
        damping,
        image_weights.reshape(1, -1),
        own.reshape(flat),
        regions.reshape(flat[1:]),
    )
    late_regions, info = lax.optimization_barrier((regions, info))
    reg_p = around(late_regions, 1)
    own_p, info = lax.optimization_barrier((own_p, info))
    first_p = swapped(own_p, "img", 0, False)
    second_p = swapped(own_p, "img", 1, False)
    packed = jax.ShapeDtypeStruct((2 * comps + 1, tiles) + vreg, f32)
    part, near, one, two = pl.pallas_call(
        functools.partial(gather_kernel, ny, tiles),
        out_shape=(
            jax.ShapeDtypeStruct((devices, LANES), f32),
            jax.ShapeDtypeStruct(flat, f32),
            packed,
            packed,
        ),
        in_specs=[vmem] * 6,
        out_specs=(vmem,) * 4,
        compiler_params=limit,
        name="gather_images",
    )(info, own.reshape(flat), first.reshape(flat), second.reshape(flat), left, right)
    one = swapped(one, "gx", 0, True)
    two = swapped(two, "gx", 1, True)
    one, reg_p = lax.optimization_barrier((one, reg_p))
    strips = pl.pallas_call(
        merge_kernel,
        out_shape=jax.ShapeDtypeStruct((2,) + packed.shape, f32),
        in_specs=[vmem] * 2,
        out_specs=vmem,
        compiler_params=limit,
        name="merge_strips",
    )(one, two)
    strips_p = around_strips(strips)
    squares = lax.all_to_all(part, ("img", "gx", "gy"), 0, 0, tiled=True)

    window = ny + 2 * DEPTH
    out = pl.pallas_call(
        functools.partial(evolve_kernel, ny, tiles, images),
        out_shape=jax.ShapeDtypeStruct(flat, f32),
        in_specs=[vmem] * 11,
        out_specs=vmem,
        scratch_shapes=[
            pltpu.VMEM((comps, window, tiles) + vreg, f32),
            pltpu.VMEM((comps, window, tiles) + vreg, f32),
            pltpu.VMEM((comps, 2, 2, tiles) + vreg, f32),
            pltpu.VMEM((comps, 2, 2, tiles) + vreg, f32),
            pltpu.VMEM((comps, 2, tiles) + vreg, f32),
            pltpu.VMEM((comps, 2, tiles) + vreg, f32),
            pltpu.VMEM((comps, 2, tiles) + vreg, f32),
            pltpu.VMEM((3, window, tiles) + vreg, f32),
            pltpu.VMEM((3, 2, 2, tiles) + vreg, f32),
        ],
        compiler_params=limit,
        name="evolve",
    )(
        info,
        squares,
        own.reshape(flat),
        own_p.reshape(flat),
        near,
        first_p.reshape(flat),
        second_p.reshape(flat),
        regions.reshape(flat[1:]),
        reg_p.reshape(flat[1:]),
        strips,
        strips_p,
    )
    return out.reshape(magnetization.shape)


def solution(mesh):
    placed = (P("img", None, None, "gy", "gx"), P(), P(), P(None, "gy", "gx"), P(), P())
    return jax.shard_map(
        body,
        mesh=mesh,
        in_specs=placed,
        out_specs=P("img", None, None, "gy", "gx"),
        check_vma=False,
    )
```

```python
import functools

import jax
import jax.numpy as jnp
from jax import lax
from jax.experimental import pallas as pl
from jax.experimental.pallas import tpu as pltpu
from jax.sharding import PartitionSpec as P

STEPS = 4
DEPTH = 2 * STEPS

eps = 1e-06
time_step = 0.05

SUB = 8
LANES = 128
COMPS = 3
ROWS = 4


def lane_iota():
    return lax.broadcasted_iota(jnp.int32, (SUB, LANES), 1)


def sub_iota():
    return lax.broadcasted_iota(jnp.int32, (SUB, LANES), 0)


def rows_at(ny, tiles, y, t):
    return pl.ds(y + ny * t, SUB, stride=ny * tiles)


def pack_kernel(
    ny, tiles, regions, lower_ref, aniso_ref, damp_ref, share_ref, m_ref, reg_ref, left_ref, right_ref, info_ref
):
    here = lax.axis_index("img")
    lane = lane_iota()
    block = lane // DEPTH
    def pack(i, carry):
        done = []
        for u in range(2):
            y = 2 * i + u
            shift = (DEPTH * (y + 1)) & (LANES - 1)
            left = block == ((y + 1) & (ny - 1))
            right = block == y
            for t in range(tiles):
                rows = rows_at(ny, tiles, y, t)
                for c in range(COMPS + 1):
                    cells = m_ref[c, rows, :] if c < COMPS else reg_ref[rows, :].astype(jnp.float32)
                    done.append((c, t, left, right, pltpu.roll(cells, shift, 1)))
        for c, t, left, right, cells in done:
            pltpu.store(left_ref.at[c, t], cells, mask=left)
            pltpu.store(right_ref.at[c, t], cells, mask=right)
        return carry

    table_a = jnp.zeros((SUB, LANES), jnp.float32)
    table_d = jnp.zeros((SUB, LANES), jnp.float32)
    for i in range(regions):
        table_a = jnp.where(lane == i, 2.0 * aniso_ref[i], table_a)
        table_d = jnp.where(lane == i, damp_ref[i], table_d)
    info_ref[0] = table_a
    info_ref[1] = table_d
    info_ref[2] = -time_step / (1.0 + table_d * table_d)
    share = share_ref[...]
    spot = lax.broadcasted_iota(jnp.int32, share.shape, 1)
    target = jnp.sum(jnp.where(spot < here, share, 0.0), axis=1, keepdims=True) / jnp.sum(
        share, axis=1, keepdims=True
    )
    info_ref[3] = jnp.broadcast_to(target, (SUB, LANES))
    info_ref[4] = jnp.full((SUB, LANES), lower_ref[here].astype(jnp.float32))

    lax.fori_loop(0, ny // 2, pack, 0)


def merge_kernel(one_ref, two_ref, out_ref):
    turned = (lax.axis_index("gx") & 1) == 1
    one, two = one_ref[...], two_ref[...]
    out_ref[0] = jnp.where(turned, one, two)
    out_ref[1] = jnp.where(turned, two, one)


def take_first(info_ref, here):
    odd = (here & 1) == 1
    below = info_ref[4] < here.astype(jnp.float32)
    return jnp.where(below, jnp.where(odd, 1, 0), jnp.where(odd, 0, 1)) == 1, odd


def gather_kernel(
    ny, tiles, info_ref, m_ref, first_ref, second_ref, own_left_ref, own_right_ref, part_ref, near_ref, one_ref, two_ref
):
    here = lax.axis_index("img")
    pick, odd = take_first(info_ref, here)
    chunks = 4
    depth = m_ref.shape[1]

    def squares(i, sums):
        sums = list(sums)
        done = []
        for u in range(chunks):
            start = pl.multiple_of((chunks * i + u) * SUB, SUB)
            for c in range(COMPS):
                one = first_ref[c, pl.ds(start, SUB), :]
                two = second_ref[c, pl.ds(start, SUB), :]
                done.append((c, start, jnp.where(pick, one, two)))
                diff = m_ref[c, pl.ds(start, SUB), :] - jnp.where(odd, one, two)
                sums[c + COMPS * u] = sums[c + COMPS * u] + diff * diff
        for c, start, cells in done:
            near_ref[c, pl.ds(start, SUB), :] = cells
        return tuple(sums)

    zero = jnp.zeros((SUB, LANES), jnp.float32)
    sums = lax.fori_loop(0, depth // (chunks * SUB), squares, (zero,) * (chunks * COMPS))
    total = jnp.sum(functools.reduce(jnp.add, sums), axis=(0, 1), keepdims=True)
    slot = lane_iota()
    part_ref[...] = jnp.where((slot == here) & (here > 0) & (sub_iota() == 0), total, 0.0)
    turned = (lax.axis_index("gx") & 1) == 1
    one_ref[COMPS:] = jnp.where(turned, own_left_ref[...], own_right_ref[...])
    two_ref[COMPS:] = jnp.where(turned, own_right_ref[...], own_left_ref[...])
    block = lane_iota() // DEPTH

    def pack(i, carry):
        done = []
        for u in range(2):
            y = 2 * i + u
            after = (y + 1) & (ny - 1)
            one = block == jnp.where(turned, after, y)
            two = block == jnp.where(turned, y, after)
            shift = (DEPTH * (y + 1)) & (LANES - 1)
            for t in range(tiles):
                for c in range(COMPS):
                    cells = pltpu.roll(near_ref[c, rows_at(ny, tiles, y, t), :], shift, 1)
                    done.append((c, t, one, two, cells))
        for c, t, one, two, cells in done:
            pltpu.store(one_ref.at[c, t], cells, mask=one)
            pltpu.store(two_ref.at[c, t], cells, mask=two)
        return carry

    lax.fori_loop(0, ny // 2, pack, 0)


def turn(m, h, a2, b, sc):
    mx, my, mz = m
    hx, hy, hz = h
    hz = hz + a2 * mz
    gx = hx + b * (my * hz - mz * hy)
    gy = hy + b * (mz * hx - mx * hz)
    gz = hz + b * (mx * hy - my * hx)
    return (
        sc * (my * gz - mz * gy),
        sc * (mz * gx - mx * gz),
        sc * (mx * gy - my * gx),
    )


def normal(v):
    scale = lax.rsqrt(v[0] * v[0] + v[1] * v[1] + v[2] * v[2])
    return tuple(x * scale for x in v)


def evolve_kernel(
    ny,
    tiles,
    images,
    info_ref,
    sq_ref,
    m_ref,
    mp_ref,
    n_ref,
    np_ref,
    reg_ref,
    regp_ref,
    strips_ref,
    stripsp_ref,
    out_ref,
    main0,
    main1,
    strip0,
    strip1,
    edge,
    seam0,
    seam1,
    par,
    spar,
):
    main, strip, seam = (main0, main1), (strip0, strip1), (seam0, seam1)
    window = ny + 2 * DEPTH
    here = lax.axis_index("img")
    lane = lane_iota()
    sub = sub_iota()
    block = lane // DEPTH
    first_lane = lane == 0
    last_lane = lane == LANES - 1
    head_lane = lane % DEPTH == 0
    tail_lane = lane % DEPTH == DEPTH - 1
    top = sub == SUB - 1
    bottom = sub == 0

    lo = info_ref[4]
    slot = lane.astype(jnp.float32)
    squares = jnp.broadcast_to(jnp.sum(sq_ref[...], axis=0, keepdims=True), (SUB, LANES))
    lengths = jnp.where((lane >= 1) & (lane < images), jnp.sqrt(squares + eps), 0.0)
    total = jnp.sum(lengths, axis=1, keepdims=True)
    arc = jnp.sum(jnp.where(slot <= lo, lengths, 0.0), axis=1, keepdims=True)
    gap = jnp.sum(jnp.where(slot == lo + 1.0, lengths, 0.0), axis=1, keepdims=True)
    weight = jnp.clip((info_ref[3] * total - arc) / gap, -0.5, 1.5)
    below = lo < here.astype(jnp.float32)
    w_own = jnp.where(below, weight, 1.0 - weight)
    w_near = jnp.where(below, 1.0 - weight, weight)

    tables = (info_ref[0], info_ref[1], info_ref[2])

    def params(region):
        return [jnp.take_along_axis(table, region, axis=1) for table in tables]

    def ends_of(k, new):
        shift = (DEPTH * (k + 1)) & (LANES - 1)
        return [pltpu.roll(new[c], shift, 1) for c in range(COMPS)]

    def fill(k, carry):
        done = []
        for g, (own, near, reg) in enumerate(((m_ref, n_ref, reg_ref), (mp_ref, np_ref, regp_ref))):
            for t in range(tiles):
                rows = rows_at(ny, tiles, k, t)
                v = normal(
                    [
                        w_own * own[c, rows, :] + w_near * near[c, rows, :]
                        for c in range(COMPS)
                    ]
                )
                done.append((g * ny + k, t, v, params(reg[rows, :])))
        for r, t, v, p in done:
            for c in range(COMPS):
                main0[c, r, t] = v[c]
            for i in range(3):
                par[i, r, t] = p[i]
        return carry

    lax.fori_loop(0, ny, fill, 0)

    def seam_of(left, right):
        return jnp.where(head_lane, pltpu.roll(left, 1, 1), pltpu.roll(right, LANES - 1, 1))

    def fill_strips(t, carry):
        done = []
        for g, cells in enumerate((strips_ref, stripsp_ref)):
            for side in range(2):
                v = normal(
                    [w_own * cells[side, COMPS + c, t] + w_near * cells[side, c, t] for c in range(COMPS)]
                )
                done.append((side, g, v, params(cells[side, 2 * COMPS, t].astype(jnp.int32))))
        for side, g, v, p in done:
            for c in range(COMPS):
                strip0[c, side, g, t] = v[c]
            for i in range(3):
                spar[i, side, g, t] = p[i]
        for g in range(2):
            left, right = (v for _, h, v, _ in done if h == g)
            for c in range(COMPS):
                seam0[c, g, t] = seam_of(left[c], right[c])
        return carry

    lax.fori_loop(0, tiles, fill_strips, 0)

    def around_z(cells, t):
        if t + 1 < tiles:
            above = cells[t + 1]
        else:
            above = jnp.where(top, 0.0, pltpu.roll(cells[0], SUB - 1, 0))
        if t > 0:
            under = cells[t - 1]
        else:
            under = jnp.where(bottom, 0.0, pltpu.roll(cells[tiles - 1], 1, 0))
        return above + under

    def main_row(state, r):
        g = r // ny
        k = r & (ny - 1)
        after = (r + 1) & (window - 1)
        before = (r - 1) & (window - 1)
        shift = (LANES - DEPTH * (k + 1)) & (LANES - 1)
        center = [[main[state][c, r, t] for t in range(tiles)] for c in range(COMPS)]
        done = []
        for t in range(tiles):
            h = []
            for c in range(COMPS):
                cells = center[c][t]
                ends = pltpu.roll(seam[state][c, g, t], shift, 1)
                s = jnp.where(first_lane, ends, pltpu.roll(cells, 1, 1))
                s = s + jnp.where(last_lane, ends, pltpu.roll(cells, LANES - 1, 1))
                s = s + (main[state][c, after, t] + main[state][c, before, t])
                h.append(s + around_z(center[c], t))
            m = [center[c][t] for c in range(COMPS)]
            rate = turn(m, h, par[0, r, t], par[1, r, t], par[2, r, t])
            if state == 0:
                new = [m[c] + rate[c] for c in range(COMPS)]
            else:
                new = normal([main[0][c, r, t] + (m[c] + rate[c]) for c in range(COMPS)])
            done.append((r, t, new, ends_of(k, m)))
        return done

    def strip_rows(state):
        done = []
        for g in range(2):
            for side in range(2):
                start = block == side
                stop = block == (side + ny - 1) % ny
                center = [[strip[state][c, side, g, t] for t in range(tiles)] for c in range(COMPS)]
                for t in range(tiles):
                    h = []
                    for c in range(COMPS):
                        cells = center[c][t]
                        inner = edge[c, g, t]
                        other = strip[state][c, side, 1 - g, t]
                        if side == 0:
                            s = pltpu.roll(cells, 1, 1)
                            s = s + pltpu.roll(jnp.where(head_lane, inner, cells), LANES - 1, 1)
                        else:
                            s = pltpu.roll(jnp.where(tail_lane, inner, cells), 1, 1)
                            s = s + pltpu.roll(cells, LANES - 1, 1)
                        s = s + pltpu.roll(jnp.where(start, other, cells), LANES - DEPTH, 1)
                        s = s + pltpu.roll(jnp.where(stop, other, cells), DEPTH, 1)
                        h.append(s + around_z(center[c], t))
                    m = [center[c][t] for c in range(COMPS)]
                    rate = turn(
                        m, h, spar[0, side, g, t], spar[1, side, g, t], spar[2, side, g, t]
                    )
                    if state == 0:
                        new = [m[c] + rate[c] for c in range(COMPS)]
                    else:
                        new = normal(
                            [strip[0][c, side, g, t] + (m[c] + rate[c]) for c in range(COMPS)]
                        )
                    done.append((side, g, t, new))
        for side, g, t, new in done:
            for c in range(COMPS):
                strip[1 - state][c, side, g, t] = new[c]
        for g in range(2):
            for t in range(tiles):
                left, right = (new for _, h, u, new in done if (h, u) == (g, t))
                for c in range(COMPS):
                    seam[1 - state][c, g, t] = seam_of(left[c], right[c])

    def main_rows(state, first, count):
        def rows(i, carry):
            done = []
            for u in range(ROWS):
                done += main_row(state, (first + ROWS * i + u) & (window - 1))
            for r, t, new, ends in done:
                k = r & (ny - 1)
                mask = ((lane - (DEPTH * k + DEPTH - 1)) & (LANES - 1)) < 2
                for c in range(COMPS):
                    main[1 - state][c, r, t] = new[c]
                    pltpu.store(edge.at[c, r // ny, t], ends[c], mask=mask)
            return carry

        lax.fori_loop(0, count // ROWS, rows, 0)

    def step(i, carry):
        for state in range(2):
            margin = DEPTH - 2 * state - 2 * i
            main_rows(state, -margin, ny + 2 * margin)
            strip_rows(state)
        return carry

    lax.fori_loop(0, STEPS, step, 0)

    def hand_out(k, carry):
        for t in range(tiles):
            for c in range(COMPS):
                out_ref[c, rows_at(ny, tiles, k, t), :] = main[0][c, k, t]
        return carry

    lax.fori_loop(0, ny, hand_out, 0)


def shifted(cells, axis, step, closed):
    count = lax.axis_size(axis)
    pairs = [(i, (i + step) % count) for i in range(count) if closed or 0 <= i + step < count]
    return lax.ppermute(cells, axis, pairs)


def swapped(cells, axis, first, closed):
    count = lax.axis_size(axis)
    pairs = [(i, (i + 1) % count) for i in range(first, count if closed else count - 1, 2)]
    return lax.ppermute(cells, axis, pairs + [(j, i) for i, j in pairs])


def around(cells, dim):
    ny = cells.shape[dim]
    if lax.axis_size("gy") == 2:
        return shifted(cells, "gy", 1, True)
    head = lax.slice_in_dim(cells, 0, DEPTH, axis=dim)
    tail = lax.slice_in_dim(cells, ny - DEPTH, ny, axis=dim)
    return jnp.concatenate([shifted(head, "gy", -1, True), shifted(tail, "gy", 1, True)], axis=dim)


def around_strips(both):
    if lax.axis_size("gy") == 2:
        return shifted(both, "gy", 1, True)
    block = lax.broadcasted_iota(jnp.int32, both.shape, both.ndim - 1) // DEPTH
    side = lax.broadcasted_iota(jnp.int32, both.shape, 0)
    head = (block + side - 1) % (LANES // DEPTH) < DEPTH
    return jnp.where(head, shifted(both, "gy", -1, True), shifted(both, "gy", 1, True))


def body(magnetization, lower_image, image_weights, regions, anisotropy, damping):
    local, comps, nz, ny, nx = magnetization.shape
    images = local * lax.axis_size("img")
    tiles = nz // SUB
    assert lax.axis_size("gx") % 2 == 0
    assert local == 1 and comps == COMPS and nx == LANES
    assert ny == 2 * DEPTH and ny * DEPTH == LANES and tiles >= 2
    flat = (comps, nz * ny, nx)
    own = magnetization[0]
    own_p = around(own, 2)
    first = swapped(own, "img", 0, False)
    second = swapped(own, "img", 1, False)

    smem = pl.BlockSpec(memory_space=pltpu.SMEM)
    vmem = pl.BlockSpec(memory_space=pltpu.VMEM)
    f32 = jnp.float32
    limit = pltpu.CompilerParams(vmem_limit_bytes=32 * 1024 * 1024)
    vreg = (SUB, LANES)
    packed = jax.ShapeDtypeStruct((comps + 1, tiles) + vreg, f32)
    left, right, info = pl.pallas_call(
        functools.partial(pack_kernel, ny, tiles, anisotropy.shape[0]),
        out_shape=(packed, packed, jax.ShapeDtypeStruct((5,) + vreg, f32)),
        in_specs=[smem] * 3 + [vmem] * 3,
        out_specs=(vmem,) * 3,
        compiler_params=limit,
        name="pack_strips",
    )(
        lower_image,
        anisotropy,
        damping,
        image_weights.reshape(1, -1),
        own.reshape(flat),
        regions.reshape(flat[1:]),
    )
    late_regions, info = lax.optimization_barrier((regions, info))
    reg_p = around(late_regions, 1)
    info, own_p, reg_p = lax.optimization_barrier((info, own_p, reg_p))
    packed = jax.ShapeDtypeStruct((2 * comps + 1, tiles) + vreg, f32)
    part, near, one, two = pl.pallas_call(
        functools.partial(gather_kernel, ny, tiles),
        out_shape=(
            jax.ShapeDtypeStruct(vreg, f32),
            jax.ShapeDtypeStruct(flat, f32),
            packed,
            packed,
        ),
        in_specs=[vmem] * 6,
        out_specs=(vmem,) * 4,
        compiler_params=limit,
        name="gather_images",
    )(info, own.reshape(flat), first.reshape(flat), second.reshape(flat), left, right)
    near_p = around(near.reshape(own.shape), 2)
    one = swapped(one, "gx", 0, True)
    two = swapped(two, "gx", 1, True)
    strips = pl.pallas_call(
        merge_kernel,
        out_shape=jax.ShapeDtypeStruct((2,) + packed.shape, f32),
        in_specs=[vmem] * 2,
        out_specs=vmem,
        compiler_params=limit,
        name="merge_strips",
    )(one, two)
    strips_p = around_strips(strips)
    squares = lax.all_gather(part, ("img", "gx", "gy"), axis=0, tiled=True)

    window = ny + 2 * DEPTH
    out = pl.pallas_call(
        functools.partial(evolve_kernel, ny, tiles, images),
        out_shape=jax.ShapeDtypeStruct(flat, f32),
        in_specs=[vmem] * 10,
        out_specs=vmem,
        scratch_shapes=[
            pltpu.VMEM((comps, window, tiles) + vreg, f32),
            pltpu.VMEM((comps, window, tiles) + vreg, f32),
            pltpu.VMEM((comps, 2, 2, tiles) + vreg, f32),
            pltpu.VMEM((comps, 2, 2, tiles) + vreg, f32),
            pltpu.VMEM((comps, 2, tiles) + vreg, f32),
            pltpu.VMEM((comps, 2, tiles) + vreg, f32),
            pltpu.VMEM((comps, 2, tiles) + vreg, f32),
            pltpu.VMEM((3, window, tiles) + vreg, f32),
            pltpu.VMEM((3, 2, 2, tiles) + vreg, f32),
        ],
        compiler_params=limit,
        name="evolve",
    )(
        info,
        squares,
        own.reshape(flat),
        own_p.reshape(flat),
        near,
        near_p.reshape(flat),
        regions.reshape(flat[1:]),
        reg_p.reshape(flat[1:]),
        strips,
        strips_p,
    )
    return out.reshape(magnetization.shape)


def solution(mesh):
    placed = (P("img", None, None, "gy", "gx"), P(), P(), P(None, "gy", "gx"), P(), P())
    return jax.shard_map(
        body,
        mesh=mesh,
        in_specs=placed,
        out_specs=P("img", None, None, "gy", "gx"),
        check_vma=False,
    )
```

```python
import functools

import jax
import jax.numpy as jnp
from jax import lax
from jax.experimental import pallas as pl
from jax.experimental.pallas import tpu as pltpu
from jax.sharding import PartitionSpec as P

STEPS = 4
DEPTH = 2 * STEPS

eps = 1e-06
time_step = 0.05

SUB = 8
LANES = 128
COMPS = 3
ROWS = 4


def lane_iota():
    return lax.broadcasted_iota(jnp.int32, (SUB, LANES), 1)


def sub_iota():
    return lax.broadcasted_iota(jnp.int32, (SUB, LANES), 0)


def rows_at(ny, tiles, y, t):
    return pl.ds(y + ny * t, SUB, stride=ny * tiles)


def info_kernel(regions, lower_ref, aniso_ref, damp_ref, share_ref, info_ref):
    here = lax.axis_index("img")
    lane = lane_iota()
    table_a = jnp.zeros((SUB, LANES), jnp.float32)
    table_d = jnp.zeros((SUB, LANES), jnp.float32)
    for i in range(regions):
        table_a = jnp.where(lane == i, 2.0 * aniso_ref[i], table_a)
        table_d = jnp.where(lane == i, damp_ref[i], table_d)
    info_ref[0] = table_a
    info_ref[1] = table_d
    info_ref[2] = -time_step / (1.0 + table_d * table_d)
    share = share_ref[...]
    spot = lax.broadcasted_iota(jnp.int32, share.shape, 1)
    target = jnp.sum(jnp.where(spot < here, share, 0.0), axis=1, keepdims=True) / jnp.sum(
        share, axis=1, keepdims=True
    )
    info_ref[3] = jnp.broadcast_to(target, (SUB, LANES))
    info_ref[4] = jnp.full((SUB, LANES), lower_ref[here].astype(jnp.float32))


def take_first(info_ref, here):
    odd = (here & 1) == 1
    below = info_ref[4] < here.astype(jnp.float32)
    return jnp.where(below, jnp.where(odd, 1, 0), jnp.where(odd, 0, 1)) == 1, odd


def gather_kernel(info_ref, m_ref, first_ref, second_ref, part_ref, near_ref):
    here = lax.axis_index("img")
    pick, odd = take_first(info_ref, here)
    chunks = 4
    depth = m_ref.shape[1]

    def squares(i, sums):
        sums = list(sums)
        done = []
        for u in range(chunks):
            start = pl.multiple_of((chunks * i + u) * SUB, SUB)
            for c in range(COMPS):
                one = first_ref[c, pl.ds(start, SUB), :]
                two = second_ref[c, pl.ds(start, SUB), :]
                done.append((c, start, jnp.where(pick, one, two)))
                diff = m_ref[c, pl.ds(start, SUB), :] - jnp.where(odd, one, two)
                sums[c + COMPS * u] = sums[c + COMPS * u] + diff * diff
        for c, start, cells in done:
            near_ref[c, pl.ds(start, SUB), :] = cells
        return tuple(sums)

    zero = jnp.zeros((SUB, LANES), jnp.float32)
    sums = lax.fori_loop(0, depth // (chunks * SUB), squares, (zero,) * (chunks * COMPS))
    total = jnp.sum(functools.reduce(jnp.add, sums), axis=(0, 1), keepdims=True)
    slot = lax.broadcasted_iota(jnp.int32, part_ref.shape, 1)
    part_ref[...] = jnp.where((slot == here) & (here > 0), total, 0.0)


def is_turned():
    return (lax.axis_index("gx") & 1) == 1


def turn(m, h, a2, b, sc):
    mx, my, mz = m
    hx, hy, hz = h
    hz = hz + a2 * mz
    gx = hx + b * (my * hz - mz * hy)
    gy = hy + b * (mz * hx - mx * hz)
    gz = hz + b * (mx * hy - my * hx)
    return (
        sc * (my * gz - mz * gy),
        sc * (mz * gx - mx * gz),
        sc * (mx * gy - my * gx),
    )


def normal(v):
    scale = lax.rsqrt(v[0] * v[0] + v[1] * v[1] + v[2] * v[2])
    return tuple(x * scale for x in v)


def start_kernel(
    ny, tiles, images, info_ref, sq_ref, m_ref, mp_ref, n_ref, np1_ref, np2_ref, reg_ref, regp_ref, main_ref, one_ref, two_ref
):
    here = lax.axis_index("img")
    lane = lane_iota()
    block = lane // DEPTH
    turned = is_turned()
    pick, _ = take_first(info_ref, here)
    lo = info_ref[4]
    slot = lane.astype(jnp.float32)
    squares = jnp.broadcast_to(jnp.sum(sq_ref[...], axis=0, keepdims=True), (SUB, LANES))
    lengths = jnp.where((lane >= 1) & (lane < images), jnp.sqrt(squares + eps), 0.0)
    total = jnp.sum(lengths, axis=1, keepdims=True)
    arc = jnp.sum(jnp.where(slot <= lo, lengths, 0.0), axis=1, keepdims=True)
    gap = jnp.sum(jnp.where(slot == lo + 1.0, lengths, 0.0), axis=1, keepdims=True)
    weight = jnp.clip((info_ref[3] * total - arc) / gap, -0.5, 1.5)
    below = lo < here.astype(jnp.float32)
    w_own = jnp.where(below, weight, 1.0 - weight)
    w_near = jnp.where(below, 1.0 - weight, weight)

    def fill(k, carry):
        done = []
        after = (k + 1) & (ny - 1)
        one = block == jnp.where(turned, after, k)
        two = block == jnp.where(turned, k, after)
        shift = (DEPTH * (k + 1)) & (LANES - 1)
        for g, (own, reg) in enumerate(((m_ref, reg_ref), (mp_ref, regp_ref))):
            for t in range(tiles):
                rows = rows_at(ny, tiles, k, t)
                if g == 0:
                    near = [n_ref[c, rows, :] for c in range(COMPS)]
                else:
                    near = [
                        jnp.where(pick, np1_ref[c, rows, :], np2_ref[c, rows, :]) for c in range(COMPS)
                    ]
                v = normal([w_own * own[c, rows, :] + w_near * near[c] for c in range(COMPS)])
                v = list(v) + [reg[rows, :].astype(jnp.float32)]
                done.append((g, t, v, [pltpu.roll(x, shift, 1) for x in v]))
        for g, t, v, ends in done:
            for c in range(COMPS):
                main_ref[c, g * ny + k, t] = v[c]
            for c in range(COMPS + 1):
                pltpu.store(one_ref.at[g, c, t], ends[c], mask=one)
                pltpu.store(two_ref.at[g, c, t], ends[c], mask=two)
        return carry

    lax.fori_loop(0, ny, fill, 0)


def look_up(info_ref, region):
    return [jnp.take_along_axis(info_ref[i], region, axis=1) for i in range(3)]


def look_up_kernel(ny, tiles, info_ref, reg_ref, regp_ref, par_ref):
    def fill(k, carry):
        done = []
        for g, reg in enumerate((reg_ref, regp_ref)):
            for t in range(tiles):
                done.append((g * ny + k, t, look_up(info_ref, reg[rows_at(ny, tiles, k, t), :])))
        for r, t, p in done:
            for i in range(3):
                par_ref[i, r, t] = p[i]
        return carry

    lax.fori_loop(0, ny, fill, 0)


def evolve_kernel(
    ny,
    tiles,
    info_ref,
    start_ref,
    par,
    one_ref,
    two_ref,
    out_ref,
    main0,
    main1,
    strip0,
    strip1,
    edge,
    seam0,
    seam1,
    spar,
):
    main, strip, seam = (main0, main1), (strip0, strip1), (seam0, seam1)
    window = ny + 2 * DEPTH
    lane = lane_iota()
    sub = sub_iota()
    block = lane // DEPTH
    first_lane = lane == 0
    last_lane = lane == LANES - 1
    head_lane = lane % DEPTH == 0
    tail_lane = lane % DEPTH == DEPTH - 1
    top = sub == SUB - 1
    bottom = sub == 0
    turned = is_turned()

    def ends_of(k, new):
        shift = (DEPTH * (k + 1)) & (LANES - 1)
        return [pltpu.roll(new[c], shift, 1) for c in range(COMPS)]

    def copy(r, carry):
        for u in range(2):
            for t in range(tiles):
                for c in range(COMPS):
                    main0[c, 2 * r + u, t] = start_ref[c, 2 * r + u, t]
        return carry

    lax.fori_loop(0, window // 2, copy, 0)

    def seam_of(left, right):
        return jnp.where(head_lane, pltpu.roll(left, 1, 1), pltpu.roll(right, LANES - 1, 1))

    def fill_strips(t, carry):
        done = []
        for g in range(2):
            one = [one_ref[g, c, t] for c in range(COMPS + 1)]
            two = [two_ref[g, c, t] for c in range(COMPS + 1)]
            left = [jnp.where(turned, x, y) for x, y in zip(one, two)]
            right = [jnp.where(turned, y, x) for x, y in zip(one, two)]
            for side, cells in enumerate((left, right)):
                p = look_up(info_ref, cells[COMPS].astype(jnp.int32))
                done.append((side, g, cells[:COMPS], p))
        for side, g, v, p in done:
            for c in range(COMPS):
                strip0[c, side, g, t] = v[c]
            for i in range(3):
                spar[i, side, g, t] = p[i]
        for g in range(2):
            left, right = (v for _, h, v, _ in done if h == g)
            for c in range(COMPS):
                seam0[c, g, t] = seam_of(left[c], right[c])
        return carry

    lax.fori_loop(0, tiles, fill_strips, 0)

    def around_z(cells, t):
        if t + 1 < tiles:
            above = cells[t + 1]
        else:
            above = jnp.where(top, 0.0, pltpu.roll(cells[0], SUB - 1, 0))
        if t > 0:
            under = cells[t - 1]
        else:
            under = jnp.where(bottom, 0.0, pltpu.roll(cells[tiles - 1], 1, 0))
        return above + under

    def main_row(state, r):
        g = r // ny
        k = r & (ny - 1)
        after = (r + 1) & (window - 1)
        before = (r - 1) & (window - 1)
        shift = (LANES - DEPTH * (k + 1)) & (LANES - 1)
        center = [[main[state][c, r, t] for t in range(tiles)] for c in range(COMPS)]
        done = []
        for t in range(tiles):
            h = []
            for c in range(COMPS):
                cells = center[c][t]
                ends = pltpu.roll(seam[state][c, g, t], shift, 1)
                s = jnp.where(first_lane, ends, pltpu.roll(cells, 1, 1))
                s = s + jnp.where(last_lane, ends, pltpu.roll(cells, LANES - 1, 1))
                s = s + (main[state][c, after, t] + main[state][c, before, t])
                h.append(s + around_z(center[c], t))
            m = [center[c][t] for c in range(COMPS)]
            rate = turn(m, h, par[0, r, t], par[1, r, t], par[2, r, t])
            if state == 0:
                new = [m[c] + rate[c] for c in range(COMPS)]
            else:
                new = normal([main[0][c, r, t] + (m[c] + rate[c]) for c in range(COMPS)])
            done.append((r, t, new, ends_of(k, m)))
        return done

    def strip_rows(state):
        done = []
        for g in range(2):
            for side in range(2):
                start = block == side
                stop = block == (side + ny - 1) % ny
                center = [[strip[state][c, side, g, t] for t in range(tiles)] for c in range(COMPS)]
                for t in range(tiles):
                    h = []
                    for c in range(COMPS):
                        cells = center[c][t]
                        inner = edge[c, g, t]
                        other = strip[state][c, side, 1 - g, t]
                        if side == 0:
                            s = pltpu.roll(cells, 1, 1)
                            s = s + pltpu.roll(jnp.where(head_lane, inner, cells), LANES - 1, 1)
                        else:
                            s = pltpu.roll(jnp.where(tail_lane, inner, cells), 1, 1)
                            s = s + pltpu.roll(cells, LANES - 1, 1)
                        s = s + pltpu.roll(jnp.where(start, other, cells), LANES - DEPTH, 1)
                        s = s + pltpu.roll(jnp.where(stop, other, cells), DEPTH, 1)
                        h.append(s + around_z(center[c], t))
                    m = [center[c][t] for c in range(COMPS)]
                    rate = turn(
                        m, h, spar[0, side, g, t], spar[1, side, g, t], spar[2, side, g, t]
                    )
                    if state == 0:
                        new = [m[c] + rate[c] for c in range(COMPS)]
                    else:
                        new = normal(
                            [strip[0][c, side, g, t] + (m[c] + rate[c]) for c in range(COMPS)]
                        )
                    done.append((side, g, t, new))
        for side, g, t, new in done:
            for c in range(COMPS):
                strip[1 - state][c, side, g, t] = new[c]
        for g in range(2):
            for t in range(tiles):
                left, right = (new for _, h, u, new in done if (h, u) == (g, t))
                for c in range(COMPS):
                    seam[1 - state][c, g, t] = seam_of(left[c], right[c])

    def main_rows(state, first, count):
        def rows(i, carry):
            done = []
            for u in range(ROWS):
                done += main_row(state, (first + ROWS * i + u) & (window - 1))
            for r, t, new, ends in done:
                k = r & (ny - 1)
                mask = ((lane - (DEPTH * k + DEPTH - 1)) & (LANES - 1)) < 2
                for c in range(COMPS):
                    main[1 - state][c, r, t] = new[c]
                    pltpu.store(edge.at[c, r // ny, t], ends[c], mask=mask)
            return carry

        lax.fori_loop(0, count // ROWS, rows, 0)

    def step(i, carry):
        for state in range(2):
            margin = DEPTH - 2 * state - 2 * i
            main_rows(state, -margin, ny + 2 * margin)
            strip_rows(state)
        return carry

    lax.fori_loop(0, STEPS, step, 0)

    def hand_out(k, carry):
        for t in range(tiles):
            for c in range(COMPS):
                out_ref[c, rows_at(ny, tiles, k, t), :] = main[0][c, k, t]
        return carry

    lax.fori_loop(0, ny, hand_out, 0)


def shifted(cells, axis, step, closed):
    count = lax.axis_size(axis)
    pairs = [(i, (i + step) % count) for i in range(count) if closed or 0 <= i + step < count]
    return lax.ppermute(cells, axis, pairs)


def swapped(cells, axis, first, closed):
    count = lax.axis_size(axis)
    pairs = [(i, (i + 1) % count) for i in range(first, count if closed else count - 1, 2)]
    return lax.ppermute(cells, axis, pairs + [(j, i) for i, j in pairs])


def around(cells, dim):
    ny = cells.shape[dim]
    if lax.axis_size("gy") == 2:
        return shifted(cells, "gy", 1, True)
    head = lax.slice_in_dim(cells, 0, DEPTH, axis=dim)
    tail = lax.slice_in_dim(cells, ny - DEPTH, ny, axis=dim)
    return jnp.concatenate([shifted(head, "gy", -1, True), shifted(tail, "gy", 1, True)], axis=dim)


def body(magnetization, lower_image, image_weights, regions, anisotropy, damping):
    local, comps, nz, ny, nx = magnetization.shape
    images = local * lax.axis_size("img")
    tiles = nz // SUB
    devices = lax.axis_size(("img", "gx", "gy"))
    assert lax.axis_size("gx") % 2 == 0
    assert local == 1 and comps == COMPS and nx == LANES
    assert ny == 2 * DEPTH and ny * DEPTH == LANES and tiles >= 2
    flat = (comps, nz * ny, nx)
    own = magnetization[0]
    own_p = around(own, 2)
    first = swapped(own, "img", 0, False)
    second = swapped(own, "img", 1, False)

    smem = pl.BlockSpec(memory_space=pltpu.SMEM)
    vmem = pl.BlockSpec(memory_space=pltpu.VMEM)
    f32 = jnp.float32
    limit = pltpu.CompilerParams(vmem_limit_bytes=32 * 1024 * 1024)
    vreg = (SUB, LANES)
    info = pl.pallas_call(
        functools.partial(info_kernel, anisotropy.shape[0]),
        out_shape=jax.ShapeDtypeStruct((5,) + vreg, f32),
        in_specs=[smem] * 3 + [vmem],
        out_specs=vmem,
        compiler_params=limit,
        name="small_arguments",
    )(lower_image, anisotropy, damping, image_weights.reshape(1, -1))
    own_p, info = lax.optimization_barrier((own_p, info))
    first_p = swapped(own_p, "img", 0, False)
    second_p = swapped(own_p, "img", 1, False)
    late_regions, info = lax.optimization_barrier((regions, info))
    reg_p = around(late_regions, 1)
    part, near = pl.pallas_call(
        gather_kernel,
        out_shape=(jax.ShapeDtypeStruct((devices, LANES), f32), jax.ShapeDtypeStruct(flat, f32)),
        in_specs=[vmem] * 4,
        out_specs=(vmem,) * 2,
        compiler_params=limit,
        name="gather_images",
    )(info, own.reshape(flat), first.reshape(flat), second.reshape(flat))
    squares = lax.all_to_all(part, ("img", "gx", "gy"), 0, 0, tiled=True)

    window = ny + 2 * DEPTH
    tile_rows = (regions.reshape(flat[1:]), reg_p.reshape(flat[1:]))
    packed = jax.ShapeDtypeStruct((2, comps + 1, tiles) + vreg, f32)
    start, one, two = pl.pallas_call(
        functools.partial(start_kernel, ny, tiles, images),
        out_shape=(jax.ShapeDtypeStruct((comps, window, tiles) + vreg, f32), packed, packed),
        in_specs=[vmem] * 9,
        out_specs=(vmem,) * 3,
        compiler_params=limit,
        name="start",
    )(
        info,
        squares,
        own.reshape(flat),
        own_p.reshape(flat),
        near,
        first_p.reshape(flat),
        second_p.reshape(flat),
        *tile_rows,
    )
    one = swapped(one, "gx", 0, True)
    two = swapped(two, "gx", 1, True)
    par = pl.pallas_call(
        functools.partial(look_up_kernel, ny, tiles),
        out_shape=jax.ShapeDtypeStruct((3, window, tiles) + vreg, f32),
        in_specs=[vmem] * 3,
        out_specs=vmem,
        compiler_params=limit,
        name="parameters",
    )(info, *tile_rows)
    out = pl.pallas_call(
        functools.partial(evolve_kernel, ny, tiles),
        out_shape=jax.ShapeDtypeStruct(flat, f32),
        in_specs=[vmem] * 5,
        out_specs=vmem,
        scratch_shapes=[
            pltpu.VMEM((comps, window, tiles) + vreg, f32),
            pltpu.VMEM((comps, window, tiles) + vreg, f32),
            pltpu.VMEM((comps, 2, 2, tiles) + vreg, f32),
            pltpu.VMEM((comps, 2, 2, tiles) + vreg, f32),
            pltpu.VMEM((comps, 2, tiles) + vreg, f32),
            pltpu.VMEM((comps, 2, tiles) + vreg, f32),
            pltpu.VMEM((comps, 2, tiles) + vreg, f32),
            pltpu.VMEM((3, 2, 2, tiles) + vreg, f32),
        ],
        compiler_params=limit,
        name="evolve",
    )(info, start, par, one, two)
    return out.reshape(magnetization.shape)


def solution(mesh):
    placed = (P("img", None, None, "gy", "gx"), P(), P(), P(None, "gy", "gx"), P(), P())
    return jax.shard_map(
        body,
        mesh=mesh,
        in_specs=placed,
        out_specs=P("img", None, None, "gy", "gx"),
        check_vma=False,
    )
```

```python
import functools

import jax
import jax.numpy as jnp
from jax import lax
from jax.experimental import pallas as pl
from jax.experimental.pallas import tpu as pltpu
from jax.sharding import PartitionSpec as P

STEPS = 4
DEPTH = 2 * STEPS

eps = 1e-06
time_step = 0.05

SUB = 8
LANES = 128
COMPS = 3
ALONG_Z = 2
ROWS = 4


def lane_iota():
    return lax.broadcasted_iota(jnp.int32, (SUB, LANES), 1)


def sub_iota():
    return lax.broadcasted_iota(jnp.int32, (SUB, LANES), 0)


def rows_at(ny, tiles, y, t):
    return pl.ds(y + ny * t, SUB, stride=ny * tiles)


def info_kernel(regions, lower_ref, aniso_ref, damp_ref, share_ref, m_ref, reg_ref, info_ref):
    here = lax.axis_index("img")
    lane = lane_iota()
    table_a = jnp.zeros((SUB, LANES), jnp.float32)
    table_d = jnp.zeros((SUB, LANES), jnp.float32)
    for i in range(regions):
        table_a = jnp.where(lane == i, 2.0 * aniso_ref[i], table_a)
        table_d = jnp.where(lane == i, damp_ref[i], table_d)
    info_ref[0] = table_a
    info_ref[1] = table_d
    info_ref[2] = -time_step / (1.0 + table_d * table_d)
    share = share_ref[...]
    spot = lax.broadcasted_iota(jnp.int32, share.shape, 1)
    target = jnp.sum(jnp.where(spot < here, share, 0.0), axis=1, keepdims=True) / jnp.sum(
        share, axis=1, keepdims=True
    )
    info_ref[3] = jnp.broadcast_to(target, (SUB, LANES))
    info_ref[4] = jnp.full((SUB, LANES), lower_ref[here].astype(jnp.float32))


def take_first(info_ref, here):
    odd = (here & 1) == 1
    below = info_ref[4] < here.astype(jnp.float32)
    return jnp.where(below, jnp.where(odd, 1, 0), jnp.where(odd, 0, 1)) == 1, odd


def gather_kernel(info_ref, m_ref, first_ref, second_ref, part_ref, near_ref, sent_ref):
    here = lax.axis_index("img")
    pick, odd = take_first(info_ref, here)
    chunks = 4
    depth = m_ref.shape[1]

    def squares(i, sums):
        sums = list(sums)
        done = []
        for u in range(chunks):
            start = pl.multiple_of((chunks * i + u) * SUB, SUB)
            for c in range(COMPS):
                one = first_ref[c, pl.ds(start, SUB), :]
                two = second_ref[c, pl.ds(start, SUB), :]
                done.append((c, start, jnp.where(pick, one, two)))
                diff = m_ref[c, pl.ds(start, SUB), :] - jnp.where(odd, one, two)
                sums[c + COMPS * u] = sums[c + COMPS * u] + diff * diff
        for c, start, cells in done:
            near_ref[c, pl.ds(start, SUB), :] = cells
            if c >= ALONG_Z:
                sent_ref[c - ALONG_Z, pl.ds(start, SUB), :] = cells
        return tuple(sums)

    zero = jnp.zeros((SUB, LANES), jnp.float32)
    sums = lax.fori_loop(0, depth // (chunks * SUB), squares, (zero,) * (chunks * COMPS))
    total = jnp.sum(functools.reduce(jnp.add, sums), axis=(0, 1), keepdims=True)
    slot = lax.broadcasted_iota(jnp.int32, part_ref.shape, 1)
    part_ref[...] = jnp.where((slot == here) & (here > 0), total, 0.0)


def is_turned():
    return (lax.axis_index("gx") & 1) == 1


def turn(m, h, a2, b, sc):
    mx, my, mz = m
    hx, hy, hz = h
    hz = hz + a2 * mz
    gx = hx + b * (my * hz - mz * hy)
    gy = hy + b * (mz * hx - mx * hz)
    gz = hz + b * (mx * hy - my * hx)
    return (
        sc * (my * gz - mz * gy),
        sc * (mz * gx - mx * gz),
        sc * (mx * gy - my * gx),
    )


def normal(v):
    scale = lax.rsqrt(v[0] * v[0] + v[1] * v[1] + v[2] * v[2])
    return tuple(x * scale for x in v)


def start_kernel(
    ny, tiles, images, info_ref, sq_ref, m_ref, mp_ref, n_ref, np1_ref, np2_ref, np3_ref, reg_ref, regp_ref, main_ref, one_ref, two_ref
):
    here = lax.axis_index("img")
    lane = lane_iota()
    block = lane // DEPTH
    turned = is_turned()
    pick, _ = take_first(info_ref, here)
    lo = info_ref[4]
    slot = lane.astype(jnp.float32)
    squares = jnp.broadcast_to(jnp.sum(sq_ref[...], axis=0, keepdims=True), (SUB, LANES))
    lengths = jnp.where((lane >= 1) & (lane < images), jnp.sqrt(squares + eps), 0.0)
    total = jnp.sum(lengths, axis=1, keepdims=True)
    arc = jnp.sum(jnp.where(slot <= lo, lengths, 0.0), axis=1, keepdims=True)
    gap = jnp.sum(jnp.where(slot == lo + 1.0, lengths, 0.0), axis=1, keepdims=True)
    weight = jnp.clip((info_ref[3] * total - arc) / gap, -0.5, 1.5)
    below = lo < here.astype(jnp.float32)
    w_own = jnp.where(below, weight, 1.0 - weight)
    w_near = jnp.where(below, 1.0 - weight, weight)

    def fill(k, carry):
        done = []
        after = (k + 1) & (ny - 1)
        one = block == jnp.where(turned, after, k)
        two = block == jnp.where(turned, k, after)
        shift = (DEPTH * (k + 1)) & (LANES - 1)
        for g, (own, reg) in enumerate(((m_ref, reg_ref), (mp_ref, regp_ref))):
            for t in range(tiles):
                rows = rows_at(ny, tiles, k, t)
                if g == 0:
                    near = [n_ref[c, rows, :] for c in range(COMPS)]
                else:
                    near = [
                        jnp.where(pick, np1_ref[c, rows, :], np2_ref[c, rows, :])
                        if c < ALONG_Z
                        else np3_ref[c - ALONG_Z, rows, :]
                        for c in range(COMPS)
                    ]
                v = normal([w_own * own[c, rows, :] + w_near * near[c] for c in range(COMPS)])
                v = list(v) + [reg[rows, :].astype(jnp.float32)]
                done.append((g, t, v, [pltpu.roll(x, shift, 1) for x in v]))
        for g, t, v, ends in done:
            for c in range(COMPS):
                main_ref[c, g * ny + k, t] = v[c]
            for c in range(COMPS + 1):
                pltpu.store(one_ref.at[g, c, t], ends[c], mask=one)
                pltpu.store(two_ref.at[g, c, t], ends[c], mask=two)
        return carry

    lax.fori_loop(0, ny, fill, 0)


def look_up(info_ref, region):
    return [jnp.take_along_axis(info_ref[i], region, axis=1) for i in range(3)]


def look_up_kernel(ny, tiles, info_ref, reg_ref, regp_ref, par_ref):
    def fill(k, carry):
        done = []
        for g, reg in enumerate((reg_ref, regp_ref)):
            for t in range(tiles):
                done.append((g * ny + k, t, look_up(info_ref, reg[rows_at(ny, tiles, k, t), :])))
        for r, t, p in done:
            for i in range(3):
                par_ref[i, r, t] = p[i]
        return carry

    lax.fori_loop(0, ny, fill, 0)


def evolve_kernel(
    ny,
    tiles,
    info_ref,
    start_ref,
    par,
    one_ref,
    two_ref,
    out_ref,
    main0,
    main1,
    strip0,
    strip1,
    edge,
    seam0,
    seam1,
    spar,
):
    main, strip, seam = (main0, main1), (strip0, strip1), (seam0, seam1)
    window = ny + 2 * DEPTH
    lane = lane_iota()
    sub = sub_iota()
    block = lane // DEPTH
    first_lane = lane == 0
    last_lane = lane == LANES - 1
    head_lane = lane % DEPTH == 0
    tail_lane = lane % DEPTH == DEPTH - 1
    top = sub == SUB - 1
    bottom = sub == 0
    turned = is_turned()

    def ends_of(k, new):
        shift = (DEPTH * (k + 1)) & (LANES - 1)
        return [pltpu.roll(new[c], shift, 1) for c in range(COMPS)]

    def seam_of(left, right):
        return jnp.where(head_lane, pltpu.roll(left, 1, 1), pltpu.roll(right, LANES - 1, 1))

    def fill_strips(t, carry):
        done = []
        for g in range(2):
            one = [one_ref[g, c, t] for c in range(COMPS + 1)]
            two = [two_ref[g, c, t] for c in range(COMPS + 1)]
            left = [jnp.where(turned, x, y) for x, y in zip(one, two)]
            right = [jnp.where(turned, y, x) for x, y in zip(one, two)]
            for side, cells in enumerate((left, right)):
                p = look_up(info_ref, cells[COMPS].astype(jnp.int32))
                done.append((side, g, cells[:COMPS], p))
        for side, g, v, p in done:
            for c in range(COMPS):
                strip0[c, side, g, t] = v[c]
            for i in range(3):
                spar[i, side, g, t] = p[i]
        for g in range(2):
            left, right = (v for _, h, v, _ in done if h == g)
            for c in range(COMPS):
                seam0[c, g, t] = seam_of(left[c], right[c])
        return carry

    lax.fori_loop(0, tiles, fill_strips, 0)

    def around_z(cells, t):
        if t + 1 < tiles:
            above = cells[t + 1]
        else:
            above = jnp.where(top, 0.0, pltpu.roll(cells[0], SUB - 1, 0))
        if t > 0:
            under = cells[t - 1]
        else:
            under = jnp.where(bottom, 0.0, pltpu.roll(cells[tiles - 1], 1, 0))
        return above + under

    def main_row(state, r):
        g = r // ny
        k = r & (ny - 1)
        after = (r + 1) & (window - 1)
        before = (r - 1) & (window - 1)
        shift = (LANES - DEPTH * (k + 1)) & (LANES - 1)
        center = [[main[state][c, r, t] for t in range(tiles)] for c in range(COMPS)]
        done = []
        for t in range(tiles):
            h = []
            for c in range(COMPS):
                cells = center[c][t]
                ends = pltpu.roll(seam[state][c, g, t], shift, 1)
                s = jnp.where(first_lane, ends, pltpu.roll(cells, 1, 1))
                s = s + jnp.where(last_lane, ends, pltpu.roll(cells, LANES - 1, 1))
                s = s + (main[state][c, after, t] + main[state][c, before, t])
                h.append(s + around_z(center[c], t))
            m = [center[c][t] for c in range(COMPS)]
            rate = turn(m, h, par[0, r, t], par[1, r, t], par[2, r, t])
            if state == 0:
                new = [m[c] + rate[c] for c in range(COMPS)]
            else:
                new = normal([main[0][c, r, t] + (m[c] + rate[c]) for c in range(COMPS)])
            done.append((r, t, new, ends_of(k, m)))
        return done

    def strip_rows(state):
        done = []
        for g in range(2):
            for side in range(2):
                start = block == side
                stop = block == (side + ny - 1) % ny
                center = [[strip[state][c, side, g, t] for t in range(tiles)] for c in range(COMPS)]
                for t in range(tiles):
                    h = []
                    for c in range(COMPS):
                        cells = center[c][t]
                        inner = edge[c, g, t]
                        other = strip[state][c, side, 1 - g, t]
                        if side == 0:
                            s = pltpu.roll(cells, 1, 1)
                            s = s + pltpu.roll(jnp.where(head_lane, inner, cells), LANES - 1, 1)
                        else:
                            s = pltpu.roll(jnp.where(tail_lane, inner, cells), 1, 1)
                            s = s + pltpu.roll(cells, LANES - 1, 1)
                        s = s + pltpu.roll(jnp.where(start, other, cells), LANES - DEPTH, 1)
                        s = s + pltpu.roll(jnp.where(stop, other, cells), DEPTH, 1)
                        h.append(s + around_z(center[c], t))
                    m = [center[c][t] for c in range(COMPS)]
                    rate = turn(
                        m, h, spar[0, side, g, t], spar[1, side, g, t], spar[2, side, g, t]
                    )
                    if state == 0:
                        new = [m[c] + rate[c] for c in range(COMPS)]
                    else:
                        new = normal(
                            [strip[0][c, side, g, t] + (m[c] + rate[c]) for c in range(COMPS)]
                        )
                    done.append((side, g, t, new))
        for side, g, t, new in done:
            for c in range(COMPS):
                strip[1 - state][c, side, g, t] = new[c]
        for g in range(2):
            for t in range(tiles):
                left, right = (new for _, h, u, new in done if (h, u) == (g, t))
                for c in range(COMPS):
                    seam[1 - state][c, g, t] = seam_of(left[c], right[c])

    def main_rows(state, first, count):
        def rows(i, carry):
            done = []
            for u in range(ROWS):
                done += main_row(state, (first + ROWS * i + u) & (window - 1))
            for r, t, new, ends in done:
                k = r & (ny - 1)
                mask = ((lane - (DEPTH * k + DEPTH - 1)) & (LANES - 1)) < 2
                for c in range(COMPS):
                    main[1 - state][c, r, t] = new[c]
                    pltpu.store(edge.at[c, r // ny, t], ends[c], mask=mask)
            return carry

        lax.fori_loop(0, count // ROWS, rows, 0)

    def step(i, carry):
        for state in range(2):
            margin = DEPTH - 2 * state - 2 * i
            main_rows(state, -margin, ny + 2 * margin)
            strip_rows(state)
        return carry

    lax.fori_loop(0, STEPS, step, 0)

    def hand_out(k, carry):
        for t in range(tiles):
            for c in range(COMPS):
                out_ref[c, rows_at(ny, tiles, k, t), :] = main[0][c, k, t]
        return carry

    lax.fori_loop(0, ny, hand_out, 0)


def shifted(cells, axis, step, closed):
    count = lax.axis_size(axis)
    pairs = [(i, (i + step) % count) for i in range(count) if closed or 0 <= i + step < count]
    return lax.ppermute(cells, axis, pairs)


def swapped(cells, axis, first, closed):
    count = lax.axis_size(axis)
    pairs = [(i, (i + 1) % count) for i in range(first, count if closed else count - 1, 2)]
    return lax.ppermute(cells, axis, pairs + [(j, i) for i, j in pairs])


def around(cells, dim):
    ny = cells.shape[dim]
    if lax.axis_size("gy") == 2:
        return shifted(cells, "gy", 1, True)
    head = lax.slice_in_dim(cells, 0, DEPTH, axis=dim)
    tail = lax.slice_in_dim(cells, ny - DEPTH, ny, axis=dim)
    return jnp.concatenate([shifted(head, "gy", -1, True), shifted(tail, "gy", 1, True)], axis=dim)


def body(magnetization, lower_image, image_weights, regions, anisotropy, damping):
    local, comps, nz, ny, nx = magnetization.shape
    images = local * lax.axis_size("img")
    tiles = nz // SUB
    devices = lax.axis_size(("img", "gx", "gy"))
    assert lax.axis_size("gx") % 2 == 0
    assert local == 1 and comps == COMPS and nx == LANES
    assert ny == 2 * DEPTH and ny * DEPTH == LANES and tiles >= 2
    flat = (comps, nz * ny, nx)
    own = magnetization[0]
    own_p = around(own, 2)
    first = swapped(own, "img", 0, False)
    second = swapped(own, "img", 1, False)

    smem = pl.BlockSpec(memory_space=pltpu.SMEM)
    vmem = pl.BlockSpec(memory_space=pltpu.VMEM)
    f32 = jnp.float32
    limit = pltpu.CompilerParams(vmem_limit_bytes=32 * 1024 * 1024)
    vreg = (SUB, LANES)
    info = pl.pallas_call(
        functools.partial(info_kernel, anisotropy.shape[0]),
        out_shape=jax.ShapeDtypeStruct((5,) + vreg, f32),
        in_specs=[smem] * 3 + [vmem] * 3,
        out_specs=vmem,
        compiler_params=limit,
        name="small_arguments",
    )(
        lower_image,
        anisotropy,
        damping,
        image_weights.reshape(1, -1),
        own.reshape(flat),
        regions.reshape(flat[1:]),
    )
    own_p, info = lax.optimization_barrier((own_p, info))
    first_p = swapped(own_p[:ALONG_Z], "img", 0, False)
    second_p = swapped(own_p[:ALONG_Z], "img", 1, False)
    late_regions, info = lax.optimization_barrier((regions, info))
    reg_p = around(late_regions, 1)
    info, reg_p = lax.optimization_barrier((info, reg_p))
    part, near, sent = pl.pallas_call(
        gather_kernel,
        out_shape=(
            jax.ShapeDtypeStruct((devices, LANES), f32),
            jax.ShapeDtypeStruct(flat, f32),
            jax.ShapeDtypeStruct((comps - ALONG_Z,) + flat[1:], f32),
        ),
        in_specs=[vmem] * 4,
        out_specs=(vmem,) * 3,
        compiler_params=limit,
        name="gather_images",
    )(info, own.reshape(flat), first.reshape(flat), second.reshape(flat))
    sent_p = around(sent.reshape((comps - ALONG_Z,) + own.shape[1:]), 2)
    squares = lax.all_to_all(part, ("img", "gx", "gy"), 0, 0, tiled=True)

    window = ny + 2 * DEPTH
    tile_rows = (regions.reshape(flat[1:]), reg_p.reshape(flat[1:]))
    packed = jax.ShapeDtypeStruct((2, comps + 1, tiles) + vreg, f32)
    start, one, two = pl.pallas_call(
        functools.partial(start_kernel, ny, tiles, images),
        out_shape=(jax.ShapeDtypeStruct((comps, window, tiles) + vreg, f32), packed, packed),
        in_specs=[vmem] * 10,
        out_specs=(vmem,) * 3,
        compiler_params=limit,
        name="start",
    )(
        info,
        squares,
        own.reshape(flat),
        own_p.reshape(flat),
        near,
        first_p.reshape((ALONG_Z,) + flat[1:]),
        second_p.reshape((ALONG_Z,) + flat[1:]),
        sent_p.reshape((comps - ALONG_Z,) + flat[1:]),
        *tile_rows,
    )
    one = swapped(one, "gx", 0, True)
    two = swapped(two, "gx", 1, True)
    par = pl.pallas_call(
        functools.partial(look_up_kernel, ny, tiles),
        out_shape=jax.ShapeDtypeStruct((3, window, tiles) + vreg, f32),
        in_specs=[vmem] * 3,
        out_specs=vmem,
        compiler_params=limit,
        name="parameters",
    )(info, *tile_rows)
    out, _ = pl.pallas_call(
        functools.partial(evolve_kernel, ny, tiles),
        out_shape=(jax.ShapeDtypeStruct(flat, f32), jax.ShapeDtypeStruct(start.shape, f32)),
        in_specs=[vmem] * 5,
        out_specs=(vmem,) * 2,
        input_output_aliases={1: 1},
        scratch_shapes=[
            pltpu.VMEM((comps, window, tiles) + vreg, f32),
            pltpu.VMEM((comps, 2, 2, tiles) + vreg, f32),
            pltpu.VMEM((comps, 2, 2, tiles) + vreg, f32),
            pltpu.VMEM((comps, 2, tiles) + vreg, f32),
            pltpu.VMEM((comps, 2, tiles) + vreg, f32),
            pltpu.VMEM((comps, 2, tiles) + vreg, f32),
            pltpu.VMEM((3, 2, 2, tiles) + vreg, f32),
        ],
        compiler_params=limit,
        name="evolve",
    )(info, start, par, one, two)
    return out.reshape(magnetization.shape)


def solution(mesh):
    placed = (P("img", None, None, "gy", "gx"), P(), P(), P(None, "gy", "gx"), P(), P())
    return jax.shard_map(
        body,
        mesh=mesh,
        in_specs=placed,
        out_specs=P("img", None, None, "gy", "gx"),
        check_vma=False,
    )
```

```python
import functools

import jax
import jax.numpy as jnp
from jax import lax
from jax.experimental import pallas as pl
from jax.experimental.pallas import tpu as pltpu
from jax.sharding import PartitionSpec as P

STEPS = 4
DEPTH = 2 * STEPS

eps = 1e-06
time_step = 0.05

SUB = 8
LANES = 128
COMPS = 3
ALONG_Z = 2
ROWS = 4


def lane_iota():
    return lax.broadcasted_iota(jnp.int32, (SUB, LANES), 1)


def sub_iota():
    return lax.broadcasted_iota(jnp.int32, (SUB, LANES), 0)


def rows_at(ny, tiles, y, t):
    return pl.ds(y + ny * t, SUB, stride=ny * tiles)


def info_kernel(regions, lower_ref, aniso_ref, damp_ref, share_ref, m_ref, reg_ref, info_ref):
    here = lax.axis_index("img")
    lane = lane_iota()
    table_a = jnp.zeros((SUB, LANES), jnp.float32)
    table_d = jnp.zeros((SUB, LANES), jnp.float32)
    for i in range(regions):
        table_a = jnp.where(lane == i, 2.0 * aniso_ref[i], table_a)
        table_d = jnp.where(lane == i, damp_ref[i], table_d)
    info_ref[0] = table_a
    info_ref[1] = table_d
    info_ref[2] = -time_step / (1.0 + table_d * table_d)
    share = share_ref[...]
    spot = lax.broadcasted_iota(jnp.int32, share.shape, 1)
    target = jnp.sum(jnp.where(spot < here, share, 0.0), axis=1, keepdims=True) / jnp.sum(
        share, axis=1, keepdims=True
    )
    info_ref[3] = jnp.broadcast_to(target, (SUB, LANES))
    info_ref[4] = jnp.full((SUB, LANES), lower_ref[here].astype(jnp.float32))


def take_first(info_ref, here):
    odd = (here & 1) == 1
    below = info_ref[4] < here.astype(jnp.float32)
    return jnp.where(below, jnp.where(odd, 1, 0), jnp.where(odd, 0, 1)) == 1, odd


def gather_kernel(info_ref, m_ref, first_ref, second_ref, part_ref, near_ref, sent_ref):
    here = lax.axis_index("img")
    pick, odd = take_first(info_ref, here)
    chunks = 4
    depth = m_ref.shape[1]

    def squares(i, sums):
        sums = list(sums)
        done = []
        for u in range(chunks):
            start = pl.multiple_of((chunks * i + u) * SUB, SUB)
            for c in range(COMPS):
                one = first_ref[c, pl.ds(start, SUB), :]
                two = second_ref[c, pl.ds(start, SUB), :]
                done.append((c, start, jnp.where(pick, one, two)))
                diff = m_ref[c, pl.ds(start, SUB), :] - jnp.where(odd, one, two)
                sums[c + COMPS * u] = sums[c + COMPS * u] + diff * diff
        for c, start, cells in done:
            near_ref[c, pl.ds(start, SUB), :] = cells
            if c >= ALONG_Z:
                sent_ref[c - ALONG_Z, pl.ds(start, SUB), :] = cells
        return tuple(sums)

    zero = jnp.zeros((SUB, LANES), jnp.float32)
    sums = lax.fori_loop(0, depth // (chunks * SUB), squares, (zero,) * (chunks * COMPS))
    total = jnp.sum(functools.reduce(jnp.add, sums), axis=(0, 1), keepdims=True)
    slot = lax.broadcasted_iota(jnp.int32, part_ref.shape, 1)
    part_ref[...] = jnp.where((slot == here) & (here > 0), total, 0.0)


def is_turned():
    return (lax.axis_index("gx") & 1) == 1


def turn(m, h, a2, b, sc):
    mx, my, mz = m
    hx, hy, hz = h
    hz = hz + a2 * mz
    gx = hx + b * (my * hz - mz * hy)
    gy = hy + b * (mz * hx - mx * hz)
    gz = hz + b * (mx * hy - my * hx)
    return (
        sc * (my * gz - mz * gy),
        sc * (mz * gx - mx * gz),
        sc * (mx * gy - my * gx),
    )


def normal(v):
    scale = lax.rsqrt(v[0] * v[0] + v[1] * v[1] + v[2] * v[2])
    return tuple(x * scale for x in v)


def start_kernel(
    ny, tiles, images, info_ref, sq_ref, m_ref, mp_ref, n_ref, np1_ref, np2_ref, np3_ref, reg_ref, regp_ref, main_ref, one_ref, two_ref
):
    here = lax.axis_index("img")
    lane = lane_iota()
    block = lane // DEPTH
    turned = is_turned()
    pick, _ = take_first(info_ref, here)
    lo = info_ref[4]
    slot = lane.astype(jnp.float32)
    squares = jnp.broadcast_to(jnp.sum(sq_ref[...], axis=0, keepdims=True), (SUB, LANES))
    lengths = jnp.where((lane >= 1) & (lane < images), jnp.sqrt(squares + eps), 0.0)
    total = jnp.sum(lengths, axis=1, keepdims=True)
    arc = jnp.sum(jnp.where(slot <= lo, lengths, 0.0), axis=1, keepdims=True)
    gap = jnp.sum(jnp.where(slot == lo + 1.0, lengths, 0.0), axis=1, keepdims=True)
    weight = jnp.clip((info_ref[3] * total - arc) / gap, -0.5, 1.5)
    below = lo < here.astype(jnp.float32)
    w_own = jnp.where(below, weight, 1.0 - weight)
    w_near = jnp.where(below, 1.0 - weight, weight)

    def fill(i, carry):
        done = []
        for k in (2 * i, 2 * i + 1):
            after = (k + 1) & (ny - 1)
            one = block == jnp.where(turned, after, k)
            two = block == jnp.where(turned, k, after)
            shift = (DEPTH * (k + 1)) & (LANES - 1)
            for g, (own, reg) in enumerate(((m_ref, reg_ref), (mp_ref, regp_ref))):
                for t in range(tiles):
                    rows = rows_at(ny, tiles, k, t)
                    if g == 0:
                        near = [n_ref[c, rows, :] for c in range(COMPS)]
                    else:
                        near = [
                            jnp.where(pick, np1_ref[c, rows, :], np2_ref[c, rows, :])
                            if c < ALONG_Z
                            else np3_ref[c - ALONG_Z, rows, :]
                            for c in range(COMPS)
                        ]
                    v = normal([w_own * own[c, rows, :] + w_near * near[c] for c in range(COMPS)])
                    v = list(v) + [reg[rows, :].astype(jnp.float32)]
                    done.append((k, g, t, one, two, v, [pltpu.roll(x, shift, 1) for x in v]))
        for k, g, t, one, two, v, ends in done:
            for c in range(COMPS):
                main_ref[c, g * ny + k, t] = v[c]
            for c in range(COMPS + 1):
                pltpu.store(one_ref.at[g, c, t], ends[c], mask=one)
                pltpu.store(two_ref.at[g, c, t], ends[c], mask=two)
        return carry

    lax.fori_loop(0, ny // 2, fill, 0)


def look_up(info_ref, region):
    return [jnp.take_along_axis(info_ref[i], region, axis=1) for i in range(3)]


def look_up_kernel(ny, tiles, info_ref, reg_ref, regp_ref, par_ref):
    def fill(k, carry):
        done = []
        for g, reg in enumerate((reg_ref, regp_ref)):
            for t in range(tiles):
                done.append((g * ny + k, t, look_up(info_ref, reg[rows_at(ny, tiles, k, t), :])))
        for r, t, p in done:
            for i in range(3):
                par_ref[i, r, t] = p[i]
        return carry

    lax.fori_loop(0, ny, fill, 0)


def evolve_kernel(
    ny,
    tiles,
    info_ref,
    start_ref,
    par,
    one_ref,
    two_ref,
    out_ref,
    main0,
    main1,
    strip0,
    strip1,
    edge,
    seam0,
    seam1,
    spar,
):
    main, strip, seam = (main0, main1), (strip0, strip1), (seam0, seam1)
    window = ny + 2 * DEPTH
    lane = lane_iota()
    sub = sub_iota()
    block = lane // DEPTH
    first_lane = lane == 0
    last_lane = lane == LANES - 1
    head_lane = lane % DEPTH == 0
    tail_lane = lane % DEPTH == DEPTH - 1
    top = sub == SUB - 1
    bottom = sub == 0
    turned = is_turned()

    def ends_of(k, new):
        shift = (DEPTH * (k + 1)) & (LANES - 1)
        return [pltpu.roll(new[c], shift, 1) for c in range(COMPS)]

    def seam_of(left, right):
        return jnp.where(head_lane, pltpu.roll(left, 1, 1), pltpu.roll(right, LANES - 1, 1))

    def fill_strips(t, carry):
        done = []
        for g in range(2):
            one = [one_ref[g, c, t] for c in range(COMPS + 1)]
            two = [two_ref[g, c, t] for c in range(COMPS + 1)]
            left = [jnp.where(turned, x, y) for x, y in zip(one, two)]
            right = [jnp.where(turned, y, x) for x, y in zip(one, two)]
            for side, cells in enumerate((left, right)):
                p = look_up(info_ref, cells[COMPS].astype(jnp.int32))
                done.append((side, g, cells[:COMPS], p))
        for side, g, v, p in done:
            for c in range(COMPS):
                strip0[c, side, g, t] = v[c]
            for i in range(3):
                spar[i, side, g, t] = p[i]
        for g in range(2):
            left, right = (v for _, h, v, _ in done if h == g)
            for c in range(COMPS):
                seam0[c, g, t] = seam_of(left[c], right[c])
        return carry

    lax.fori_loop(0, tiles, fill_strips, 0)

    def around_z(cells, t):
        if t + 1 < tiles:
            above = cells[t + 1]
        else:
            above = jnp.where(top, 0.0, pltpu.roll(cells[0], SUB - 1, 0))
        if t > 0:
            under = cells[t - 1]
        else:
            under = jnp.where(bottom, 0.0, pltpu.roll(cells[tiles - 1], 1, 0))
        return above + under

    def main_row(state, r):
        g = r // ny
        k = r & (ny - 1)
        after = (r + 1) & (window - 1)
        before = (r - 1) & (window - 1)
        shift = (LANES - DEPTH * (k + 1)) & (LANES - 1)
        center = [[main[state][c, r, t] for t in range(tiles)] for c in range(COMPS)]
        done = []
        for t in range(tiles):
            h = []
            for c in range(COMPS):
                cells = center[c][t]
                ends = pltpu.roll(seam[state][c, g, t], shift, 1)
                s = jnp.where(first_lane, ends, pltpu.roll(cells, 1, 1))
                s = s + jnp.where(last_lane, ends, pltpu.roll(cells, LANES - 1, 1))
                s = s + (main[state][c, after, t] + main[state][c, before, t])
                h.append(s + around_z(center[c], t))
            m = [center[c][t] for c in range(COMPS)]
            rate = turn(m, h, par[0, r, t], par[1, r, t], par[2, r, t])
            if state == 0:
                new = [m[c] + rate[c] for c in range(COMPS)]
            else:
                new = normal([main[0][c, r, t] + (m[c] + rate[c]) for c in range(COMPS)])
            done.append((r, t, new, ends_of(k, m)))
        return done

    def strip_rows(state):
        done = []
        for g in range(2):
            for side in range(2):
                start = block == side
                stop = block == (side + ny - 1) % ny
                center = [[strip[state][c, side, g, t] for t in range(tiles)] for c in range(COMPS)]
                for t in range(tiles):
                    h = []
                    for c in range(COMPS):
                        cells = center[c][t]
                        inner = edge[c, g, t]
                        other = strip[state][c, side, 1 - g, t]
                        if side == 0:
                            s = pltpu.roll(cells, 1, 1)
                            s = s + pltpu.roll(jnp.where(head_lane, inner, cells), LANES - 1, 1)
                        else:
                            s = pltpu.roll(jnp.where(tail_lane, inner, cells), 1, 1)
                            s = s + pltpu.roll(cells, LANES - 1, 1)
                        s = s + pltpu.roll(jnp.where(start, other, cells), LANES - DEPTH, 1)
                        s = s + pltpu.roll(jnp.where(stop, other, cells), DEPTH, 1)
                        h.append(s + around_z(center[c], t))
                    m = [center[c][t] for c in range(COMPS)]
                    rate = turn(
                        m, h, spar[0, side, g, t], spar[1, side, g, t], spar[2, side, g, t]
                    )
                    if state == 0:
                        new = [m[c] + rate[c] for c in range(COMPS)]
                    else:
                        new = normal(
                            [strip[0][c, side, g, t] + (m[c] + rate[c]) for c in range(COMPS)]
                        )
                    done.append((side, g, t, new))
        for side, g, t, new in done:
            for c in range(COMPS):
                strip[1 - state][c, side, g, t] = new[c]
        for g in range(2):
            for t in range(tiles):
                left, right = (new for _, h, u, new in done if (h, u) == (g, t))
                for c in range(COMPS):
                    seam[1 - state][c, g, t] = seam_of(left[c], right[c])

    def main_rows(state, first, count):
        def rows(i, carry):
            done = []
            for u in range(ROWS):
                done += main_row(state, (first + ROWS * i + u) & (window - 1))
            for r, t, new, ends in done:
                k = r & (ny - 1)
                mask = ((lane - (DEPTH * k + DEPTH - 1)) & (LANES - 1)) < 2
                for c in range(COMPS):
                    main[1 - state][c, r, t] = new[c]
                    pltpu.store(edge.at[c, r // ny, t], ends[c], mask=mask)
            return carry

        lax.fori_loop(0, count // ROWS, rows, 0)

    def step(i, carry):
        for state in range(2):
            margin = DEPTH - 2 * state - 2 * i
            main_rows(state, -margin, ny + 2 * margin)
            strip_rows(state)
        return carry

    lax.fori_loop(0, STEPS, step, 0)

    def hand_out(k, carry):
        for t in range(tiles):
            for c in range(COMPS):
                out_ref[c, rows_at(ny, tiles, k, t), :] = main[0][c, k, t]
        return carry

    lax.fori_loop(0, ny, hand_out, 0)


def shifted(cells, axis, step, closed):
    count = lax.axis_size(axis)
    pairs = [(i, (i + step) % count) for i in range(count) if closed or 0 <= i + step < count]
    return lax.ppermute(cells, axis, pairs)


def swapped(cells, axis, first, closed):
    count = lax.axis_size(axis)
    pairs = [(i, (i + 1) % count) for i in range(first, count if closed else count - 1, 2)]
    return lax.ppermute(cells, axis, pairs + [(j, i) for i, j in pairs])


def around(cells, dim):
    ny = cells.shape[dim]
    if lax.axis_size("gy") == 2:
        return shifted(cells, "gy", 1, True)
    head = lax.slice_in_dim(cells, 0, DEPTH, axis=dim)
    tail = lax.slice_in_dim(cells, ny - DEPTH, ny, axis=dim)
    return jnp.concatenate([shifted(head, "gy", -1, True), shifted(tail, "gy", 1, True)], axis=dim)


def body(magnetization, lower_image, image_weights, regions, anisotropy, damping):
    local, comps, nz, ny, nx = magnetization.shape
    images = local * lax.axis_size("img")
    tiles = nz // SUB
    devices = lax.axis_size(("img", "gx", "gy"))
    assert lax.axis_size("gx") % 2 == 0
    assert local == 1 and comps == COMPS and nx == LANES
    assert ny == 2 * DEPTH and ny * DEPTH == LANES and tiles >= 2
    flat = (comps, nz * ny, nx)
    own = magnetization[0]
    own_p = around(own, 2)
    first = swapped(own, "img", 0, False)
    second = swapped(own, "img", 1, False)

    smem = pl.BlockSpec(memory_space=pltpu.SMEM)
    vmem = pl.BlockSpec(memory_space=pltpu.VMEM)
    f32 = jnp.float32
    limit = pltpu.CompilerParams(vmem_limit_bytes=32 * 1024 * 1024)
    vreg = (SUB, LANES)
    info = pl.pallas_call(
        functools.partial(info_kernel, anisotropy.shape[0]),
        out_shape=jax.ShapeDtypeStruct((5,) + vreg, f32),
        in_specs=[smem] * 3 + [vmem] * 3,
        out_specs=vmem,
        compiler_params=limit,
        name="small_arguments",
    )(
        lower_image,
        anisotropy,
        damping,
        image_weights.reshape(1, -1),
        own.reshape(flat),
        regions.reshape(flat[1:]),
    )
    own_p, info = lax.optimization_barrier((own_p, info))
    first_p = swapped(own_p[:ALONG_Z], "img", 0, False)
    second_p = swapped(own_p[:ALONG_Z], "img", 1, False)
    late_regions, info = lax.optimization_barrier((regions, info))
    reg_p = around(late_regions, 1)
    part, near, sent = pl.pallas_call(
        gather_kernel,
        out_shape=(
            jax.ShapeDtypeStruct((devices, LANES), f32),
            jax.ShapeDtypeStruct(flat, f32),
            jax.ShapeDtypeStruct((comps - ALONG_Z,) + flat[1:], f32),
        ),
        in_specs=[vmem] * 4,
        out_specs=(vmem,) * 3,
        compiler_params=limit,
        name="gather_images",
    )(info, own.reshape(flat), first.reshape(flat), second.reshape(flat))
    sent_p = around(sent.reshape((comps - ALONG_Z,) + own.shape[1:]), 2)
    squares = lax.all_to_all(part, ("img", "gx", "gy"), 0, 0, tiled=True)

    window = ny + 2 * DEPTH
    tile_rows = (regions.reshape(flat[1:]), reg_p.reshape(flat[1:]))
    packed = jax.ShapeDtypeStruct((2, comps + 1, tiles) + vreg, f32)
    start, one, two = pl.pallas_call(
        functools.partial(start_kernel, ny, tiles, images),
        out_shape=(jax.ShapeDtypeStruct((comps, window, tiles) + vreg, f32), packed, packed),
        in_specs=[vmem] * 10,
        out_specs=(vmem,) * 3,
        compiler_params=limit,
        name="start",
    )(
        info,
        squares,
        own.reshape(flat),
        own_p.reshape(flat),
        near,
        first_p.reshape((ALONG_Z,) + flat[1:]),
        second_p.reshape((ALONG_Z,) + flat[1:]),
        sent_p.reshape((comps - ALONG_Z,) + flat[1:]),
        *tile_rows,
    )
    one = swapped(one, "gx", 0, True)
    two = swapped(two, "gx", 1, True)
    par = pl.pallas_call(
        functools.partial(look_up_kernel, ny, tiles),
        out_shape=jax.ShapeDtypeStruct((3, window, tiles) + vreg, f32),
        in_specs=[vmem] * 3,
        out_specs=vmem,
        compiler_params=limit,
        name="parameters",
    )(info, *tile_rows)
    out, _ = pl.pallas_call(
        functools.partial(evolve_kernel, ny, tiles),
        out_shape=(jax.ShapeDtypeStruct(flat, f32), jax.ShapeDtypeStruct(start.shape, f32)),
        in_specs=[vmem] * 5,
        out_specs=(vmem,) * 2,
        input_output_aliases={1: 1},
        scratch_shapes=[
            pltpu.VMEM((comps, window, tiles) + vreg, f32),
            pltpu.VMEM((comps, 2, 2, tiles) + vreg, f32),
            pltpu.VMEM((comps, 2, 2, tiles) + vreg, f32),
            pltpu.VMEM((comps, 2, tiles) + vreg, f32),
            pltpu.VMEM((comps, 2, tiles) + vreg, f32),
            pltpu.VMEM((comps, 2, tiles) + vreg, f32),
            pltpu.VMEM((3, 2, 2, tiles) + vreg, f32),
        ],
        compiler_params=limit,
        name="evolve",
    )(info, start, par, one, two)
    return out.reshape(magnetization.shape)


def solution(mesh):
    placed = (P("img", None, None, "gy", "gx"), P(), P(), P(None, "gy", "gx"), P(), P())
    return jax.shard_map(
        body,
        mesh=mesh,
        in_specs=placed,
        out_specs=P("img", None, None, "gy", "gx"),
        check_vma=False,
    )
```

```python
import functools

import jax
import jax.numpy as jnp
from jax import lax
from jax.experimental import pallas as pl
from jax.experimental.pallas import tpu as pltpu
from jax.sharding import PartitionSpec as P

STEPS = 4
DEPTH = 2 * STEPS

eps = 1e-06
time_step = 0.05

SUB = 8
LANES = 128
COMPS = 3
ROWS = 4


def lane_iota():
    return lax.broadcasted_iota(jnp.int32, (SUB, LANES), 1)


def sub_iota():
    return lax.broadcasted_iota(jnp.int32, (SUB, LANES), 0)


def rows_at(ny, tiles, y, t):
    return pl.ds(y + ny * t, SUB, stride=ny * tiles)


def pack_kernel(
    ny, tiles, regions, lower_ref, aniso_ref, damp_ref, share_ref, m_ref, reg_ref, left_ref, right_ref, info_ref
):
    here = lax.axis_index("img")
    lane = lane_iota()
    block = lane // DEPTH
    def pack(i, carry):
        done = []
        for u in range(2):
            y = 2 * i + u
            shift = (DEPTH * (y + 1)) & (LANES - 1)
            left = block == ((y + 1) & (ny - 1))
            right = block == y
            for t in range(tiles):
                rows = rows_at(ny, tiles, y, t)
                for c in range(COMPS + 1):
                    cells = m_ref[c, rows, :] if c < COMPS else reg_ref[rows, :].astype(jnp.float32)
                    done.append((c, t, left, right, pltpu.roll(cells, shift, 1)))
        for c, t, left, right, cells in done:
            pltpu.store(left_ref.at[c, t], cells, mask=left)
            pltpu.store(right_ref.at[c, t], cells, mask=right)
        return carry

    table_a = jnp.zeros((SUB, LANES), jnp.float32)
    table_d = jnp.zeros((SUB, LANES), jnp.float32)
    for i in range(regions):
        table_a = jnp.where(lane == i, 2.0 * aniso_ref[i], table_a)
        table_d = jnp.where(lane == i, damp_ref[i], table_d)
    info_ref[0] = table_a
    info_ref[1] = table_d
    info_ref[2] = -time_step / (1.0 + table_d * table_d)
    share = share_ref[...]
    spot = lax.broadcasted_iota(jnp.int32, share.shape, 1)
    target = jnp.sum(jnp.where(spot < here, share, 0.0), axis=1, keepdims=True) / jnp.sum(
        share, axis=1, keepdims=True
    )
    info_ref[3] = jnp.broadcast_to(target, (SUB, LANES))
    info_ref[4] = jnp.full((SUB, LANES), lower_ref[here].astype(jnp.float32))

    lax.fori_loop(0, ny // 2, pack, 0)


def merge_kernel(one_ref, two_ref, out_ref):
    turned = (lax.axis_index("gx") & 1) == 1
    one, two = one_ref[...], two_ref[...]
    out_ref[0] = jnp.where(turned, one, two)
    out_ref[1] = jnp.where(turned, two, one)


def take_first(info_ref, here):
    odd = (here & 1) == 1
    below = info_ref[4] < here.astype(jnp.float32)
    return jnp.where(below, jnp.where(odd, 1, 0), jnp.where(odd, 0, 1)) == 1, odd


def gather_kernel(
    ny, tiles, info_ref, m_ref, first_ref, second_ref, own_left_ref, own_right_ref, part_ref, near_ref, one_ref, two_ref
):
    here = lax.axis_index("img")
    pick, odd = take_first(info_ref, here)
    chunks = 4
    depth = m_ref.shape[1]

    def squares(i, sums):
        sums = list(sums)
        done = []
        for u in range(chunks):
            start = pl.multiple_of((chunks * i + u) * SUB, SUB)
            for c in range(COMPS):
                one = first_ref[c, pl.ds(start, SUB), :]
                two = second_ref[c, pl.ds(start, SUB), :]
                done.append((c, start, jnp.where(pick, one, two)))
                diff = m_ref[c, pl.ds(start, SUB), :] - jnp.where(odd, one, two)
                sums[c + COMPS * u] = sums[c + COMPS * u] + diff * diff
        for c, start, cells in done:
            near_ref[c, pl.ds(start, SUB), :] = cells
        return tuple(sums)

    zero = jnp.zeros((SUB, LANES), jnp.float32)
    sums = lax.fori_loop(0, depth // (chunks * SUB), squares, (zero,) * (chunks * COMPS))
    total = jnp.sum(functools.reduce(jnp.add, sums), axis=(0, 1), keepdims=True)
    slot = lax.broadcasted_iota(jnp.int32, part_ref.shape, 1)
    part_ref[...] = jnp.where((slot == here) & (here > 0), total, 0.0)
    turned = (lax.axis_index("gx") & 1) == 1
    one_ref[COMPS:] = jnp.where(turned, own_left_ref[...], own_right_ref[...])
    two_ref[COMPS:] = jnp.where(turned, own_right_ref[...], own_left_ref[...])
    block = lane_iota() // DEPTH

    def pack(i, carry):
        done = []
        for u in range(2):
            y = 2 * i + u
            after = (y + 1) & (ny - 1)
            one = block == jnp.where(turned, after, y)
            two = block == jnp.where(turned, y, after)
            shift = (DEPTH * (y + 1)) & (LANES - 1)
            for t in range(tiles):
                for c in range(COMPS):
                    cells = pltpu.roll(near_ref[c, rows_at(ny, tiles, y, t), :], shift, 1)
                    done.append((c, t, one, two, cells))
        for c, t, one, two, cells in done:
            pltpu.store(one_ref.at[c, t], cells, mask=one)
            pltpu.store(two_ref.at[c, t], cells, mask=two)
        return carry

    lax.fori_loop(0, ny // 2, pack, 0)


def turn(m, h, a2, b, sc):
    mx, my, mz = m
    hx, hy, hz = h
    hz = hz + a2 * mz
    gx = hx + b * (my * hz - mz * hy)
    gy = hy + b * (mz * hx - mx * hz)
    gz = hz + b * (mx * hy - my * hx)
    return (
        sc * (my * gz - mz * gy),
        sc * (mz * gx - mx * gz),
        sc * (mx * gy - my * gx),
    )


def normal(v):
    scale = lax.rsqrt(v[0] * v[0] + v[1] * v[1] + v[2] * v[2])
    return tuple(x * scale for x in v)


def look_up(info_ref, region):
    return [jnp.take_along_axis(info_ref[i], region, axis=1) for i in range(3)]


def look_up_kernel(ny, tiles, info_ref, reg_ref, regp_ref, par_ref):
    def fill(i, carry):
        done = []
        for k in (2 * i, 2 * i + 1):
            for g, reg in enumerate((reg_ref, regp_ref)):
                for t in range(tiles):
                    done.append((g * ny + k, t, look_up(info_ref, reg[rows_at(ny, tiles, k, t), :])))
        for r, t, p in done:
            for i in range(3):
                par_ref[i, r, t] = p[i]
        return carry

    lax.fori_loop(0, ny // 2, fill, 0)


def evolve_kernel(
    ny,
    tiles,
    images,
    info_ref,
    sq_ref,
    m_ref,
    mp_ref,
    n_ref,
    np_ref,
    par,
    strips_ref,
    stripsp_ref,
    out_ref,
    main0,
    main1,
    strip0,
    strip1,
    edge,
    seam0,
    seam1,
    spar,
):
    main, strip, seam = (main0, main1), (strip0, strip1), (seam0, seam1)
    window = ny + 2 * DEPTH
    here = lax.axis_index("img")
    lane = lane_iota()
    sub = sub_iota()
    block = lane // DEPTH
    first_lane = lane == 0
    last_lane = lane == LANES - 1
    head_lane = lane % DEPTH == 0
    tail_lane = lane % DEPTH == DEPTH - 1
    top = sub == SUB - 1
    bottom = sub == 0

    lo = info_ref[4]
    slot = lane.astype(jnp.float32)
    squares = jnp.broadcast_to(jnp.sum(sq_ref[...], axis=0, keepdims=True), (SUB, LANES))
    lengths = jnp.where((lane >= 1) & (lane < images), jnp.sqrt(squares + eps), 0.0)
    total = jnp.sum(lengths, axis=1, keepdims=True)
    arc = jnp.sum(jnp.where(slot <= lo, lengths, 0.0), axis=1, keepdims=True)
    gap = jnp.sum(jnp.where(slot == lo + 1.0, lengths, 0.0), axis=1, keepdims=True)
    weight = jnp.clip((info_ref[3] * total - arc) / gap, -0.5, 1.5)
    below = lo < here.astype(jnp.float32)
    w_own = jnp.where(below, weight, 1.0 - weight)
    w_near = jnp.where(below, 1.0 - weight, weight)

    def ends_of(k, new):
        shift = (DEPTH * (k + 1)) & (LANES - 1)
        return [pltpu.roll(new[c], shift, 1) for c in range(COMPS)]

    def fill(i, carry):
        done = []
        for k in (2 * i, 2 * i + 1):
            for g, (own, near) in enumerate(((m_ref, n_ref), (mp_ref, np_ref))):
                for t in range(tiles):
                    rows = rows_at(ny, tiles, k, t)
                    v = normal(
                        [w_own * own[c, rows, :] + w_near * near[c, rows, :] for c in range(COMPS)]
                    )
                    done.append((g * ny + k, t, v))
        for r, t, v in done:
            for c in range(COMPS):
                main0[c, r, t] = v[c]
        return carry

    lax.fori_loop(0, ny // 2, fill, 0)

    def seam_of(left, right):
        return jnp.where(head_lane, pltpu.roll(left, 1, 1), pltpu.roll(right, LANES - 1, 1))

    def fill_strips(t, carry):
        done = []
        for g, cells in enumerate((strips_ref, stripsp_ref)):
            for side in range(2):
                v = normal(
                    [w_own * cells[side, COMPS + c, t] + w_near * cells[side, c, t] for c in range(COMPS)]
                )
                done.append((side, g, v, look_up(info_ref, cells[side, 2 * COMPS, t].astype(jnp.int32))))
        for side, g, v, p in done:
            for c in range(COMPS):
                strip0[c, side, g, t] = v[c]
            for i in range(3):
                spar[i, side, g, t] = p[i]
        for g in range(2):
            left, right = (v for _, h, v, _ in done if h == g)
            for c in range(COMPS):
                seam0[c, g, t] = seam_of(left[c], right[c])
        return carry

    lax.fori_loop(0, tiles, fill_strips, 0)

    def around_z(cells, t):
        if t + 1 < tiles:
            above = cells[t + 1]
        else:
            above = jnp.where(top, 0.0, pltpu.roll(cells[0], SUB - 1, 0))
        if t > 0:
            under = cells[t - 1]
        else:
            under = jnp.where(bottom, 0.0, pltpu.roll(cells[tiles - 1], 1, 0))
        return above + under

    def main_row(state, r):
        g = r // ny
        k = r & (ny - 1)
        after = (r + 1) & (window - 1)
        before = (r - 1) & (window - 1)
        shift = (LANES - DEPTH * (k + 1)) & (LANES - 1)
        center = [[main[state][c, r, t] for t in range(tiles)] for c in range(COMPS)]
        done = []
        for t in range(tiles):
            h = []
            for c in range(COMPS):
                cells = center[c][t]
                ends = pltpu.roll(seam[state][c, g, t], shift, 1)
                s = jnp.where(first_lane, ends, pltpu.roll(cells, 1, 1))
                s = s + jnp.where(last_lane, ends, pltpu.roll(cells, LANES - 1, 1))
                s = s + (main[state][c, after, t] + main[state][c, before, t])
                h.append(s + around_z(center[c], t))
            m = [center[c][t] for c in range(COMPS)]
            rate = turn(m, h, par[0, r, t], par[1, r, t], par[2, r, t])
            if state == 0:
                new = [m[c] + rate[c] for c in range(COMPS)]
            else:
                new = normal([main[0][c, r, t] + (m[c] + rate[c]) for c in range(COMPS)])
            done.append((r, t, new, ends_of(k, m)))
        return done

    def strip_rows(state):
        done = []
        for g in range(2):
            for side in range(2):
                start = block == side
                stop = block == (side + ny - 1) % ny
                center = [[strip[state][c, side, g, t] for t in range(tiles)] for c in range(COMPS)]
                for t in range(tiles):
                    h = []
                    for c in range(COMPS):
                        cells = center[c][t]
                        inner = edge[c, g, t]
                        other = strip[state][c, side, 1 - g, t]
                        if side == 0:
                            s = pltpu.roll(cells, 1, 1)
                            s = s + pltpu.roll(jnp.where(head_lane, inner, cells), LANES - 1, 1)
                        else:
                            s = pltpu.roll(jnp.where(tail_lane, inner, cells), 1, 1)
                            s = s + pltpu.roll(cells, LANES - 1, 1)
                        s = s + pltpu.roll(jnp.where(start, other, cells), LANES - DEPTH, 1)
                        s = s + pltpu.roll(jnp.where(stop, other, cells), DEPTH, 1)
                        h.append(s + around_z(center[c], t))
                    m = [center[c][t] for c in range(COMPS)]
                    rate = turn(
                        m, h, spar[0, side, g, t], spar[1, side, g, t], spar[2, side, g, t]
                    )
                    if state == 0:
                        new = [m[c] + rate[c] for c in range(COMPS)]
                    else:
                        new = normal(
                            [strip[0][c, side, g, t] + (m[c] + rate[c]) for c in range(COMPS)]
                        )
                    done.append((side, g, t, new))
        for side, g, t, new in done:
            for c in range(COMPS):
                strip[1 - state][c, side, g, t] = new[c]
        for g in range(2):
            for t in range(tiles):
                left, right = (new for _, h, u, new in done if (h, u) == (g, t))
                for c in range(COMPS):
                    seam[1 - state][c, g, t] = seam_of(left[c], right[c])

    def main_rows(state, first, count):
        def rows(i, carry):
            done = []
            for u in range(ROWS):
                done += main_row(state, (first + ROWS * i + u) & (window - 1))
            for r, t, new, ends in done:
                k = r & (ny - 1)
                mask = ((lane - (DEPTH * k + DEPTH - 1)) & (LANES - 1)) < 2
                for c in range(COMPS):
                    main[1 - state][c, r, t] = new[c]
                    pltpu.store(edge.at[c, r // ny, t], ends[c], mask=mask)
            return carry

        lax.fori_loop(0, count // ROWS, rows, 0)

    def step(i, carry):
        for state in range(2):
            margin = DEPTH - 2 * state - 2 * i
            main_rows(state, -margin, ny + 2 * margin)
            strip_rows(state)
        return carry

    lax.fori_loop(0, STEPS, step, 0)

    def hand_out(i, carry):
        for k in (2 * i, 2 * i + 1):
            for t in range(tiles):
                for c in range(COMPS):
                    out_ref[c, rows_at(ny, tiles, k, t), :] = main0[c, k, t]
        return carry

    lax.fori_loop(0, ny // 2, hand_out, 0)


def shifted(cells, axis, step, closed):
    count = lax.axis_size(axis)
    pairs = [(i, (i + step) % count) for i in range(count) if closed or 0 <= i + step < count]
    return lax.ppermute(cells, axis, pairs)


def swapped(cells, axis, first, closed):
    count = lax.axis_size(axis)
    pairs = [(i, (i + 1) % count) for i in range(first, count if closed else count - 1, 2)]
    return lax.ppermute(cells, axis, pairs + [(j, i) for i, j in pairs])


def around(cells, dim):
    ny = cells.shape[dim]
    if lax.axis_size("gy") == 2:
        return shifted(cells, "gy", 1, True)
    head = lax.slice_in_dim(cells, 0, DEPTH, axis=dim)
    tail = lax.slice_in_dim(cells, ny - DEPTH, ny, axis=dim)
    return jnp.concatenate([shifted(head, "gy", -1, True), shifted(tail, "gy", 1, True)], axis=dim)


def around_strips(both):
    if lax.axis_size("gy") == 2:
        return shifted(both, "gy", 1, True)
    block = lax.broadcasted_iota(jnp.int32, both.shape, both.ndim - 1) // DEPTH
    side = lax.broadcasted_iota(jnp.int32, both.shape, 0)
    head = (block + side - 1) % (LANES // DEPTH) < DEPTH
    return jnp.where(head, shifted(both, "gy", -1, True), shifted(both, "gy", 1, True))


def body(magnetization, lower_image, image_weights, regions, anisotropy, damping):
    local, comps, nz, ny, nx = magnetization.shape
    images = local * lax.axis_size("img")
    tiles = nz // SUB
    devices = lax.axis_size(("img", "gx", "gy"))
    assert lax.axis_size("gx") % 2 == 0
    assert local == 1 and comps == COMPS and nx == LANES
    assert ny == 2 * DEPTH and ny * DEPTH == LANES and tiles >= 2
    flat = (comps, nz * ny, nx)
    own = magnetization[0]
    own_p = around(own, 2)
    first = swapped(own, "img", 0, False)
    second = swapped(own, "img", 1, False)

    smem = pl.BlockSpec(memory_space=pltpu.SMEM)
    vmem = pl.BlockSpec(memory_space=pltpu.VMEM)
    f32 = jnp.float32
    limit = pltpu.CompilerParams(vmem_limit_bytes=32 * 1024 * 1024)
    vreg = (SUB, LANES)
    packed = jax.ShapeDtypeStruct((comps + 1, tiles) + vreg, f32)
    left, right, info = pl.pallas_call(
        functools.partial(pack_kernel, ny, tiles, anisotropy.shape[0]),
        out_shape=(packed, packed, jax.ShapeDtypeStruct((5,) + vreg, f32)),
        in_specs=[smem] * 3 + [vmem] * 3,
        out_specs=(vmem,) * 3,
        compiler_params=limit,
        name="pack_strips",
    )(
        lower_image,
        anisotropy,
        damping,
        image_weights.reshape(1, -1),
        own.reshape(flat),
        regions.reshape(flat[1:]),
    )
    late_regions, info = lax.optimization_barrier((regions, info))
    reg_p = around(late_regions, 1)
    info, own_p, reg_p = lax.optimization_barrier((info, own_p, reg_p))
    packed = jax.ShapeDtypeStruct((2 * comps + 1, tiles) + vreg, f32)
    part, near, one, two = pl.pallas_call(
        functools.partial(gather_kernel, ny, tiles),
        out_shape=(
            jax.ShapeDtypeStruct((devices, LANES), f32),
            jax.ShapeDtypeStruct(flat, f32),
            packed,
            packed,
        ),
        in_specs=[vmem] * 6,
        out_specs=(vmem,) * 4,
        compiler_params=limit,
        name="gather_images",
    )(info, own.reshape(flat), first.reshape(flat), second.reshape(flat), left, right)
    near_p = around(near.reshape(own.shape), 2)
    one = swapped(one, "gx", 0, True)
    two = swapped(two, "gx", 1, True)
    window = ny + 2 * DEPTH
    par = pl.pallas_call(
        functools.partial(look_up_kernel, ny, tiles),
        out_shape=jax.ShapeDtypeStruct((3, window, tiles) + vreg, f32),
        in_specs=[vmem] * 3,
        out_specs=vmem,
        compiler_params=limit,
        name="parameters",
    )(info, regions.reshape(flat[1:]), reg_p.reshape(flat[1:]))
    one, par = lax.optimization_barrier((one, par))
    strips = pl.pallas_call(
        merge_kernel,
        out_shape=jax.ShapeDtypeStruct((2,) + packed.shape, f32),
        in_specs=[vmem] * 2,
        out_specs=vmem,
        compiler_params=limit,
        name="merge_strips",
    )(one, two)
    strips_p = around_strips(strips)
    squares = lax.all_to_all(part, ("img", "gx", "gy"), 0, 0, tiled=True)

    out = pl.pallas_call(
        functools.partial(evolve_kernel, ny, tiles, images),
        out_shape=jax.ShapeDtypeStruct(flat, f32),
        in_specs=[vmem] * 9,
        out_specs=vmem,
        scratch_shapes=[
            pltpu.VMEM((comps, window, tiles) + vreg, f32),
            pltpu.VMEM((comps, window, tiles) + vreg, f32),
            pltpu.VMEM((comps, 2, 2, tiles) + vreg, f32),
            pltpu.VMEM((comps, 2, 2, tiles) + vreg, f32),
            pltpu.VMEM((comps, 2, tiles) + vreg, f32),
            pltpu.VMEM((comps, 2, tiles) + vreg, f32),
            pltpu.VMEM((comps, 2, tiles) + vreg, f32),
            pltpu.VMEM((3, 2, 2, tiles) + vreg, f32),
        ],
        compiler_params=limit,
        name="evolve",
    )(
        info,
        squares,
        own.reshape(flat),
        own_p.reshape(flat),
        near,
        near_p.reshape(flat),
        par,
        strips,
        strips_p,
    )
    return out.reshape(magnetization.shape)


def solution(mesh):
    placed = (P("img", None, None, "gy", "gx"), P(), P(), P(None, "gy", "gx"), P(), P())
    return jax.shard_map(
        body,
        mesh=mesh,
        in_specs=placed,
        out_specs=P("img", None, None, "gy", "gx"),
        check_vma=False,
    )
```

```python
import functools

import jax
import jax.numpy as jnp
from jax import lax
from jax.experimental import pallas as pl
from jax.experimental.pallas import tpu as pltpu
from jax.sharding import PartitionSpec as P

STEPS = 4
DEPTH = 2 * STEPS

eps = 1e-06
time_step = 0.05

SUB = 8
LANES = 128
COMPS = 3
ROWS = 4


def lane_iota():
    return lax.broadcasted_iota(jnp.int32, (SUB, LANES), 1)


def sub_iota():
    return lax.broadcasted_iota(jnp.int32, (SUB, LANES), 0)


def rows_at(ny, tiles, y, t):
    return pl.ds(y + ny * t, SUB, stride=ny * tiles)


def is_turned():
    return (lax.axis_index("gx") & 1) == 1


def rims(ny, y):
    block = lane_iota() // DEPTH
    turned = is_turned()
    after = (y + 1) & (ny - 1)
    return block == jnp.where(turned, after, y), block == jnp.where(turned, y, after), (DEPTH * (y + 1)) & (LANES - 1)


def pack_kernel(
    ny, tiles, regions, lower_ref, aniso_ref, damp_ref, share_ref, m_ref, reg_ref, one_ref, two_ref, info_ref
):
    here = lax.axis_index("img")
    lane = lane_iota()
    def pack(i, carry):
        done = []
        for u in range(2):
            y = 2 * i + u
            one, two, shift = rims(ny, y)
            for t in range(tiles):
                rows = rows_at(ny, tiles, y, t)
                for c in range(COMPS + 1):
                    cells = m_ref[c, rows, :] if c < COMPS else reg_ref[rows, :].astype(jnp.float32)
                    done.append((c, t, one, two, pltpu.roll(cells, shift, 1)))
        for c, t, one, two, cells in done:
            pltpu.store(one_ref.at[c, t], cells, mask=one)
            pltpu.store(two_ref.at[c, t], cells, mask=two)
        return carry

    table_a = jnp.zeros((SUB, LANES), jnp.float32)
    table_d = jnp.zeros((SUB, LANES), jnp.float32)
    for i in range(regions):
        table_a = jnp.where(lane == i, 2.0 * aniso_ref[i], table_a)
        table_d = jnp.where(lane == i, damp_ref[i], table_d)
    info_ref[0] = table_a
    info_ref[1] = table_d
    info_ref[2] = -time_step / (1.0 + table_d * table_d)
    share = share_ref[...]
    spot = lax.broadcasted_iota(jnp.int32, share.shape, 1)
    target = jnp.sum(jnp.where(spot < here, share, 0.0), axis=1, keepdims=True) / jnp.sum(
        share, axis=1, keepdims=True
    )
    info_ref[3] = jnp.broadcast_to(target, (SUB, LANES))
    info_ref[4] = jnp.full((SUB, LANES), lower_ref[here].astype(jnp.float32))

    lax.fori_loop(0, ny // 2, pack, 0)


def merge_kernel(one_ref, two_ref, own_one_ref, own_two_ref, out_ref):
    turned = is_turned()
    for first, (one_ref, two_ref) in ((0, (one_ref, two_ref)), (COMPS, (own_one_ref, own_two_ref))):
        one, two = one_ref[...], two_ref[...]
        out_ref[0, first : first + one.shape[0]] = jnp.where(turned, one, two)
        out_ref[1, first : first + one.shape[0]] = jnp.where(turned, two, one)


def take_first(info_ref, here):
    odd = (here & 1) == 1
    below = info_ref[4] < here.astype(jnp.float32)
    return jnp.where(below, jnp.where(odd, 1, 0), jnp.where(odd, 0, 1)) == 1, odd


def gather_kernel(
    ny, tiles, info_ref, m_ref, first_ref, second_ref, part_ref, near_ref, one_ref, two_ref
):
    here = lax.axis_index("img")
    pick, odd = take_first(info_ref, here)
    chunks = 4
    depth = m_ref.shape[1]

    def squares(i, sums):
        sums = list(sums)
        done = []
        for u in range(chunks):
            start = pl.multiple_of((chunks * i + u) * SUB, SUB)
            for c in range(COMPS):
                one = first_ref[c, pl.ds(start, SUB), :]
                two = second_ref[c, pl.ds(start, SUB), :]
                done.append((c, start, jnp.where(pick, one, two)))
                diff = m_ref[c, pl.ds(start, SUB), :] - jnp.where(odd, one, two)
                sums[c + COMPS * u] = sums[c + COMPS * u] + diff * diff
        for c, start, cells in done:
            near_ref[c, pl.ds(start, SUB), :] = cells
        return tuple(sums)

    zero = jnp.zeros((SUB, LANES), jnp.float32)
    sums = lax.fori_loop(0, depth // (chunks * SUB), squares, (zero,) * (chunks * COMPS))
    total = jnp.sum(functools.reduce(jnp.add, sums), axis=(0, 1), keepdims=True)
    slot = lax.broadcasted_iota(jnp.int32, part_ref.shape, 1)
    part_ref[...] = jnp.where((slot == here) & (here > 0), total, 0.0)
    def pack(i, carry):
        done = []
        for u in range(2):
            y = 2 * i + u
            one, two, shift = rims(ny, y)
            for t in range(tiles):
                for c in range(COMPS):
                    cells = pltpu.roll(near_ref[c, rows_at(ny, tiles, y, t), :], shift, 1)
                    done.append((c, t, one, two, cells))
        for c, t, one, two, cells in done:
            pltpu.store(one_ref.at[c, t], cells, mask=one)
            pltpu.store(two_ref.at[c, t], cells, mask=two)
        return carry

    lax.fori_loop(0, ny // 2, pack, 0)


def turn(m, h, a2, b, sc):
    mx, my, mz = m
    hx, hy, hz = h
    hz = hz + a2 * mz
    gx = hx + b * (my * hz - mz * hy)
    gy = hy + b * (mz * hx - mx * hz)
    gz = hz + b * (mx * hy - my * hx)
    return (
        sc * (my * gz - mz * gy),
        sc * (mz * gx - mx * gz),
        sc * (mx * gy - my * gx),
    )


def normal(v):
    scale = lax.rsqrt(v[0] * v[0] + v[1] * v[1] + v[2] * v[2])
    return tuple(x * scale for x in v)


def look_up(info_ref, region):
    return [jnp.take_along_axis(info_ref[i], region, axis=1) for i in range(3)]


def look_up_kernel(ny, tiles, info_ref, reg_ref, regp_ref, par_ref):
    def fill(i, carry):
        done = []
        for k in (2 * i, 2 * i + 1):
            for g, reg in enumerate((reg_ref, regp_ref)):
                for t in range(tiles):
                    done.append((g * ny + k, t, look_up(info_ref, reg[rows_at(ny, tiles, k, t), :])))
        for r, t, p in done:
            for i in range(3):
                par_ref[i, r, t] = p[i]
        return carry

    lax.fori_loop(0, ny // 2, fill, 0)


def evolve_kernel(
    ny,
    tiles,
    images,
    info_ref,
    sq_ref,
    m_ref,
    mp_ref,
    n_ref,
    np_ref,
    par,
    strips_ref,
    stripsp_ref,
    out_ref,
    main0,
    main1,
    strip0,
    strip1,
    edge,
    seam0,
    seam1,
    spar,
):
    main, strip, seam = (main0, main1), (strip0, strip1), (seam0, seam1)
    window = ny + 2 * DEPTH
    here = lax.axis_index("img")
    lane = lane_iota()
    sub = sub_iota()
    block = lane // DEPTH
    first_lane = lane == 0
    last_lane = lane == LANES - 1
    head_lane = lane % DEPTH == 0
    tail_lane = lane % DEPTH == DEPTH - 1
    top = sub == SUB - 1
    bottom = sub == 0

    lo = info_ref[4]
    slot = lane.astype(jnp.float32)
    squares = jnp.broadcast_to(jnp.sum(sq_ref[...], axis=0, keepdims=True), (SUB, LANES))
    lengths = jnp.where((lane >= 1) & (lane < images), jnp.sqrt(squares + eps), 0.0)
    total = jnp.sum(lengths, axis=1, keepdims=True)
    arc = jnp.sum(jnp.where(slot <= lo, lengths, 0.0), axis=1, keepdims=True)
    gap = jnp.sum(jnp.where(slot == lo + 1.0, lengths, 0.0), axis=1, keepdims=True)
    weight = jnp.clip((info_ref[3] * total - arc) / gap, -0.5, 1.5)
    below = lo < here.astype(jnp.float32)
    w_own = jnp.where(below, weight, 1.0 - weight)
    w_near = jnp.where(below, 1.0 - weight, weight)

    def ends_of(k, new):
        shift = (DEPTH * (k + 1)) & (LANES - 1)
        return [pltpu.roll(new[c], shift, 1) for c in range(COMPS)]

    def fill(i, carry):
        done = []
        for k in (2 * i, 2 * i + 1):
            for g, (own, near) in enumerate(((m_ref, n_ref), (mp_ref, np_ref))):
                for t in range(tiles):
                    rows = rows_at(ny, tiles, k, t)
                    v = normal(
                        [w_own * own[c, rows, :] + w_near * near[c, rows, :] for c in range(COMPS)]
                    )
                    done.append((g * ny + k, t, v))
        for r, t, v in done:
            for c in range(COMPS):
                main0[c, r, t] = v[c]
        return carry

    lax.fori_loop(0, ny // 2, fill, 0)

    def seam_of(left, right):
        return jnp.where(head_lane, pltpu.roll(left, 1, 1), pltpu.roll(right, LANES - 1, 1))

    def fill_strips(t, carry):
        done = []
        for g, cells in enumerate((strips_ref, stripsp_ref)):
            for side in range(2):
                v = normal(
                    [w_own * cells[side, COMPS + c, t] + w_near * cells[side, c, t] for c in range(COMPS)]
                )
                done.append((side, g, v, look_up(info_ref, cells[side, 2 * COMPS, t].astype(jnp.int32))))
        for side, g, v, p in done:
            for c in range(COMPS):
                strip0[c, side, g, t] = v[c]
            for i in range(3):
                spar[i, side, g, t] = p[i]
        for g in range(2):
            left, right = (v for _, h, v, _ in done if h == g)
            for c in range(COMPS):
                seam0[c, g, t] = seam_of(left[c], right[c])
        return carry

    lax.fori_loop(0, tiles, fill_strips, 0)

    def around_z(cells, t):
        if t + 1 < tiles:
            above = cells[t + 1]
        else:
            above = jnp.where(top, 0.0, pltpu.roll(cells[0], SUB - 1, 0))
        if t > 0:
            under = cells[t - 1]
        else:
            under = jnp.where(bottom, 0.0, pltpu.roll(cells[tiles - 1], 1, 0))
        return above + under

    def main_row(state, r):
        g = r // ny
        k = r & (ny - 1)
        after = (r + 1) & (window - 1)
        before = (r - 1) & (window - 1)
        shift = (LANES - DEPTH * (k + 1)) & (LANES - 1)
        center = [[main[state][c, r, t] for t in range(tiles)] for c in range(COMPS)]
        done = []
        for t in range(tiles):
            h = []
            for c in range(COMPS):
                cells = center[c][t]
                ends = pltpu.roll(seam[state][c, g, t], shift, 1)
                s = jnp.where(first_lane, ends, pltpu.roll(cells, 1, 1))
                s = s + jnp.where(last_lane, ends, pltpu.roll(cells, LANES - 1, 1))
                s = s + (main[state][c, after, t] + main[state][c, before, t])
                h.append(s + around_z(center[c], t))
            m = [center[c][t] for c in range(COMPS)]
            rate = turn(m, h, par[0, r, t], par[1, r, t], par[2, r, t])
            if state == 0:
                new = [m[c] + rate[c] for c in range(COMPS)]
            else:
                new = normal([main[0][c, r, t] + (m[c] + rate[c]) for c in range(COMPS)])
            done.append((r, t, new, ends_of(k, m)))
        return done

    def strip_rows(state):
        done = []
        for g in range(2):
            for side in range(2):
                start = block == side
                stop = block == (side + ny - 1) % ny
                center = [[strip[state][c, side, g, t] for t in range(tiles)] for c in range(COMPS)]
                for t in range(tiles):
                    h = []
                    for c in range(COMPS):
                        cells = center[c][t]
                        inner = edge[c, g, t]
                        other = strip[state][c, side, 1 - g, t]
                        if side == 0:
                            s = pltpu.roll(cells, 1, 1)
                            s = s + pltpu.roll(jnp.where(head_lane, inner, cells), LANES - 1, 1)
                        else:
                            s = pltpu.roll(jnp.where(tail_lane, inner, cells), 1, 1)
                            s = s + pltpu.roll(cells, LANES - 1, 1)
                        s = s + pltpu.roll(jnp.where(start, other, cells), LANES - DEPTH, 1)
                        s = s + pltpu.roll(jnp.where(stop, other, cells), DEPTH, 1)
                        h.append(s + around_z(center[c], t))
                    m = [center[c][t] for c in range(COMPS)]
                    rate = turn(
                        m, h, spar[0, side, g, t], spar[1, side, g, t], spar[2, side, g, t]
                    )
                    if state == 0:
                        new = [m[c] + rate[c] for c in range(COMPS)]
                    else:
                        new = normal(
                            [strip[0][c, side, g, t] + (m[c] + rate[c]) for c in range(COMPS)]
                        )
                    done.append((side, g, t, new))
        for side, g, t, new in done:
            for c in range(COMPS):
                strip[1 - state][c, side, g, t] = new[c]
        for g in range(2):
            for t in range(tiles):
                left, right = (new for _, h, u, new in done if (h, u) == (g, t))
                for c in range(COMPS):
                    seam[1 - state][c, g, t] = seam_of(left[c], right[c])

    def main_rows(state, first, count):
        def rows(i, carry):
            done = []
            for u in range(ROWS):
                done += main_row(state, (first + ROWS * i + u) & (window - 1))
            for r, t, new, ends in done:
                k = r & (ny - 1)
                mask = ((lane - (DEPTH * k + DEPTH - 1)) & (LANES - 1)) < 2
                for c in range(COMPS):
                    main[1 - state][c, r, t] = new[c]
                    pltpu.store(edge.at[c, r // ny, t], ends[c], mask=mask)
            return carry

        lax.fori_loop(0, count // ROWS, rows, 0)

    def step(i, carry):
        for state in range(2):
            margin = DEPTH - 2 * state - 2 * i
            main_rows(state, -margin, ny + 2 * margin)
            strip_rows(state)
        return carry

    lax.fori_loop(0, STEPS, step, 0)

    def hand_out(i, carry):
        for k in (2 * i, 2 * i + 1):
            for t in range(tiles):
                for c in range(COMPS):
                    out_ref[c, rows_at(ny, tiles, k, t), :] = main0[c, k, t]
        return carry

    lax.fori_loop(0, ny // 2, hand_out, 0)


def shifted(cells, axis, step, closed):
    count = lax.axis_size(axis)
    pairs = [(i, (i + step) % count) for i in range(count) if closed or 0 <= i + step < count]
    return lax.ppermute(cells, axis, pairs)


def swapped(cells, axis, first, closed):
    count = lax.axis_size(axis)
    pairs = [(i, (i + 1) % count) for i in range(first, count if closed else count - 1, 2)]
    return lax.ppermute(cells, axis, pairs + [(j, i) for i, j in pairs])


def around(cells, dim):
    ny = cells.shape[dim]
    if lax.axis_size("gy") == 2:
        return shifted(cells, "gy", 1, True)
    head = lax.slice_in_dim(cells, 0, DEPTH, axis=dim)
    tail = lax.slice_in_dim(cells, ny - DEPTH, ny, axis=dim)
    return jnp.concatenate([shifted(head, "gy", -1, True), shifted(tail, "gy", 1, True)], axis=dim)


def around_strips(both):
    if lax.axis_size("gy") == 2:
        return shifted(both, "gy", 1, True)
    block = lax.broadcasted_iota(jnp.int32, both.shape, both.ndim - 1) // DEPTH
    side = lax.broadcasted_iota(jnp.int32, both.shape, 0)
    head = (block + side - 1) % (LANES // DEPTH) < DEPTH
    return jnp.where(head, shifted(both, "gy", -1, True), shifted(both, "gy", 1, True))


def body(magnetization, lower_image, image_weights, regions, anisotropy, damping):
    local, comps, nz, ny, nx = magnetization.shape
    images = local * lax.axis_size("img")
    tiles = nz // SUB
    devices = lax.axis_size(("img", "gx", "gy"))
    assert lax.axis_size("gx") % 2 == 0
    assert local == 1 and comps == COMPS and nx == LANES
    assert ny == 2 * DEPTH and ny * DEPTH == LANES and tiles >= 2
    flat = (comps, nz * ny, nx)
    own = magnetization[0]
    own_p = around(own, 2)
    first = swapped(own, "img", 0, False)
    second = swapped(own, "img", 1, False)

    smem = pl.BlockSpec(memory_space=pltpu.SMEM)
    vmem = pl.BlockSpec(memory_space=pltpu.VMEM)
    f32 = jnp.float32
    limit = pltpu.CompilerParams(vmem_limit_bytes=32 * 1024 * 1024)
    vreg = (SUB, LANES)
    packed = jax.ShapeDtypeStruct((comps + 1, tiles) + vreg, f32)
    own_one, own_two, info = pl.pallas_call(
        functools.partial(pack_kernel, ny, tiles, anisotropy.shape[0]),
        out_shape=(packed, packed, jax.ShapeDtypeStruct((5,) + vreg, f32)),
        in_specs=[smem] * 3 + [vmem] * 3,
        out_specs=(vmem,) * 3,
        compiler_params=limit,
        name="pack_strips",
    )(
        lower_image,
        anisotropy,
        damping,
        image_weights.reshape(1, -1),
        own.reshape(flat),
        regions.reshape(flat[1:]),
    )
    own_one = swapped(own_one, "gx", 0, True)
    own_two = swapped(own_two, "gx", 1, True)
    late_regions, info = lax.optimization_barrier((regions, info))
    reg_p = around(late_regions, 1)
    info, own_p, reg_p, own_one, own_two = lax.optimization_barrier((info, own_p, reg_p, own_one, own_two))
    packed = jax.ShapeDtypeStruct((comps, tiles) + vreg, f32)
    part, near, one, two = pl.pallas_call(
        functools.partial(gather_kernel, ny, tiles),
        out_shape=(
            jax.ShapeDtypeStruct((devices, LANES), f32),
            jax.ShapeDtypeStruct(flat, f32),
            packed,
            packed,
        ),
        in_specs=[vmem] * 4,
        out_specs=(vmem,) * 4,
        compiler_params=limit,
        name="gather_images",
    )(info, own.reshape(flat), first.reshape(flat), second.reshape(flat))
    near_p = around(near.reshape(own.shape), 2)
    one = swapped(one, "gx", 0, True)
    two = swapped(two, "gx", 1, True)
    window = ny + 2 * DEPTH
    par = pl.pallas_call(
        functools.partial(look_up_kernel, ny, tiles),
        out_shape=jax.ShapeDtypeStruct((3, window, tiles) + vreg, f32),
        in_specs=[vmem] * 3,
        out_specs=vmem,
        compiler_params=limit,
        name="parameters",
    )(info, regions.reshape(flat[1:]), reg_p.reshape(flat[1:]))
    one, par = lax.optimization_barrier((one, par))
    strips = pl.pallas_call(
        merge_kernel,
        out_shape=jax.ShapeDtypeStruct((2, 2 * comps + 1, tiles) + vreg, f32),
        in_specs=[vmem] * 4,
        out_specs=vmem,
        compiler_params=limit,
        name="merge_strips",
    )(one, two, own_one, own_two)
    strips_p = around_strips(strips)
    squares = lax.all_to_all(part, ("img", "gx", "gy"), 0, 0, tiled=True)

    out = pl.pallas_call(
        functools.partial(evolve_kernel, ny, tiles, images),
        out_shape=jax.ShapeDtypeStruct(flat, f32),
        in_specs=[vmem] * 9,
        out_specs=vmem,
        scratch_shapes=[
            pltpu.VMEM((comps, window, tiles) + vreg, f32),
            pltpu.VMEM((comps, window, tiles) + vreg, f32),
            pltpu.VMEM((comps, 2, 2, tiles) + vreg, f32),
            pltpu.VMEM((comps, 2, 2, tiles) + vreg, f32),
            pltpu.VMEM((comps, 2, tiles) + vreg, f32),
            pltpu.VMEM((comps, 2, tiles) + vreg, f32),
            pltpu.VMEM((comps, 2, tiles) + vreg, f32),
            pltpu.VMEM((3, 2, 2, tiles) + vreg, f32),
        ],
        compiler_params=limit,
        name="evolve",
    )(
        info,
        squares,
        own.reshape(flat),
        own_p.reshape(flat),
        near,
        near_p.reshape(flat),
        par,
        strips,
        strips_p,
    )
    return out.reshape(magnetization.shape)


def solution(mesh):
    placed = (P("img", None, None, "gy", "gx"), P(), P(), P(None, "gy", "gx"), P(), P())
    return jax.shard_map(
        body,
        mesh=mesh,
        in_specs=placed,
        out_specs=P("img", None, None, "gy", "gx"),
        check_vma=False,
    )
```

```python
import functools

import jax
import jax.numpy as jnp
from jax import lax
from jax.experimental import pallas as pl
from jax.experimental.pallas import tpu as pltpu
from jax.sharding import PartitionSpec as P

STEPS = 4
DEPTH = 2 * STEPS

eps = 1e-06
time_step = 0.05

SUB = 8
LANES = 128
COMPS = 3
ROWS = 4


def lane_iota():
    return lax.broadcasted_iota(jnp.int32, (SUB, LANES), 1)


def sub_iota():
    return lax.broadcasted_iota(jnp.int32, (SUB, LANES), 0)


def rows_at(ny, tiles, y, t):
    return pl.ds(y + ny * t, SUB, stride=ny * tiles)


def is_turned():
    return (lax.axis_index("gx") & 1) == 1


def rims(ny, y):
    block = lane_iota() // DEPTH
    turned = is_turned()
    after = (y + 1) & (ny - 1)
    return block == jnp.where(turned, after, y), block == jnp.where(turned, y, after), (DEPTH * (y + 1)) & (LANES - 1)


def pack_rows(ny, tiles, one_ref, two_ref, comps, cells_at):
    def pack(i, carry):
        done = []
        for u in range(2):
            y = 2 * i + u
            one, two, shift = rims(ny, y)
            for t in range(tiles):
                for c in range(comps):
                    cells = cells_at(c, rows_at(ny, tiles, y, t))
                    done.append((c, t, one, two, pltpu.roll(cells, shift, 1)))
        for c, t, one, two, cells in done:
            pltpu.store(one_ref.at[c, t], cells, mask=one)
            pltpu.store(two_ref.at[c, t], cells, mask=two)
        return carry

    lax.fori_loop(0, ny // 2, pack, 0)


def pack_kernel(ny, tiles, m_ref, one_ref, two_ref):
    pack_rows(ny, tiles, one_ref, two_ref, COMPS, lambda c, rows: m_ref[c, rows, :])


def info_kernel(
    ny, tiles, regions, lower_ref, aniso_ref, damp_ref, share_ref, reg_ref, one_ref, two_ref, info_ref
):
    here = lax.axis_index("img")
    lane = lane_iota()
    pack_rows(ny, tiles, one_ref, two_ref, 1, lambda c, rows: reg_ref[rows, :].astype(jnp.float32))

    table_a = jnp.zeros((SUB, LANES), jnp.float32)
    table_d = jnp.zeros((SUB, LANES), jnp.float32)
    for i in range(regions):
        table_a = jnp.where(lane == i, 2.0 * aniso_ref[i], table_a)
        table_d = jnp.where(lane == i, damp_ref[i], table_d)
    info_ref[0] = table_a
    info_ref[1] = table_d
    info_ref[2] = -time_step / (1.0 + table_d * table_d)
    share = share_ref[...]
    spot = lax.broadcasted_iota(jnp.int32, share.shape, 1)
    target = jnp.sum(jnp.where(spot < here, share, 0.0), axis=1, keepdims=True) / jnp.sum(
        share, axis=1, keepdims=True
    )
    info_ref[3] = jnp.broadcast_to(target, (SUB, LANES))
    info_ref[4] = jnp.full((SUB, LANES), lower_ref[here].astype(jnp.float32))


def merge_kernel(one_ref, two_ref, own_one_ref, own_two_ref, out_ref):
    turned = is_turned()
    for first, (one_ref, two_ref) in ((0, (one_ref, two_ref)), (COMPS + 1, (own_one_ref, own_two_ref))):
        one, two = one_ref[...], two_ref[...]
        out_ref[0, first : first + one.shape[0]] = jnp.where(turned, one, two)
        out_ref[1, first : first + one.shape[0]] = jnp.where(turned, two, one)


def take_first(info_ref, here):
    odd = (here & 1) == 1
    below = info_ref[4] < here.astype(jnp.float32)
    return jnp.where(below, jnp.where(odd, 1, 0), jnp.where(odd, 0, 1)) == 1, odd


def gather_kernel(
    ny, tiles, info_ref, m_ref, first_ref, second_ref, reg_one_ref, reg_two_ref, part_ref, near_ref, one_ref, two_ref
):
    here = lax.axis_index("img")
    pick, odd = take_first(info_ref, here)
    chunks = 4
    depth = m_ref.shape[1]

    def squares(i, sums):
        sums = list(sums)
        done = []
        for u in range(chunks):
            start = pl.multiple_of((chunks * i + u) * SUB, SUB)
            for c in range(COMPS):
                one = first_ref[c, pl.ds(start, SUB), :]
                two = second_ref[c, pl.ds(start, SUB), :]
                done.append((c, start, jnp.where(pick, one, two)))
                diff = m_ref[c, pl.ds(start, SUB), :] - jnp.where(odd, one, two)
                sums[c + COMPS * u] = sums[c + COMPS * u] + diff * diff
        for c, start, cells in done:
            near_ref[c, pl.ds(start, SUB), :] = cells
        return tuple(sums)

    zero = jnp.zeros((SUB, LANES), jnp.float32)
    sums = lax.fori_loop(0, depth // (chunks * SUB), squares, (zero,) * (chunks * COMPS))
    total = jnp.sum(functools.reduce(jnp.add, sums), axis=(0, 1), keepdims=True)
    slot = lax.broadcasted_iota(jnp.int32, part_ref.shape, 1)
    part_ref[...] = jnp.where((slot == here) & (here > 0), total, 0.0)
    one_ref[COMPS:] = reg_one_ref[...]
    two_ref[COMPS:] = reg_two_ref[...]
    pack_rows(ny, tiles, one_ref, two_ref, COMPS, lambda c, rows: near_ref[c, rows, :])


def turn(m, h, a2, b, sc):
    mx, my, mz = m
    hx, hy, hz = h
    hz = hz + a2 * mz
    gx = hx + b * (my * hz - mz * hy)
    gy = hy + b * (mz * hx - mx * hz)
    gz = hz + b * (mx * hy - my * hx)
    return (
        sc * (my * gz - mz * gy),
        sc * (mz * gx - mx * gz),
        sc * (mx * gy - my * gx),
    )


def normal(v):
    scale = lax.rsqrt(v[0] * v[0] + v[1] * v[1] + v[2] * v[2])
    return tuple(x * scale for x in v)


def look_up(info_ref, region):
    return [jnp.take_along_axis(info_ref[i], region, axis=1) for i in range(3)]


def look_up_kernel(ny, tiles, info_ref, reg_ref, regp_ref, par_ref):
    def fill(i, carry):
        done = []
        for k in (2 * i, 2 * i + 1):
            for g, reg in enumerate((reg_ref, regp_ref)):
                for t in range(tiles):
                    done.append((g * ny + k, t, look_up(info_ref, reg[rows_at(ny, tiles, k, t), :])))
        for r, t, p in done:
            for i in range(3):
                par_ref[i, r, t] = p[i]
        return carry

    lax.fori_loop(0, ny // 2, fill, 0)


def evolve_kernel(
    ny,
    tiles,
    images,
    info_ref,
    sq_ref,
    m_ref,
    mp_ref,
    n_ref,
    np_ref,
    par,
    strips_ref,
    stripsp_ref,
    out_ref,
    main0,
    main1,
    strip0,
    strip1,
    edge,
    seam0,
    seam1,
    spar,
):
    main, strip, seam = (main0, main1), (strip0, strip1), (seam0, seam1)
    window = ny + 2 * DEPTH
    here = lax.axis_index("img")
    lane = lane_iota()
    sub = sub_iota()
    block = lane // DEPTH
    first_lane = lane == 0
    last_lane = lane == LANES - 1
    head_lane = lane % DEPTH == 0
    tail_lane = lane % DEPTH == DEPTH - 1
    top = sub == SUB - 1
    bottom = sub == 0

    lo = info_ref[4]
    slot = lane.astype(jnp.float32)
    squares = jnp.broadcast_to(jnp.sum(sq_ref[...], axis=0, keepdims=True), (SUB, LANES))
    lengths = jnp.where((lane >= 1) & (lane < images), jnp.sqrt(squares + eps), 0.0)
    total = jnp.sum(lengths, axis=1, keepdims=True)
    arc = jnp.sum(jnp.where(slot <= lo, lengths, 0.0), axis=1, keepdims=True)
    gap = jnp.sum(jnp.where(slot == lo + 1.0, lengths, 0.0), axis=1, keepdims=True)
    weight = jnp.clip((info_ref[3] * total - arc) / gap, -0.5, 1.5)
    below = lo < here.astype(jnp.float32)
    w_own = jnp.where(below, weight, 1.0 - weight)
    w_near = jnp.where(below, 1.0 - weight, weight)

    def ends_of(k, new):
        shift = (DEPTH * (k + 1)) & (LANES - 1)
        return [pltpu.roll(new[c], shift, 1) for c in range(COMPS)]

    def fill(i, carry):
        done = []
        for k in (2 * i, 2 * i + 1):
            for g, (own, near) in enumerate(((m_ref, n_ref), (mp_ref, np_ref))):
                for t in range(tiles):
                    rows = rows_at(ny, tiles, k, t)
                    v = normal(
                        [w_own * own[c, rows, :] + w_near * near[c, rows, :] for c in range(COMPS)]
                    )
                    done.append((g * ny + k, t, v))
        for r, t, v in done:
            for c in range(COMPS):
                main0[c, r, t] = v[c]
        return carry

    lax.fori_loop(0, ny // 2, fill, 0)

    def seam_of(left, right):
        return jnp.where(head_lane, pltpu.roll(left, 1, 1), pltpu.roll(right, LANES - 1, 1))

    def fill_strips(t, carry):
        done = []
        for g, cells in enumerate((strips_ref, stripsp_ref)):
            for side in range(2):
                v = normal(
                    [w_own * cells[side, COMPS + 1 + c, t] + w_near * cells[side, c, t] for c in range(COMPS)]
                )
                done.append((side, g, v, look_up(info_ref, cells[side, COMPS, t].astype(jnp.int32))))
        for side, g, v, p in done:
            for c in range(COMPS):
                strip0[c, side, g, t] = v[c]
            for i in range(3):
                spar[i, side, g, t] = p[i]
        for g in range(2):
            left, right = (v for _, h, v, _ in done if h == g)
            for c in range(COMPS):
                seam0[c, g, t] = seam_of(left[c], right[c])
        return carry

    lax.fori_loop(0, tiles, fill_strips, 0)

    def around_z(cells, t):
        if t + 1 < tiles:
            above = cells[t + 1]
        else:
            above = jnp.where(top, 0.0, pltpu.roll(cells[0], SUB - 1, 0))
        if t > 0:
            under = cells[t - 1]
        else:
            under = jnp.where(bottom, 0.0, pltpu.roll(cells[tiles - 1], 1, 0))
        return above + under

    def main_row(state, r):
        g = r // ny
        k = r & (ny - 1)
        after = (r + 1) & (window - 1)
        before = (r - 1) & (window - 1)
        shift = (LANES - DEPTH * (k + 1)) & (LANES - 1)
        center = [[main[state][c, r, t] for t in range(tiles)] for c in range(COMPS)]
        done = []
        for t in range(tiles):
            h = []
            for c in range(COMPS):
                cells = center[c][t]
                ends = pltpu.roll(seam[state][c, g, t], shift, 1)
                s = jnp.where(first_lane, ends, pltpu.roll(cells, 1, 1))
                s = s + jnp.where(last_lane, ends, pltpu.roll(cells, LANES - 1, 1))
                s = s + (main[state][c, after, t] + main[state][c, before, t])
                h.append(s + around_z(center[c], t))
            m = [center[c][t] for c in range(COMPS)]
            rate = turn(m, h, par[0, r, t], par[1, r, t], par[2, r, t])
            if state == 0:
                new = [m[c] + rate[c] for c in range(COMPS)]
            else:
                new = normal([main[0][c, r, t] + (m[c] + rate[c]) for c in range(COMPS)])
            done.append((r, t, new, ends_of(k, m)))
        return done

    def strip_rows(state):
        done = []
        for g in range(2):
            for side in range(2):
                start = block == side
                stop = block == (side + ny - 1) % ny
                center = [[strip[state][c, side, g, t] for t in range(tiles)] for c in range(COMPS)]
                for t in range(tiles):
                    h = []
                    for c in range(COMPS):
                        cells = center[c][t]
                        inner = edge[c, g, t]
                        other = strip[state][c, side, 1 - g, t]
                        if side == 0:
                            s = pltpu.roll(cells, 1, 1)
                            s = s + pltpu.roll(jnp.where(head_lane, inner, cells), LANES - 1, 1)
                        else:
                            s = pltpu.roll(jnp.where(tail_lane, inner, cells), 1, 1)
                            s = s + pltpu.roll(cells, LANES - 1, 1)
                        s = s + pltpu.roll(jnp.where(start, other, cells), LANES - DEPTH, 1)
                        s = s + pltpu.roll(jnp.where(stop, other, cells), DEPTH, 1)
                        h.append(s + around_z(center[c], t))
                    m = [center[c][t] for c in range(COMPS)]
                    rate = turn(
                        m, h, spar[0, side, g, t], spar[1, side, g, t], spar[2, side, g, t]
                    )
                    if state == 0:
                        new = [m[c] + rate[c] for c in range(COMPS)]
                    else:
                        new = normal(
                            [strip[0][c, side, g, t] + (m[c] + rate[c]) for c in range(COMPS)]
                        )
                    done.append((side, g, t, new))
        for side, g, t, new in done:
            for c in range(COMPS):
                strip[1 - state][c, side, g, t] = new[c]
        for g in range(2):
            for t in range(tiles):
                left, right = (new for _, h, u, new in done if (h, u) == (g, t))
                for c in range(COMPS):
                    seam[1 - state][c, g, t] = seam_of(left[c], right[c])

    def main_rows(state, first, count):
        def rows(i, carry):
            done = []
            for u in range(ROWS):
                done += main_row(state, (first + ROWS * i + u) & (window - 1))
            for r, t, new, ends in done:
                k = r & (ny - 1)
                mask = ((lane - (DEPTH * k + DEPTH - 1)) & (LANES - 1)) < 2
                for c in range(COMPS):
                    main[1 - state][c, r, t] = new[c]
                    pltpu.store(edge.at[c, r // ny, t], ends[c], mask=mask)
            return carry

        lax.fori_loop(0, count // ROWS, rows, 0)

    def step(i, carry):
        for state in range(2):
            margin = DEPTH - 2 * state - 2 * i
            main_rows(state, -margin, ny + 2 * margin)
            strip_rows(state)
        return carry

    lax.fori_loop(0, STEPS, step, 0)

    def hand_out(i, carry):
        for k in (2 * i, 2 * i + 1):
            for t in range(tiles):
                for c in range(COMPS):
                    out_ref[c, rows_at(ny, tiles, k, t), :] = main0[c, k, t]
        return carry

    lax.fori_loop(0, ny // 2, hand_out, 0)


def shifted(cells, axis, step, closed):
    count = lax.axis_size(axis)
    pairs = [(i, (i + step) % count) for i in range(count) if closed or 0 <= i + step < count]
    return lax.ppermute(cells, axis, pairs)


def swapped(cells, axis, first, closed):
    count = lax.axis_size(axis)
    pairs = [(i, (i + 1) % count) for i in range(first, count if closed else count - 1, 2)]
    return lax.ppermute(cells, axis, pairs + [(j, i) for i, j in pairs])


def around(cells, dim):
    ny = cells.shape[dim]
    if lax.axis_size("gy") == 2:
        return shifted(cells, "gy", 1, True)
    head = lax.slice_in_dim(cells, 0, DEPTH, axis=dim)
    tail = lax.slice_in_dim(cells, ny - DEPTH, ny, axis=dim)
    return jnp.concatenate([shifted(head, "gy", -1, True), shifted(tail, "gy", 1, True)], axis=dim)


def around_strips(both):
    if lax.axis_size("gy") == 2:
        return shifted(both, "gy", 1, True)
    block = lax.broadcasted_iota(jnp.int32, both.shape, both.ndim - 1) // DEPTH
    side = lax.broadcasted_iota(jnp.int32, both.shape, 0)
    head = (block + side - 1) % (LANES // DEPTH) < DEPTH
    return jnp.where(head, shifted(both, "gy", -1, True), shifted(both, "gy", 1, True))


def body(magnetization, lower_image, image_weights, regions, anisotropy, damping):
    local, comps, nz, ny, nx = magnetization.shape
    images = local * lax.axis_size("img")
    tiles = nz // SUB
    devices = lax.axis_size(("img", "gx", "gy"))
    assert lax.axis_size("gx") % 2 == 0
    assert local == 1 and comps == COMPS and nx == LANES
    assert ny == 2 * DEPTH and ny * DEPTH == LANES and tiles >= 2
    flat = (comps, nz * ny, nx)
    own = magnetization[0]
    own_p = around(own, 2)
    first = swapped(own, "img", 0, False)
    second = swapped(own, "img", 1, False)

    smem = pl.BlockSpec(memory_space=pltpu.SMEM)
    vmem = pl.BlockSpec(memory_space=pltpu.VMEM)
    f32 = jnp.float32
    limit = pltpu.CompilerParams(vmem_limit_bytes=32 * 1024 * 1024)
    vreg = (SUB, LANES)
    packed = [jax.ShapeDtypeStruct((count, tiles) + vreg, f32) for count in range(comps + 2)]
    own_one, own_two = pl.pallas_call(
        functools.partial(pack_kernel, ny, tiles),
        out_shape=(packed[comps],) * 2,
        in_specs=[vmem],
        out_specs=(vmem,) * 2,
        compiler_params=limit,
        name="pack_strips",
    )(own.reshape(flat))
    own_one = swapped(own_one, "gx", 0, True)
    own_two = swapped(own_two, "gx", 1, True)
    reg_one, reg_two, info = pl.pallas_call(
        functools.partial(info_kernel, ny, tiles, anisotropy.shape[0]),
        out_shape=(packed[1], packed[1], jax.ShapeDtypeStruct((5,) + vreg, f32)),
        in_specs=[smem] * 3 + [vmem] * 2,
        out_specs=(vmem,) * 3,
        compiler_params=limit,
        name="small_arguments",
    )(lower_image, anisotropy, damping, image_weights.reshape(1, -1), regions.reshape(flat[1:]))
    late_regions, own_one = lax.optimization_barrier((regions, own_one))
    reg_p = around(late_regions, 1)
    info, own_p, reg_p, own_one, own_two = lax.optimization_barrier((info, own_p, reg_p, own_one, own_two))
    part, near, one, two = pl.pallas_call(
        functools.partial(gather_kernel, ny, tiles),
        out_shape=(
            jax.ShapeDtypeStruct((devices, LANES), f32),
            jax.ShapeDtypeStruct(flat, f32),
            packed[comps + 1],
            packed[comps + 1],
        ),
        in_specs=[vmem] * 6,
        out_specs=(vmem,) * 4,
        compiler_params=limit,
        name="gather_images",
    )(info, own.reshape(flat), first.reshape(flat), second.reshape(flat), reg_one, reg_two)
    near_p = around(near.reshape(own.shape), 2)
    one = swapped(one, "gx", 0, True)
    two = swapped(two, "gx", 1, True)
    window = ny + 2 * DEPTH
    par = pl.pallas_call(
        functools.partial(look_up_kernel, ny, tiles),
        out_shape=jax.ShapeDtypeStruct((3, window, tiles) + vreg, f32),
        in_specs=[vmem] * 3,
        out_specs=vmem,
        compiler_params=limit,
        name="parameters",
    )(info, regions.reshape(flat[1:]), reg_p.reshape(flat[1:]))
    one, par = lax.optimization_barrier((one, par))
    strips = pl.pallas_call(
        merge_kernel,
        out_shape=jax.ShapeDtypeStruct((2, 2 * comps + 1, tiles) + vreg, f32),
        in_specs=[vmem] * 4,
        out_specs=vmem,
        compiler_params=limit,
        name="merge_strips",
    )(one, two, own_one, own_two)
    strips_p = around_strips(strips)
    squares = lax.all_to_all(part, ("img", "gx", "gy"), 0, 0, tiled=True)

    out = pl.pallas_call(
        functools.partial(evolve_kernel, ny, tiles, images),
        out_shape=jax.ShapeDtypeStruct(flat, f32),
        in_specs=[vmem] * 9,
        out_specs=vmem,
        scratch_shapes=[
            pltpu.VMEM((comps, window, tiles) + vreg, f32),
            pltpu.VMEM((comps, window, tiles) + vreg, f32),
            pltpu.VMEM((comps, 2, 2, tiles) + vreg, f32),
            pltpu.VMEM((comps, 2, 2, tiles) + vreg, f32),
            pltpu.VMEM((comps, 2, tiles) + vreg, f32),
            pltpu.VMEM((comps, 2, tiles) + vreg, f32),
            pltpu.VMEM((comps, 2, tiles) + vreg, f32),
            pltpu.VMEM((3, 2, 2, tiles) + vreg, f32),
        ],
        compiler_params=limit,
        name="evolve",
    )(
        info,
        squares,
        own.reshape(flat),
        own_p.reshape(flat),
        near,
        near_p.reshape(flat),
        par,
        strips,
        strips_p,
    )
    return out.reshape(magnetization.shape)


def solution(mesh):
    placed = (P("img", None, None, "gy", "gx"), P(), P(), P(None, "gy", "gx"), P(), P())
    return jax.shard_map(
        body,
        mesh=mesh,
        in_specs=placed,
        out_specs=P("img", None, None, "gy", "gx"),
        check_vma=False,
    )
```

```python
import functools

import jax
import jax.numpy as jnp
from jax import lax
from jax.experimental import pallas as pl
from jax.experimental.pallas import tpu as pltpu
from jax.sharding import PartitionSpec as P

STEPS = 4
DEPTH = 2 * STEPS

eps = 1e-06
time_step = 0.05

SUB = 8
LANES = 128
COMPS = 3
ROWS = 8


def lane_iota():
    return lax.broadcasted_iota(jnp.int32, (SUB, LANES), 1)


def sub_iota():
    return lax.broadcasted_iota(jnp.int32, (SUB, LANES), 0)


def rows_at(ny, tiles, y, t):
    return pl.ds(y + ny * t, SUB, stride=ny * tiles)


def is_turned():
    return (lax.axis_index("gx") & 1) == 1


def rims(ny, y):
    block = lane_iota() // DEPTH
    turned = is_turned()
    after = (y + 1) & (ny - 1)
    return block == jnp.where(turned, after, y), block == jnp.where(turned, y, after), (DEPTH * (y + 1)) & (LANES - 1)


def pack_kernel(
    ny, tiles, regions, lower_ref, aniso_ref, damp_ref, share_ref, m_ref, reg_ref, one_ref, two_ref, info_ref
):
    here = lax.axis_index("img")
    lane = lane_iota()
    def pack(i, carry):
        done = []
        for u in range(2):
            y = 2 * i + u
            one, two, shift = rims(ny, y)
            for t in range(tiles):
                rows = rows_at(ny, tiles, y, t)
                for c in range(COMPS + 1):
                    cells = m_ref[c, rows, :] if c < COMPS else reg_ref[rows, :].astype(jnp.float32)
                    done.append((c, t, one, two, pltpu.roll(cells, shift, 1)))
        for c, t, one, two, cells in done:
            pltpu.store(one_ref.at[c, t], cells, mask=one)
            pltpu.store(two_ref.at[c, t], cells, mask=two)
        return carry

    table_a = jnp.zeros((SUB, LANES), jnp.float32)
    table_d = jnp.zeros((SUB, LANES), jnp.float32)
    for i in range(regions):
        table_a = jnp.where(lane == i, 2.0 * aniso_ref[i], table_a)
        table_d = jnp.where(lane == i, damp_ref[i], table_d)
    info_ref[0] = table_a
    info_ref[1] = table_d
    info_ref[2] = -time_step / (1.0 + table_d * table_d)
    share = share_ref[...]
    spot = lax.broadcasted_iota(jnp.int32, share.shape, 1)
    target = jnp.sum(jnp.where(spot < here, share, 0.0), axis=1, keepdims=True) / jnp.sum(
        share, axis=1, keepdims=True
    )
    info_ref[3] = jnp.broadcast_to(target, (SUB, LANES))
    info_ref[4] = jnp.full((SUB, LANES), lower_ref[here].astype(jnp.float32))

    lax.fori_loop(0, ny // 2, pack, 0)


def merge_kernel(one_ref, two_ref, own_one_ref, own_two_ref, out_ref):
    turned = is_turned()
    for first, (one_ref, two_ref) in ((0, (one_ref, two_ref)), (COMPS, (own_one_ref, own_two_ref))):
        one, two = one_ref[...], two_ref[...]
        out_ref[0, first : first + one.shape[0]] = jnp.where(turned, one, two)
        out_ref[1, first : first + one.shape[0]] = jnp.where(turned, two, one)


def take_first(info_ref, here):
    odd = (here & 1) == 1
    below = info_ref[4] < here.astype(jnp.float32)
    return jnp.where(below, jnp.where(odd, 1, 0), jnp.where(odd, 0, 1)) == 1, odd


def gather_kernel(
    ny, tiles, info_ref, m_ref, first_ref, second_ref, part_ref, near_ref, one_ref, two_ref
):
    here = lax.axis_index("img")
    pick, odd = take_first(info_ref, here)
    chunks = 4
    depth = m_ref.shape[1]

    def squares(i, sums):
        sums = list(sums)
        done = []
        for u in range(chunks):
            start = pl.multiple_of((chunks * i + u) * SUB, SUB)
            for c in range(COMPS):
                one = first_ref[c, pl.ds(start, SUB), :]
                two = second_ref[c, pl.ds(start, SUB), :]
                done.append((c, start, jnp.where(pick, one, two)))
                diff = m_ref[c, pl.ds(start, SUB), :] - jnp.where(odd, one, two)
                sums[c + COMPS * u] = sums[c + COMPS * u] + diff * diff
        for c, start, cells in done:
            near_ref[c, pl.ds(start, SUB), :] = cells
        return tuple(sums)

    zero = jnp.zeros((SUB, LANES), jnp.float32)
    sums = lax.fori_loop(0, depth // (chunks * SUB), squares, (zero,) * (chunks * COMPS))
    total = jnp.sum(functools.reduce(jnp.add, sums), axis=(0, 1), keepdims=True)
    slot = lax.broadcasted_iota(jnp.int32, part_ref.shape, 1)
    part_ref[...] = jnp.where((slot == here) & (here > 0), total, 0.0)
    def pack(i, carry):
        done = []
        for u in range(2):
            y = 2 * i + u
            one, two, shift = rims(ny, y)
            for t in range(tiles):
                for c in range(COMPS):
                    cells = pltpu.roll(near_ref[c, rows_at(ny, tiles, y, t), :], shift, 1)
                    done.append((c, t, one, two, cells))
        for c, t, one, two, cells in done:
            pltpu.store(one_ref.at[c, t], cells, mask=one)
            pltpu.store(two_ref.at[c, t], cells, mask=two)
        return carry

    lax.fori_loop(0, ny // 2, pack, 0)


def turn(m, h, a2, b, sc):
    mx, my, mz = m
    hx, hy, hz = h
    hz = hz + a2 * mz
    gx = hx + b * (my * hz - mz * hy)
    gy = hy + b * (mz * hx - mx * hz)
    gz = hz + b * (mx * hy - my * hx)
    return (
        sc * (my * gz - mz * gy),
        sc * (mz * gx - mx * gz),
        sc * (mx * gy - my * gx),
    )


def normal(v):
    scale = lax.rsqrt(v[0] * v[0] + v[1] * v[1] + v[2] * v[2])
    return tuple(x * scale for x in v)


def look_up(info_ref, region):
    return [jnp.take_along_axis(info_ref[i], region, axis=1) for i in range(3)]


def look_up_kernel(ny, tiles, info_ref, reg_ref, regp_ref, par_ref):
    def fill(i, carry):
        done = []
        for k in (2 * i, 2 * i + 1):
            for g, reg in enumerate((reg_ref, regp_ref)):
                for t in range(tiles):
                    done.append((g * ny + k, t, look_up(info_ref, reg[rows_at(ny, tiles, k, t), :])))
        for r, t, p in done:
            for i in range(3):
                par_ref[i, r, t] = p[i]
        return carry

    lax.fori_loop(0, ny // 2, fill, 0)


def evolve_kernel(
    ny,
    tiles,
    images,
    info_ref,
    sq_ref,
    m_ref,
    mp_ref,
    n_ref,
    np_ref,
    par,
    strips_ref,
    stripsp_ref,
    out_ref,
    main0,
    main1,
    strip0,
    strip1,
    edge,
    seam0,
    seam1,
    spar,
):
    main, strip, seam = (main0, main1), (strip0, strip1), (seam0, seam1)
    window = ny + 2 * DEPTH
    here = lax.axis_index("img")
    lane = lane_iota()
    sub = sub_iota()
    block = lane // DEPTH
    first_lane = lane == 0
    last_lane = lane == LANES - 1
    head_lane = lane % DEPTH == 0
    tail_lane = lane % DEPTH == DEPTH - 1
    top = sub == SUB - 1
    bottom = sub == 0

    lo = info_ref[4]
    slot = lane.astype(jnp.float32)
    squares = jnp.broadcast_to(jnp.sum(sq_ref[...], axis=0, keepdims=True), (SUB, LANES))
    lengths = jnp.where((lane >= 1) & (lane < images), jnp.sqrt(squares + eps), 0.0)
    total = jnp.sum(lengths, axis=1, keepdims=True)
    arc = jnp.sum(jnp.where(slot <= lo, lengths, 0.0), axis=1, keepdims=True)
    gap = jnp.sum(jnp.where(slot == lo + 1.0, lengths, 0.0), axis=1, keepdims=True)
    weight = jnp.clip((info_ref[3] * total - arc) / gap, -0.5, 1.5)
    below = lo < here.astype(jnp.float32)
    w_own = jnp.where(below, weight, 1.0 - weight)
    w_near = jnp.where(below, 1.0 - weight, weight)

    def ends_of(k, new):
        shift = (DEPTH * (k + 1)) & (LANES - 1)
        return [pltpu.roll(new[c], shift, 1) for c in range(COMPS)]

    def fill(i, carry):
        done = []
        for k in (2 * i, 2 * i + 1):
            for g, (own, near) in enumerate(((m_ref, n_ref), (mp_ref, np_ref))):
                for t in range(tiles):
                    rows = rows_at(ny, tiles, k, t)
                    v = normal(
                        [w_own * own[c, rows, :] + w_near * near[c, rows, :] for c in range(COMPS)]
                    )
                    done.append((g * ny + k, t, v))
        for r, t, v in done:
            for c in range(COMPS):
                main0[c, r, t] = v[c]
        return carry

    lax.fori_loop(0, ny // 2, fill, 0)

    def seam_of(left, right):
        return jnp.where(head_lane, pltpu.roll(left, 1, 1), pltpu.roll(right, LANES - 1, 1))

    def fill_strips(t, carry):
        done = []
        for g, cells in enumerate((strips_ref, stripsp_ref)):
            for side in range(2):
                v = normal(
                    [w_own * cells[side, COMPS + c, t] + w_near * cells[side, c, t] for c in range(COMPS)]
                )
                done.append((side, g, v, look_up(info_ref, cells[side, 2 * COMPS, t].astype(jnp.int32))))
        for side, g, v, p in done:
            for c in range(COMPS):
                strip0[c, side, g, t] = v[c]
            for i in range(3):
                spar[i, side, g, t] = p[i]
        for g in range(2):
            left, right = (v for _, h, v, _ in done if h == g)
            for c in range(COMPS):
                seam0[c, g, t] = seam_of(left[c], right[c])
        return carry

    lax.fori_loop(0, tiles, fill_strips, 0)

    def around_z(cells, t):
        if t + 1 < tiles:
            above = cells[t + 1]
        else:
            above = jnp.where(top, 0.0, pltpu.roll(cells[0], SUB - 1, 0))
        if t > 0:
            under = cells[t - 1]
        else:
            under = jnp.where(bottom, 0.0, pltpu.roll(cells[tiles - 1], 1, 0))
        return above + under

    def main_row(state, r):
        g = r // ny
        k = r & (ny - 1)
        after = (r + 1) & (window - 1)
        before = (r - 1) & (window - 1)
        shift = (LANES - DEPTH * (k + 1)) & (LANES - 1)
        center = [[main[state][c, r, t] for t in range(tiles)] for c in range(COMPS)]
        done = []
        for t in range(tiles):
            h = []
            for c in range(COMPS):
                cells = center[c][t]
                ends = pltpu.roll(seam[state][c, g, t], shift, 1)
                s = jnp.where(first_lane, ends, pltpu.roll(cells, 1, 1))
                s = s + jnp.where(last_lane, ends, pltpu.roll(cells, LANES - 1, 1))
                s = s + (main[state][c, after, t] + main[state][c, before, t])
                h.append(s + around_z(center[c], t))
            m = [center[c][t] for c in range(COMPS)]
            rate = turn(m, h, par[0, r, t], par[1, r, t], par[2, r, t])
            if state == 0:
                new = [m[c] + rate[c] for c in range(COMPS)]
            else:
                new = normal([main[0][c, r, t] + (m[c] + rate[c]) for c in range(COMPS)])
            done.append((r, t, new, ends_of(k, m)))
        return done

    def strip_rows(state):
        done = []
        for g in range(2):
            for side in range(2):
                start = block == side
                stop = block == (side + ny - 1) % ny
                center = [[strip[state][c, side, g, t] for t in range(tiles)] for c in range(COMPS)]
                for t in range(tiles):
                    h = []
                    for c in range(COMPS):
                        cells = center[c][t]
                        inner = edge[c, g, t]
                        other = strip[state][c, side, 1 - g, t]
                        if side == 0:
                            s = pltpu.roll(cells, 1, 1)
                            s = s + pltpu.roll(jnp.where(head_lane, inner, cells), LANES - 1, 1)
                        else:
                            s = pltpu.roll(jnp.where(tail_lane, inner, cells), 1, 1)
                            s = s + pltpu.roll(cells, LANES - 1, 1)
                        s = s + pltpu.roll(jnp.where(start, other, cells), LANES - DEPTH, 1)
                        s = s + pltpu.roll(jnp.where(stop, other, cells), DEPTH, 1)
                        h.append(s + around_z(center[c], t))
                    m = [center[c][t] for c in range(COMPS)]
                    rate = turn(
                        m, h, spar[0, side, g, t], spar[1, side, g, t], spar[2, side, g, t]
                    )
                    if state == 0:
                        new = [m[c] + rate[c] for c in range(COMPS)]
                    else:
                        new = normal(
                            [strip[0][c, side, g, t] + (m[c] + rate[c]) for c in range(COMPS)]
                        )
                    done.append((side, g, t, new))
        for side, g, t, new in done:
            for c in range(COMPS):
                strip[1 - state][c, side, g, t] = new[c]
        for g in range(2):
            for t in range(tiles):
                left, right = (new for _, h, u, new in done if (h, u) == (g, t))
                for c in range(COMPS):
                    seam[1 - state][c, g, t] = seam_of(left[c], right[c])

    def main_rows(state, first, count):
        def rows(i, carry):
            done = []
            for u in range(ROWS):
                done += main_row(state, (first + ROWS * i + u) & (window - 1))
            for r, t, new, ends in done:
                k = r & (ny - 1)
                mask = ((lane - (DEPTH * k + DEPTH - 1)) & (LANES - 1)) < 2
                for c in range(COMPS):
                    main[1 - state][c, r, t] = new[c]
                    pltpu.store(edge.at[c, r // ny, t], ends[c], mask=mask)
            return carry

        lax.fori_loop(0, (count + ROWS - 1) // ROWS, rows, 0)

    def step(i, carry):
        for state in range(2):
            margin = DEPTH - 2 * state - 2 * i
            main_rows(state, -margin, ny + 2 * margin)
            strip_rows(state)
        return carry

    lax.fori_loop(0, STEPS, step, 0)

    def hand_out(i, carry):
        for k in (2 * i, 2 * i + 1):
            for t in range(tiles):
                for c in range(COMPS):
                    out_ref[c, rows_at(ny, tiles, k, t), :] = main0[c, k, t]
        return carry

    lax.fori_loop(0, ny // 2, hand_out, 0)


def shifted(cells, axis, step, closed):
    count = lax.axis_size(axis)
    pairs = [(i, (i + step) % count) for i in range(count) if closed or 0 <= i + step < count]
    return lax.ppermute(cells, axis, pairs)


def swapped(cells, axis, first, closed):
    count = lax.axis_size(axis)
    pairs = [(i, (i + 1) % count) for i in range(first, count if closed else count - 1, 2)]
    return lax.ppermute(cells, axis, pairs + [(j, i) for i, j in pairs])


def around(cells, dim):
    ny = cells.shape[dim]
    if lax.axis_size("gy") == 2:
        return shifted(cells, "gy", 1, True)
    head = lax.slice_in_dim(cells, 0, DEPTH, axis=dim)
    tail = lax.slice_in_dim(cells, ny - DEPTH, ny, axis=dim)
    return jnp.concatenate([shifted(head, "gy", -1, True), shifted(tail, "gy", 1, True)], axis=dim)


def around_strips(both):
    if lax.axis_size("gy") == 2:
        return shifted(both, "gy", 1, True)
    block = lax.broadcasted_iota(jnp.int32, both.shape, both.ndim - 1) // DEPTH
    side = lax.broadcasted_iota(jnp.int32, both.shape, 0)
    head = (block + side - 1) % (LANES // DEPTH) < DEPTH
    return jnp.where(head, shifted(both, "gy", -1, True), shifted(both, "gy", 1, True))


def body(magnetization, lower_image, image_weights, regions, anisotropy, damping):
    local, comps, nz, ny, nx = magnetization.shape
    images = local * lax.axis_size("img")
    tiles = nz // SUB
    devices = lax.axis_size(("img", "gx", "gy"))
    assert lax.axis_size("gx") % 2 == 0
    assert local == 1 and comps == COMPS and nx == LANES
    assert ny == 2 * DEPTH and ny * DEPTH == LANES and tiles >= 2
    flat = (comps, nz * ny, nx)
    own = magnetization[0]
    own_p = around(own, 2)
    first = swapped(own, "img", 0, False)
    second = swapped(own, "img", 1, False)

    smem = pl.BlockSpec(memory_space=pltpu.SMEM)
    vmem = pl.BlockSpec(memory_space=pltpu.VMEM)
    f32 = jnp.float32
    limit = pltpu.CompilerParams(vmem_limit_bytes=32 * 1024 * 1024)
    vreg = (SUB, LANES)
    packed = jax.ShapeDtypeStruct((comps + 1, tiles) + vreg, f32)
    own_one, own_two, info = pl.pallas_call(
        functools.partial(pack_kernel, ny, tiles, anisotropy.shape[0]),
        out_shape=(packed, packed, jax.ShapeDtypeStruct((5,) + vreg, f32)),
        in_specs=[smem] * 3 + [vmem] * 3,
        out_specs=(vmem,) * 3,
        compiler_params=limit,
        name="pack_strips",
    )(
        lower_image,
        anisotropy,
        damping,
        image_weights.reshape(1, -1),
        own.reshape(flat),
        regions.reshape(flat[1:]),
    )
    own_one = swapped(own_one, "gx", 0, True)
    own_two = swapped(own_two, "gx", 1, True)
    late_regions, info = lax.optimization_barrier((regions, info))
    reg_p = around(late_regions, 1)
    info, own_p, reg_p, own_one, own_two = lax.optimization_barrier((info, own_p, reg_p, own_one, own_two))
    packed = jax.ShapeDtypeStruct((comps, tiles) + vreg, f32)
    part, near, one, two = pl.pallas_call(
        functools.partial(gather_kernel, ny, tiles),
        out_shape=(
            jax.ShapeDtypeStruct((devices, LANES), f32),
            jax.ShapeDtypeStruct(flat, f32),
            packed,
            packed,
        ),
        in_specs=[vmem] * 4,
        out_specs=(vmem,) * 4,
        compiler_params=limit,
        name="gather_images",
    )(info, own.reshape(flat), first.reshape(flat), second.reshape(flat))
    near_p = around(near.reshape(own.shape), 2)
    one = swapped(one, "gx", 0, True)
    two = swapped(two, "gx", 1, True)
    window = ny + 2 * DEPTH
    par = pl.pallas_call(
        functools.partial(look_up_kernel, ny, tiles),
        out_shape=jax.ShapeDtypeStruct((3, window, tiles) + vreg, f32),
        in_specs=[vmem] * 3,
        out_specs=vmem,
        compiler_params=limit,
        name="parameters",
    )(info, regions.reshape(flat[1:]), reg_p.reshape(flat[1:]))
    one, par = lax.optimization_barrier((one, par))
    strips = pl.pallas_call(
        merge_kernel,
        out_shape=jax.ShapeDtypeStruct((2, 2 * comps + 1, tiles) + vreg, f32),
        in_specs=[vmem] * 4,
        out_specs=vmem,
        compiler_params=limit,
        name="merge_strips",
    )(one, two, own_one, own_two)
    strips_p = around_strips(strips)
    squares = lax.all_to_all(part, ("img", "gx", "gy"), 0, 0, tiled=True)

    out = pl.pallas_call(
        functools.partial(evolve_kernel, ny, tiles, images),
        out_shape=jax.ShapeDtypeStruct(flat, f32),
        in_specs=[vmem] * 9,
        out_specs=vmem,
        scratch_shapes=[
            pltpu.VMEM((comps, window, tiles) + vreg, f32),
            pltpu.VMEM((comps, window, tiles) + vreg, f32),
            pltpu.VMEM((comps, 2, 2, tiles) + vreg, f32),
            pltpu.VMEM((comps, 2, 2, tiles) + vreg, f32),
            pltpu.VMEM((comps, 2, tiles) + vreg, f32),
            pltpu.VMEM((comps, 2, tiles) + vreg, f32),
            pltpu.VMEM((comps, 2, tiles) + vreg, f32),
            pltpu.VMEM((3, 2, 2, tiles) + vreg, f32),
        ],
        compiler_params=limit,
        name="evolve",
    )(
        info,
        squares,
        own.reshape(flat),
        own_p.reshape(flat),
        near,
        near_p.reshape(flat),
        par,
        strips,
        strips_p,
    )
    return out.reshape(magnetization.shape)


def solution(mesh):
    placed = (P("img", None, None, "gy", "gx"), P(), P(), P(None, "gy", "gx"), P(), P())
    return jax.shard_map(
        body,
        mesh=mesh,
        in_specs=placed,
        out_specs=P("img", None, None, "gy", "gx"),
        check_vma=False,
    )
```

```python
import functools

import jax
import jax.numpy as jnp
from jax import lax
from jax.experimental import pallas as pl
from jax.experimental.pallas import tpu as pltpu
from jax.sharding import PartitionSpec as P

STEPS = 4
DEPTH = 2 * STEPS

eps = 1e-06
time_step = 0.05

SUB = 8
LANES = 128
COMPS = 3
ROWS = 10


def lane_iota():
    return lax.broadcasted_iota(jnp.int32, (SUB, LANES), 1)


def sub_iota():
    return lax.broadcasted_iota(jnp.int32, (SUB, LANES), 0)


def rows_at(ny, tiles, y, t):
    return pl.ds(y + ny * t, SUB, stride=ny * tiles)


def is_turned():
    return (lax.axis_index("gx") & 1) == 1


def rims(ny, y):
    block = lane_iota() // DEPTH
    turned = is_turned()
    after = (y + 1) & (ny - 1)
    return block == jnp.where(turned, after, y), block == jnp.where(turned, y, after), (DEPTH * (y + 1)) & (LANES - 1)


def pack_kernel(
    ny, tiles, regions, lower_ref, aniso_ref, damp_ref, share_ref, m_ref, reg_ref, one_ref, two_ref, info_ref
):
    here = lax.axis_index("img")
    lane = lane_iota()
    def pack(i, carry):
        done = []
        for u in range(2):
            y = 2 * i + u
            one, two, shift = rims(ny, y)
            for t in range(tiles):
                rows = rows_at(ny, tiles, y, t)
                for c in range(COMPS + 1):
                    cells = m_ref[c, rows, :] if c < COMPS else reg_ref[rows, :].astype(jnp.float32)
                    done.append((c, t, one, two, pltpu.roll(cells, shift, 1)))
        for c, t, one, two, cells in done:
            pltpu.store(one_ref.at[c, t], cells, mask=one)
            pltpu.store(two_ref.at[c, t], cells, mask=two)
        return carry

    table_a = jnp.zeros((SUB, LANES), jnp.float32)
    table_d = jnp.zeros((SUB, LANES), jnp.float32)
    for i in range(regions):
        table_a = jnp.where(lane == i, 2.0 * aniso_ref[i], table_a)
        table_d = jnp.where(lane == i, damp_ref[i], table_d)
    info_ref[0] = table_a
    info_ref[1] = table_d
    info_ref[2] = -time_step / (1.0 + table_d * table_d)
    share = share_ref[...]
    spot = lax.broadcasted_iota(jnp.int32, share.shape, 1)
    target = jnp.sum(jnp.where(spot < here, share, 0.0), axis=1, keepdims=True) / jnp.sum(
        share, axis=1, keepdims=True
    )
    info_ref[3] = jnp.broadcast_to(target, (SUB, LANES))
    info_ref[4] = jnp.full((SUB, LANES), lower_ref[here].astype(jnp.float32))

    lax.fori_loop(0, ny // 2, pack, 0)


def merge_kernel(one_ref, two_ref, own_one_ref, own_two_ref, out_ref):
    turned = is_turned()
    for first, (one_ref, two_ref) in ((0, (one_ref, two_ref)), (COMPS, (own_one_ref, own_two_ref))):
        one, two = one_ref[...], two_ref[...]
        out_ref[0, first : first + one.shape[0]] = jnp.where(turned, one, two)
        out_ref[1, first : first + one.shape[0]] = jnp.where(turned, two, one)


def take_first(info_ref, here):
    odd = (here & 1) == 1
    below = info_ref[4] < here.astype(jnp.float32)
    return jnp.where(below, jnp.where(odd, 1, 0), jnp.where(odd, 0, 1)) == 1, odd


def gather_kernel(
    ny, tiles, info_ref, m_ref, first_ref, second_ref, part_ref, near_ref, one_ref, two_ref
):
    here = lax.axis_index("img")
    pick, odd = take_first(info_ref, here)
    chunks = 8
    depth = m_ref.shape[1]

    def squares(i, sums):
        sums = list(sums)
        done = []
        for u in range(chunks):
            start = pl.multiple_of((chunks * i + u) * SUB, SUB)
            for c in range(COMPS):
                one = first_ref[c, pl.ds(start, SUB), :]
                two = second_ref[c, pl.ds(start, SUB), :]
                done.append((c, start, jnp.where(pick, one, two)))
                diff = m_ref[c, pl.ds(start, SUB), :] - jnp.where(odd, one, two)
                sums[c + COMPS * (u % 4)] = sums[c + COMPS * (u % 4)] + diff * diff
        for c, start, cells in done:
            near_ref[c, pl.ds(start, SUB), :] = cells
        return tuple(sums)

    zero = jnp.zeros((SUB, LANES), jnp.float32)
    sums = lax.fori_loop(0, depth // (chunks * SUB), squares, (zero,) * (4 * COMPS))
    total = jnp.sum(functools.reduce(jnp.add, sums), axis=(0, 1), keepdims=True)
    slot = lax.broadcasted_iota(jnp.int32, part_ref.shape, 1)
    part_ref[...] = jnp.where((slot == here) & (here > 0), total, 0.0)
    def pack(i, carry):
        done = []
        for u in range(4):
            y = 4 * i + u
            one, two, shift = rims(ny, y)
            for t in range(tiles):
                for c in range(COMPS):
                    cells = pltpu.roll(near_ref[c, rows_at(ny, tiles, y, t), :], shift, 1)
                    done.append((c, t, one, two, cells))
        for c, t, one, two, cells in done:
            pltpu.store(one_ref.at[c, t], cells, mask=one)
            pltpu.store(two_ref.at[c, t], cells, mask=two)
        return carry

    lax.fori_loop(0, ny // 4, pack, 0)


def turn(m, h, a2, b, sc):
    mx, my, mz = m
    hx, hy, hz = h
    hz = hz + a2 * mz
    gx = hx + b * (my * hz - mz * hy)
    gy = hy + b * (mz * hx - mx * hz)
    gz = hz + b * (mx * hy - my * hx)
    return (
        sc * (my * gz - mz * gy),
        sc * (mz * gx - mx * gz),
        sc * (mx * gy - my * gx),
    )


def normal(v):
    scale = lax.rsqrt(v[0] * v[0] + v[1] * v[1] + v[2] * v[2])
    return tuple(x * scale for x in v)


def look_up(info_ref, region):
    return [jnp.take_along_axis(info_ref[i], region, axis=1) for i in range(3)]


def look_up_kernel(ny, tiles, info_ref, reg_ref, regp_ref, par_ref):
    def fill(i, carry):
        done = []
        for k in (2 * i, 2 * i + 1):
            for g, reg in enumerate((reg_ref, regp_ref)):
                for t in range(tiles):
                    done.append((g * ny + k, t, look_up(info_ref, reg[rows_at(ny, tiles, k, t), :])))
        for r, t, p in done:
            for i in range(3):
                par_ref[i, r, t] = p[i]
        return carry

    lax.fori_loop(0, ny // 2, fill, 0)


def evolve_kernel(
    ny,
    tiles,
    images,
    info_ref,
    sq_ref,
    m_ref,
    mp_ref,
    n_ref,
    np_ref,
    par,
    strips_ref,
    stripsp_ref,
    out_ref,
    main0,
    main1,
    strip0,
    strip1,
    edge,
    seam0,
    seam1,
    spar,
):
    main, strip, seam = (main0, main1), (strip0, strip1), (seam0, seam1)
    window = ny + 2 * DEPTH
    here = lax.axis_index("img")
    lane = lane_iota()
    sub = sub_iota()
    block = lane // DEPTH
    first_lane = lane == 0
    last_lane = lane == LANES - 1
    head_lane = lane % DEPTH == 0
    tail_lane = lane % DEPTH == DEPTH - 1
    top = sub == SUB - 1
    bottom = sub == 0

    lo = info_ref[4]
    slot = lane.astype(jnp.float32)
    squares = jnp.broadcast_to(jnp.sum(sq_ref[...], axis=0, keepdims=True), (SUB, LANES))
    lengths = jnp.where((lane >= 1) & (lane < images), jnp.sqrt(squares + eps), 0.0)
    total = jnp.sum(lengths, axis=1, keepdims=True)
    arc = jnp.sum(jnp.where(slot <= lo, lengths, 0.0), axis=1, keepdims=True)
    gap = jnp.sum(jnp.where(slot == lo + 1.0, lengths, 0.0), axis=1, keepdims=True)
    weight = jnp.clip((info_ref[3] * total - arc) / gap, -0.5, 1.5)
    below = lo < here.astype(jnp.float32)
    w_own = jnp.where(below, weight, 1.0 - weight)
    w_near = jnp.where(below, 1.0 - weight, weight)

    def ends_of(k, new):
        shift = (DEPTH * (k + 1)) & (LANES - 1)
        return [pltpu.roll(new[c], shift, 1) for c in range(COMPS)]

    def fill(i, carry):
        done = []
        for k in [4 * i + u for u in range(4)]:
            for g, (own, near) in enumerate(((m_ref, n_ref), (mp_ref, np_ref))):
                for t in range(tiles):
                    rows = rows_at(ny, tiles, k, t)
                    v = normal(
                        [w_own * own[c, rows, :] + w_near * near[c, rows, :] for c in range(COMPS)]
                    )
                    done.append((g * ny + k, t, v))
        for r, t, v in done:
            for c in range(COMPS):
                main0[c, r, t] = v[c]
        return carry

    lax.fori_loop(0, ny // 4, fill, 0)

    def seam_of(left, right):
        return jnp.where(head_lane, pltpu.roll(left, 1, 1), pltpu.roll(right, LANES - 1, 1))

    def fill_strips(t, carry):
        done = []
        for g, cells in enumerate((strips_ref, stripsp_ref)):
            for side in range(2):
                v = normal(
                    [w_own * cells[side, COMPS + c, t] + w_near * cells[side, c, t] for c in range(COMPS)]
                )
                done.append((side, g, v, look_up(info_ref, cells[side, 2 * COMPS, t].astype(jnp.int32))))
        for side, g, v, p in done:
            for c in range(COMPS):
                strip0[c, side, g, t] = v[c]
            for i in range(3):
                spar[i, side, g, t] = p[i]
        for g in range(2):
            left, right = (v for _, h, v, _ in done if h == g)
            for c in range(COMPS):
                seam0[c, g, t] = seam_of(left[c], right[c])
        return carry

    lax.fori_loop(0, tiles, fill_strips, 0)

    def around_z(cells, t):
        if t + 1 < tiles:
            above = cells[t + 1]
        else:
            above = jnp.where(top, 0.0, pltpu.roll(cells[0], SUB - 1, 0))
        if t > 0:
            under = cells[t - 1]
        else:
            under = jnp.where(bottom, 0.0, pltpu.roll(cells[tiles - 1], 1, 0))
        return above + under

    def main_row(state, r):
        g = r // ny
        k = r & (ny - 1)
        after = (r + 1) & (window - 1)
        before = (r - 1) & (window - 1)
        shift = (LANES - DEPTH * (k + 1)) & (LANES - 1)
        center = [[main[state][c, r, t] for t in range(tiles)] for c in range(COMPS)]
        done = []
        for t in range(tiles):
            h = []
            for c in range(COMPS):
                cells = center[c][t]
                ends = pltpu.roll(seam[state][c, g, t], shift, 1)
                s = jnp.where(first_lane, ends, pltpu.roll(cells, 1, 1))
                s = s + jnp.where(last_lane, ends, pltpu.roll(cells, LANES - 1, 1))
                s = s + (main[state][c, after, t] + main[state][c, before, t])
                h.append(s + around_z(center[c], t))
            m = [center[c][t] for c in range(COMPS)]
            rate = turn(m, h, par[0, r, t], par[1, r, t], par[2, r, t])
            if state == 0:
                new = [m[c] + rate[c] for c in range(COMPS)]
            else:
                new = normal([main[0][c, r, t] + (m[c] + rate[c]) for c in range(COMPS)])
            done.append((r, t, new, ends_of(k, m)))
        return done

    def strip_rows(state):
        done = []
        for g in range(2):
            for side in range(2):
                start = block == side
                stop = block == (side + ny - 1) % ny
                center = [[strip[state][c, side, g, t] for t in range(tiles)] for c in range(COMPS)]
                for t in range(tiles):
                    h = []
                    for c in range(COMPS):
                        cells = center[c][t]
                        inner = edge[c, g, t]
                        other = strip[state][c, side, 1 - g, t]
                        if side == 0:
                            s = pltpu.roll(cells, 1, 1)
                            s = s + pltpu.roll(jnp.where(head_lane, inner, cells), LANES - 1, 1)
                        else:
                            s = pltpu.roll(jnp.where(tail_lane, inner, cells), 1, 1)
                            s = s + pltpu.roll(cells, LANES - 1, 1)
                        s = s + pltpu.roll(jnp.where(start, other, cells), LANES - DEPTH, 1)
                        s = s + pltpu.roll(jnp.where(stop, other, cells), DEPTH, 1)
                        h.append(s + around_z(center[c], t))
                    m = [center[c][t] for c in range(COMPS)]
                    rate = turn(
                        m, h, spar[0, side, g, t], spar[1, side, g, t], spar[2, side, g, t]
                    )
                    if state == 0:
                        new = [m[c] + rate[c] for c in range(COMPS)]
                    else:
                        new = normal(
                            [strip[0][c, side, g, t] + (m[c] + rate[c]) for c in range(COMPS)]
                        )
                    done.append((side, g, t, new))
        for side, g, t, new in done:
            for c in range(COMPS):
                strip[1 - state][c, side, g, t] = new[c]
        for g in range(2):
            for t in range(tiles):
                left, right = (new for _, h, u, new in done if (h, u) == (g, t))
                for c in range(COMPS):
                    seam[1 - state][c, g, t] = seam_of(left[c], right[c])

    def main_rows(state, first, count):
        def rows(i, carry):
            done = []
            for u in range(ROWS):
                done += main_row(state, (first + ROWS * i + u) & (window - 1))
            for r, t, new, ends in done:
                k = r & (ny - 1)
                mask = ((lane - (DEPTH * k + DEPTH - 1)) & (LANES - 1)) < 2
                for c in range(COMPS):
                    main[1 - state][c, r, t] = new[c]
                    pltpu.store(edge.at[c, r // ny, t], ends[c], mask=mask)
            return carry

        lax.fori_loop(0, (count + ROWS - 1) // ROWS, rows, 0)

    def step(i, carry):
        for state in range(2):
            margin = DEPTH - 1 - state - 2 * i
            main_rows(state, -margin, ny + 2 * margin)
            strip_rows(state)
        return carry

    lax.fori_loop(0, STEPS, step, 0)

    def hand_out(i, carry):
        for k in (2 * i, 2 * i + 1):
            for t in range(tiles):
                for c in range(COMPS):
                    out_ref[c, rows_at(ny, tiles, k, t), :] = main0[c, k, t]
        return carry

    lax.fori_loop(0, ny // 2, hand_out, 0)


def shifted(cells, axis, step, closed):
    count = lax.axis_size(axis)
    pairs = [(i, (i + step) % count) for i in range(count) if closed or 0 <= i + step < count]
    return lax.ppermute(cells, axis, pairs)


def swapped(cells, axis, first, closed):
    count = lax.axis_size(axis)
    pairs = [(i, (i + 1) % count) for i in range(first, count if closed else count - 1, 2)]
    return lax.ppermute(cells, axis, pairs + [(j, i) for i, j in pairs])


def around(cells, dim):
    ny = cells.shape[dim]
    if lax.axis_size("gy") == 2:
        return shifted(cells, "gy", 1, True)
    head = lax.slice_in_dim(cells, 0, DEPTH, axis=dim)
    tail = lax.slice_in_dim(cells, ny - DEPTH, ny, axis=dim)
    return jnp.concatenate([shifted(head, "gy", -1, True), shifted(tail, "gy", 1, True)], axis=dim)


def around_strips(both):
    if lax.axis_size("gy") == 2:
        return shifted(both, "gy", 1, True)
    block = lax.broadcasted_iota(jnp.int32, both.shape, both.ndim - 1) // DEPTH
    side = lax.broadcasted_iota(jnp.int32, both.shape, 0)
    head = (block + side - 1) % (LANES // DEPTH) < DEPTH
    return jnp.where(head, shifted(both, "gy", -1, True), shifted(both, "gy", 1, True))


def body(magnetization, lower_image, image_weights, regions, anisotropy, damping):
    local, comps, nz, ny, nx = magnetization.shape
    images = local * lax.axis_size("img")
    tiles = nz // SUB
    devices = lax.axis_size(("img", "gx", "gy"))
    assert lax.axis_size("gx") % 2 == 0
    assert local == 1 and comps == COMPS and nx == LANES
    assert ny == 2 * DEPTH and ny * DEPTH == LANES and tiles >= 2
    flat = (comps, nz * ny, nx)
    own = magnetization[0]
    own_p = around(own, 2)
    first = swapped(own, "img", 0, False)
    second = swapped(own, "img", 1, False)

    smem = pl.BlockSpec(memory_space=pltpu.SMEM)
    vmem = pl.BlockSpec(memory_space=pltpu.VMEM)
    f32 = jnp.float32
    limit = pltpu.CompilerParams(vmem_limit_bytes=32 * 1024 * 1024)
    vreg = (SUB, LANES)
    packed = jax.ShapeDtypeStruct((comps + 1, tiles) + vreg, f32)
    own_one, own_two, info = pl.pallas_call(
        functools.partial(pack_kernel, ny, tiles, anisotropy.shape[0]),
        out_shape=(packed, packed, jax.ShapeDtypeStruct((5,) + vreg, f32)),
        in_specs=[smem] * 3 + [vmem] * 3,
        out_specs=(vmem,) * 3,
        compiler_params=limit,
        name="pack_strips",
    )(
        lower_image,
        anisotropy,
        damping,
        image_weights.reshape(1, -1),
        own.reshape(flat),
        regions.reshape(flat[1:]),
    )
    own_one = swapped(own_one, "gx", 0, True)
    own_two = swapped(own_two, "gx", 1, True)
    late_regions, info = lax.optimization_barrier((regions, info))
    reg_p = around(late_regions, 1)
    info, own_p, reg_p, own_one, own_two = lax.optimization_barrier((info, own_p, reg_p, own_one, own_two))
    packed = jax.ShapeDtypeStruct((comps, tiles) + vreg, f32)
    part, near, one, two = pl.pallas_call(
        functools.partial(gather_kernel, ny, tiles),
        out_shape=(
            jax.ShapeDtypeStruct((devices, LANES), f32),
            jax.ShapeDtypeStruct(flat, f32),
            packed,
            packed,
        ),
        in_specs=[vmem] * 4,
        out_specs=(vmem,) * 4,
        compiler_params=limit,
        name="gather_images",
    )(info, own.reshape(flat), first.reshape(flat), second.reshape(flat))
    near_p = around(near.reshape(own.shape), 2)
    one = swapped(one, "gx", 0, True)
    two = swapped(two, "gx", 1, True)
    window = ny + 2 * DEPTH
    par = pl.pallas_call(
        functools.partial(look_up_kernel, ny, tiles),
        out_shape=jax.ShapeDtypeStruct((3, window, tiles) + vreg, f32),
        in_specs=[vmem] * 3,
        out_specs=vmem,
        compiler_params=limit,
        name="parameters",
    )(info, regions.reshape(flat[1:]), reg_p.reshape(flat[1:]))
    one, par = lax.optimization_barrier((one, par))
    strips = pl.pallas_call(
        merge_kernel,
        out_shape=jax.ShapeDtypeStruct((2, 2 * comps + 1, tiles) + vreg, f32),
        in_specs=[vmem] * 4,
        out_specs=vmem,
        compiler_params=limit,
        name="merge_strips",
    )(one, two, own_one, own_two)
    strips_p = around_strips(strips)
    squares = lax.all_to_all(part, ("img", "gx", "gy"), 0, 0, tiled=True)

    out = pl.pallas_call(
        functools.partial(evolve_kernel, ny, tiles, images),
        out_shape=jax.ShapeDtypeStruct(flat, f32),
        in_specs=[vmem] * 9,
        out_specs=vmem,
        scratch_shapes=[
            pltpu.VMEM((comps, window, tiles) + vreg, f32),
            pltpu.VMEM((comps, window, tiles) + vreg, f32),
            pltpu.VMEM((comps, 2, 2, tiles) + vreg, f32),
            pltpu.VMEM((comps, 2, 2, tiles) + vreg, f32),
            pltpu.VMEM((comps, 2, tiles) + vreg, f32),
            pltpu.VMEM((comps, 2, tiles) + vreg, f32),
            pltpu.VMEM((comps, 2, tiles) + vreg, f32),
            pltpu.VMEM((3, 2, 2, tiles) + vreg, f32),
        ],
        compiler_params=limit,
        name="evolve",
    )(
        info,
        squares,
        own.reshape(flat),
        own_p.reshape(flat),
        near,
        near_p.reshape(flat),
        par,
        strips,
        strips_p,
    )
    return out.reshape(magnetization.shape)


def solution(mesh):
    placed = (P("img", None, None, "gy", "gx"), P(), P(), P(None, "gy", "gx"), P(), P())
    return jax.shard_map(
        body,
        mesh=mesh,
        in_specs=placed,
        out_specs=P("img", None, None, "gy", "gx"),
        check_vma=False,
    )
```

```python
import functools

import jax
import jax.numpy as jnp
from jax import lax
from jax.experimental import pallas as pl
from jax.experimental.pallas import tpu as pltpu
from jax.sharding import PartitionSpec as P

STEPS = 4
DEPTH = 2 * STEPS

eps = 1e-06
time_step = 0.05

SUB = 8
LANES = 128
COMPS = 3
ROWS = 10


def lane_iota():
    return lax.broadcasted_iota(jnp.int32, (SUB, LANES), 1)


def sub_iota():
    return lax.broadcasted_iota(jnp.int32, (SUB, LANES), 0)


def rows_at(ny, tiles, y, t):
    return pl.ds(y + ny * t, SUB, stride=ny * tiles)


def is_turned():
    return (lax.axis_index("gx") & 1) == 1


def rims(ny, y):
    block = lane_iota() // DEPTH
    turned = is_turned()
    after = (y + 1) & (ny - 1)
    return block == jnp.where(turned, after, y), block == jnp.where(turned, y, after), (DEPTH * (y + 1)) & (LANES - 1)


def pack_kernel(
    ny, tiles, regions, lower_ref, aniso_ref, damp_ref, share_ref, m_ref, reg_ref, one_ref, two_ref, info_ref
):
    here = lax.axis_index("img")
    lane = lane_iota()
    def pack(i, carry):
        done = []
        for u in range(2):
            y = 2 * i + u
            one, two, shift = rims(ny, y)
            for t in range(tiles):
                rows = rows_at(ny, tiles, y, t)
                for c in range(COMPS + 1):
                    cells = m_ref[c, rows, :] if c < COMPS else reg_ref[rows, :].astype(jnp.float32)
                    done.append((c, t, one, two, pltpu.roll(cells, shift, 1)))
        for c, t, one, two, cells in done:
            pltpu.store(one_ref.at[c, t], cells, mask=one)
            pltpu.store(two_ref.at[c, t], cells, mask=two)
        return carry

    table_a = jnp.zeros((SUB, LANES), jnp.float32)
    table_d = jnp.zeros((SUB, LANES), jnp.float32)
    for i in range(regions):
        table_a = jnp.where(lane == i, 2.0 * aniso_ref[i], table_a)
        table_d = jnp.where(lane == i, damp_ref[i], table_d)
    info_ref[0] = table_a
    info_ref[1] = table_d
    info_ref[2] = -time_step / (1.0 + table_d * table_d)
    share = share_ref[...]
    spot = lax.broadcasted_iota(jnp.int32, share.shape, 1)
    target = jnp.sum(jnp.where(spot < here, share, 0.0), axis=1, keepdims=True) / jnp.sum(
        share, axis=1, keepdims=True
    )
    info_ref[3] = jnp.broadcast_to(target, (SUB, LANES))
    info_ref[4] = jnp.full((SUB, LANES), lower_ref[here].astype(jnp.float32))

    lax.fori_loop(0, ny // 2, pack, 0)


def merge_kernel(one_ref, two_ref, own_one_ref, own_two_ref, out_ref):
    turned = is_turned()
    for first, (one_ref, two_ref) in ((0, (one_ref, two_ref)), (COMPS, (own_one_ref, own_two_ref))):
        one, two = one_ref[...], two_ref[...]
        out_ref[0, first : first + one.shape[0]] = jnp.where(turned, one, two)
        out_ref[1, first : first + one.shape[0]] = jnp.where(turned, two, one)


def take_first(info_ref, here):
    odd = (here & 1) == 1
    below = info_ref[4] < here.astype(jnp.float32)
    return jnp.where(below, jnp.where(odd, 1, 0), jnp.where(odd, 0, 1)) == 1, odd


def gather_kernel(
    ny, tiles, info_ref, m_ref, first_ref, second_ref, part_ref, near_ref, one_ref, two_ref
):
    here = lax.axis_index("img")
    pick, odd = take_first(info_ref, here)
    chunks = 8
    depth = m_ref.shape[1]

    def squares(i, sums):
        sums = list(sums)
        done = []
        for u in range(chunks):
            start = pl.multiple_of((chunks * i + u) * SUB, SUB)
            for c in range(COMPS):
                one = first_ref[c, pl.ds(start, SUB), :]
                two = second_ref[c, pl.ds(start, SUB), :]
                done.append((c, start, jnp.where(pick, one, two)))
                diff = m_ref[c, pl.ds(start, SUB), :] - jnp.where(odd, one, two)
                sums[c + COMPS * (u % 4)] = sums[c + COMPS * (u % 4)] + diff * diff
        for c, start, cells in done:
            near_ref[c, pl.ds(start, SUB), :] = cells
        return tuple(sums)

    zero = jnp.zeros((SUB, LANES), jnp.float32)
    sums = lax.fori_loop(0, depth // (chunks * SUB), squares, (zero,) * (4 * COMPS))
    total = jnp.sum(functools.reduce(jnp.add, sums), axis=(0, 1), keepdims=True)
    slot = lax.broadcasted_iota(jnp.int32, part_ref.shape, 1)
    part_ref[...] = jnp.where((slot == here) & (here > 0), total, 0.0)
    def pack(i, carry):
        done = []
        for u in range(4):
            y = 4 * i + u
            one, two, shift = rims(ny, y)
            for t in range(tiles):
                for c in range(COMPS):
                    cells = pltpu.roll(near_ref[c, rows_at(ny, tiles, y, t), :], shift, 1)
                    done.append((c, t, one, two, cells))
        for c, t, one, two, cells in done:
            pltpu.store(one_ref.at[c, t], cells, mask=one)
            pltpu.store(two_ref.at[c, t], cells, mask=two)
        return carry

    lax.fori_loop(0, ny // 4, pack, 0)


def turn(m, h, a2, b, sc):
    mx, my, mz = m
    hx, hy, hz = h
    hz = hz + a2 * mz
    gx = hx + b * (my * hz - mz * hy)
    gy = hy + b * (mz * hx - mx * hz)
    gz = hz + b * (mx * hy - my * hx)
    return (
        sc * (my * gz - mz * gy),
        sc * (mz * gx - mx * gz),
        sc * (mx * gy - my * gx),
    )


def normal(v):
    scale = lax.rsqrt(v[0] * v[0] + v[1] * v[1] + v[2] * v[2])
    return tuple(x * scale for x in v)


def look_up(info_ref, region):
    return [jnp.take_along_axis(info_ref[i], region, axis=1) for i in range(3)]


def look_up_kernel(ny, tiles, info_ref, reg_ref, regp_ref, par_ref):
    def fill(i, carry):
        done = []
        for k in (2 * i, 2 * i + 1):
            for g, reg in enumerate((reg_ref, regp_ref)):
                for t in range(tiles):
                    done.append((g * ny + k, t, look_up(info_ref, reg[rows_at(ny, tiles, k, t), :])))
        for r, t, p in done:
            for i in range(3):
                par_ref[i, r, t] = p[i]
        return carry

    lax.fori_loop(0, ny // 2, fill, 0)


def evolve_kernel(
    ny,
    tiles,
    images,
    info_ref,
    sq_ref,
    m_ref,
    mp_ref,
    n_ref,
    np_ref,
    par,
    strips_ref,
    stripsp_ref,
    out_ref,
    main0,
    main1,
    strip0,
    strip1,
    edge,
    seam0,
    seam1,
    spar,
):
    main, strip, seam = (main0, main1), (strip0, strip1), (seam0, seam1)
    window = ny + 2 * DEPTH
    here = lax.axis_index("img")
    lane = lane_iota()
    sub = sub_iota()
    block = lane // DEPTH
    first_lane = lane == 0
    last_lane = lane == LANES - 1
    head_lane = lane % DEPTH == 0
    tail_lane = lane % DEPTH == DEPTH - 1
    top = sub == SUB - 1
    bottom = sub == 0

    lo = info_ref[4]
    slot = lane.astype(jnp.float32)
    squares = jnp.broadcast_to(jnp.sum(sq_ref[...], axis=0, keepdims=True), (SUB, LANES))
    lengths = jnp.where((lane >= 1) & (lane < images), jnp.sqrt(squares + eps), 0.0)
    total = jnp.sum(lengths, axis=1, keepdims=True)
    arc = jnp.sum(jnp.where(slot <= lo, lengths, 0.0), axis=1, keepdims=True)
    gap = jnp.sum(jnp.where(slot == lo + 1.0, lengths, 0.0), axis=1, keepdims=True)
    weight = jnp.clip((info_ref[3] * total - arc) / gap, -0.5, 1.5)
    below = lo < here.astype(jnp.float32)
    w_own = jnp.where(below, weight, 1.0 - weight)
    w_near = jnp.where(below, 1.0 - weight, weight)

    def ends_of(k, new):
        shift = (DEPTH * (k + 1)) & (LANES - 1)
        return [pltpu.roll(new[c], shift, 1) for c in range(COMPS)]

    def fill(i, carry):
        done = []
        for k in [4 * i + u for u in range(4)]:
            for g, (own, near) in enumerate(((m_ref, n_ref), (mp_ref, np_ref))):
                for t in range(tiles):
                    rows = rows_at(ny, tiles, k, t)
                    v = normal(
                        [w_own * own[c, rows, :] + w_near * near[c, rows, :] for c in range(COMPS)]
                    )
                    done.append((g * ny + k, t, v))
        for r, t, v in done:
            for c in range(COMPS):
                main0[c, r, t] = v[c]
        return carry

    lax.fori_loop(0, ny // 4, fill, 0)

    def seam_of(left, right):
        return jnp.where(head_lane, pltpu.roll(left, 1, 1), pltpu.roll(right, LANES - 1, 1))

    def fill_strips(t, carry):
        done = []
        for g, cells in enumerate((strips_ref, stripsp_ref)):
            for side in range(2):
                v = normal(
                    [w_own * cells[side, COMPS + c, t] + w_near * cells[side, c, t] for c in range(COMPS)]
                )
                done.append((side, g, v, look_up(info_ref, cells[side, 2 * COMPS, t].astype(jnp.int32))))
        for side, g, v, p in done:
            for c in range(COMPS):
                strip0[c, side, g, t] = v[c]
            for i in range(3):
                spar[i, side, g, t] = p[i]
        for g in range(2):
            left, right = (v for _, h, v, _ in done if h == g)
            for c in range(COMPS):
                seam0[c, g, t] = seam_of(left[c], right[c])
        return carry

    lax.fori_loop(0, tiles, fill_strips, 0)

    def around_z(cells, t):
        if t + 1 < tiles:
            above = cells[t + 1]
        else:
            above = jnp.where(top, 0.0, pltpu.roll(cells[0], SUB - 1, 0))
        if t > 0:
            under = cells[t - 1]
        else:
            under = jnp.where(bottom, 0.0, pltpu.roll(cells[tiles - 1], 1, 0))
        return above + under

    def main_row(state, r):
        g = r // ny
        k = r & (ny - 1)
        after = (r + 1) & (window - 1)
        before = (r - 1) & (window - 1)
        shift = (LANES - DEPTH * (k + 1)) & (LANES - 1)
        center = [[main[state][c, r, t] for t in range(tiles)] for c in range(COMPS)]
        done = []
        for t in range(tiles):
            h = []
            for c in range(COMPS):
                cells = center[c][t]
                ends = pltpu.roll(seam[state][c, g, t], shift, 1)
                s = jnp.where(first_lane, ends, pltpu.roll(cells, 1, 1))
                s = s + jnp.where(last_lane, ends, pltpu.roll(cells, LANES - 1, 1))
                s = s + (main[state][c, after, t] + main[state][c, before, t])
                h.append(s + around_z(center[c], t))
            m = [center[c][t] for c in range(COMPS)]
            rate = turn(m, h, par[0, r, t], par[1, r, t], par[2, r, t])
            if state == 0:
                new = [m[c] + rate[c] for c in range(COMPS)]
            else:
                new = normal([main[0][c, r, t] + (m[c] + rate[c]) for c in range(COMPS)])
            done.append((r, t, new, ends_of(k, m)))
        return done

    def strip_rows(state):
        done = []
        for g in range(2):
            for side in range(2):
                start = block == side
                stop = block == (side + ny - 1) % ny
                center = [[strip[state][c, side, g, t] for t in range(tiles)] for c in range(COMPS)]
                for t in range(tiles):
                    h = []
                    for c in range(COMPS):
                        cells = center[c][t]
                        inner = edge[c, g, t]
                        other = strip[state][c, side, 1 - g, t]
                        if side == 0:
                            s = pltpu.roll(cells, 1, 1)
                            s = s + pltpu.roll(jnp.where(head_lane, inner, cells), LANES - 1, 1)
                        else:
                            s = pltpu.roll(jnp.where(tail_lane, inner, cells), 1, 1)
                            s = s + pltpu.roll(cells, LANES - 1, 1)
                        s = s + pltpu.roll(jnp.where(start, other, cells), LANES - DEPTH, 1)
                        s = s + pltpu.roll(jnp.where(stop, other, cells), DEPTH, 1)
                        h.append(s + around_z(center[c], t))
                    m = [center[c][t] for c in range(COMPS)]
                    rate = turn(
                        m, h, spar[0, side, g, t], spar[1, side, g, t], spar[2, side, g, t]
                    )
                    if state == 0:
                        new = [m[c] + rate[c] for c in range(COMPS)]
                    else:
                        new = normal(
                            [strip[0][c, side, g, t] + (m[c] + rate[c]) for c in range(COMPS)]
                        )
                    done.append((side, g, t, new))
        for side, g, t, new in done:
            for c in range(COMPS):
                strip[1 - state][c, side, g, t] = new[c]
        for g in range(2):
            for t in range(tiles):
                left, right = (new for _, h, u, new in done if (h, u) == (g, t))
                for c in range(COMPS):
                    seam[1 - state][c, g, t] = seam_of(left[c], right[c])

    def main_rows(state, first, count):
        def rows(i, carry):
            done = []
            for u in range(ROWS):
                done += main_row(state, (first + ROWS * i + u) & (window - 1))
            for r, t, new, ends in done:
                k = r & (ny - 1)
                mask = ((lane - (DEPTH * k + DEPTH - 1)) & (LANES - 1)) < 2
                for c in range(COMPS):
                    main[1 - state][c, r, t] = new[c]
                    pltpu.store(edge.at[c, r // ny, t], ends[c], mask=mask)
            return carry

        lax.fori_loop(0, (count + ROWS - 1) // ROWS, rows, 0)

    def step(i, carry):
        for state in range(2):
            margin = DEPTH - 1 - state - 2 * i
            main_rows(state, -margin, ny + 2 * margin)
            strip_rows(state)
        return carry

    lax.fori_loop(0, STEPS, step, 0)

    def hand_out(i, carry):
        for k in [4 * i + u for u in range(4)]:
            for t in range(tiles):
                for c in range(COMPS):
                    out_ref[c, rows_at(ny, tiles, k, t), :] = main0[c, k, t]
        return carry

    lax.fori_loop(0, ny // 4, hand_out, 0)


def shifted(cells, axis, step, closed):
    count = lax.axis_size(axis)
    pairs = [(i, (i + step) % count) for i in range(count) if closed or 0 <= i + step < count]
    return lax.ppermute(cells, axis, pairs)


def swapped(cells, axis, first, closed):
    count = lax.axis_size(axis)
    pairs = [(i, (i + 1) % count) for i in range(first, count if closed else count - 1, 2)]
    return lax.ppermute(cells, axis, pairs + [(j, i) for i, j in pairs])


def around(cells, dim):
    ny = cells.shape[dim]
    if lax.axis_size("gy") == 2:
        return shifted(cells, "gy", 1, True)
    head = lax.slice_in_dim(cells, 0, DEPTH, axis=dim)
    tail = lax.slice_in_dim(cells, ny - DEPTH, ny, axis=dim)
    return jnp.concatenate([shifted(head, "gy", -1, True), shifted(tail, "gy", 1, True)], axis=dim)


def around_strips(both):
    if lax.axis_size("gy") == 2:
        return shifted(both, "gy", 1, True)
    block = lax.broadcasted_iota(jnp.int32, both.shape, both.ndim - 1) // DEPTH
    side = lax.broadcasted_iota(jnp.int32, both.shape, 0)
    head = (block + side - 1) % (LANES // DEPTH) < DEPTH
    return jnp.where(head, shifted(both, "gy", -1, True), shifted(both, "gy", 1, True))


def body(magnetization, lower_image, image_weights, regions, anisotropy, damping):
    local, comps, nz, ny, nx = magnetization.shape
    images = local * lax.axis_size("img")
    tiles = nz // SUB
    devices = lax.axis_size(("img", "gx", "gy"))
    assert lax.axis_size("gx") % 2 == 0
    assert local == 1 and comps == COMPS and nx == LANES
    assert ny == 2 * DEPTH and ny * DEPTH == LANES and tiles >= 2
    flat = (comps, nz * ny, nx)
    own = magnetization[0]
    own_p = around(own, 2)
    first = swapped(own, "img", 0, False)
    second = swapped(own, "img", 1, False)

    smem = pl.BlockSpec(memory_space=pltpu.SMEM)
    vmem = pl.BlockSpec(memory_space=pltpu.VMEM)
    f32 = jnp.float32
    limit = pltpu.CompilerParams(vmem_limit_bytes=32 * 1024 * 1024)
    vreg = (SUB, LANES)
    packed = jax.ShapeDtypeStruct((comps + 1, tiles) + vreg, f32)
    own_one, own_two, info = pl.pallas_call(
        functools.partial(pack_kernel, ny, tiles, anisotropy.shape[0]),
        out_shape=(packed, packed, jax.ShapeDtypeStruct((5,) + vreg, f32)),
        in_specs=[smem] * 3 + [vmem] * 3,
        out_specs=(vmem,) * 3,
        compiler_params=limit,
        name="pack_strips",
    )(
        lower_image,
        anisotropy,
        damping,
        image_weights.reshape(1, -1),
        own.reshape(flat),
        regions.reshape(flat[1:]),
    )
    own_two = swapped(own_two, "gx", 1, True)
    own_one = swapped(own_one, "gx", 0, True)
    late_regions, info = lax.optimization_barrier((regions, info))
    reg_p = around(late_regions, 1)
    info, own_p, reg_p, own_one, own_two = lax.optimization_barrier((info, own_p, reg_p, own_one, own_two))
    packed = jax.ShapeDtypeStruct((comps, tiles) + vreg, f32)
    part, near, one, two = pl.pallas_call(
        functools.partial(gather_kernel, ny, tiles),
        out_shape=(
            jax.ShapeDtypeStruct((devices, LANES), f32),
            jax.ShapeDtypeStruct(flat, f32),
            packed,
            packed,
        ),
        in_specs=[vmem] * 4,
        out_specs=(vmem,) * 4,
        compiler_params=limit,
        name="gather_images",
    )(info, own.reshape(flat), first.reshape(flat), second.reshape(flat))
    near_p = around(near.reshape(own.shape), 2)
    two = swapped(two, "gx", 1, True)
    window = ny + 2 * DEPTH
    par = pl.pallas_call(
        functools.partial(look_up_kernel, ny, tiles),
        out_shape=jax.ShapeDtypeStruct((3, window, tiles) + vreg, f32),
        in_specs=[vmem] * 3,
        out_specs=vmem,
        compiler_params=limit,
        name="parameters",
    )(info, regions.reshape(flat[1:]), reg_p.reshape(flat[1:]))
    one, par = lax.optimization_barrier((one, par))
    one = swapped(one, "gx", 0, True)
    strips = pl.pallas_call(
        merge_kernel,
        out_shape=jax.ShapeDtypeStruct((2, 2 * comps + 1, tiles) + vreg, f32),
        in_specs=[vmem] * 4,
        out_specs=vmem,
        compiler_params=limit,
        name="merge_strips",
    )(one, two, own_one, own_two)
    strips_p = around_strips(strips)
    squares = lax.all_to_all(part, ("img", "gx", "gy"), 0, 0, tiled=True)

    out = pl.pallas_call(
        functools.partial(evolve_kernel, ny, tiles, images),
        out_shape=jax.ShapeDtypeStruct(flat, f32),
        in_specs=[vmem] * 9,
        out_specs=vmem,
        scratch_shapes=[
            pltpu.VMEM((comps, window, tiles) + vreg, f32),
            pltpu.VMEM((comps, window, tiles) + vreg, f32),
            pltpu.VMEM((comps, 2, 2, tiles) + vreg, f32),
            pltpu.VMEM((comps, 2, 2, tiles) + vreg, f32),
            pltpu.VMEM((comps, 2, tiles) + vreg, f32),
            pltpu.VMEM((comps, 2, tiles) + vreg, f32),
            pltpu.VMEM((comps, 2, tiles) + vreg, f32),
            pltpu.VMEM((3, 2, 2, tiles) + vreg, f32),
        ],
        compiler_params=limit,
        name="evolve",
    )(
        info,
        squares,
        own.reshape(flat),
        own_p.reshape(flat),
        near,
        near_p.reshape(flat),
        par,
        strips,
        strips_p,
    )
    return out.reshape(magnetization.shape)


def solution(mesh):
    placed = (P("img", None, None, "gy", "gx"), P(), P(), P(None, "gy", "gx"), P(), P())
    return jax.shard_map(
        body,
        mesh=mesh,
        in_specs=placed,
        out_specs=P("img", None, None, "gy", "gx"),
        check_vma=False,
    )
```

```python
import functools

import jax
import jax.numpy as jnp
from jax import lax
from jax.experimental import pallas as pl
from jax.experimental.pallas import tpu as pltpu
from jax.sharding import PartitionSpec as P

STEPS = 4
DEPTH = 2 * STEPS

eps = 1e-06
time_step = 0.05

SUB = 8
LANES = 128
COMPS = 3
ROWS = 10


def lane_iota():
    return lax.broadcasted_iota(jnp.int32, (SUB, LANES), 1)


def sub_iota():
    return lax.broadcasted_iota(jnp.int32, (SUB, LANES), 0)


def rows_at(ny, tiles, y, t):
    return pl.ds(y + ny * t, SUB, stride=ny * tiles)


def is_turned():
    return (lax.axis_index("gx") & 1) == 1


def rims(ny, y):
    block = lane_iota() // DEPTH
    turned = is_turned()
    after = (y + 1) & (ny - 1)
    return block == jnp.where(turned, after, y), block == jnp.where(turned, y, after), (DEPTH * (y + 1)) & (LANES - 1)


def pack_rows(ny, tiles, one_ref, two_ref, comps, cells_at):
    def pack(i, carry):
        done = []
        for u in range(4):
            y = 4 * i + u
            one, two, shift = rims(ny, y)
            for t in range(tiles):
                for c in range(comps):
                    cells = cells_at(c, rows_at(ny, tiles, y, t))
                    done.append((c, t, one, two, pltpu.roll(cells, shift, 1)))
        for c, t, one, two, cells in done:
            pltpu.store(one_ref.at[c, t], cells, mask=one)
            pltpu.store(two_ref.at[c, t], cells, mask=two)
        return carry

    lax.fori_loop(0, ny // 4, pack, 0)


def pack_kernel(ny, tiles, m_ref, one_ref, two_ref):
    pack_rows(ny, tiles, one_ref, two_ref, COMPS, lambda c, rows: m_ref[c, rows, :])


def info_kernel(
    ny, tiles, regions, lower_ref, aniso_ref, damp_ref, share_ref, reg_ref, one_ref, two_ref, info_ref
):
    here = lax.axis_index("img")
    lane = lane_iota()
    pack_rows(ny, tiles, one_ref, two_ref, 1, lambda c, rows: reg_ref[rows, :].astype(jnp.float32))

    table_a = jnp.zeros((SUB, LANES), jnp.float32)
    table_d = jnp.zeros((SUB, LANES), jnp.float32)
    for i in range(regions):
        table_a = jnp.where(lane == i, 2.0 * aniso_ref[i], table_a)
        table_d = jnp.where(lane == i, damp_ref[i], table_d)
    info_ref[0] = table_a
    info_ref[1] = table_d
    info_ref[2] = -time_step / (1.0 + table_d * table_d)
    share = share_ref[...]
    spot = lax.broadcasted_iota(jnp.int32, share.shape, 1)
    target = jnp.sum(jnp.where(spot < here, share, 0.0), axis=1, keepdims=True) / jnp.sum(
        share, axis=1, keepdims=True
    )
    info_ref[3] = jnp.broadcast_to(target, (SUB, LANES))
    info_ref[4] = jnp.full((SUB, LANES), lower_ref[here].astype(jnp.float32))


def merge_kernel(one_ref, two_ref, own_one_ref, own_two_ref, out_ref):
    turned = is_turned()
    for first, (one_ref, two_ref) in ((0, (one_ref, two_ref)), (COMPS + 1, (own_one_ref, own_two_ref))):
        one, two = one_ref[...], two_ref[...]
        out_ref[0, first : first + one.shape[0]] = jnp.where(turned, one, two)
        out_ref[1, first : first + one.shape[0]] = jnp.where(turned, two, one)


def take_first(info_ref, here):
    odd = (here & 1) == 1
    below = info_ref[4] < here.astype(jnp.float32)
    return jnp.where(below, jnp.where(odd, 1, 0), jnp.where(odd, 0, 1)) == 1, odd


def gather_kernel(
    ny, tiles, info_ref, m_ref, first_ref, second_ref, reg_one_ref, reg_two_ref, part_ref, near_ref, one_ref, two_ref
):
    here = lax.axis_index("img")
    pick, odd = take_first(info_ref, here)
    chunks = 8
    depth = m_ref.shape[1]

    def squares(i, sums):
        sums = list(sums)
        done = []
        for u in range(chunks):
            start = pl.multiple_of((chunks * i + u) * SUB, SUB)
            for c in range(COMPS):
                one = first_ref[c, pl.ds(start, SUB), :]
                two = second_ref[c, pl.ds(start, SUB), :]
                done.append((c, start, jnp.where(pick, one, two)))
                diff = m_ref[c, pl.ds(start, SUB), :] - jnp.where(odd, one, two)
                sums[c + COMPS * (u % 4)] = sums[c + COMPS * (u % 4)] + diff * diff
        for c, start, cells in done:
            near_ref[c, pl.ds(start, SUB), :] = cells
        return tuple(sums)

    zero = jnp.zeros((SUB, LANES), jnp.float32)
    sums = lax.fori_loop(0, depth // (chunks * SUB), squares, (zero,) * (4 * COMPS))
    total = jnp.sum(functools.reduce(jnp.add, sums), axis=(0, 1), keepdims=True)
    slot = lax.broadcasted_iota(jnp.int32, part_ref.shape, 1)
    part_ref[...] = jnp.where((slot == here) & (here > 0), total, 0.0)
    one_ref[COMPS:] = reg_one_ref[...]
    two_ref[COMPS:] = reg_two_ref[...]
    pack_rows(ny, tiles, one_ref, two_ref, COMPS, lambda c, rows: near_ref[c, rows, :])


def turn(m, h, a2, b, sc):
    mx, my, mz = m
    hx, hy, hz = h
    hz = hz + a2 * mz
    gx = hx + b * (my * hz - mz * hy)
    gy = hy + b * (mz * hx - mx * hz)
    gz = hz + b * (mx * hy - my * hx)
    return (
        sc * (my * gz - mz * gy),
        sc * (mz * gx - mx * gz),
        sc * (mx * gy - my * gx),
    )


def normal(v):
    scale = lax.rsqrt(v[0] * v[0] + v[1] * v[1] + v[2] * v[2])
    return tuple(x * scale for x in v)


def look_up(info_ref, region):
    return [jnp.take_along_axis(info_ref[i], region, axis=1) for i in range(3)]


def look_up_kernel(ny, tiles, info_ref, reg_ref, regp_ref, par_ref):
    def fill(i, carry):
        done = []
        for k in (2 * i, 2 * i + 1):
            for g, reg in enumerate((reg_ref, regp_ref)):
                for t in range(tiles):
                    done.append((g * ny + k, t, look_up(info_ref, reg[rows_at(ny, tiles, k, t), :])))
        for r, t, p in done:
            for i in range(3):
                par_ref[i, r, t] = p[i]
        return carry

    lax.fori_loop(0, ny // 2, fill, 0)


def evolve_kernel(
    ny,
    tiles,
    images,
    info_ref,
    sq_ref,
    m_ref,
    mp_ref,
    n_ref,
    np_ref,
    par,
    strips_ref,
    stripsp_ref,
    out_ref,
    main0,
    main1,
    strip0,
    strip1,
    edge,
    seam0,
    seam1,
    spar,
):
    main, strip, seam = (main0, main1), (strip0, strip1), (seam0, seam1)
    window = ny + 2 * DEPTH
    here = lax.axis_index("img")
    lane = lane_iota()
    sub = sub_iota()
    block = lane // DEPTH
    first_lane = lane == 0
    last_lane = lane == LANES - 1
    head_lane = lane % DEPTH == 0
    tail_lane = lane % DEPTH == DEPTH - 1
    top = sub == SUB - 1
    bottom = sub == 0

    lo = info_ref[4]
    slot = lane.astype(jnp.float32)
    squares = jnp.broadcast_to(jnp.sum(sq_ref[...], axis=0, keepdims=True), (SUB, LANES))
    lengths = jnp.where((lane >= 1) & (lane < images), jnp.sqrt(squares + eps), 0.0)
    total = jnp.sum(lengths, axis=1, keepdims=True)
    arc = jnp.sum(jnp.where(slot <= lo, lengths, 0.0), axis=1, keepdims=True)
    gap = jnp.sum(jnp.where(slot == lo + 1.0, lengths, 0.0), axis=1, keepdims=True)
    weight = jnp.clip((info_ref[3] * total - arc) / gap, -0.5, 1.5)
    below = lo < here.astype(jnp.float32)
    w_own = jnp.where(below, weight, 1.0 - weight)
    w_near = jnp.where(below, 1.0 - weight, weight)

    def ends_of(k, new):
        shift = (DEPTH * (k + 1)) & (LANES - 1)
        return [pltpu.roll(new[c], shift, 1) for c in range(COMPS)]

    def fill(i, carry):
        done = []
        for k in [4 * i + u for u in range(4)]:
            for g, (own, near) in enumerate(((m_ref, n_ref), (mp_ref, np_ref))):
                for t in range(tiles):
                    rows = rows_at(ny, tiles, k, t)
                    v = normal(
                        [w_own * own[c, rows, :] + w_near * near[c, rows, :] for c in range(COMPS)]
                    )
                    done.append((g * ny + k, t, v))
        for r, t, v in done:
            for c in range(COMPS):
                main0[c, r, t] = v[c]
        return carry

    lax.fori_loop(0, ny // 4, fill, 0)

    def seam_of(left, right):
        return jnp.where(head_lane, pltpu.roll(left, 1, 1), pltpu.roll(right, LANES - 1, 1))

    def fill_strips(t, carry):
        done = []
        for g, cells in enumerate((strips_ref, stripsp_ref)):
            for side in range(2):
                v = normal(
                    [w_own * cells[side, COMPS + 1 + c, t] + w_near * cells[side, c, t] for c in range(COMPS)]
                )
                done.append((side, g, v, look_up(info_ref, cells[side, COMPS, t].astype(jnp.int32))))
        for side, g, v, p in done:
            for c in range(COMPS):
                strip0[c, side, g, t] = v[c]
            for i in range(3):
                spar[i, side, g, t] = p[i]
        for g in range(2):
            left, right = (v for _, h, v, _ in done if h == g)
            for c in range(COMPS):
                seam0[c, g, t] = seam_of(left[c], right[c])
        return carry

    lax.fori_loop(0, tiles, fill_strips, 0)

    def around_z(cells, t):
        if t + 1 < tiles:
            above = cells[t + 1]
        else:
            above = jnp.where(top, 0.0, pltpu.roll(cells[0], SUB - 1, 0))
        if t > 0:
            under = cells[t - 1]
        else:
            under = jnp.where(bottom, 0.0, pltpu.roll(cells[tiles - 1], 1, 0))
        return above + under

    def main_row(state, r):
        g = r // ny
        k = r & (ny - 1)
        after = (r + 1) & (window - 1)
        before = (r - 1) & (window - 1)
        shift = (LANES - DEPTH * (k + 1)) & (LANES - 1)
        center = [[main[state][c, r, t] for t in range(tiles)] for c in range(COMPS)]
        done = []
        for t in range(tiles):
            h = []
            for c in range(COMPS):
                cells = center[c][t]
                ends = pltpu.roll(seam[state][c, g, t], shift, 1)
                s = jnp.where(first_lane, ends, pltpu.roll(cells, 1, 1))
                s = s + jnp.where(last_lane, ends, pltpu.roll(cells, LANES - 1, 1))
                s = s + (main[state][c, after, t] + main[state][c, before, t])
                h.append(s + around_z(center[c], t))
            m = [center[c][t] for c in range(COMPS)]
            rate = turn(m, h, par[0, r, t], par[1, r, t], par[2, r, t])
            if state == 0:
                new = [m[c] + rate[c] for c in range(COMPS)]
            else:
                new = normal([main[0][c, r, t] + (m[c] + rate[c]) for c in range(COMPS)])
            done.append((r, t, new, ends_of(k, m)))
        return done

    def strip_rows(state):
        done = []
        for g in range(2):
            for side in range(2):
                start = block == side
                stop = block == (side + ny - 1) % ny
                center = [[strip[state][c, side, g, t] for t in range(tiles)] for c in range(COMPS)]
                for t in range(tiles):
                    h = []
                    for c in range(COMPS):
                        cells = center[c][t]
                        inner = edge[c, g, t]
                        other = strip[state][c, side, 1 - g, t]
                        if side == 0:
                            s = pltpu.roll(cells, 1, 1)
                            s = s + pltpu.roll(jnp.where(head_lane, inner, cells), LANES - 1, 1)
                        else:
                            s = pltpu.roll(jnp.where(tail_lane, inner, cells), 1, 1)
                            s = s + pltpu.roll(cells, LANES - 1, 1)
                        s = s + pltpu.roll(jnp.where(start, other, cells), LANES - DEPTH, 1)
                        s = s + pltpu.roll(jnp.where(stop, other, cells), DEPTH, 1)
                        h.append(s + around_z(center[c], t))
                    m = [center[c][t] for c in range(COMPS)]
                    rate = turn(
                        m, h, spar[0, side, g, t], spar[1, side, g, t], spar[2, side, g, t]
                    )
                    if state == 0:
                        new = [m[c] + rate[c] for c in range(COMPS)]
                    else:
                        new = normal(
                            [strip[0][c, side, g, t] + (m[c] + rate[c]) for c in range(COMPS)]
                        )
                    done.append((side, g, t, new))
        for side, g, t, new in done:
            for c in range(COMPS):
                strip[1 - state][c, side, g, t] = new[c]
        for g in range(2):
            for t in range(tiles):
                left, right = (new for _, h, u, new in done if (h, u) == (g, t))
                for c in range(COMPS):
                    seam[1 - state][c, g, t] = seam_of(left[c], right[c])

    def main_rows(state, first, count):
        def rows(i, carry):
            done = []
            for u in range(ROWS):
                done += main_row(state, (first + ROWS * i + u) & (window - 1))
            for r, t, new, ends in done:
                k = r & (ny - 1)
                mask = ((lane - (DEPTH * k + DEPTH - 1)) & (LANES - 1)) < 2
                for c in range(COMPS):
                    main[1 - state][c, r, t] = new[c]
                    pltpu.store(edge.at[c, r // ny, t], ends[c], mask=mask)
            return carry

        lax.fori_loop(0, (count + ROWS - 1) // ROWS, rows, 0)

    def step(i, carry):
        for state in range(2):
            margin = DEPTH - 1 - state - 2 * i
            main_rows(state, -margin, ny + 2 * margin)
            strip_rows(state)
        return carry

    lax.fori_loop(0, STEPS, step, 0)

    def hand_out(i, carry):
        for k in (2 * i, 2 * i + 1):
            for t in range(tiles):
                for c in range(COMPS):
                    out_ref[c, rows_at(ny, tiles, k, t), :] = main0[c, k, t]
        return carry

    lax.fori_loop(0, ny // 2, hand_out, 0)


def shifted(cells, axis, step, closed):
    count = lax.axis_size(axis)
    pairs = [(i, (i + step) % count) for i in range(count) if closed or 0 <= i + step < count]
    return lax.ppermute(cells, axis, pairs)


def swapped(cells, axis, first, closed):
    count = lax.axis_size(axis)
    pairs = [(i, (i + 1) % count) for i in range(first, count if closed else count - 1, 2)]
    return lax.ppermute(cells, axis, pairs + [(j, i) for i, j in pairs])


def around(cells, dim):
    ny = cells.shape[dim]
    if lax.axis_size("gy") == 2:
        return shifted(cells, "gy", 1, True)
    head = lax.slice_in_dim(cells, 0, DEPTH, axis=dim)
    tail = lax.slice_in_dim(cells, ny - DEPTH, ny, axis=dim)
    return jnp.concatenate([shifted(head, "gy", -1, True), shifted(tail, "gy", 1, True)], axis=dim)


def around_strips(both):
    if lax.axis_size("gy") == 2:
        return shifted(both, "gy", 1, True)
    block = lax.broadcasted_iota(jnp.int32, both.shape, both.ndim - 1) // DEPTH
    side = lax.broadcasted_iota(jnp.int32, both.shape, 0)
    head = (block + side - 1) % (LANES // DEPTH) < DEPTH
    return jnp.where(head, shifted(both, "gy", -1, True), shifted(both, "gy", 1, True))


def body(magnetization, lower_image, image_weights, regions, anisotropy, damping):
    local, comps, nz, ny, nx = magnetization.shape
    images = local * lax.axis_size("img")
    tiles = nz // SUB
    devices = lax.axis_size(("img", "gx", "gy"))
    assert lax.axis_size("gx") % 2 == 0
    assert local == 1 and comps == COMPS and nx == LANES
    assert ny == 2 * DEPTH and ny * DEPTH == LANES and tiles >= 2
    flat = (comps, nz * ny, nx)
    own = magnetization[0]
    own_p = around(own, 2)
    first = swapped(own, "img", 0, False)
    second = swapped(own, "img", 1, False)

    smem = pl.BlockSpec(memory_space=pltpu.SMEM)
    vmem = pl.BlockSpec(memory_space=pltpu.VMEM)
    f32 = jnp.float32
    limit = pltpu.CompilerParams(vmem_limit_bytes=32 * 1024 * 1024)
    vreg = (SUB, LANES)
    packed = [jax.ShapeDtypeStruct((count, tiles) + vreg, f32) for count in range(comps + 2)]
    own_one, own_two = pl.pallas_call(
        functools.partial(pack_kernel, ny, tiles),
        out_shape=(packed[comps],) * 2,
        in_specs=[vmem],
        out_specs=(vmem,) * 2,
        compiler_params=limit,
        name="pack_strips",
    )(own.reshape(flat))
    own_one = swapped(own_one, "gx", 0, True)
    own_two = swapped(own_two, "gx", 1, True)
    reg_one, reg_two, info = pl.pallas_call(
        functools.partial(info_kernel, ny, tiles, anisotropy.shape[0]),
        out_shape=(packed[1], packed[1], jax.ShapeDtypeStruct((5,) + vreg, f32)),
        in_specs=[smem] * 3 + [vmem] * 2,
        out_specs=(vmem,) * 3,
        compiler_params=limit,
        name="small_arguments",
    )(lower_image, anisotropy, damping, image_weights.reshape(1, -1), regions.reshape(flat[1:]))
    late_regions, own_one = lax.optimization_barrier((regions, own_one))
    reg_p = around(late_regions, 1)
    info, own_p, reg_p, own_one, own_two = lax.optimization_barrier((info, own_p, reg_p, own_one, own_two))
    part, near, one, two = pl.pallas_call(
        functools.partial(gather_kernel, ny, tiles),
        out_shape=(
            jax.ShapeDtypeStruct((devices, LANES), f32),
            jax.ShapeDtypeStruct(flat, f32),
            packed[comps + 1],
            packed[comps + 1],
        ),
        in_specs=[vmem] * 6,
        out_specs=(vmem,) * 4,
        compiler_params=limit,
        name="gather_images",
    )(info, own.reshape(flat), first.reshape(flat), second.reshape(flat), reg_one, reg_two)
    near_p = around(near.reshape(own.shape), 2)
    one = swapped(one, "gx", 0, True)
    two = swapped(two, "gx", 1, True)
    window = ny + 2 * DEPTH
    par = pl.pallas_call(
        functools.partial(look_up_kernel, ny, tiles),
        out_shape=jax.ShapeDtypeStruct((3, window, tiles) + vreg, f32),
        in_specs=[vmem] * 3,
        out_specs=vmem,
        compiler_params=limit,
        name="parameters",
    )(info, regions.reshape(flat[1:]), reg_p.reshape(flat[1:]))
    one, par = lax.optimization_barrier((one, par))
    strips = pl.pallas_call(
        merge_kernel,
        out_shape=jax.ShapeDtypeStruct((2, 2 * comps + 1, tiles) + vreg, f32),
        in_specs=[vmem] * 4,
        out_specs=vmem,
        compiler_params=limit,
        name="merge_strips",
    )(one, two, own_one, own_two)
    strips_p = around_strips(strips)
    squares = lax.all_to_all(part, ("img", "gx", "gy"), 0, 0, tiled=True)

    out = pl.pallas_call(
        functools.partial(evolve_kernel, ny, tiles, images),
        out_shape=jax.ShapeDtypeStruct(flat, f32),
        in_specs=[vmem] * 9,
        out_specs=vmem,
        scratch_shapes=[
            pltpu.VMEM((comps, window, tiles) + vreg, f32),
            pltpu.VMEM((comps, window, tiles) + vreg, f32),
            pltpu.VMEM((comps, 2, 2, tiles) + vreg, f32),
            pltpu.VMEM((comps, 2, 2, tiles) + vreg, f32),
            pltpu.VMEM((comps, 2, tiles) + vreg, f32),
            pltpu.VMEM((comps, 2, tiles) + vreg, f32),
            pltpu.VMEM((comps, 2, tiles) + vreg, f32),
            pltpu.VMEM((3, 2, 2, tiles) + vreg, f32),
        ],
        compiler_params=limit,
        name="evolve",
    )(
        info,
        squares,
        own.reshape(flat),
        own_p.reshape(flat),
        near,
        near_p.reshape(flat),
        par,
        strips,
        strips_p,
    )
    return out.reshape(magnetization.shape)


def solution(mesh):
    placed = (P("img", None, None, "gy", "gx"), P(), P(), P(None, "gy", "gx"), P(), P())
    return jax.shard_map(
        body,
        mesh=mesh,
        in_specs=placed,
        out_specs=P("img", None, None, "gy", "gx"),
        check_vma=False,
    )
```

```python
import functools

import jax
import jax.numpy as jnp
from jax import lax
from jax.experimental import pallas as pl
from jax.experimental.pallas import tpu as pltpu
from jax.sharding import PartitionSpec as P

STEPS = 4
DEPTH = 2 * STEPS

eps = 1e-06
time_step = 0.05

SUB = 8
LANES = 128
COMPS = 3
ROWS = 10


def lane_iota():
    return lax.broadcasted_iota(jnp.int32, (SUB, LANES), 1)


def sub_iota():
    return lax.broadcasted_iota(jnp.int32, (SUB, LANES), 0)


def rows_at(ny, tiles, y, t):
    return pl.ds(y + ny * t, SUB, stride=ny * tiles)


def is_turned():
    return (lax.axis_index("gx") & 1) == 1


def rims(ny, y):
    block = lane_iota() // DEPTH
    turned = is_turned()
    after = (y + 1) & (ny - 1)
    return block == jnp.where(turned, after, y), block == jnp.where(turned, y, after), (DEPTH * (y + 1)) & (LANES - 1)


def pack_kernel(
    ny, tiles, regions, lower_ref, aniso_ref, damp_ref, share_ref, m_ref, reg_ref, one_ref, two_ref, info_ref
):
    here = lax.axis_index("img")
    lane = lane_iota()
    def pack(i, carry):
        done = []
        for u in range(2):
            y = 2 * i + u
            one, two, shift = rims(ny, y)
            for t in range(tiles):
                rows = rows_at(ny, tiles, y, t)
                for c in range(COMPS + 1):
                    cells = m_ref[c, rows, :] if c < COMPS else reg_ref[rows, :].astype(jnp.float32)
                    done.append((c, t, one, two, pltpu.roll(cells, shift, 1)))
        for c, t, one, two, cells in done:
            pltpu.store(one_ref.at[c, t], cells, mask=one)
            pltpu.store(two_ref.at[c, t], cells, mask=two)
        return carry

    table_a = jnp.zeros((SUB, LANES), jnp.float32)
    table_d = jnp.zeros((SUB, LANES), jnp.float32)
    for i in range(regions):
        table_a = jnp.where(lane == i, 2.0 * aniso_ref[i], table_a)
        table_d = jnp.where(lane == i, damp_ref[i], table_d)
    info_ref[0] = table_a
    info_ref[1] = table_d
    info_ref[2] = -time_step / (1.0 + table_d * table_d)
    share = share_ref[...]
    spot = lax.broadcasted_iota(jnp.int32, share.shape, 1)
    target = jnp.sum(jnp.where(spot < here, share, 0.0), axis=1, keepdims=True) / jnp.sum(
        share, axis=1, keepdims=True
    )
    info_ref[3] = jnp.broadcast_to(target, (SUB, LANES))
    info_ref[4] = jnp.full((SUB, LANES), lower_ref[here].astype(jnp.float32))

    lax.fori_loop(0, ny // 2, pack, 0)


def merge_kernel(one_ref, two_ref, own_one_ref, own_two_ref, out_ref):
    turned = is_turned()
    for first, (one_ref, two_ref) in ((0, (one_ref, two_ref)), (COMPS, (own_one_ref, own_two_ref))):
        one, two = one_ref[...], two_ref[...]
        out_ref[0, first : first + one.shape[0]] = jnp.where(turned, one, two)
        out_ref[1, first : first + one.shape[0]] = jnp.where(turned, two, one)


def take_first(info_ref, here):
    odd = (here & 1) == 1
    below = info_ref[4] < here.astype(jnp.float32)
    return jnp.where(below, jnp.where(odd, 1, 0), jnp.where(odd, 0, 1)) == 1, odd


def gather_kernel(
    ny, tiles, info_ref, m_ref, first_ref, second_ref, part_ref, near_ref, one_ref, two_ref
):
    here = lax.axis_index("img")
    pick, odd = take_first(info_ref, here)
    chunks = 8
    depth = m_ref.shape[1]

    def squares(i, sums):
        sums = list(sums)
        done = []
        for u in range(chunks):
            start = pl.multiple_of((chunks * i + u) * SUB, SUB)
            for c in range(COMPS):
                one = first_ref[c, pl.ds(start, SUB), :]
                two = second_ref[c, pl.ds(start, SUB), :]
                done.append((c, start, jnp.where(pick, one, two)))
                diff = m_ref[c, pl.ds(start, SUB), :] - jnp.where(odd, one, two)
                sums[c + COMPS * (u % 4)] = sums[c + COMPS * (u % 4)] + diff * diff
        for c, start, cells in done:
            near_ref[c, pl.ds(start, SUB), :] = cells
        return tuple(sums)

    zero = jnp.zeros((SUB, LANES), jnp.float32)
    sums = lax.fori_loop(0, depth // (chunks * SUB), squares, (zero,) * (4 * COMPS))
    total = jnp.sum(functools.reduce(jnp.add, sums), axis=(0, 1), keepdims=True)
    slot = lax.broadcasted_iota(jnp.int32, part_ref.shape, 1)
    part_ref[...] = jnp.where((slot == here) & (here > 0), total, 0.0)
    def pack(i, carry):
        done = []
        for u in range(4):
            y = 4 * i + u
            one, two, shift = rims(ny, y)
            for t in range(tiles):
                for c in range(COMPS):
                    cells = pltpu.roll(near_ref[c, rows_at(ny, tiles, y, t), :], shift, 1)
                    done.append((c, t, one, two, cells))
        for c, t, one, two, cells in done:
            pltpu.store(one_ref.at[c, t], cells, mask=one)
            pltpu.store(two_ref.at[c, t], cells, mask=two)
        return carry

    lax.fori_loop(0, ny // 4, pack, 0)


def turn(m, h, a2, b, sc):
    mx, my, mz = m
    hx, hy, hz = h
    hz = hz + a2 * mz
    gx = hx + b * (my * hz - mz * hy)
    gy = hy + b * (mz * hx - mx * hz)
    gz = hz + b * (mx * hy - my * hx)
    return (
        sc * (my * gz - mz * gy),
        sc * (mz * gx - mx * gz),
        sc * (mx * gy - my * gx),
    )


def normal(v):
    scale = lax.rsqrt(v[0] * v[0] + v[1] * v[1] + v[2] * v[2])
    return tuple(x * scale for x in v)


def look_up(info_ref, region):
    return [jnp.take_along_axis(info_ref[i], region, axis=1) for i in range(3)]


def look_up_kernel(ny, tiles, info_ref, reg_ref, regp_ref, par_ref):
    def fill(i, carry):
        done = []
        for k in (2 * i, 2 * i + 1):
            for g, reg in enumerate((reg_ref, regp_ref)):
                for t in range(tiles):
                    done.append((g * ny + k, t, look_up(info_ref, reg[rows_at(ny, tiles, k, t), :])))
        for r, t, p in done:
            for i in range(3):
                par_ref[i, r, t] = p[i]
        return carry

    lax.fori_loop(0, ny // 2, fill, 0)


def evolve_kernel(
    ny,
    tiles,
    images,
    info_ref,
    sq_ref,
    m_ref,
    mp_ref,
    n_ref,
    np_ref,
    par,
    strips_ref,
    stripsp_ref,
    out_ref,
    main0,
    main1,
    strip0,
    strip1,
    edge,
    seam0,
    seam1,
    spar,
):
    main, strip, seam = (main0, main1), (strip0, strip1), (seam0, seam1)
    window = ny + 2 * DEPTH
    here = lax.axis_index("img")
    lane = lane_iota()
    sub = sub_iota()
    block = lane // DEPTH
    first_lane = lane == 0
    last_lane = lane == LANES - 1
    head_lane = lane % DEPTH == 0
    tail_lane = lane % DEPTH == DEPTH - 1
    top = sub == SUB - 1
    bottom = sub == 0

    lo = info_ref[4]
    slot = lane.astype(jnp.float32)
    squares = jnp.broadcast_to(jnp.sum(sq_ref[...], axis=0, keepdims=True), (SUB, LANES))
    lengths = jnp.where((lane >= 1) & (lane < images), jnp.sqrt(squares + eps), 0.0)
    total = jnp.sum(lengths, axis=1, keepdims=True)
    arc = jnp.sum(jnp.where(slot <= lo, lengths, 0.0), axis=1, keepdims=True)
    gap = jnp.sum(jnp.where(slot == lo + 1.0, lengths, 0.0), axis=1, keepdims=True)
    weight = jnp.clip((info_ref[3] * total - arc) / gap, -0.5, 1.5)
    below = lo < here.astype(jnp.float32)
    w_own = jnp.where(below, weight, 1.0 - weight)
    w_near = jnp.where(below, 1.0 - weight, weight)

    def ends_of(k, new):
        shift = (DEPTH * (k + 1)) & (LANES - 1)
        return [pltpu.roll(new[c], shift, 1) for c in range(COMPS)]

    def fill(i, carry):
        done = []
        for k in [8 * i + u for u in range(8)]:
            for g, (own, near) in enumerate(((m_ref, n_ref), (mp_ref, np_ref))):
                for t in range(tiles):
                    rows = rows_at(ny, tiles, k, t)
                    v = normal(
                        [w_own * own[c, rows, :] + w_near * near[c, rows, :] for c in range(COMPS)]
                    )
                    done.append((g * ny + k, t, v))
        for r, t, v in done:
            for c in range(COMPS):
                main0[c, r, t] = v[c]
        return carry

    lax.fori_loop(0, ny // 8, fill, 0)

    def seam_of(left, right):
        return jnp.where(head_lane, pltpu.roll(left, 1, 1), pltpu.roll(right, LANES - 1, 1))

    def fill_strips(t, carry):
        done = []
        for g, cells in enumerate((strips_ref, stripsp_ref)):
            for side in range(2):
                v = normal(
                    [w_own * cells[side, COMPS + c, t] + w_near * cells[side, c, t] for c in range(COMPS)]
                )
                done.append((side, g, v, look_up(info_ref, cells[side, 2 * COMPS, t].astype(jnp.int32))))
        for side, g, v, p in done:
            for c in range(COMPS):
                strip0[c, side, g, t] = v[c]
            for i in range(3):
                spar[i, side, g, t] = p[i]
        for g in range(2):
            left, right = (v for _, h, v, _ in done if h == g)
            for c in range(COMPS):
                seam0[c, g, t] = seam_of(left[c], right[c])
        return carry

    lax.fori_loop(0, tiles, fill_strips, 0)

    def around_z(cells, t):
        if t + 1 < tiles:
            above = cells[t + 1]
        else:
            above = jnp.where(top, 0.0, pltpu.roll(cells[0], SUB - 1, 0))
        if t > 0:
            under = cells[t - 1]
        else:
            under = jnp.where(bottom, 0.0, pltpu.roll(cells[tiles - 1], 1, 0))
        return above + under

    def main_row(state, r):
        g = r // ny
        k = r & (ny - 1)
        after = (r + 1) & (window - 1)
        before = (r - 1) & (window - 1)
        shift = (LANES - DEPTH * (k + 1)) & (LANES - 1)
        center = [[main[state][c, r, t] for t in range(tiles)] for c in range(COMPS)]
        done = []
        for t in range(tiles):
            h = []
            for c in range(COMPS):
                cells = center[c][t]
                ends = pltpu.roll(seam[state][c, g, t], shift, 1)
                s = jnp.where(first_lane, ends, pltpu.roll(cells, 1, 1))
                s = s + jnp.where(last_lane, ends, pltpu.roll(cells, LANES - 1, 1))
                s = s + (main[state][c, after, t] + main[state][c, before, t])
                h.append(s + around_z(center[c], t))
            m = [center[c][t] for c in range(COMPS)]
            rate = turn(m, h, par[0, r, t], par[1, r, t], par[2, r, t])
            if state == 0:
                new = [m[c] + rate[c] for c in range(COMPS)]
            else:
                new = normal([main[0][c, r, t] + (m[c] + rate[c]) for c in range(COMPS)])
            done.append((r, t, new, ends_of(k, m)))
        return done

    def strip_rows(state):
        done = []
        for g in range(2):
            for side in range(2):
                start = block == side
                stop = block == (side + ny - 1) % ny
                center = [[strip[state][c, side, g, t] for t in range(tiles)] for c in range(COMPS)]
                for t in range(tiles):
                    h = []
                    for c in range(COMPS):
                        cells = center[c][t]
                        inner = edge[c, g, t]
                        other = strip[state][c, side, 1 - g, t]
                        if side == 0:
                            s = pltpu.roll(cells, 1, 1)
                            s = s + pltpu.roll(jnp.where(head_lane, inner, cells), LANES - 1, 1)
                        else:
                            s = pltpu.roll(jnp.where(tail_lane, inner, cells), 1, 1)
                            s = s + pltpu.roll(cells, LANES - 1, 1)
                        s = s + pltpu.roll(jnp.where(start, other, cells), LANES - DEPTH, 1)
                        s = s + pltpu.roll(jnp.where(stop, other, cells), DEPTH, 1)
                        h.append(s + around_z(center[c], t))
                    m = [center[c][t] for c in range(COMPS)]
                    rate = turn(
                        m, h, spar[0, side, g, t], spar[1, side, g, t], spar[2, side, g, t]
                    )
                    if state == 0:
                        new = [m[c] + rate[c] for c in range(COMPS)]
                    else:
                        new = normal(
                            [strip[0][c, side, g, t] + (m[c] + rate[c]) for c in range(COMPS)]
                        )
                    done.append((side, g, t, new))
        for side, g, t, new in done:
            for c in range(COMPS):
                strip[1 - state][c, side, g, t] = new[c]
        for g in range(2):
            for t in range(tiles):
                left, right = (new for _, h, u, new in done if (h, u) == (g, t))
                for c in range(COMPS):
                    seam[1 - state][c, g, t] = seam_of(left[c], right[c])

    def main_rows(state, first, count):
        def rows(i, carry):
            done = []
            for u in range(ROWS):
                done += main_row(state, (first + ROWS * i + u) & (window - 1))
            for r, t, new, ends in done:
                k = r & (ny - 1)
                mask = ((lane - (DEPTH * k + DEPTH - 1)) & (LANES - 1)) < 2
                for c in range(COMPS):
                    main[1 - state][c, r, t] = new[c]
                    pltpu.store(edge.at[c, r // ny, t], ends[c], mask=mask)
            return carry

        lax.fori_loop(0, (count + ROWS - 1) // ROWS, rows, 0)

    def step(i, carry):
        for state in range(2):
            margin = DEPTH - 1 - state - 2 * i
            main_rows(state, -margin, ny + 2 * margin)
            strip_rows(state)
        return carry

    lax.fori_loop(0, STEPS, step, 0)

    def hand_out(i, carry):
        for k in [8 * i + u for u in range(8)]:
            for t in range(tiles):
                for c in range(COMPS):
                    out_ref[c, rows_at(ny, tiles, k, t), :] = main0[c, k, t]
        return carry

    lax.fori_loop(0, ny // 8, hand_out, 0)


def shifted(cells, axis, step, closed):
    count = lax.axis_size(axis)
    pairs = [(i, (i + step) % count) for i in range(count) if closed or 0 <= i + step < count]
    return lax.ppermute(cells, axis, pairs)


def swapped(cells, axis, first, closed):
    count = lax.axis_size(axis)
    pairs = [(i, (i + 1) % count) for i in range(first, count if closed else count - 1, 2)]
    return lax.ppermute(cells, axis, pairs + [(j, i) for i, j in pairs])


def around(cells, dim):
    ny = cells.shape[dim]
    if lax.axis_size("gy") == 2:
        return shifted(cells, "gy", 1, True)
    head = lax.slice_in_dim(cells, 0, DEPTH, axis=dim)
    tail = lax.slice_in_dim(cells, ny - DEPTH, ny, axis=dim)
    return jnp.concatenate([shifted(head, "gy", -1, True), shifted(tail, "gy", 1, True)], axis=dim)


def around_strips(both):
    if lax.axis_size("gy") == 2:
        return shifted(both, "gy", 1, True)
    block = lax.broadcasted_iota(jnp.int32, both.shape, both.ndim - 1) // DEPTH
    side = lax.broadcasted_iota(jnp.int32, both.shape, 0)
    head = (block + side - 1) % (LANES // DEPTH) < DEPTH
    return jnp.where(head, shifted(both, "gy", -1, True), shifted(both, "gy", 1, True))


def body(magnetization, lower_image, image_weights, regions, anisotropy, damping):
    local, comps, nz, ny, nx = magnetization.shape
    images = local * lax.axis_size("img")
    tiles = nz // SUB
    devices = lax.axis_size(("img", "gx", "gy"))
    assert lax.axis_size("gx") % 2 == 0
    assert local == 1 and comps == COMPS and nx == LANES
    assert ny == 2 * DEPTH and ny * DEPTH == LANES and tiles >= 2
    flat = (comps, nz * ny, nx)
    own = magnetization[0]
    own_p = around(own, 2)
    first = swapped(own, "img", 0, False)
    second = swapped(own, "img", 1, False)

    smem = pl.BlockSpec(memory_space=pltpu.SMEM)
    vmem = pl.BlockSpec(memory_space=pltpu.VMEM)
    f32 = jnp.float32
    limit = pltpu.CompilerParams(vmem_limit_bytes=32 * 1024 * 1024)
    vreg = (SUB, LANES)
    packed = jax.ShapeDtypeStruct((comps + 1, tiles) + vreg, f32)
    own_one, own_two, info = pl.pallas_call(
        functools.partial(pack_kernel, ny, tiles, anisotropy.shape[0]),
        out_shape=(packed, packed, jax.ShapeDtypeStruct((5,) + vreg, f32)),
        in_specs=[smem] * 3 + [vmem] * 3,
        out_specs=(vmem,) * 3,
        compiler_params=limit,
        name="pack_strips",
    )(
        lower_image,
        anisotropy,
        damping,
        image_weights.reshape(1, -1),
        own.reshape(flat),
        regions.reshape(flat[1:]),
    )
    own_one = swapped(own_one, "gx", 0, True)
    own_two = swapped(own_two, "gx", 1, True)
    late_regions, info = lax.optimization_barrier((regions, info))
    reg_p = around(late_regions, 1)
    info, own_p, reg_p, own_one, own_two = lax.optimization_barrier((info, own_p, reg_p, own_one, own_two))
    packed = jax.ShapeDtypeStruct((comps, tiles) + vreg, f32)
    part, near, one, two = pl.pallas_call(
        functools.partial(gather_kernel, ny, tiles),
        out_shape=(
            jax.ShapeDtypeStruct((devices, LANES), f32),
            jax.ShapeDtypeStruct(flat, f32),
            packed,
            packed,
        ),
        in_specs=[vmem] * 4,
        out_specs=(vmem,) * 4,
        compiler_params=limit,
        name="gather_images",
    )(info, own.reshape(flat), first.reshape(flat), second.reshape(flat))
    near_p = around(near.reshape(own.shape), 2)
    one = swapped(one, "gx", 0, True)
    two = swapped(two, "gx", 1, True)
    window = ny + 2 * DEPTH
    par = pl.pallas_call(
        functools.partial(look_up_kernel, ny, tiles),
        out_shape=jax.ShapeDtypeStruct((3, window, tiles) + vreg, f32),
        in_specs=[vmem] * 3,
        out_specs=vmem,
        compiler_params=limit,
        name="parameters",
    )(info, regions.reshape(flat[1:]), reg_p.reshape(flat[1:]))
    one, par = lax.optimization_barrier((one, par))
    strips = pl.pallas_call(
        merge_kernel,
        out_shape=jax.ShapeDtypeStruct((2, 2 * comps + 1, tiles) + vreg, f32),
        in_specs=[vmem] * 4,
        out_specs=vmem,
        compiler_params=limit,
        name="merge_strips",
    )(one, two, own_one, own_two)
    strips_p = around_strips(strips)
    squares = lax.all_to_all(part, ("img", "gx", "gy"), 0, 0, tiled=True)

    out = pl.pallas_call(
        functools.partial(evolve_kernel, ny, tiles, images),
        out_shape=jax.ShapeDtypeStruct(flat, f32),
        in_specs=[vmem] * 9,
        out_specs=vmem,
        scratch_shapes=[
            pltpu.VMEM((comps, window, tiles) + vreg, f32),
            pltpu.VMEM((comps, window, tiles) + vreg, f32),
            pltpu.VMEM((comps, 2, 2, tiles) + vreg, f32),
            pltpu.VMEM((comps, 2, 2, tiles) + vreg, f32),
            pltpu.VMEM((comps, 2, tiles) + vreg, f32),
            pltpu.VMEM((comps, 2, tiles) + vreg, f32),
            pltpu.VMEM((comps, 2, tiles) + vreg, f32),
            pltpu.VMEM((3, 2, 2, tiles) + vreg, f32),
        ],
        compiler_params=limit,
        name="evolve",
    )(
        info,
        squares,
        own.reshape(flat),
        own_p.reshape(flat),
        near,
        near_p.reshape(flat),
        par,
        strips,
        strips_p,
    )
    return out.reshape(magnetization.shape)


def solution(mesh):
    placed = (P("img", None, None, "gy", "gx"), P(), P(), P(None, "gy", "gx"), P(), P())
    return jax.shard_map(
        body,
        mesh=mesh,
        in_specs=placed,
        out_specs=P("img", None, None, "gy", "gx"),
        check_vma=False,
    )
```

```python
import functools

import jax
import jax.numpy as jnp
from jax import lax
from jax.experimental import pallas as pl
from jax.experimental.pallas import tpu as pltpu
from jax.sharding import PartitionSpec as P

STEPS = 4
DEPTH = 2 * STEPS

eps = 1e-06
time_step = 0.05

SUB = 8
LANES = 128
COMPS = 3
ROWS = 10


def lane_iota():
    return lax.broadcasted_iota(jnp.int32, (SUB, LANES), 1)


def sub_iota():
    return lax.broadcasted_iota(jnp.int32, (SUB, LANES), 0)


def rows_at(ny, tiles, y, t):
    return pl.ds(y + ny * t, SUB, stride=ny * tiles)


def is_turned():
    return (lax.axis_index("gx") & 1) == 1


def rims(ny, y):
    block = lane_iota() // DEPTH
    turned = is_turned()
    after = (y + 1) & (ny - 1)
    return block == jnp.where(turned, after, y), block == jnp.where(turned, y, after), (DEPTH * (y + 1)) & (LANES - 1)


def pack_kernel(
    ny, tiles, regions, lower_ref, aniso_ref, damp_ref, share_ref, m_ref, reg_ref, one_ref, two_ref, info_ref
):
    here = lax.axis_index("img")
    lane = lane_iota()
    def pack(i, carry):
        done = []
        for u in range(2):
            y = 2 * i + u
            one, two, shift = rims(ny, y)
            for t in range(tiles):
                rows = rows_at(ny, tiles, y, t)
                for c in range(COMPS + 1):
                    cells = m_ref[c, rows, :] if c < COMPS else reg_ref[rows, :].astype(jnp.float32)
                    done.append((c, t, one, two, pltpu.roll(cells, shift, 1)))
        for c, t, one, two, cells in done:
            pltpu.store(one_ref.at[c, t], cells, mask=one)
            pltpu.store(two_ref.at[c, t], cells, mask=two)
        return carry

    table_a = jnp.zeros((SUB, LANES), jnp.float32)
    table_d = jnp.zeros((SUB, LANES), jnp.float32)
    for i in range(regions):
        table_a = jnp.where(lane == i, 2.0 * aniso_ref[i], table_a)
        table_d = jnp.where(lane == i, damp_ref[i], table_d)
    info_ref[0] = table_a
    info_ref[1] = table_d
    info_ref[2] = -time_step / (1.0 + table_d * table_d)
    share = share_ref[...]
    spot = lax.broadcasted_iota(jnp.int32, share.shape, 1)
    target = jnp.sum(jnp.where(spot < here, share, 0.0), axis=1, keepdims=True) / jnp.sum(
        share, axis=1, keepdims=True
    )
    info_ref[3] = jnp.broadcast_to(target, (SUB, LANES))
    info_ref[4] = jnp.full((SUB, LANES), lower_ref[here].astype(jnp.float32))

    lax.fori_loop(0, ny // 2, pack, 0)


def merge_kernel(one_ref, two_ref, own_one_ref, own_two_ref, out_ref):
    turned = is_turned()
    for first, (one_ref, two_ref) in ((0, (one_ref, two_ref)), (COMPS, (own_one_ref, own_two_ref))):
        one, two = one_ref[...], two_ref[...]
        out_ref[0, first : first + one.shape[0]] = jnp.where(turned, one, two)
        out_ref[1, first : first + one.shape[0]] = jnp.where(turned, two, one)


def take_first(info_ref, here):
    odd = (here & 1) == 1
    below = info_ref[4] < here.astype(jnp.float32)
    return jnp.where(below, jnp.where(odd, 1, 0), jnp.where(odd, 0, 1)) == 1, odd


def gather_kernel(
    ny, tiles, info_ref, m_ref, first_ref, second_ref, part_ref, near_ref, one_ref, two_ref
):
    here = lax.axis_index("img")
    pick, odd = take_first(info_ref, here)
    chunks = 16
    depth = m_ref.shape[1]

    def squares(i, sums):
        sums = list(sums)
        done = []
        for u in range(chunks):
            start = pl.multiple_of((chunks * i + u) * SUB, SUB)
            for c in range(COMPS):
                one = first_ref[c, pl.ds(start, SUB), :]
                two = second_ref[c, pl.ds(start, SUB), :]
                done.append((c, start, jnp.where(pick, one, two)))
                diff = m_ref[c, pl.ds(start, SUB), :] - jnp.where(odd, one, two)
                sums[c + COMPS * (u % 4)] = sums[c + COMPS * (u % 4)] + diff * diff
        for c, start, cells in done:
            near_ref[c, pl.ds(start, SUB), :] = cells
        return tuple(sums)

    zero = jnp.zeros((SUB, LANES), jnp.float32)
    sums = lax.fori_loop(0, depth // (chunks * SUB), squares, (zero,) * (4 * COMPS))
    total = jnp.sum(functools.reduce(jnp.add, sums), axis=(0, 1), keepdims=True)
    slot = lax.broadcasted_iota(jnp.int32, part_ref.shape, 1)
    part_ref[...] = jnp.where((slot == here) & (here > 0), total, 0.0)
    def pack(i, carry):
        done = []
        for u in range(8):
            y = 8 * i + u
            one, two, shift = rims(ny, y)
            for t in range(tiles):
                for c in range(COMPS):
                    cells = pltpu.roll(near_ref[c, rows_at(ny, tiles, y, t), :], shift, 1)
                    done.append((c, t, one, two, cells))
        for c, t, one, two, cells in done:
            pltpu.store(one_ref.at[c, t], cells, mask=one)
            pltpu.store(two_ref.at[c, t], cells, mask=two)
        return carry

    lax.fori_loop(0, ny // 8, pack, 0)


def turn(m, h, a2, b, sc):
    mx, my, mz = m
    hx, hy, hz = h
    hz = hz + a2 * mz
    gx = hx + b * (my * hz - mz * hy)
    gy = hy + b * (mz * hx - mx * hz)
    gz = hz + b * (mx * hy - my * hx)
    return (
        sc * (my * gz - mz * gy),
        sc * (mz * gx - mx * gz),
        sc * (mx * gy - my * gx),
    )


def normal(v):
    scale = lax.rsqrt(v[0] * v[0] + v[1] * v[1] + v[2] * v[2])
    return tuple(x * scale for x in v)


def look_up(info_ref, region):
    return [jnp.take_along_axis(info_ref[i], region, axis=1) for i in range(3)]


def look_up_kernel(ny, tiles, info_ref, reg_ref, regp_ref, par_ref):
    def fill(i, carry):
        done = []
        for k in (2 * i, 2 * i + 1):
            for g, reg in enumerate((reg_ref, regp_ref)):
                for t in range(tiles):
                    done.append((g * ny + k, t, look_up(info_ref, reg[rows_at(ny, tiles, k, t), :])))
        for r, t, p in done:
            for i in range(3):
                par_ref[i, r, t] = p[i]
        return carry

    lax.fori_loop(0, ny // 2, fill, 0)


def evolve_kernel(
    ny,
    tiles,
    images,
    info_ref,
    sq_ref,
    m_ref,
    mp_ref,
    n_ref,
    np_ref,
    par,
    strips_ref,
    stripsp_ref,
    out_ref,
    main0,
    main1,
    strip0,
    strip1,
    edge,
    seam0,
    seam1,
    spar,
):
    main, strip, seam = (main0, main1), (strip0, strip1), (seam0, seam1)
    window = ny + 2 * DEPTH
    here = lax.axis_index("img")
    lane = lane_iota()
    sub = sub_iota()
    block = lane // DEPTH
    first_lane = lane == 0
    last_lane = lane == LANES - 1
    head_lane = lane % DEPTH == 0
    tail_lane = lane % DEPTH == DEPTH - 1
    top = sub == SUB - 1
    bottom = sub == 0

    lo = info_ref[4]
    slot = lane.astype(jnp.float32)
    squares = jnp.broadcast_to(jnp.sum(sq_ref[...], axis=0, keepdims=True), (SUB, LANES))
    lengths = jnp.where((lane >= 1) & (lane < images), jnp.sqrt(squares + eps), 0.0)
    total = jnp.sum(lengths, axis=1, keepdims=True)
    arc = jnp.sum(jnp.where(slot <= lo, lengths, 0.0), axis=1, keepdims=True)
    gap = jnp.sum(jnp.where(slot == lo + 1.0, lengths, 0.0), axis=1, keepdims=True)
    weight = jnp.clip((info_ref[3] * total - arc) / gap, -0.5, 1.5)
    below = lo < here.astype(jnp.float32)
    w_own = jnp.where(below, weight, 1.0 - weight)
    w_near = jnp.where(below, 1.0 - weight, weight)

    def ends_of(k, new):
        shift = (DEPTH * (k + 1)) & (LANES - 1)
        return [pltpu.roll(new[c], shift, 1) for c in range(COMPS)]

    def fill(i, carry):
        done = []
        for k in [4 * i + u for u in range(4)]:
            for g, (own, near) in enumerate(((m_ref, n_ref), (mp_ref, np_ref))):
                for t in range(tiles):
                    rows = rows_at(ny, tiles, k, t)
                    v = normal(
                        [w_own * own[c, rows, :] + w_near * near[c, rows, :] for c in range(COMPS)]
                    )
                    done.append((g * ny + k, t, v))
        for r, t, v in done:
            for c in range(COMPS):
                main0[c, r, t] = v[c]
        return carry

    lax.fori_loop(0, ny // 4, fill, 0)

    def seam_of(left, right):
        return jnp.where(head_lane, pltpu.roll(left, 1, 1), pltpu.roll(right, LANES - 1, 1))

    def fill_strips(t, carry):
        done = []
        for g, cells in enumerate((strips_ref, stripsp_ref)):
            for side in range(2):
                v = normal(
                    [w_own * cells[side, COMPS + c, t] + w_near * cells[side, c, t] for c in range(COMPS)]
                )
                done.append((side, g, v, look_up(info_ref, cells[side, 2 * COMPS, t].astype(jnp.int32))))
        for side, g, v, p in done:
            for c in range(COMPS):
                strip0[c, side, g, t] = v[c]
            for i in range(3):
                spar[i, side, g, t] = p[i]
        for g in range(2):
            left, right = (v for _, h, v, _ in done if h == g)
            for c in range(COMPS):
                seam0[c, g, t] = seam_of(left[c], right[c])
        return carry

    lax.fori_loop(0, tiles, fill_strips, 0)

    def around_z(cells, t):
        if t + 1 < tiles:
            above = cells[t + 1]
        else:
            above = jnp.where(top, 0.0, pltpu.roll(cells[0], SUB - 1, 0))
        if t > 0:
            under = cells[t - 1]
        else:
            under = jnp.where(bottom, 0.0, pltpu.roll(cells[tiles - 1], 1, 0))
        return above + under

    def main_row(state, r):
        g = r // ny
        k = r & (ny - 1)
        after = (r + 1) & (window - 1)
        before = (r - 1) & (window - 1)
        shift = (LANES - DEPTH * (k + 1)) & (LANES - 1)
        center = [[main[state][c, r, t] for t in range(tiles)] for c in range(COMPS)]
        done = []
        for t in range(tiles):
            h = []
            for c in range(COMPS):
                cells = center[c][t]
                ends = pltpu.roll(seam[state][c, g, t], shift, 1)
                s = jnp.where(first_lane, ends, pltpu.roll(cells, 1, 1))
                s = s + jnp.where(last_lane, ends, pltpu.roll(cells, LANES - 1, 1))
                s = s + (main[state][c, after, t] + main[state][c, before, t])
                h.append(s + around_z(center[c], t))
            m = [center[c][t] for c in range(COMPS)]
            rate = turn(m, h, par[0, r, t], par[1, r, t], par[2, r, t])
            if state == 0:
                new = [m[c] + rate[c] for c in range(COMPS)]
            else:
                new = normal([main[0][c, r, t] + (m[c] + rate[c]) for c in range(COMPS)])
            done.append((r, t, new, ends_of(k, m)))
        return done

    def strip_rows(state):
        done = []
        for g in range(2):
            for side in range(2):
                start = block == side
                stop = block == (side + ny - 1) % ny
                center = [[strip[state][c, side, g, t] for t in range(tiles)] for c in range(COMPS)]
                for t in range(tiles):
                    h = []
                    for c in range(COMPS):
                        cells = center[c][t]
                        inner = edge[c, g, t]
                        other = strip[state][c, side, 1 - g, t]
                        if side == 0:
                            s = pltpu.roll(cells, 1, 1)
                            s = s + pltpu.roll(jnp.where(head_lane, inner, cells), LANES - 1, 1)
                        else:
                            s = pltpu.roll(jnp.where(tail_lane, inner, cells), 1, 1)
                            s = s + pltpu.roll(cells, LANES - 1, 1)
                        s = s + pltpu.roll(jnp.where(start, other, cells), LANES - DEPTH, 1)
                        s = s + pltpu.roll(jnp.where(stop, other, cells), DEPTH, 1)
                        h.append(s + around_z(center[c], t))
                    m = [center[c][t] for c in range(COMPS)]
                    rate = turn(
                        m, h, spar[0, side, g, t], spar[1, side, g, t], spar[2, side, g, t]
                    )
                    if state == 0:
                        new = [m[c] + rate[c] for c in range(COMPS)]
                    else:
                        new = normal(
                            [strip[0][c, side, g, t] + (m[c] + rate[c]) for c in range(COMPS)]
                        )
                    done.append((side, g, t, new))
        for side, g, t, new in done:
            for c in range(COMPS):
                strip[1 - state][c, side, g, t] = new[c]
        for g in range(2):
            for t in range(tiles):
                left, right = (new for _, h, u, new in done if (h, u) == (g, t))
                for c in range(COMPS):
                    seam[1 - state][c, g, t] = seam_of(left[c], right[c])

    def main_rows(state, first, count):
        def rows(i, carry):
            done = []
            for u in range(ROWS):
                done += main_row(state, (first + ROWS * i + u) & (window - 1))
            for r, t, new, ends in done:
                k = r & (ny - 1)
                mask = ((lane - (DEPTH * k + DEPTH - 1)) & (LANES - 1)) < 2
                for c in range(COMPS):
                    main[1 - state][c, r, t] = new[c]
                    pltpu.store(edge.at[c, r // ny, t], ends[c], mask=mask)
            return carry

        lax.fori_loop(0, (count + ROWS - 1) // ROWS, rows, 0)

    def step(i, carry):
        for state in range(2):
            margin = DEPTH - 1 - state - 2 * i
            main_rows(state, -margin, ny + 2 * margin)
            strip_rows(state)
        return carry

    lax.fori_loop(0, STEPS, step, 0)

    def hand_out(i, carry):
        for k in (2 * i, 2 * i + 1):
            for t in range(tiles):
                for c in range(COMPS):
                    out_ref[c, rows_at(ny, tiles, k, t), :] = main0[c, k, t]
        return carry

    lax.fori_loop(0, ny // 2, hand_out, 0)


def shifted(cells, axis, step, closed):
    count = lax.axis_size(axis)
    pairs = [(i, (i + step) % count) for i in range(count) if closed or 0 <= i + step < count]
    return lax.ppermute(cells, axis, pairs)


def swapped(cells, axis, first, closed):
    count = lax.axis_size(axis)
    pairs = [(i, (i + 1) % count) for i in range(first, count if closed else count - 1, 2)]
    return lax.ppermute(cells, axis, pairs + [(j, i) for i, j in pairs])


def around(cells, dim):
    ny = cells.shape[dim]
    if lax.axis_size("gy") == 2:
        return shifted(cells, "gy", 1, True)
    head = lax.slice_in_dim(cells, 0, DEPTH, axis=dim)
    tail = lax.slice_in_dim(cells, ny - DEPTH, ny, axis=dim)
    return jnp.concatenate([shifted(head, "gy", -1, True), shifted(tail, "gy", 1, True)], axis=dim)


def around_strips(both):
    if lax.axis_size("gy") == 2:
        return shifted(both, "gy", 1, True)
    block = lax.broadcasted_iota(jnp.int32, both.shape, both.ndim - 1) // DEPTH
    side = lax.broadcasted_iota(jnp.int32, both.shape, 0)
    head = (block + side - 1) % (LANES // DEPTH) < DEPTH
    return jnp.where(head, shifted(both, "gy", -1, True), shifted(both, "gy", 1, True))


def body(magnetization, lower_image, image_weights, regions, anisotropy, damping):
    local, comps, nz, ny, nx = magnetization.shape
    images = local * lax.axis_size("img")
    tiles = nz // SUB
    devices = lax.axis_size(("img", "gx", "gy"))
    assert lax.axis_size("gx") % 2 == 0
    assert local == 1 and comps == COMPS and nx == LANES
    assert ny == 2 * DEPTH and ny * DEPTH == LANES and tiles >= 2
    flat = (comps, nz * ny, nx)
    own = magnetization[0]
    own_p = around(own, 2)
    first = swapped(own, "img", 0, False)
    second = swapped(own, "img", 1, False)

    smem = pl.BlockSpec(memory_space=pltpu.SMEM)
    vmem = pl.BlockSpec(memory_space=pltpu.VMEM)
    f32 = jnp.float32
    limit = pltpu.CompilerParams(vmem_limit_bytes=32 * 1024 * 1024)
    vreg = (SUB, LANES)
    packed = jax.ShapeDtypeStruct((comps + 1, tiles) + vreg, f32)
    own_one, own_two, info = pl.pallas_call(
        functools.partial(pack_kernel, ny, tiles, anisotropy.shape[0]),
        out_shape=(packed, packed, jax.ShapeDtypeStruct((5,) + vreg, f32)),
        in_specs=[smem] * 3 + [vmem] * 3,
        out_specs=(vmem,) * 3,
        compiler_params=limit,
        name="pack_strips",
    )(
        lower_image,
        anisotropy,
        damping,
        image_weights.reshape(1, -1),
        own.reshape(flat),
        regions.reshape(flat[1:]),
    )
    own_one = swapped(own_one, "gx", 0, True)
    own_two = swapped(own_two, "gx", 1, True)
    late_regions, info = lax.optimization_barrier((regions, info))
    reg_p = around(late_regions, 1)
    info, own_p, reg_p, own_one, own_two = lax.optimization_barrier((info, own_p, reg_p, own_one, own_two))
    packed = jax.ShapeDtypeStruct((comps, tiles) + vreg, f32)
    part, near, one, two = pl.pallas_call(
        functools.partial(gather_kernel, ny, tiles),
        out_shape=(
            jax.ShapeDtypeStruct((devices, LANES), f32),
            jax.ShapeDtypeStruct(flat, f32),
            packed,
            packed,
        ),
        in_specs=[vmem] * 4,
        out_specs=(vmem,) * 4,
        compiler_params=limit,
        name="gather_images",
    )(info, own.reshape(flat), first.reshape(flat), second.reshape(flat))
    near_p = around(near.reshape(own.shape), 2)
    one = swapped(one, "gx", 0, True)
    two = swapped(two, "gx", 1, True)
    window = ny + 2 * DEPTH
    par = pl.pallas_call(
        functools.partial(look_up_kernel, ny, tiles),
        out_shape=jax.ShapeDtypeStruct((3, window, tiles) + vreg, f32),
        in_specs=[vmem] * 3,
        out_specs=vmem,
        compiler_params=limit,
        name="parameters",
    )(info, regions.reshape(flat[1:]), reg_p.reshape(flat[1:]))
    one, par = lax.optimization_barrier((one, par))
    strips = pl.pallas_call(
        merge_kernel,
        out_shape=jax.ShapeDtypeStruct((2, 2 * comps + 1, tiles) + vreg, f32),
        in_specs=[vmem] * 4,
        out_specs=vmem,
        compiler_params=limit,
        name="merge_strips",
    )(one, two, own_one, own_two)
    strips_p = around_strips(strips)
    squares = lax.all_to_all(part, ("img", "gx", "gy"), 0, 0, tiled=True)

    out = pl.pallas_call(
        functools.partial(evolve_kernel, ny, tiles, images),
        out_shape=jax.ShapeDtypeStruct(flat, f32),
        in_specs=[vmem] * 9,
        out_specs=vmem,
        scratch_shapes=[
            pltpu.VMEM((comps, window, tiles) + vreg, f32),
            pltpu.VMEM((comps, window, tiles) + vreg, f32),
            pltpu.VMEM((comps, 2, 2, tiles) + vreg, f32),
            pltpu.VMEM((comps, 2, 2, tiles) + vreg, f32),
            pltpu.VMEM((comps, 2, tiles) + vreg, f32),
            pltpu.VMEM((comps, 2, tiles) + vreg, f32),
            pltpu.VMEM((comps, 2, tiles) + vreg, f32),
            pltpu.VMEM((3, 2, 2, tiles) + vreg, f32),
        ],
        compiler_params=limit,
        name="evolve",
    )(
        info,
        squares,
        own.reshape(flat),
        own_p.reshape(flat),
        near,
        near_p.reshape(flat),
        par,
        strips,
        strips_p,
    )
    return out.reshape(magnetization.shape)


def solution(mesh):
    placed = (P("img", None, None, "gy", "gx"), P(), P(), P(None, "gy", "gx"), P(), P())
    return jax.shard_map(
        body,
        mesh=mesh,
        in_specs=placed,
        out_specs=P("img", None, None, "gy", "gx"),
        check_vma=False,
    )
```
